32 devices in a mesh: patch: 4 (over y, x), shot: 8 (over z, core).
Axes of the slice: x: 2, y: 2, z: 4, core: 2. Of those that a mesh axis runs over, the one named last changes fastest.
Arguments:
- estimate: bfloat16 [256, 512, 1024], P('shot', 'patch'), may hold values from -6 to 6
- observed: bfloat16 [256, 512, 1024], P('shot', 'patch'), may hold values from -6 to 6
- random_source_delays: int32 [256], replicated, may hold values from 0 to 255
- thresholds: float32 [512], replicated, may hold values from 0.5 to 3
Outputs:
- updated: float32 [256, 512, 1024], P('shot', 'patch')
- misfit: float32 [256], P('shot')
The draws below stay inside these ranges and needn't reach their ends.
All inputs are finite; a program needn't handle non-finite values.
Results may differ from the reference program's by a relative error of at most 0.0084.
Values may be sent and summed in bfloat16 or wider, within the bound.
No kernel may reach another device: no remote copies, remote signals or barrier semaphores. Data moves between devices by JAX's collectives and lax.ppermute only.
A program may use at most 256 MiB of HBM per device.

```python
import math
import jax
import jax.numpy as jnp
from jax import lax

S = 256
R = 512
NT = 1024
F = 512
SOURCE_SPACING = 512
JITTER = 256


def plant(drawn, key, smallest, high):
    shape = drawn.shape
    spot = [jax.random.randint(jax.random.fold_in(key, axis), (), 0, shape[axis]) for axis in range(len(shape))]
    drawn = drawn.at[tuple(spot)].set(smallest)
    longest = shape.index(max(shape))
    spot[longest] = (spot[longest] + 1) % shape[longest]
    return drawn.at[tuple(spot)].set(high)


def levels(key, dims, shards, low, high):
    def one(position, blocks):
        steps = jax.random.uniform(jax.random.fold_in(jax.random.fold_in(key, 6), position), (blocks,), jnp.float32, low / len(shards), high / len(shards))
        return jnp.repeat(jnp.exp(steps), dims[position] // blocks).reshape((-1,) + (1,) * (len(dims) - position - 1))

    loudness = one(*shards[0])
    for cut in shards[1:]:
        loudness = loudness * one(*cut)
    return loudness


def bell_draw(own_key, extent, scale, reach, split=(), held_as=jnp.bfloat16):
    entries = jax.random.normal(own_key, extent, jnp.float32) * scale
    if len(split) > 0:
        entries = levels(own_key, extent, split, -0.22, 0.18) * entries
    return jnp.clip(entries, min=-reach, max=reach).astype(held_as)


def setup_inputs(seed: int = 0) -> dict:
    key_of = jax.random.split(jax.random.key(seed), 5)
    estimate = bell_draw(key_of[0], (S, R, NT), 1.0, 6.0, ((0, 8), (1, 4)))
    observed = bell_draw(key_of[1], (S, R, NT), 1.0, 6.0, ((0, 8), (1, 4)))
    random_source_delays = plant(jax.random.randint(key_of[2], (S,), 0, JITTER), jax.random.fold_in(key_of[2], 1), 0, JITTER - 1).astype(jnp.int32)
    thresholds = jnp.clip(jnp.exp(jax.random.uniform(key_of[3], (F,), jnp.float32, math.log(0.5), math.log(3.0))), 0.5, 3.0)
    return {"estimate": estimate, "observed": observed, "random_source_delays": random_source_delays, "thresholds": thresholds}


correction_step_length = 0.5

def delayed(traces, offset):
    length = traces.shape[-1]
    padded = jnp.pad(traces, ((0, 0), (length, length)))
    return lax.dynamic_slice_in_dim(padded, (length - offset).astype(jnp.int32), length, 1)

def combined_data_panel(field, random_source_delays):
    source_panels = field.shape[0]
    source_onset_moments = (jnp.arange(source_panels, dtype=jnp.int32) * SOURCE_SPACING + random_source_delays).astype(jnp.int32)
    padded = jnp.pad(field, ((1, 1), (0, 0), (0, 0)))

    def one_shot(source_position):
        before = lax.dynamic_index_in_dim(padded, source_position, 0, keepdims=False)
        center = lax.dynamic_index_in_dim(padded, source_position + 1, 0, keepdims=False)
        after = lax.dynamic_index_in_dim(padded, source_position + 2, 0, keepdims=False)
        subsequent_source_position = jnp.minimum(source_position + 1, source_panels - 1).astype(jnp.int32)
        prior_source_position = jnp.maximum(source_position - 1, 0).astype(jnp.int32)
        subsequent_source_panel = source_onset_moments[subsequent_source_position] - source_onset_moments[source_position]
        prior_source_panel = source_onset_moments[source_position] - source_onset_moments[prior_source_position]
        return center + delayed(after, subsequent_source_panel) + delayed(before, -prior_source_panel)
    return lax.map(one_shot, jnp.arange(source_panels, dtype=jnp.int32))

def time_tables():
    freq = jnp.arange(F, dtype=jnp.int32)
    sample = jnp.arange(NT, dtype=jnp.int32)
    phase = (freq[:, None] * sample[None, :] % NT).astype(jnp.float32)
    angle = 2.0 * jnp.pi * phase / NT
    root = jnp.sqrt(jnp.float32(NT))
    forward = jnp.stack([jnp.cos(angle) / root, -jnp.sin(angle) / root]).astype(jnp.bfloat16)
    weight = jnp.where(freq == 0, 1.0, 2.0).astype(jnp.float32)[:, None] / root
    inverse = jnp.stack([weight * jnp.cos(angle), -weight * jnp.sin(angle)]).astype(jnp.bfloat16)
    return (forward, inverse)

def shot_tables(source_panels):
    index = jnp.arange(source_panels, dtype=jnp.int32)
    phase = (index[:, None] * index[None, :] % source_panels).astype(jnp.float32)
    angle = 2.0 * jnp.pi * phase / source_panels
    root = jnp.sqrt(jnp.float32(source_panels))
    cosine = jnp.cos(angle) / root
    sine = jnp.sin(angle) / root
    across = jnp.stack([jnp.stack([cosine, sine]), jnp.stack([-sine, cosine])]).astype(jnp.bfloat16)
    back = jnp.stack([jnp.stack([cosine, -sine]), jnp.stack([sine, cosine])]).astype(jnp.bfloat16)
    return (across, back)

def shrink(wavenum, level):
    magnitude = jnp.sqrt(wavenum[0] * wavenum[0] + wavenum[1] * wavenum[1])
    factor = jnp.maximum(magnitude - level, 0.0) / jnp.maximum(magnitude, level)
    return (wavenum * factor[None]).astype(jnp.bfloat16)

def reference(estimate, observed, random_source_delays, thresholds):
    present_gather = estimate.astype(jnp.float32)
    resid = observed.astype(jnp.float32) - combined_data_panel(present_gather, random_source_delays)
    misfit = lax.optimization_barrier(jnp.sum(resid * resid, axis=(1, 2))) / (R * NT)
    advanced_estimate = (present_gather + correction_step_length * combined_data_panel(resid, random_source_delays)).astype(jnp.bfloat16)
    forward, inverse = time_tables()
    spectra = jnp.einsum('srt,pft->pfsr', advanced_estimate.astype(jnp.float32), forward.astype(jnp.float32)).astype(jnp.bfloat16)
    across, back = shot_tables(S)
    wavenum = jnp.einsum('pqks,qfsr->pfkr', across.astype(jnp.float32), spectra.astype(jnp.float32))
    shrunk = shrink(wavenum, thresholds[:, None, None])
    restored = jnp.einsum('pqks,qfsr->pfkr', back.astype(jnp.float32), shrunk.astype(jnp.float32)).astype(jnp.bfloat16)
    updated = jnp.einsum('pft,pfsr->srt', inverse.astype(jnp.float32), restored.astype(jnp.float32))
    return (updated, misfit)
```

```python
import functools

import jax
import jax.numpy as jnp
import ml_dtypes
import numpy as np
from jax import lax
from jax.experimental import pallas as pl
from jax.experimental.pallas import tpu as pltpu
from jax.sharding import PartitionSpec as P

F = 512
SOURCE_SPACING = 512
JITTER = 256
STEP = 0.5
LANES = 128
NEAR = SOURCE_SPACING - JITTER
FAR = SOURCE_SPACING + JITTER
HALO = 3


def time_tables(samples, blocks):
    freq = np.arange(F, dtype=np.int32)
    sample = np.arange(samples, dtype=np.int32)
    phase = (freq[:, None] * sample[None, :] % samples).astype(np.float32)
    angle = np.float32(2.0 * np.pi) * phase / np.float32(samples)
    root = np.sqrt(np.float32(samples))
    weight = np.where(freq == 0, 1.0, 2.0).astype(np.float32)[:, None] / root
    forward = np.stack([np.cos(angle) / root, -np.sin(angle) / root])
    inverse = np.stack([weight * np.cos(angle), -weight * np.sin(angle)])

    def ordered(table):
        table = table.astype(np.float32).astype(ml_dtypes.bfloat16)
        table = table.reshape(2, blocks, F // blocks, samples).transpose(1, 0, 2, 3)
        return table.reshape(2 * F, samples)

    return np.ascontiguousarray(ordered(forward).T), ordered(inverse)


def shot_table(shots):
    index = np.arange(shots, dtype=np.int32)
    phase = (index[:, None] * index[None, :] % shots).astype(np.float32)
    angle = np.float32(2.0 * np.pi) * phase / np.float32(shots)
    root = np.sqrt(np.float32(shots))
    table = np.concatenate([np.cos(angle) / root, np.sin(angle) / root])
    return table.astype(np.float32).astype(ml_dtypes.bfloat16)


def blend_into(
    first_ref, delay_ref, est_ref, obs_ref, before_ref, after_ref, energy_ref, est32, res32, store
):
    shots, rows, samples = est_ref.shape
    columns = samples // LANES
    margin = (FAR - NEAR) // LANES
    inner = (samples - NEAR) // LANES
    skip = NEAR // LANES
    total = delay_ref.shape[0]
    first = first_ref[0]
    lane = lax.broadcasted_iota(jnp.int32, (1, rows, LANES), 2)

    def ahead(shot):
        shot = jnp.clip(shot, 0, total - 2)
        return jnp.clip(SOURCE_SPACING + delay_ref[shot + 1] - delay_ref[shot], NEAR + 1, FAR - 1)

    def window(field, slot, start):
        column, rest = start // LANES, start % LANES
        wide = field[slot, pl.ds(column, inner + 1)]
        turned = pltpu.roll(
            wide.reshape((inner + 1) * rows, LANES), (LANES - rest) % LANES, 1
        ).reshape(inner + 1, rows, LANES)
        return jnp.where(lane < LANES - rest, turned[:-1], turned[1:])

    def blended(field, slot, shot):
        later = window(field, slot + 1, margin * LANES + NEAR - ahead(shot))
        earlier = window(field, slot - 1, margin * LANES + ahead(shot - 1))
        return later, earlier

    def fill(field, slot, values):
        blank = jnp.zeros((margin, rows, LANES), jnp.float32)
        field[slot, pl.ds(0, margin)] = blank
        field[slot, pl.ds(margin + columns, margin)] = blank
        for column in range(columns):
            field[slot, margin + column] = values(column)

    def cut(ref, shot):
        return lambda column: ref[shot, :, column * LANES : (column + 1) * LANES].astype(jnp.float32)

    for slot in range(2):
        fill(est32, slot, cut(before_ref, slot))
        fill(est32, shots + 2 + slot, cut(after_ref, slot))

    def load(shot, carry):
        fill(est32, shot + 2, cut(est_ref, shot))
        return carry

    lax.fori_loop(0, shots, load, 0)

    def residual(place, values):
        shot = first + place - 1
        inside = jnp.logical_and(shot >= 0, shot < total)
        later, earlier = blended(est32, place + 1, shot)
        power = jnp.zeros((rows, LANES), jnp.float32)
        cells = []
        for column in range(columns):
            cell = est32[place + 1, margin + column]
            if column >= skip:
                cell = cell + later[column - skip]
            if column < inner:
                cell = cell + earlier[column]
            cell = jnp.where(inside, values(column) - cell, 0.0)
            power = power + cell * cell
            cells.append(cell)
        fill(res32, place, lambda column: cells[column])
        return power

    residual(0, cut(before_ref, 2))
    residual(shots + 1, cut(after_ref, 2))

    def middle(shot, carry):
        power = residual(shot + 1, cut(obs_ref, shot))
        energy_ref[pl.ds(shot, 1), :] = jnp.sum(power, axis=0, keepdims=True)
        return carry

    lax.fori_loop(0, shots, middle, 0)

    def step(shot, carry):
        later, earlier = blended(res32, shot + 1, first + shot)
        for column in range(columns):
            cell = res32[shot + 1, margin + column]
            if column >= skip:
                cell = cell + later[column - skip]
            if column < inner:
                cell = cell + earlier[column]
            cell = est32[shot + 2, margin + column] + STEP * cell
            store(shot, column, cell.astype(jnp.bfloat16))
        return carry

    lax.fori_loop(0, shots, step, 0)


def spectra_kernel(
    first_ref, delay_ref, est_ref, obs_ref, before_ref, after_ref, table_ref, out_ref, energy_ref,
    est32, res32, stepped,
):
    shots, rows, samples = est_ref.shape
    blocks, _, _, width = out_ref.shape

    def store(shot, column, values):
        start = pl.multiple_of(shot * rows, rows)
        stepped[pl.ds(start, rows), column * LANES : (column + 1) * LANES] = values

    blend_into(
        first_ref, delay_ref, est_ref, obs_ref, before_ref, after_ref, energy_ref, est32, res32, store
    )
    group = min(shots, max(1, 256 // rows))

    def transform(part, carry):
        start = pl.multiple_of(part * (group * rows), group * rows)
        result = jnp.dot(
            stepped[pl.ds(start, group * rows), :], table_ref[...], preferred_element_type=jnp.float32
        ).astype(jnp.bfloat16)
        for block in range(blocks):
            out_ref[block, pl.ds(part * group, group)] = result[
                :, block * width : (block + 1) * width
            ].reshape(group, rows, width)
        return carry

    lax.fori_loop(0, shots // group, transform, 0)


def step_kernel(
    first_ref, delay_ref, est_ref, obs_ref, before_ref, after_ref, out_ref, energy_ref, est32, res32
):
    def store(shot, column, values):
        out_ref[shot, :, column * LANES : (column + 1) * LANES] = values

    blend_into(
        first_ref, delay_ref, est_ref, obs_ref, before_ref, after_ref, energy_ref, est32, res32, store
    )


def shots_kernel(spectra_ref, table_ref, level_ref, out_ref, wide, back):
    blocks, held, rows, width = spectra_ref.shape
    shots = blocks * held
    half = width // 2
    wide[...] = spectra_ref[...].reshape(shots * rows, width).astype(jnp.float32)
    level = level_ref[...]
    sign = jnp.where(
        lax.broadcasted_iota(jnp.int32, (1, width), 1) < half, jnp.float32(1.0), jnp.float32(-1.0)
    )

    def pair(index, carry):
        picks = [pl.ds(index * 2 + turn, shots, stride=rows) for turn in range(2)]
        block = jnp.concatenate([wide[pick, :] for pick in picks], axis=1).astype(jnp.bfloat16)
        both = jnp.dot(table_ref[...], block, preferred_element_type=jnp.float32)
        kept = []
        for turn in range(2):
            own = both[:, turn * width : (turn + 1) * width]
            wave = own[:shots] + sign * pltpu.roll(own[shots:], half, 1)
            power = wave * wave
            power = power + pltpu.roll(power, half, 1)
            factor = jnp.maximum(1.0 - level * lax.rsqrt(power), 0.0)
            kept.append((wave * factor).astype(jnp.bfloat16))
        both = jnp.dot(table_ref[...], jnp.concatenate(kept, axis=1), preferred_element_type=jnp.float32)
        for turn in range(2):
            own = both[:, turn * width : (turn + 1) * width]
            back[picks[turn], :] = own[:shots] - sign * pltpu.roll(own[shots:], half, 1)
        return carry

    lax.fori_loop(0, rows // 2, pair, 0)
    out_ref[...] = back[...].astype(jnp.bfloat16).reshape(out_ref.shape)


def update_kernel(*refs):
    restored_ref, table_ref, out_ref = refs[0], refs[1], refs[-1]
    blocks, held, rows, width = restored_ref.shape
    block = jnp.concatenate(
        [restored_ref[index].reshape(held * rows, width) for index in range(blocks)], axis=1
    )
    out_ref[...] = jnp.dot(block, table_ref[...], preferred_element_type=jnp.float32).reshape(out_ref.shape)


def whole(shape):
    return pl.BlockSpec(shape, lambda *_: (0,) * len(shape))


def blend_specs(shots, rows, samples, chunk):
    at = lambda *_: (0, chunk, 0)
    return [
        pl.BlockSpec(memory_space=pltpu.SMEM),
        pl.BlockSpec(memory_space=pltpu.SMEM),
        pl.BlockSpec((shots, rows, samples), at),
        pl.BlockSpec((shots, rows, samples), at),
        pl.BlockSpec((HALO, rows, samples), at),
        pl.BlockSpec((HALO, rows, samples), at),
    ]


def blend_scratch(shots, rows, samples):
    columns = (samples + 2 * (FAR - NEAR)) // LANES
    return [
        pltpu.VMEM((shots + 4, columns, rows, LANES), jnp.float32),
        pltpu.VMEM((shots + 2, columns, rows, LANES), jnp.float32),
    ]


PARAMS = pltpu.CompilerParams(vmem_limit_bytes=48 * 1024 * 1024)


def spectra_of(first, delays, fields, table, rows, chunk, blocks):
    shots, _, samples = fields[0].shape
    width = 2 * F // blocks
    return pl.pallas_call(
        spectra_kernel,
        grid=(1,),
        in_specs=blend_specs(shots, rows, samples, chunk) + [whole(table.shape)],
        out_specs=[whole((blocks, shots, rows, width)), whole((shots, LANES))],
        out_shape=[
            jax.ShapeDtypeStruct((blocks, shots, rows, width), jnp.bfloat16),
            jax.ShapeDtypeStruct((shots, LANES), jnp.float32),
        ],
        scratch_shapes=blend_scratch(shots, rows, samples)
        + [pltpu.VMEM((shots * rows, samples), jnp.bfloat16)],
        compiler_params=PARAMS,
        cost_estimate=pl.CostEstimate(
            flops=4 * F * shots * rows * samples,
            bytes_accessed=3 * 2 * shots * rows * samples + table.size * 2,
            transcendentals=0,
        ),
        name="spectra",
    )(first, delays, *fields, table)


def stepped_of(first, delays, fields, rows, chunk):
    shots, _, samples = fields[0].shape
    return pl.pallas_call(
        step_kernel,
        grid=(1,),
        in_specs=blend_specs(shots, rows, samples, chunk),
        out_specs=[whole((shots, rows, samples)), whole((shots, LANES))],
        out_shape=[
            jax.ShapeDtypeStruct((shots, rows, samples), jnp.bfloat16),
            jax.ShapeDtypeStruct((shots, LANES), jnp.float32),
        ],
        scratch_shapes=blend_scratch(shots, rows, samples),
        compiler_params=PARAMS,
        name="stepped",
    )(first, delays, *fields)


def shrunk_of(spectra, table, level):
    blocks, held, rows, width = spectra.shape
    shots = blocks * held
    return pl.pallas_call(
        shots_kernel,
        grid=(1,),
        in_specs=[whole(spectra.shape), whole(table.shape), whole(level.shape)],
        out_specs=whole(spectra.shape),
        out_shape=jax.ShapeDtypeStruct(spectra.shape, jnp.bfloat16),
        scratch_shapes=[pltpu.VMEM((shots * rows, width), jnp.float32)] * 2,
        compiler_params=PARAMS,
        cost_estimate=pl.CostEstimate(
            flops=8 * shots * shots * rows * width,
            bytes_accessed=2 * 2 * spectra.size + table.size * 2,
            transcendentals=spectra.size,
        ),
        name="shrink",
    )(spectra, table, level)


def updated_of(restored, table, chunk, receivers, onto):
    blocks, shots, rows, width = restored.shape
    samples = table.shape[1]
    group = min(shots, max(1, 256 // rows))
    in_specs = [
        pl.BlockSpec((blocks, group, rows, width), lambda step: (0, step, 0, 0)),
        whole(table.shape),
    ]
    operands = [restored, table]
    if onto is not None:
        in_specs.append(pl.BlockSpec(memory_space=pl.ANY))
        operands.append(onto)
    return pl.pallas_call(
        update_kernel,
        grid=(shots // group,),
        in_specs=in_specs,
        out_specs=pl.BlockSpec((group, rows, samples), lambda step: (step, chunk, 0)),
        out_shape=jax.ShapeDtypeStruct((shots, receivers, samples), jnp.float32),
        input_output_aliases={} if onto is None else {2: 0},
        compiler_params=PARAMS,
        cost_estimate=pl.CostEstimate(
            flops=4 * F * shots * rows * samples,
            bytes_accessed=2 * restored.size + 2 * table.size + 4 * shots * rows * samples,
            transcendentals=0,
        ),
        name="update",
    )(*operands)


def swapped(array):
    return lax.all_to_all(array, "shot", split_axis=0, concat_axis=0, tiled=True)


def spectral_by_einsum(stepped, forward, inverse, table, level, peers):
    shots, receivers, samples = stepped.shape
    total = table.shape[1]
    share = F // peers
    spectra = jnp.einsum(
        "srt,tdpf->dpfsr",
        stepped,
        forward.reshape(samples, peers, 2, share),
        preferred_element_type=jnp.float32,
    ).astype(jnp.bfloat16)
    mixed = swapped(spectra).transpose(1, 2, 0, 3, 4).reshape(2, share, total, receivers)
    cosine, sine = table[:total], table[total:]
    across = jnp.stack([jnp.stack([cosine, sine]), jnp.stack([-sine, cosine])])
    wave = jnp.einsum("pqks,qfsr->pfkr", across, mixed, preferred_element_type=jnp.float32)
    magnitude = jnp.sqrt(wave[0] * wave[0] + wave[1] * wave[1])
    bound = level[:, None, None]
    factor = jnp.maximum(magnitude - bound, 0.0) / jnp.maximum(magnitude, bound)
    shrunk = (wave * factor[None]).astype(jnp.bfloat16)
    back = jnp.stack([jnp.stack([cosine, -sine]), jnp.stack([sine, cosine])])
    restored = jnp.einsum(
        "pqks,qfkr->pfsr", back, shrunk, preferred_element_type=jnp.float32
    ).astype(jnp.bfloat16)
    restored = restored.reshape(2, share, peers, shots, receivers).transpose(2, 0, 1, 3, 4)
    return jnp.einsum(
        "dpft,dpfsr->srt",
        inverse.reshape(peers, 2, share, samples),
        swapped(restored),
        preferred_element_type=jnp.float32,
    )


def local(estimate, observed, random_source_delays, thresholds):
    shots, receivers, samples = estimate.shape
    peers = lax.axis_size("shot")
    rank = lax.axis_index("shot")
    total = random_source_delays.shape[0]
    share = F // peers
    rows = min(16, receivers)
    chunks = receivers // rows
    first = jnp.reshape(rank * shots, (1,)).astype(jnp.int32)
    up = [(i, i + 1) for i in range(peers - 1)]
    down = [(j, i) for i, j in up]
    tail = jnp.concatenate([estimate[shots - 2 :], observed[shots - 1 :]])
    head = jnp.concatenate([estimate[:2], observed[:1]])
    before = lax.ppermute(tail, "shot", up)
    after = lax.ppermute(head, "shot", down)
    fields = (estimate, observed, before, after)
    forward, inverse = (jnp.asarray(table) for table in time_tables(samples, peers))
    table = jnp.asarray(shot_table(total))
    level = lax.dynamic_slice_in_dim(thresholds, rank * share, share)
    energy = 0.0
    if (2 * share) % LANES == 0:
        levels = jnp.tile(level, 2)[None, :]
        updated = None
        for chunk in range(chunks):
            spectra, power = spectra_of(
                first, random_source_delays, fields, forward, rows, chunk, peers
            )
            energy = energy + power
            restored = shrunk_of(swapped(spectra), table, levels)
            updated = updated_of(swapped(restored), inverse, chunk, receivers, updated)
    else:
        parts = []
        for chunk in range(chunks):
            part, power = stepped_of(first, random_source_delays, fields, rows, chunk)
            energy = energy + power
            parts.append(part)
        updated = spectral_by_einsum(
            jnp.concatenate(parts, axis=1), forward, inverse, table, level, peers
        )
    misfit = lax.psum(jnp.sum(energy, axis=1), "patch") / (
        receivers * lax.axis_size("patch") * samples
    )
    return updated, misfit


def solution(mesh):
    in_specs = (P("shot", "patch", None), P("shot", "patch", None), P(), P())
    out_specs = (P("shot", "patch", None), P("shot"))
    return jax.shard_map(local, mesh=mesh, in_specs=in_specs, out_specs=out_specs, check_vma=False)
```

```python
import functools

import jax
import jax.numpy as jnp
import ml_dtypes
import numpy as np
from jax import lax
from jax.experimental import pallas as pl
from jax.experimental.pallas import tpu as pltpu
from jax.sharding import PartitionSpec as P

F = 512
SOURCE_SPACING = 512
JITTER = 256
STEP = 0.5
LANES = 128
NEAR = SOURCE_SPACING - JITTER
FAR = SOURCE_SPACING + JITTER
HALO = 3


def time_tables(samples, blocks):
    freq = np.arange(F, dtype=np.int32)
    sample = np.arange(samples, dtype=np.int32)
    phase = (freq[:, None] * sample[None, :] % samples).astype(np.float32)
    angle = np.float32(2.0 * np.pi) * phase / np.float32(samples)
    root = np.sqrt(np.float32(samples))
    weight = np.where(freq == 0, 1.0, 2.0).astype(np.float32)[:, None] / root
    forward = np.stack([np.cos(angle) / root, -np.sin(angle) / root])
    inverse = np.stack([weight * np.cos(angle), -weight * np.sin(angle)])

    def ordered(table):
        table = table.astype(np.float32).astype(ml_dtypes.bfloat16)
        table = table.reshape(2, blocks, F // blocks, samples).transpose(1, 0, 2, 3)
        return table.reshape(2 * F, samples)

    return np.ascontiguousarray(ordered(forward).T), ordered(inverse)


def shot_table(shots):
    index = np.arange(shots, dtype=np.int32)
    phase = (index[:, None] * index[None, :] % shots).astype(np.float32)
    angle = np.float32(2.0 * np.pi) * phase / np.float32(shots)
    root = np.sqrt(np.float32(shots))
    table = np.concatenate([np.cos(angle) / root, np.sin(angle) / root])
    return table.astype(np.float32).astype(ml_dtypes.bfloat16)


def blend_into(
    first_ref, delay_ref, est_ref, obs_ref, before_ref, after_ref, energy_ref, est32, res32, store
):
    shots, rows, samples = est_ref.shape
    columns = samples // LANES
    margin = (FAR - NEAR) // LANES
    inner = (samples - NEAR) // LANES
    skip = NEAR // LANES
    total = delay_ref.shape[0]
    first = first_ref[0]
    lane = lax.broadcasted_iota(jnp.int32, (1, rows, LANES), 2)

    def ahead(shot):
        shot = jnp.clip(shot, 0, total - 2)
        return jnp.clip(SOURCE_SPACING + delay_ref[shot + 1] - delay_ref[shot], NEAR + 1, FAR - 1)

    def window(field, slot, start):
        column, rest = start // LANES, start % LANES
        wide = field[slot, pl.ds(column, inner + 1)]
        turned = pltpu.roll(
            wide.reshape((inner + 1) * rows, LANES), (LANES - rest) % LANES, 1
        ).reshape(inner + 1, rows, LANES)
        return jnp.where(lane < LANES - rest, turned[:-1], turned[1:])

    def blended(field, slot, shot):
        later = window(field, slot + 1, margin * LANES + NEAR - ahead(shot))
        earlier = window(field, slot - 1, margin * LANES + ahead(shot - 1))
        return later, earlier

    def fill(field, slot, values):
        blank = jnp.zeros((margin, rows, LANES), jnp.float32)
        field[slot, pl.ds(0, margin)] = blank
        field[slot, pl.ds(margin + columns, margin)] = blank
        for column in range(columns):
            field[slot, margin + column] = values(column)

    def cut(ref, shot):
        return lambda column: ref[shot, :, column * LANES : (column + 1) * LANES].astype(jnp.float32)

    for slot in range(2):
        fill(est32, slot, cut(before_ref, slot))
        fill(est32, shots + 2 + slot, cut(after_ref, slot))

    def load(shot, carry):
        fill(est32, shot + 2, cut(est_ref, shot))
        return carry

    lax.fori_loop(0, shots, load, 0)

    def residual(place, values):
        shot = first + place - 1
        inside = jnp.logical_and(shot >= 0, shot < total)
        later, earlier = blended(est32, place + 1, shot)
        power = jnp.zeros((rows, LANES), jnp.float32)
        cells = []
        for column in range(columns):
            cell = est32[place + 1, margin + column]
            if column >= skip:
                cell = cell + later[column - skip]
            if column < inner:
                cell = cell + earlier[column]
            cell = jnp.where(inside, values(column) - cell, 0.0)
            power = power + cell * cell
            cells.append(cell)
        fill(res32, place, lambda column: cells[column])
        return power

    residual(0, cut(before_ref, 2))
    residual(shots + 1, cut(after_ref, 2))

    def middle(shot, carry):
        power = residual(shot + 1, cut(obs_ref, shot))
        energy_ref[pl.ds(shot, 1), :] = jnp.sum(power, axis=0, keepdims=True)
        return carry

    lax.fori_loop(0, shots, middle, 0)

    def step(shot, carry):
        later, earlier = blended(res32, shot + 1, first + shot)
        for column in range(columns):
            cell = res32[shot + 1, margin + column]
            if column >= skip:
                cell = cell + later[column - skip]
            if column < inner:
                cell = cell + earlier[column]
            cell = est32[shot + 2, margin + column] + STEP * cell
            store(shot, column, cell.astype(jnp.bfloat16))
        return carry

    lax.fori_loop(0, shots, step, 0)


def spectra_kernel(
    first_ref, delay_ref, est_ref, obs_ref, before_ref, after_ref, table_ref, _, *refs
):
    *out_refs, energy_ref, est32, res32, stepped = refs
    shots, rows, samples = est_ref.shape
    width = out_refs[0].shape[2]

    def store(shot, column, values):
        start = pl.multiple_of(shot * rows, rows)
        stepped[pl.ds(start, rows), column * LANES : (column + 1) * LANES] = values

    blend_into(
        first_ref, delay_ref, est_ref, obs_ref, before_ref, after_ref, energy_ref, est32, res32, store
    )
    group = min(shots, max(1, 256 // rows))

    def transform(part, carry):
        start = pl.multiple_of(part * (group * rows), group * rows)
        result = jnp.dot(
            stepped[pl.ds(start, group * rows), :], table_ref[...], preferred_element_type=jnp.float32
        ).astype(jnp.bfloat16)
        for slot, out_ref in enumerate(out_refs):
            out_ref[pl.ds(part * group, group)] = result[
                :, slot * width : (slot + 1) * width
            ].reshape(group, rows, width)
        return carry

    lax.fori_loop(0, shots // group, transform, 0)


def step_kernel(
    first_ref, delay_ref, est_ref, obs_ref, before_ref, after_ref, out_ref, energy_ref, est32, res32
):
    def store(shot, column, values):
        out_ref[shot, :, column * LANES : (column + 1) * LANES] = values

    blend_into(
        first_ref, delay_ref, est_ref, obs_ref, before_ref, after_ref, energy_ref, est32, res32, store
    )


def shots_kernel(across_ref, back_ref, level_ref, _, *refs):
    peers = (len(refs) - 2) // 2
    spectra_refs, out_refs, (wide, back) = refs[:peers], refs[peers : 2 * peers], refs[2 * peers :]
    held, rows, width = spectra_refs[0].shape
    shots = peers * held
    half = width // 2
    for slot, ref in enumerate(spectra_refs):
        wide[pl.ds(slot * held * rows, held * rows), :] = (
            ref[...].reshape(held * rows, width).astype(jnp.float32)
        )
    level = level_ref[...]
    sign = jnp.where(
        lax.broadcasted_iota(jnp.int32, (1, width), 1) < half, jnp.float32(1.0), jnp.float32(-1.0)
    )

    def pair(index, carry):
        picks = [pl.ds(index * 2 + turn, shots, stride=rows) for turn in range(2)]
        block = jnp.concatenate([wide[pick, :] for pick in picks], axis=1).astype(jnp.bfloat16)
        both = jnp.dot(across_ref[...], block, preferred_element_type=jnp.float32)
        kept = []
        for turn in range(2):
            own = both[:, turn * width : (turn + 1) * width]
            wave = own[:shots] + sign * pltpu.roll(own[shots:], half, 1)
            power = wave * wave
            power = power + pltpu.roll(power, half, 1)
            factor = jnp.maximum(1.0 - level * lax.rsqrt(power), 0.0)
            kept.append((wave * factor).astype(jnp.bfloat16))
        both = jnp.dot(back_ref[...], jnp.concatenate(kept, axis=1), preferred_element_type=jnp.float32)
        for turn in range(2):
            own = both[:, turn * width : (turn + 1) * width]
            back[picks[turn], :] = own[:shots] - sign * pltpu.roll(own[shots:], half, 1)
        return carry

    lax.fori_loop(0, rows // 2, pair, 0)
    for slot, ref in enumerate(out_refs):
        ref[...] = (
            back[pl.ds(slot * held * rows, held * rows), :].astype(jnp.bfloat16).reshape(ref.shape)
        )


def update_kernel(peers, table_ref, _, *refs):
    restored_refs, (out_ref, turn_ref) = refs[:peers], refs[-2:]
    held, rows, width = restored_refs[0].shape
    block = jnp.concatenate(
        [ref[...].reshape(held * rows, width) for ref in restored_refs], axis=1
    )
    out_ref[...] = jnp.dot(block, table_ref[...], preferred_element_type=jnp.float32).reshape(out_ref.shape)
    turn_ref[...] = jnp.zeros_like(turn_ref)


def whole(shape):
    return pl.BlockSpec(shape, lambda *_: (0,) * len(shape))


def blend_specs(shots, rows, samples, chunk):
    at = lambda *_: (0, chunk, 0)
    return [
        pl.BlockSpec(memory_space=pltpu.SMEM),
        pl.BlockSpec(memory_space=pltpu.SMEM),
        pl.BlockSpec((shots, rows, samples), at),
        pl.BlockSpec((shots, rows, samples), at),
        pl.BlockSpec((HALO, rows, samples), at),
        pl.BlockSpec((HALO, rows, samples), at),
    ]


def blend_scratch(shots, rows, samples):
    columns = (samples + 2 * (FAR - NEAR)) // LANES
    return [
        pltpu.VMEM((shots + 4, columns, rows, LANES), jnp.float32),
        pltpu.VMEM((shots + 2, columns, rows, LANES), jnp.float32),
    ]


PARAMS = pltpu.CompilerParams(vmem_limit_bytes=48 * 1024 * 1024)


ANYWHERE = pl.BlockSpec(memory_space=pl.ANY)


def spectra_of(first, delays, fields, table, rows, chunk, peers, after):
    shots, _, samples = fields[0].shape
    block = (shots, rows, 2 * F // peers)
    *spectra, energy = pl.pallas_call(
        spectra_kernel,
        grid=(1,),
        in_specs=blend_specs(shots, rows, samples, chunk) + [whole(table.shape), ANYWHERE],
        out_specs=[whole(block)] * peers + [whole((shots, LANES))],
        out_shape=[jax.ShapeDtypeStruct(block, jnp.bfloat16)] * peers
        + [jax.ShapeDtypeStruct((shots, LANES), jnp.float32)],
        scratch_shapes=blend_scratch(shots, rows, samples)
        + [pltpu.VMEM((shots * rows, samples), jnp.bfloat16)],
        compiler_params=PARAMS,
        cost_estimate=pl.CostEstimate(
            flops=4 * F * shots * rows * samples,
            bytes_accessed=3 * 2 * shots * rows * samples + table.size * 2,
            transcendentals=0,
        ),
        name="spectra",
    )(first, delays, *fields, table, after)
    return spectra, energy


def stepped_of(first, delays, fields, rows, chunk):
    shots, _, samples = fields[0].shape
    return pl.pallas_call(
        step_kernel,
        grid=(1,),
        in_specs=blend_specs(shots, rows, samples, chunk),
        out_specs=[whole((shots, rows, samples)), whole((shots, LANES))],
        out_shape=[
            jax.ShapeDtypeStruct((shots, rows, samples), jnp.bfloat16),
            jax.ShapeDtypeStruct((shots, LANES), jnp.float32),
        ],
        scratch_shapes=blend_scratch(shots, rows, samples),
        compiler_params=PARAMS,
        name="stepped",
    )(first, delays, *fields)


def shrunk_of(spectra, across, back, level, after):
    held, rows, width = spectra[0].shape
    peers = len(spectra)
    shots = peers * held
    size = spectra[0].size * peers
    return pl.pallas_call(
        shots_kernel,
        grid=(1,),
        in_specs=[whole(across.shape), whole(back.shape), whole(level.shape), ANYWHERE]
        + [whole(spectra[0].shape)] * peers,
        out_specs=[whole(spectra[0].shape)] * peers,
        out_shape=[jax.ShapeDtypeStruct(spectra[0].shape, jnp.bfloat16)] * peers,
        scratch_shapes=[pltpu.VMEM((shots * rows, width), jnp.float32)] * 2,
        compiler_params=PARAMS,
        cost_estimate=pl.CostEstimate(
            flops=8 * shots * size, bytes_accessed=4 * size + 4 * across.size, transcendentals=size
        ),
        name="shrink",
    )(across, back, level, after, *spectra)


def updated_of(restored, table, chunk, receivers, onto, after):
    shots, rows, width = restored[0].shape
    peers = len(restored)
    samples = table.shape[1]
    group = min(shots, max(1, 256 // rows))
    in_specs = [whole(table.shape), ANYWHERE]
    in_specs += [pl.BlockSpec((group, rows, width), lambda step: (step, 0, 0))] * peers
    operands = [table, after, *restored]
    if onto is not None:
        in_specs.append(ANYWHERE)
        operands.append(onto)
    return pl.pallas_call(
        functools.partial(update_kernel, peers),
        grid=(shots // group,),
        in_specs=in_specs,
        out_specs=[
            pl.BlockSpec((group, rows, samples), lambda step: (step, chunk, 0)),
            whole((8, LANES)),
        ],
        out_shape=[
            jax.ShapeDtypeStruct((shots, receivers, samples), jnp.float32),
            jax.ShapeDtypeStruct((8, LANES), jnp.float32),
        ],
        input_output_aliases={} if onto is None else {len(operands) - 1: 0},
        compiler_params=PARAMS,
        cost_estimate=pl.CostEstimate(
            flops=4 * F * shots * rows * samples,
            bytes_accessed=2 * restored[0].size * peers + 2 * table.size + 4 * shots * rows * samples,
            transcendentals=0,
        ),
        name="update",
    )(*operands)


def exchanged(blocks):
    peers = len(blocks)
    return [
        block if slot == 0 else lax.ppermute(block, "shot", [(i, i ^ slot) for i in range(peers)])
        for slot, block in enumerate(blocks)
    ]


def chunks_of(receivers):
    if receivers == 128:
        return [(16, 0), (16, 1), (32, 1), (32, 2), (16, 6), (16, 7)]
    rows = min(16, receivers)
    return [(rows, index) for index in range(receivers // rows)]


def swapped(array):
    return lax.all_to_all(array, "shot", split_axis=0, concat_axis=0, tiled=True)


def spectral_by_einsum(stepped, forward, inverse, table, level, peers):
    shots, receivers, samples = stepped.shape
    total = table.shape[1]
    share = F // peers
    spectra = jnp.einsum(
        "srt,tdpf->dpfsr",
        stepped,
        forward.reshape(samples, peers, 2, share),
        preferred_element_type=jnp.float32,
    ).astype(jnp.bfloat16)
    mixed = swapped(spectra).transpose(1, 2, 0, 3, 4).reshape(2, share, total, receivers)
    cosine, sine = table[:total], table[total:]
    across = jnp.stack([jnp.stack([cosine, sine]), jnp.stack([-sine, cosine])])
    wave = jnp.einsum("pqks,qfsr->pfkr", across, mixed, preferred_element_type=jnp.float32)
    magnitude = jnp.sqrt(wave[0] * wave[0] + wave[1] * wave[1])
    bound = level[:, None, None]
    factor = jnp.maximum(magnitude - bound, 0.0) / jnp.maximum(magnitude, bound)
    shrunk = (wave * factor[None]).astype(jnp.bfloat16)
    back = jnp.stack([jnp.stack([cosine, -sine]), jnp.stack([sine, cosine])])
    restored = jnp.einsum(
        "pqks,qfkr->pfsr", back, shrunk, preferred_element_type=jnp.float32
    ).astype(jnp.bfloat16)
    restored = restored.reshape(2, share, peers, shots, receivers).transpose(2, 0, 1, 3, 4)
    return jnp.einsum(
        "dpft,dpfsr->srt",
        inverse.reshape(peers, 2, share, samples),
        swapped(restored),
        preferred_element_type=jnp.float32,
    )


def local(estimate, observed, random_source_delays, thresholds):
    shots, receivers, samples = estimate.shape
    peers = lax.axis_size("shot")
    rank = lax.axis_index("shot")
    total = random_source_delays.shape[0]
    share = F // peers
    first = jnp.reshape(rank * shots, (1,)).astype(jnp.int32)
    up = [(i, i + 1) for i in range(peers - 1)]
    down = [(j, i) for i, j in up]
    tail = jnp.concatenate([estimate[shots - 2 :], observed[shots - 1 :]])
    head = jnp.concatenate([estimate[:2], observed[:1]])
    before = lax.ppermute(tail, "shot", up)
    after = lax.ppermute(head, "shot", down)
    fields = (estimate, observed, before, after)
    forward, inverse = (jnp.asarray(table) for table in time_tables(samples, peers))
    table = jnp.asarray(shot_table(total))
    level = lax.dynamic_slice_in_dim(thresholds, rank * share, share)
    chunks = chunks_of(receivers)
    energy = 0.0
    if (2 * share) % LANES == 0 and peers & (peers - 1) == 0:
        order = rank ^ jnp.arange(peers, dtype=jnp.int32)
        forward = jnp.take(forward.reshape(samples, peers, 2 * share), order, axis=1)
        forward = forward.reshape(samples, 2 * F)
        inverse = jnp.take(inverse.reshape(peers, 2 * share, samples), order, axis=0)
        inverse = inverse.reshape(2 * F, samples)
        across = jnp.take(table.reshape(2 * total, peers, shots), order, axis=1)
        across = across.reshape(2 * total, total)
        back = jnp.take(table.reshape(2, peers, shots, total), order, axis=1)
        back = back.reshape(2 * total, total)
        levels = jnp.tile(level, 2)[None, :]
        updated, last = None, levels
        lag = 2
        ahead, behind = {}, {}
        for turn in range(len(chunks) + 2 * lag):
            if turn < len(chunks):
                rows, index = chunks[turn]
                spectra, power = spectra_of(
                    first, random_source_delays, fields, forward, rows, index, peers, last
                )
                last = power
                energy = energy + power
                ahead[turn] = exchanged(spectra)
            place = turn - lag
            if place in ahead:
                shrunk = shrunk_of(ahead.pop(place), across, back, levels, last)
                last = shrunk[0]
                behind[place] = exchanged(shrunk)
            place = turn - 2 * lag
            if place in behind:
                updated, last = updated_of(
                    behind.pop(place), inverse, chunks[place][1], receivers, updated, last
                )
    else:
        parts = []
        for rows, index in chunks:
            part, power = stepped_of(first, random_source_delays, fields, rows, index)
            energy = energy + power
            parts.append(part)
        updated = spectral_by_einsum(
            jnp.concatenate(parts, axis=1), forward, inverse, table, level, peers
        )
    misfit = lax.psum(jnp.sum(energy, axis=1), "patch") / (
        receivers * lax.axis_size("patch") * samples
    )
    return updated, misfit


def solution(mesh):
    in_specs = (P("shot", "patch", None), P("shot", "patch", None), P(), P())
    out_specs = (P("shot", "patch", None), P("shot"))
    return jax.shard_map(local, mesh=mesh, in_specs=in_specs, out_specs=out_specs, check_vma=False)
```

```python
import functools

import jax
import jax.numpy as jnp
import ml_dtypes
import numpy as np
from jax import lax
from jax.experimental import pallas as pl
from jax.experimental.pallas import tpu as pltpu
from jax.sharding import PartitionSpec as P

F = 512
SOURCE_SPACING = 512
JITTER = 256
STEP = 0.5
LANES = 128
NEAR = SOURCE_SPACING - JITTER
FAR = SOURCE_SPACING + JITTER
HALO = 3


def time_tables(samples, blocks):
    freq = np.arange(F, dtype=np.int32)
    sample = np.arange(samples, dtype=np.int32)
    phase = (freq[:, None] * sample[None, :] % samples).astype(np.float32)
    angle = np.float32(2.0 * np.pi) * phase / np.float32(samples)
    root = np.sqrt(np.float32(samples))
    weight = np.where(freq == 0, 1.0, 2.0).astype(np.float32)[:, None] / root
    forward = np.stack([np.cos(angle) / root, -np.sin(angle) / root])
    inverse = np.stack([weight * np.cos(angle), -weight * np.sin(angle)])

    def ordered(table):
        table = table.astype(np.float32).astype(ml_dtypes.bfloat16)
        table = table.reshape(2, blocks, F // blocks, samples).transpose(1, 0, 2, 3)
        return table.reshape(2 * F, samples)

    return np.ascontiguousarray(ordered(forward).T), ordered(inverse)


def shot_table(shots):
    index = np.arange(shots, dtype=np.int32)
    phase = (index[:, None] * index[None, :] % shots).astype(np.float32)
    angle = np.float32(2.0 * np.pi) * phase / np.float32(shots)
    root = np.sqrt(np.float32(shots))
    table = np.concatenate([np.cos(angle) / root, np.sin(angle) / root])
    return table.astype(np.float32).astype(ml_dtypes.bfloat16)


def blend_into(
    first_ref, delay_ref, est_ref, obs_ref, before_ref, after_ref, energy_ref, est32, res32, store
):
    shots, rows, samples = est_ref.shape
    columns = samples // LANES
    margin = (FAR - NEAR) // LANES
    inner = (samples - NEAR) // LANES
    skip = NEAR // LANES
    total = delay_ref.shape[0]
    first = first_ref[0]
    lane = lax.broadcasted_iota(jnp.int32, (1, rows, LANES), 2)

    def ahead(shot):
        shot = jnp.clip(shot, 0, total - 2)
        return jnp.clip(SOURCE_SPACING + delay_ref[shot + 1] - delay_ref[shot], NEAR + 1, FAR - 1)

    def window(field, slot, start):
        column, rest = start // LANES, start % LANES
        wide = field[slot, pl.ds(column, inner + 1)]
        turned = pltpu.roll(
            wide.reshape((inner + 1) * rows, LANES), (LANES - rest) % LANES, 1
        ).reshape(inner + 1, rows, LANES)
        return jnp.where(lane < LANES - rest, turned[:-1], turned[1:])

    def blended(field, slot, shot):
        later = window(field, slot + 1, margin * LANES + NEAR - ahead(shot))
        earlier = window(field, slot - 1, margin * LANES + ahead(shot - 1))
        return later, earlier

    def fill(field, slot, values):
        blank = jnp.zeros((margin, rows, LANES), jnp.float32)
        field[slot, pl.ds(0, margin)] = blank
        field[slot, pl.ds(margin + columns, margin)] = blank
        for column in range(columns):
            field[slot, margin + column] = values(column)

    def cut(ref, shot):
        return lambda column: ref[shot, :, column * LANES : (column + 1) * LANES].astype(jnp.float32)

    for slot in range(2):
        fill(est32, slot, cut(before_ref, slot))
        fill(est32, shots + 2 + slot, cut(after_ref, slot))

    def load(shot, carry):
        fill(est32, shot + 2, cut(est_ref, shot))
        return carry

    lax.fori_loop(0, shots, load, 0, unroll=2)

    def residual(place, values):
        shot = first + place - 1
        inside = jnp.logical_and(shot >= 0, shot < total)
        later, earlier = blended(est32, place + 1, shot)
        power = jnp.zeros((rows, LANES), jnp.float32)
        cells = []
        for column in range(columns):
            cell = est32[place + 1, margin + column]
            if column >= skip:
                cell = cell + later[column - skip]
            if column < inner:
                cell = cell + earlier[column]
            cell = jnp.where(inside, values(column) - cell, 0.0)
            power = power + cell * cell
            cells.append(cell)
        fill(res32, place, lambda column: cells[column])
        return power

    residual(0, cut(before_ref, 2))
    residual(shots + 1, cut(after_ref, 2))

    def middle(shot, carry):
        power = residual(shot + 1, cut(obs_ref, shot))
        energy_ref[pl.ds(shot, 1), :] = jnp.sum(power, axis=0, keepdims=True)
        return carry

    lax.fori_loop(0, shots, middle, 0, unroll=2)

    def step(shot, carry):
        later, earlier = blended(res32, shot + 1, first + shot)
        for column in range(columns):
            cell = res32[shot + 1, margin + column]
            if column >= skip:
                cell = cell + later[column - skip]
            if column < inner:
                cell = cell + earlier[column]
            cell = est32[shot + 2, margin + column] + STEP * cell
            store(shot, column, cell.astype(jnp.bfloat16))
        return carry

    lax.fori_loop(0, shots, step, 0, unroll=2)


def blocks_in(near_ref, far_refs):
    return [near_ref.at[index] for index in range(near_ref.shape[0])] + list(far_refs)


def spectra_kernel(
    first_ref, delay_ref, est_ref, obs_ref, before_ref, after_ref, table_ref, order_ref, _, *refs
):
    near_ref, *far_refs, energy_ref, est32, res32, stepped, result = refs
    shots, rows, samples = est_ref.shape
    width = near_ref.shape[3]

    def store(shot, column, values):
        start = pl.multiple_of(shot * rows, rows)
        stepped[pl.ds(start, rows), column * LANES : (column + 1) * LANES] = values

    blend_into(
        first_ref, delay_ref, est_ref, obs_ref, before_ref, after_ref, energy_ref, est32, res32, store
    )
    held = result.shape[0]
    group = held // rows

    def transform(part, carry):
        start = pl.multiple_of(part * held, held)
        result[...] = jnp.dot(
            stepped[pl.ds(start, held), :], table_ref[...], preferred_element_type=jnp.float32
        ).astype(jnp.bfloat16)
        for slot, out_ref in enumerate(blocks_in(near_ref, far_refs)):
            lanes = pl.ds(pl.multiple_of(order_ref[slot] * width, width), width)
            out_ref[pl.ds(part * group, group)] = result[:, lanes].reshape(group, rows, width)
        return carry

    lax.fori_loop(0, shots // group, transform, 0)


def step_kernel(
    first_ref, delay_ref, est_ref, obs_ref, before_ref, after_ref, out_ref, energy_ref, est32, res32
):
    def store(shot, column, values):
        out_ref[shot, :, column * LANES : (column + 1) * LANES] = values

    blend_into(
        first_ref, delay_ref, est_ref, obs_ref, before_ref, after_ref, energy_ref, est32, res32, store
    )


def shots_kernel(order_ref, table_ref, level_ref, _, *refs):
    *refs, wide, back = refs
    spectra_refs, out_refs = refs[: len(refs) // 2], refs[len(refs) // 2 :]
    _, held, rows, width = spectra_refs[0].shape
    shots = wide.shape[0] // rows
    half = width // 2

    def place(slot):
        size = held * rows
        return pl.ds(pl.multiple_of(order_ref[slot] * size, size), size)

    for slot, ref in enumerate(blocks_in(spectra_refs[0], spectra_refs[1:])):
        wide[place(slot), :] = ref[...].reshape(held * rows, width).astype(jnp.float32)
    level = level_ref[...]
    sign = jnp.where(
        lax.broadcasted_iota(jnp.int32, (1, width), 1) < half, jnp.float32(1.0), jnp.float32(-1.0)
    )

    def pair(index, carry):
        picks = [pl.ds(index * 2 + turn, shots, stride=rows) for turn in range(2)]
        block = jnp.concatenate([wide[pick, :] for pick in picks], axis=1).astype(jnp.bfloat16)
        both = jnp.dot(table_ref[...], block, preferred_element_type=jnp.float32)
        kept = []
        for turn in range(2):
            own = both[:, turn * width : (turn + 1) * width]
            wave = own[:shots] + sign * pltpu.roll(own[shots:], half, 1)
            power = wave * wave
            power = power + pltpu.roll(power, half, 1)
            factor = jnp.maximum(1.0 - level * lax.rsqrt(power), 0.0)
            kept.append((wave * factor).astype(jnp.bfloat16))
        both = jnp.dot(table_ref[...], jnp.concatenate(kept, axis=1), preferred_element_type=jnp.float32)
        for turn in range(2):
            own = both[:, turn * width : (turn + 1) * width]
            back[picks[turn], :] = own[:shots] - sign * pltpu.roll(own[shots:], half, 1)
        return carry

    lax.fori_loop(0, rows // 2, pair, 0, unroll=2)
    for slot, ref in enumerate(blocks_in(out_refs[0], out_refs[1:])):
        ref[...] = back[place(slot), :].astype(jnp.bfloat16).reshape(held, rows, width)


def update_kernel(inputs, order_ref, table_ref, _, *refs):
    restored_refs, (out_ref, turn_ref, whole_rows) = refs[:inputs], refs[-3:]
    _, held, rows, width = restored_refs[0].shape
    for slot, ref in enumerate(blocks_in(restored_refs[0], restored_refs[1:])):
        lanes = pl.ds(pl.multiple_of(order_ref[slot] * width, width), width)
        whole_rows[:, lanes] = ref[...].reshape(held * rows, width)
    out_ref[...] = jnp.dot(
        whole_rows[...], table_ref[...], preferred_element_type=jnp.float32
    ).reshape(out_ref.shape)
    turn_ref[...] = jnp.zeros_like(turn_ref)


def whole(shape):
    return pl.BlockSpec(shape, lambda *_: (0,) * len(shape))


def blend_specs(shots, rows, samples, chunk, edge_chunk):
    at = lambda *_: (0, chunk, 0)
    edge = lambda *_: (0, edge_chunk, 0)
    return [
        pl.BlockSpec(memory_space=pltpu.SMEM),
        pl.BlockSpec(memory_space=pltpu.SMEM),
        pl.BlockSpec((shots, rows, samples), at),
        pl.BlockSpec((shots, rows, samples), at),
        pl.BlockSpec((HALO, rows, samples), edge),
        pl.BlockSpec((HALO, rows, samples), edge),
    ]


def blend_scratch(shots, rows, samples):
    columns = (samples + 2 * (FAR - NEAR)) // LANES
    return [
        pltpu.VMEM((shots + 4, columns, rows, LANES), jnp.float32),
        pltpu.VMEM((shots + 2, columns, rows, LANES), jnp.float32),
    ]


PARAMS = pltpu.CompilerParams(vmem_limit_bytes=48 * 1024 * 1024)


ANYWHERE = pl.BlockSpec(memory_space=pl.ANY)


SCALARS = pl.BlockSpec(memory_space=pltpu.SMEM)


def spectra_of(first, delays, fields, table, order, rows, chunk, edge_chunk, after):
    shots, _, samples = fields[0].shape
    peers = order.shape[0]
    block = (shots, rows, 2 * F // peers)
    blocks = [(peers // 2,) + block] + [block] * (peers - peers // 2)
    group = min(shots, max(1, 256 // rows))
    *spectra, energy = pl.pallas_call(
        spectra_kernel,
        grid=(1,),
        in_specs=blend_specs(shots, rows, samples, chunk, edge_chunk)
        + [whole(table.shape), SCALARS, ANYWHERE],
        out_specs=[whole(shape) for shape in blocks] + [whole((shots, LANES))],
        out_shape=[jax.ShapeDtypeStruct(shape, jnp.bfloat16) for shape in blocks]
        + [jax.ShapeDtypeStruct((shots, LANES), jnp.float32)],
        scratch_shapes=blend_scratch(shots, rows, samples)
        + [
            pltpu.VMEM((shots * rows, samples), jnp.bfloat16),
            pltpu.VMEM((group * rows, 2 * F), jnp.bfloat16),
        ],
        compiler_params=PARAMS,
        cost_estimate=pl.CostEstimate(
            flops=4 * F * shots * rows * samples,
            bytes_accessed=3 * 2 * shots * rows * samples + table.size * 2,
            transcendentals=0,
        ),
        name="spectra",
    )(first, delays, *fields, table, order, after)
    return spectra, energy


def stepped_of(first, delays, fields, rows, chunk):
    shots, _, samples = fields[0].shape
    return pl.pallas_call(
        step_kernel,
        grid=(1,),
        in_specs=blend_specs(shots, rows, samples, chunk, chunk),
        out_specs=[whole((shots, rows, samples)), whole((shots, LANES))],
        out_shape=[
            jax.ShapeDtypeStruct((shots, rows, samples), jnp.bfloat16),
            jax.ShapeDtypeStruct((shots, LANES), jnp.float32),
        ],
        scratch_shapes=blend_scratch(shots, rows, samples),
        compiler_params=PARAMS,
        name="stepped",
    )(first, delays, *fields)


def shrunk_of(spectra, table, level, order, after):
    _, held, rows, width = spectra[0].shape
    shots = order.shape[0] * held
    size = shots * rows * width
    return pl.pallas_call(
        shots_kernel,
        grid=(1,),
        in_specs=[SCALARS, whole(table.shape), whole(level.shape), ANYWHERE]
        + [whole(block.shape) for block in spectra],
        out_specs=[whole(block.shape) for block in spectra],
        out_shape=[jax.ShapeDtypeStruct(block.shape, jnp.bfloat16) for block in spectra],
        scratch_shapes=[pltpu.VMEM((shots * rows, width), jnp.float32)] * 2,
        compiler_params=PARAMS,
        cost_estimate=pl.CostEstimate(
            flops=8 * shots * size, bytes_accessed=4 * size + 2 * table.size, transcendentals=size
        ),
        name="shrink",
    )(order, table, level, after, *spectra)


def updated_of(restored, table, order, chunk, receivers, onto, after):
    near, shots, rows, width = restored[0].shape
    samples = table.shape[1]
    group = min(shots, max(1, 256 // rows))
    in_specs = [SCALARS, whole(table.shape), ANYWHERE]
    in_specs += [pl.BlockSpec((near, group, rows, width), lambda step: (0, step, 0, 0))]
    in_specs += [pl.BlockSpec((group, rows, width), lambda step: (step, 0, 0))] * (len(restored) - 1)
    operands = [order, table, after, *restored]
    if onto is not None:
        in_specs.append(ANYWHERE)
        operands.append(onto)
    return pl.pallas_call(
        functools.partial(update_kernel, len(restored)),
        grid=(shots // group,),
        in_specs=in_specs,
        out_specs=[
            pl.BlockSpec((group, rows, samples), lambda step: (step, chunk, 0)),
            whole((8, LANES)),
        ],
        out_shape=[
            jax.ShapeDtypeStruct((shots, receivers, samples), jnp.float32),
            jax.ShapeDtypeStruct((8, LANES), jnp.float32),
        ],
        scratch_shapes=[pltpu.VMEM((group * rows, 2 * F), jnp.bfloat16)],
        input_output_aliases={} if onto is None else {len(operands) - 1: 0},
        compiler_params=PARAMS,
        cost_estimate=pl.CostEstimate(
            flops=4 * F * shots * rows * samples,
            bytes_accessed=4 * F * shots * rows + 2 * table.size + 4 * shots * rows * samples,
            transcendentals=0,
        ),
        name="update",
    )(*operands)


def exchanged(blocks):
    near, *far = blocks
    half = near.shape[0]
    peers = half + len(far)
    far = [
        lax.ppermute(block, "shot", [(i, i ^ (half + slot)) for i in range(peers)])
        for slot, block in enumerate(far)
    ]
    groups = [list(range(half)), list(range(half, peers))]
    near = lax.all_to_all(
        near, "shot", split_axis=0, concat_axis=0, axis_index_groups=groups, tiled=True
    )
    return [near, *far]


def peers_of(rank, peers):
    half = peers // 2
    near = rank // half * half + jnp.arange(half, dtype=jnp.int32)
    return jnp.concatenate([near, rank ^ jnp.arange(half, peers, dtype=jnp.int32)])


def chunks_of(receivers):
    if receivers == 128:
        return [(16, 7), (16, 6), (32, 1), (32, 2), (16, 1), (16, 0)]
    rows = min(16, receivers)
    return [(rows, index) for index in range(receivers // rows)][::-1]


def edges(estimate, observed, start, stop):
    peers = lax.axis_size("shot")
    up = [(i, i + 1) for i in range(peers - 1)]
    down = [(j, i) for i, j in up]
    estimate, observed = estimate[:, start:stop], observed[:, start:stop]
    tail = jnp.concatenate([estimate[-2:], observed[-1:]])
    head = jnp.concatenate([estimate[:2], observed[:1]])
    return lax.ppermute(tail, "shot", up), lax.ppermute(head, "shot", down)


def swapped(array):
    return lax.all_to_all(array, "shot", split_axis=0, concat_axis=0, tiled=True)


def spectral_by_einsum(stepped, forward, inverse, table, level, peers):
    shots, receivers, samples = stepped.shape
    total = table.shape[1]
    share = F // peers
    spectra = jnp.einsum(
        "srt,tdpf->dpfsr",
        stepped,
        forward.reshape(samples, peers, 2, share),
        preferred_element_type=jnp.float32,
    ).astype(jnp.bfloat16)
    mixed = swapped(spectra).transpose(1, 2, 0, 3, 4).reshape(2, share, total, receivers)
    cosine, sine = table[:total], table[total:]
    across = jnp.stack([jnp.stack([cosine, sine]), jnp.stack([-sine, cosine])])
    wave = jnp.einsum("pqks,qfsr->pfkr", across, mixed, preferred_element_type=jnp.float32)
    magnitude = jnp.sqrt(wave[0] * wave[0] + wave[1] * wave[1])
    bound = level[:, None, None]
    factor = jnp.maximum(magnitude - bound, 0.0) / jnp.maximum(magnitude, bound)
    shrunk = (wave * factor[None]).astype(jnp.bfloat16)
    back = jnp.stack([jnp.stack([cosine, -sine]), jnp.stack([sine, cosine])])
    restored = jnp.einsum(
        "pqks,qfkr->pfsr", back, shrunk, preferred_element_type=jnp.float32
    ).astype(jnp.bfloat16)
    restored = restored.reshape(2, share, peers, shots, receivers).transpose(2, 0, 1, 3, 4)
    return jnp.einsum(
        "dpft,dpfsr->srt",
        inverse.reshape(peers, 2, share, samples),
        swapped(restored),
        preferred_element_type=jnp.float32,
    )


def local(estimate, observed, random_source_delays, thresholds):
    shots, receivers, samples = estimate.shape
    peers = lax.axis_size("shot")
    rank = lax.axis_index("shot")
    total = random_source_delays.shape[0]
    share = F // peers
    first = jnp.reshape(rank * shots, (1,)).astype(jnp.int32)
    forward, inverse = (jnp.asarray(table) for table in time_tables(samples, peers))
    table = jnp.asarray(shot_table(total))
    level = lax.dynamic_slice_in_dim(thresholds, rank * share, share)
    chunks = chunks_of(receivers)
    head_rows = chunks[0][0]
    early = edges(estimate, observed, receivers - head_rows, receivers)
    late = edges(estimate, observed, 0, receivers - head_rows) if len(chunks) > 1 else None
    energy = 0.0
    if (2 * share) % LANES == 0 and peers & (peers - 1) == 0:
        order = peers_of(rank, peers)
        levels = jnp.tile(level, 2)[None, :]
        updated, last = None, levels
        lag = 2
        ahead, behind = {}, {}
        for turn in range(len(chunks) + 2 * lag):
            if turn < len(chunks):
                rows, index = chunks[turn]
                sides, edge_index = (late, index) if turn else (early, 0)
                spectra, power = spectra_of(
                    first,
                    random_source_delays,
                    (estimate, observed, *sides),
                    forward,
                    order,
                    rows,
                    index,
                    edge_index,
                    last,
                )
                last = power
                energy = energy + power
                ahead[turn] = exchanged(spectra)
            place = turn - lag
            if place in ahead:
                shrunk = shrunk_of(ahead.pop(place), table, levels, order, last)
                last = shrunk[1]
                behind[place] = exchanged(shrunk)
            place = turn - 2 * lag
            if place in behind:
                updated, last = updated_of(
                    behind.pop(place), inverse, order, chunks[place][1], receivers, updated, last
                )
    else:
        sides = [jnp.concatenate(pair, axis=1) for pair in zip(late, early)] if late else early
        parts = {}
        for rows, index in chunks:
            part, power = stepped_of(
                first, random_source_delays, (estimate, observed, *sides), rows, index
            )
            energy = energy + power
            parts[index * rows] = part
        updated = spectral_by_einsum(
            jnp.concatenate([parts[start] for start in sorted(parts)], axis=1), forward, inverse, table, level, peers
        )
    misfit = lax.psum(jnp.sum(energy, axis=1), "patch") / (
        receivers * lax.axis_size("patch") * samples
    )
    return updated, misfit


def solution(mesh):
    in_specs = (P("shot", "patch", None), P("shot", "patch", None), P(), P())
    out_specs = (P("shot", "patch", None), P("shot"))
    return jax.shard_map(local, mesh=mesh, in_specs=in_specs, out_specs=out_specs, check_vma=False)
```

```python
import functools

import jax
import jax.numpy as jnp
import ml_dtypes
import numpy as np
from jax import lax
from jax.experimental import pallas as pl
from jax.experimental.pallas import tpu as pltpu
from jax.sharding import PartitionSpec as P

F = 512
SOURCE_SPACING = 512
JITTER = 256
STEP = 0.5
LANES = 128
NEAR = SOURCE_SPACING - JITTER
FAR = SOURCE_SPACING + JITTER
HALO = 3


def time_tables(samples, blocks):
    freq = np.arange(F, dtype=np.int32)
    sample = np.arange(samples, dtype=np.int32)
    phase = (freq[:, None] * sample[None, :] % samples).astype(np.float32)
    angle = np.float32(2.0 * np.pi) * phase / np.float32(samples)
    root = np.sqrt(np.float32(samples))
    weight = np.where(freq == 0, 1.0, 2.0).astype(np.float32)[:, None] / root
    forward = np.stack([np.cos(angle) / root, -np.sin(angle) / root])
    inverse = np.stack([weight * np.cos(angle), -weight * np.sin(angle)])

    def ordered(table):
        table = table.astype(np.float32).astype(ml_dtypes.bfloat16)
        table = table.reshape(2, blocks, F // blocks, samples).transpose(1, 0, 2, 3)
        return table.reshape(2 * F, samples)

    return np.ascontiguousarray(ordered(forward).T), ordered(inverse)


def shot_table(shots):
    index = np.arange(shots, dtype=np.int32)
    phase = (index[:, None] * index[None, :] % shots).astype(np.float32)
    angle = np.float32(2.0 * np.pi) * phase / np.float32(shots)
    root = np.sqrt(np.float32(shots))
    table = np.concatenate([np.cos(angle) / root, np.sin(angle) / root])
    return table.astype(np.float32).astype(ml_dtypes.bfloat16)


def band(meta_ref, chip, width):
    return pl.ds(pl.multiple_of(meta_ref[3 + 2 * chip] // 2 * width, width), width)


def views(refs):
    return [ref.at[index] for ref in refs for index in range(ref.shape[0])]


def blend_into(
    meta_ref, delay_ref, est_ref, obs_ref, before_ref, after_ref, energy_ref, est32, res32, store
):
    shots, rows, samples = est_ref.shape
    columns = samples // LANES
    margin = (FAR - NEAR) // LANES
    inner = (samples - NEAR) // LANES
    skip = NEAR // LANES
    total = delay_ref.shape[0]
    first = meta_ref[0]
    lane = lax.broadcasted_iota(jnp.int32, (1, rows, LANES), 2)

    def ahead(shot):
        shot = jnp.clip(shot, 0, total - 2)
        return jnp.clip(SOURCE_SPACING + delay_ref[shot + 1] - delay_ref[shot], NEAR + 1, FAR - 1)

    def window(field, slot, start):
        column, rest = start // LANES, start % LANES
        wide = field[slot, pl.ds(column, inner + 1)]
        turned = pltpu.roll(
            wide.reshape((inner + 1) * rows, LANES), (LANES - rest) % LANES, 1
        ).reshape(inner + 1, rows, LANES)
        return jnp.where(lane < LANES - rest, turned[:-1], turned[1:])

    def blended(field, slot, shot):
        later = window(field, slot + 1, margin * LANES + NEAR - ahead(shot))
        earlier = window(field, slot - 1, margin * LANES + ahead(shot - 1))
        return later, earlier

    def fill(field, slot, values):
        blank = jnp.zeros((margin, rows, LANES), jnp.float32)
        field[slot, pl.ds(0, margin)] = blank
        field[slot, pl.ds(margin + columns, margin)] = blank
        for column in range(columns):
            field[slot, margin + column] = values(column)

    def cut(ref, shot):
        return lambda column: ref[shot, :, column * LANES : (column + 1) * LANES].astype(jnp.float32)

    for slot in range(2):
        fill(est32, slot, cut(before_ref, slot))
        fill(est32, shots + 2 + slot, cut(after_ref, slot))

    def load(shot, carry):
        fill(est32, shot + 2, cut(est_ref, shot))
        return carry

    lax.fori_loop(0, shots, load, 0, unroll=2)

    def residual(place, values):
        shot = first + place - 1
        inside = jnp.logical_and(shot >= 0, shot < total)
        later, earlier = blended(est32, place + 1, shot)
        power = jnp.zeros((rows, LANES), jnp.float32)
        cells = []
        for column in range(columns):
            cell = est32[place + 1, margin + column]
            if column >= skip:
                cell = cell + later[column - skip]
            if column < inner:
                cell = cell + earlier[column]
            cell = jnp.where(inside, values(column) - cell, 0.0)
            power = power + cell * cell
            cells.append(cell)
        fill(res32, place, lambda column: cells[column])
        return power

    residual(0, cut(before_ref, 2))
    residual(shots + 1, cut(after_ref, 2))

    def middle(shot, carry):
        power = residual(shot + 1, cut(obs_ref, shot))
        energy_ref[pl.ds(shot, 1), :] = jnp.sum(power, axis=0, keepdims=True)
        return carry

    lax.fori_loop(0, shots, middle, 0, unroll=2)

    def step(shot, carry):
        later, earlier = blended(res32, shot + 1, first + shot)
        for column in range(columns):
            cell = res32[shot + 1, margin + column]
            if column >= skip:
                cell = cell + later[column - skip]
            if column < inner:
                cell = cell + earlier[column]
            cell = est32[shot + 2, margin + column] + STEP * cell
            store(shot, column, cell.astype(jnp.bfloat16))
        return carry

    lax.fori_loop(0, shots, step, 0, unroll=2)


def spectra_kernel(outputs, packed, meta_ref, delay_ref, est_ref, obs_ref, before_ref, after_ref, table_ref, _, *refs):
    *refs, energy_ref, est32, res32, stepped, result = refs
    out_refs, partner_refs = refs[-outputs:], refs[:-outputs]
    shots, rows, samples = est_ref.shape
    width = out_refs[0].shape[3]

    def store(shot, column, values):
        start = pl.multiple_of(shot * rows, rows)
        stepped[pl.ds(start, rows), column * LANES : (column + 1) * LANES] = values

    blend_into(
        meta_ref, delay_ref, est_ref, obs_ref, before_ref, after_ref, energy_ref, est32, res32, store
    )
    held = result.shape[0]
    group = held // rows
    if packed:
        targets = [out_refs[0].at[chip] for chip in range(out_refs[0].shape[0])]
    else:
        targets = [ref.at[0] for ref in out_refs]

    def transform(part, carry):
        start = pl.multiple_of(part * held, held)
        result[...] = jnp.dot(
            stepped[pl.ds(start, held), :], table_ref[...], preferred_element_type=jnp.float32
        ).astype(jnp.bfloat16)
        for chip, target in enumerate(targets):
            target[pl.ds(part * group, group)] = result[:, band(meta_ref, chip, width)].reshape(
                group, rows, width
            )
        return carry

    lax.fori_loop(0, shots // group, transform, 0)
    for partner_ref in partner_refs:
        for chip, out_ref in enumerate(out_refs):
            out_ref[1] = partner_ref[chip]


def step_kernel(
    meta_ref, delay_ref, est_ref, obs_ref, before_ref, after_ref, out_ref, energy_ref, est32, res32
):
    def store(shot, column, values):
        out_ref[shot, :, column * LANES : (column + 1) * LANES] = values

    blend_into(
        meta_ref, delay_ref, est_ref, obs_ref, before_ref, after_ref, energy_ref, est32, res32, store
    )


def shots_kernel(inputs, meta_ref, table_ref, level_ref, _, *refs):
    *refs, wide, back = refs
    _, held, rows, width = refs[0].shape
    pieces, size, _ = wide.shape
    shots = size // rows
    half = width // 2

    def place(slot):
        size = held * rows
        return pl.ds(pl.multiple_of(meta_ref[3 + slot] * size, size), size)

    for slot, ref in enumerate(views(refs[:inputs])):
        block = ref[...].reshape(held * rows, width).astype(jnp.float32)
        for piece in range(pieces):
            wide[piece, place(slot), :] = block[:, piece * LANES : (piece + 1) * LANES]
    level = level_ref[...]
    sign = jnp.where(
        lax.broadcasted_iota(jnp.int32, (1, width), 1) < half, jnp.float32(1.0), jnp.float32(-1.0)
    )

    def receiver(index, carry):
        pick = pl.ds(index, shots, stride=rows)
        block = jnp.concatenate([wide.at[piece][pick, :] for piece in range(pieces)], axis=1)
        both = jnp.dot(
            table_ref[...], block.astype(jnp.bfloat16), preferred_element_type=jnp.float32
        )
        wave = both[:shots] + sign * pltpu.roll(both[shots:], half, 1)
        power = wave * wave
        power = power + pltpu.roll(power, half, 1)
        factor = jnp.maximum(1.0 - level * lax.rsqrt(power), 0.0)
        kept = (wave * factor).astype(jnp.bfloat16)
        both = jnp.dot(table_ref[...], kept, preferred_element_type=jnp.float32)
        both = both[:shots] - sign * pltpu.roll(both[shots:], half, 1)
        for piece in range(pieces):
            back.at[piece][pick, :] = both[:, piece * LANES : (piece + 1) * LANES]
        return carry

    lax.fori_loop(0, rows, receiver, 0, unroll=2)
    for slot, ref in enumerate(views(refs[inputs:])):
        block = jnp.concatenate([back[piece, place(slot), :] for piece in range(pieces)], axis=1)
        ref[...] = block.astype(jnp.bfloat16).reshape(held, rows, width)


def update_kernel(inputs, passes, meta_ref, table_ref, _, *refs):
    restored_refs, whole_rows = refs[:inputs], refs[-1]
    outputs = refs[-4:-1] if passes else refs[-3:-1]
    own = [restored_refs[0].at[chip] for chip in range(restored_refs[0].shape[0])]
    if inputs > 1:
        own = [ref.at[0] for ref in restored_refs]
    held, rows, width = own[0].shape
    for chip, ref in enumerate(own):
        whole_rows[:, band(meta_ref, chip, width)] = ref[...].reshape(held * rows, width)
    outputs[0][...] = jnp.dot(
        whole_rows[...], table_ref[...], preferred_element_type=jnp.float32
    ).reshape(outputs[0].shape)
    outputs[1][...] = jnp.zeros_like(outputs[1])
    if passes:
        for chip, ref in enumerate(restored_refs):
            outputs[2][chip] = ref[1]


def whole(shape):
    return pl.BlockSpec(shape, lambda *_: (0,) * len(shape))


def blend_specs(shots, rows, samples, block, edge_block):
    at = lambda step, meta, delays: (0, block(meta), 0)
    edge = lambda step, meta, delays: (0, edge_block(meta), 0)
    return [
        pl.BlockSpec((shots, rows, samples), at),
        pl.BlockSpec((shots, rows, samples), at),
        pl.BlockSpec((HALO, rows, samples), edge),
        pl.BlockSpec((HALO, rows, samples), edge),
    ]


def blend_scratch(shots, rows, samples):
    columns = (samples + 2 * (FAR - NEAR)) // LANES
    return [
        pltpu.VMEM((shots + 4, columns, rows, LANES), jnp.float32),
        pltpu.VMEM((shots + 2, columns, rows, LANES), jnp.float32),
    ]


PARAMS = pltpu.CompilerParams(vmem_limit_bytes=60 * 1024 * 1024)
ANYWHERE = pl.BlockSpec(memory_space=pl.ANY)


def spectra_of(meta, delays, fields, table, block, edge_block, rows, peers, mode, partner, after):
    shots, _, samples = fields[0].shape
    chips = peers // 2
    block_shape = (shots, rows, 2 * F // chips)
    shapes = {
        "apart": [(1, *block_shape)] * chips,
        "packed": [(chips, *block_shape)],
        "joined": [(2, *block_shape)] * chips,
    }[mode]
    group = min(shots, max(1, 256 // rows))
    partners = [] if partner is None else [partner]
    *spectra, energy = pl.pallas_call(
        functools.partial(spectra_kernel, len(shapes), mode == "packed"),
        grid_spec=pltpu.PrefetchScalarGridSpec(
            num_scalar_prefetch=2,
            grid=(1,),
            in_specs=blend_specs(shots, rows, samples, block, edge_block)
            + [whole(table.shape), ANYWHERE]
            + [whole(array.shape) for array in partners],
            out_specs=[whole(shape) for shape in shapes] + [whole((shots, LANES))],
            scratch_shapes=blend_scratch(shots, rows, samples)
            + [
                pltpu.VMEM((shots * rows, samples), jnp.bfloat16),
                pltpu.VMEM((group * rows, 2 * F), jnp.bfloat16),
            ],
        ),
        out_shape=[pltpu.HBM(shape, jnp.bfloat16) for shape in shapes]
        + [pltpu.HBM((shots, LANES), jnp.float32)],
        compiler_params=PARAMS,
        cost_estimate=pl.CostEstimate(
            flops=4 * F * shots * rows * samples,
            bytes_accessed=3 * 2 * shots * rows * samples + table.size * 2,
            transcendentals=0,
        ),
        name="spectra_" + mode,
    )(meta, delays, *fields, table, after, *partners)
    return spectra, energy


def stepped_of(meta, delays, fields, rows, index):
    shots, _, samples = fields[0].shape
    block = lambda meta: index
    return pl.pallas_call(
        step_kernel,
        grid_spec=pltpu.PrefetchScalarGridSpec(
            num_scalar_prefetch=2,
            grid=(1,),
            in_specs=blend_specs(shots, rows, samples, block, block),
            out_specs=[whole((shots, rows, samples)), whole((shots, LANES))],
            scratch_shapes=blend_scratch(shots, rows, samples),
        ),
        out_shape=[
            jax.ShapeDtypeStruct((shots, rows, samples), jnp.bfloat16),
            jax.ShapeDtypeStruct((shots, LANES), jnp.float32),
        ],
        compiler_params=PARAMS,
        name="stepped",
    )(meta, delays, *fields)


def shrunk_of(meta, spectra, table, level, joined, after):
    _, held, rows, width = spectra[0].shape
    shots = table.shape[1]
    peers = shots // held
    size = shots * rows * width
    shapes = [(2, held, rows, width)] * (peers // 2) if joined else [(1, held, rows, width)] * peers
    return pl.pallas_call(
        functools.partial(shots_kernel, len(spectra)),
        grid_spec=pltpu.PrefetchScalarGridSpec(
            num_scalar_prefetch=1,
            grid=(1,),
            in_specs=[whole(table.shape), whole(level.shape), ANYWHERE]
            + [whole(block.shape) for block in spectra],
            out_specs=[whole(shape) for shape in shapes],
            scratch_shapes=[pltpu.VMEM((width // LANES, shots * rows, LANES), jnp.float32)] * 2,
        ),
        out_shape=[pltpu.HBM(shape, jnp.bfloat16) for shape in shapes],
        compiler_params=PARAMS,
        cost_estimate=pl.CostEstimate(
            flops=8 * shots * size, bytes_accessed=4 * size + 2 * table.size, transcendentals=size
        ),
        name="shrink",
    )(meta, table, level, after, *spectra)


def updated_of(meta, restored, table, block, receivers, onto, passes, after):
    _, shots, rows, width = restored[0].shape
    samples = table.shape[1]
    chips = table.shape[0] // width
    group = min(shots, max(1, 256 // rows))
    by_shots = lambda step, meta: (0, step, 0, 0)
    in_specs = [whole(table.shape), ANYWHERE]
    in_specs += [pl.BlockSpec((array.shape[0], group, rows, width), by_shots) for array in restored]
    operands = [meta, table, after, *restored]
    if onto is not None:
        in_specs.append(ANYWHERE)
        operands.append(onto)
    out_specs = [
        pl.BlockSpec((group, rows, samples), lambda step, meta: (step, block(meta), 0)),
        whole((8, LANES)),
    ]
    out_shape = [
        pltpu.HBM((shots, receivers, samples), jnp.float32),
        pltpu.HBM((8, LANES), jnp.float32),
    ]
    if passes:
        out_specs.append(pl.BlockSpec((chips, group, rows, width), by_shots))
        out_shape.append(pltpu.HBM((chips, shots, rows, width), jnp.bfloat16))
    return pl.pallas_call(
        functools.partial(update_kernel, len(restored), passes),
        grid_spec=pltpu.PrefetchScalarGridSpec(
            num_scalar_prefetch=1,
            grid=(shots // group,),
            in_specs=in_specs,
            out_specs=out_specs,
            scratch_shapes=[pltpu.VMEM((group * rows, 2 * F), jnp.bfloat16)],
        ),
        out_shape=out_shape,
        input_output_aliases={} if onto is None else {len(operands) - 1: 0},
        compiler_params=PARAMS,
        cost_estimate=pl.CostEstimate(
            flops=4 * F * shots * rows * samples,
            bytes_accessed=4 * F * shots * rows + 2 * table.size + 4 * shots * rows * samples,
            transcendentals=0,
        ),
        name="update",
    )(*operands)


def swapped(array):
    return lax.all_to_all(array, "shot", split_axis=0, concat_axis=0, tiled=True)


def sent(array, distance):
    peers = lax.axis_size("shot")
    return lax.ppermute(array, "shot", [(i, i ^ distance) for i in range(peers)])


def edges(estimate, observed):
    peers = lax.axis_size("shot")
    up = [(i, i + 1) for i in range(peers - 1)]
    down = [(j, i) for i, j in up]
    tail = jnp.concatenate([estimate[-2:], observed[-1:]])
    head = jnp.concatenate([estimate[:2], observed[:1]])
    return lax.ppermute(tail, "shot", up), lax.ppermute(head, "shot", down)


def part_of_halves(array, start, stop):
    shots, receivers, samples = array.shape
    halves = array.reshape(shots, 2, receivers // 2, samples)[:, :, start:stop]
    return halves.reshape(shots, 2 * (stop - start), samples)


def turns(steps):
    for turn in range(steps + 4):
        if turn == 0:
            yield "own", 0
            yield "other", 0
        if turn + 1 < steps:
            yield "other", turn + 1
        if 0 < turn < steps:
            yield "own", turn
        for name, lag in (("shrink", 1), ("update own", 3), ("update other", 4)):
            if 0 <= turn - lag < steps:
                yield name, turn - lag


def in_pairs(estimate, observed, delays, thresholds, rows):
    shots, receivers, samples = estimate.shape
    peers = lax.axis_size("shot")
    rank = lax.axis_index("shot")
    total = delays.shape[0]
    chips = peers // 2
    share = F // chips
    steps = receivers // 2 // rows
    core = rank % 2
    meta = jnp.concatenate(
        [jnp.stack([rank * shots, core, 1 - core]), rank ^ jnp.arange(peers, dtype=jnp.int32)]
    ).astype(jnp.int32)
    forward, inverse = (jnp.asarray(table) for table in time_tables(samples, chips))
    table = jnp.asarray(shot_table(total))
    levels = jnp.tile(lax.dynamic_slice_in_dim(thresholds, rank // 2 * share, share), 2)[None, :]
    early = edges(part_of_halves(estimate, 0, rows), part_of_halves(observed, 0, rows))
    late = None
    last, updated, energy = levels, None, 0.0
    packed, ahead, behind, passed = {}, {}, {}, {}
    for name, step in turns(steps):
        side = 1 if name.endswith("own") else 2
        block = lambda meta, side=side, step=step: meta[side] * steps + step
        if name in ("own", "other"):
            edge_block = block
            if step == 0:
                edge_block = lambda meta, side=side: meta[side]
            else:
                edge_block = lambda meta, side=side, step=step: meta[side] * (steps - 1) + step - 1
            direct = step == 0
            mode = "apart" if direct else "joined" if name == "own" else "packed"
            spectra, power = spectra_of(
                meta,
                delays,
                (estimate, observed, *(late if step else early)),
                forward,
                block,
                edge_block,
                rows,
                peers,
                mode,
                packed.pop(step) if mode == "joined" else None,
                last,
            )
            last = power
            energy = energy + power
            if mode == "packed":
                packed[step] = sent(spectra[0], 1)
            elif mode == "joined":
                far = [sent(spectra[chip], 2 * chip) for chip in range(1, chips)]
                ahead[step] = [spectra[0], *far]
            elif name == "own":
                far = [sent(spectra[chip], 2 * chip) for chip in range(1, chips)]
                ahead[step] = [spectra[0], *far]
                held_estimate, held_observed, _ = lax.optimization_barrier(
                    (estimate, observed, power)
                )
                if steps > 1:
                    late = edges(
                        part_of_halves(held_estimate, rows, receivers // 2),
                        part_of_halves(held_observed, rows, receivers // 2),
                    )
            else:
                other = [sent(spectra[chip], 2 * chip + 1) for chip in range(chips)]
                ahead[step] = [array for pair in zip(ahead[step], other) for array in pair]
        elif name == "shrink":
            direct = step == steps - 1
            shrunk = shrunk_of(meta, ahead.pop(step), table, levels, not direct, last)
            last = shrunk[0]
            unit = 1 if direct else 2
            behind[step] = [
                sent(array, unit * index) if index else array for index, array in enumerate(shrunk)
            ]
        elif name == "update own":
            direct = step == steps - 1
            restored = behind.pop(step)
            if direct:
                passed[step] = restored[1::2]
                restored = restored[::2]
            updated, last, *partner = updated_of(
                meta, restored, inverse, block, receivers, updated, not direct, last
            )
            if not direct:
                passed[step] = [sent(partner[0], 1)]
        else:
            updated, last = updated_of(
                meta, passed.pop(step), inverse, block, receivers, updated, False, last
            )
    return updated, energy


def spectral_by_einsum(stepped, forward, inverse, table, level, peers):
    shots, receivers, samples = stepped.shape
    total = table.shape[1]
    share = F // peers
    spectra = jnp.einsum(
        "srt,tdpf->dpfsr",
        stepped,
        forward.reshape(samples, peers, 2, share),
        preferred_element_type=jnp.float32,
    ).astype(jnp.bfloat16)
    mixed = swapped(spectra).transpose(1, 2, 0, 3, 4).reshape(2, share, total, receivers)
    cosine, sine = table[:total], table[total:]
    across = jnp.stack([jnp.stack([cosine, sine]), jnp.stack([-sine, cosine])])
    wave = jnp.einsum("pqks,qfsr->pfkr", across, mixed, preferred_element_type=jnp.float32)
    magnitude = jnp.sqrt(wave[0] * wave[0] + wave[1] * wave[1])
    bound = level[:, None, None]
    factor = jnp.maximum(magnitude - bound, 0.0) / jnp.maximum(magnitude, bound)
    shrunk = (wave * factor[None]).astype(jnp.bfloat16)
    back = jnp.stack([jnp.stack([cosine, -sine]), jnp.stack([sine, cosine])])
    restored = jnp.einsum(
        "pqks,qfkr->pfsr", back, shrunk, preferred_element_type=jnp.float32
    ).astype(jnp.bfloat16)
    restored = restored.reshape(2, share, peers, shots, receivers).transpose(2, 0, 1, 3, 4)
    return jnp.einsum(
        "dpft,dpfsr->srt",
        inverse.reshape(peers, 2, share, samples),
        swapped(restored),
        preferred_element_type=jnp.float32,
    )


def by_einsum(estimate, observed, delays, thresholds, rows):
    shots, receivers, samples = estimate.shape
    peers = lax.axis_size("shot")
    rank = lax.axis_index("shot")
    share = F // peers
    meta = jnp.reshape(rank * shots, (1,)).astype(jnp.int32)
    sides = edges(estimate, observed)
    energy = 0.0
    parts = []
    for index in range(receivers // rows):
        part, power = stepped_of(meta, delays, (estimate, observed, *sides), rows, index)
        energy = energy + power
        parts.append(part)
    forward, inverse = (jnp.asarray(table) for table in time_tables(samples, peers))
    table = jnp.asarray(shot_table(delays.shape[0]))
    level = lax.dynamic_slice_in_dim(thresholds, rank * share, share)
    stepped = jnp.concatenate(parts, axis=1)
    return spectral_by_einsum(stepped, forward, inverse, table, level, peers), energy


def local(estimate, observed, random_source_delays, thresholds):
    receivers, samples = estimate.shape[1:]
    peers = lax.axis_size("shot")
    rows = min(16, receivers)
    paired = (
        peers > 1
        and peers & (peers - 1) == 0
        and (4 * F // peers) % LANES == 0
        and receivers % (2 * rows) == 0
    )
    path = in_pairs if paired else by_einsum
    updated, energy = path(estimate, observed, random_source_delays, thresholds, rows)
    misfit = lax.psum(jnp.sum(energy, axis=1), "patch") / (
        receivers * lax.axis_size("patch") * samples
    )
    return updated, misfit


def solution(mesh):
    in_specs = (P("shot", "patch", None), P("shot", "patch", None), P(), P())
    out_specs = (P("shot", "patch", None), P("shot"))
    return jax.shard_map(local, mesh=mesh, in_specs=in_specs, out_specs=out_specs, check_vma=False)
```

```python
import functools

import jax
import jax.numpy as jnp
import ml_dtypes
import numpy as np
from jax import lax
from jax.experimental import pallas as pl
from jax.experimental.pallas import tpu as pltpu
from jax.sharding import PartitionSpec as P

F = 512
SOURCE_SPACING = 512
JITTER = 256
STEP = 0.5
LANES = 128
NEAR = SOURCE_SPACING - JITTER
FAR = SOURCE_SPACING + JITTER
HALO = 3


def time_tables(samples, blocks):
    freq = np.arange(F, dtype=np.int32)
    sample = np.arange(samples, dtype=np.int32)
    phase = (freq[:, None] * sample[None, :] % samples).astype(np.float32)
    angle = np.float32(2.0 * np.pi) * phase / np.float32(samples)
    root = np.sqrt(np.float32(samples))
    weight = np.where(freq == 0, 1.0, 2.0).astype(np.float32)[:, None] / root
    forward = np.stack([np.cos(angle) / root, -np.sin(angle) / root])
    inverse = np.stack([weight * np.cos(angle), -weight * np.sin(angle)])

    def ordered(table):
        table = table.astype(np.float32).astype(ml_dtypes.bfloat16)
        table = table.reshape(2, blocks, F // blocks, samples).transpose(1, 0, 2, 3)
        return table.reshape(2 * F, samples)

    return np.ascontiguousarray(ordered(forward).T), ordered(inverse)


def shot_table(shots):
    index = np.arange(shots, dtype=np.int32)
    phase = (index[:, None] * index[None, :] % shots).astype(np.float32)
    angle = np.float32(2.0 * np.pi) * phase / np.float32(shots)
    root = np.sqrt(np.float32(shots))
    table = np.concatenate([np.cos(angle) / root, np.sin(angle) / root])
    return table.astype(np.float32).astype(ml_dtypes.bfloat16)


def band(meta_ref, chip, width):
    return pl.ds(pl.multiple_of(meta_ref[3 + 2 * chip] // 2 * width, width), width)


def views(refs):
    return [ref.at[index] for ref in refs for index in range(ref.shape[0])]


def blend_into(
    meta_ref, delay_ref, est_ref, obs_ref, before_ref, after_ref, energy_ref, est32, res32, store
):
    shots, rows, samples = est_ref.shape
    columns = samples // LANES
    margin = (FAR - NEAR) // LANES
    inner = (samples - NEAR) // LANES
    skip = NEAR // LANES
    total = delay_ref.shape[0]
    first = meta_ref[0]
    lane = lax.broadcasted_iota(jnp.int32, (1, rows, LANES), 2)

    def ahead(shot):
        shot = jnp.clip(shot, 0, total - 2)
        return jnp.clip(SOURCE_SPACING + delay_ref[shot + 1] - delay_ref[shot], NEAR + 1, FAR - 1)

    def window(field, slot, start):
        column, rest = start // LANES, start % LANES
        wide = field[slot, pl.ds(column, inner + 1)]
        turned = pltpu.roll(
            wide.reshape((inner + 1) * rows, LANES), (LANES - rest) % LANES, 1
        ).reshape(inner + 1, rows, LANES)
        return jnp.where(lane < LANES - rest, turned[:-1], turned[1:])

    def blended(field, slot, shot):
        later = window(field, slot + 1, margin * LANES + NEAR - ahead(shot))
        earlier = window(field, slot - 1, margin * LANES + ahead(shot - 1))
        return later, earlier

    def fill(field, slot, values):
        blank = jnp.zeros((margin, rows, LANES), jnp.float32)
        field[slot, pl.ds(0, margin)] = blank
        field[slot, pl.ds(margin + columns, margin)] = blank
        for column in range(columns):
            field[slot, margin + column] = values(column)

    def cut(ref, shot):
        return lambda column: ref[shot, :, column * LANES : (column + 1) * LANES].astype(jnp.float32)

    for slot in range(2):
        fill(est32, slot, cut(before_ref, slot))
        fill(est32, shots + 2 + slot, cut(after_ref, slot))

    def load(shot, carry):
        fill(est32, shot + 2, cut(est_ref, shot))
        return carry

    lax.fori_loop(0, shots, load, 0, unroll=2)

    def residual(place, values):
        shot = first + place - 1
        inside = jnp.logical_and(shot >= 0, shot < total)
        later, earlier = blended(est32, place + 1, shot)
        power = jnp.zeros((rows, LANES), jnp.float32)
        cells = []
        for column in range(columns):
            cell = est32[place + 1, margin + column]
            if column >= skip:
                cell = cell + later[column - skip]
            if column < inner:
                cell = cell + earlier[column]
            cell = jnp.where(inside, values(column) - cell, 0.0)
            power = power + cell * cell
            cells.append(cell)
        fill(res32, place, lambda column: cells[column])
        return power

    residual(0, cut(before_ref, 2))
    residual(shots + 1, cut(after_ref, 2))

    def middle(shot, carry):
        power = residual(shot + 1, cut(obs_ref, shot))
        energy_ref[pl.ds(shot, 1), :] = jnp.sum(power, axis=0, keepdims=True)
        return carry

    lax.fori_loop(0, shots, middle, 0, unroll=4)

    def step(shot, carry):
        later, earlier = blended(res32, shot + 1, first + shot)
        for column in range(columns):
            cell = res32[shot + 1, margin + column]
            if column >= skip:
                cell = cell + later[column - skip]
            if column < inner:
                cell = cell + earlier[column]
            cell = est32[shot + 2, margin + column] + STEP * cell
            store(shot, column, cell.astype(jnp.bfloat16))
        return carry

    lax.fori_loop(0, shots, step, 0, unroll=4)


def spectra_kernel(outputs, packed, meta_ref, delay_ref, est_ref, obs_ref, before_ref, after_ref, table_ref, _, *refs):
    *refs, energy_ref, est32, res32, stepped, result = refs
    out_refs, partner_refs = refs[-outputs:], refs[:-outputs]
    shots, rows, samples = est_ref.shape
    width = out_refs[0].shape[3]

    def store(shot, column, values):
        start = pl.multiple_of(shot * rows, rows)
        stepped[pl.ds(start, rows), column * LANES : (column + 1) * LANES] = values

    blend_into(
        meta_ref, delay_ref, est_ref, obs_ref, before_ref, after_ref, energy_ref, est32, res32, store
    )
    held = result.shape[0]
    group = held // rows
    if packed:
        targets = [out_refs[0].at[chip] for chip in range(out_refs[0].shape[0])]
    else:
        targets = [ref.at[0] for ref in out_refs]

    def transform(part, carry):
        start = pl.multiple_of(part * held, held)
        result[...] = jnp.dot(
            stepped[pl.ds(start, held), :], table_ref[...], preferred_element_type=jnp.float32
        ).astype(jnp.bfloat16)
        for chip, target in enumerate(targets):
            target[pl.ds(part * group, group)] = result[:, band(meta_ref, chip, width)].reshape(
                group, rows, width
            )
        return carry

    lax.fori_loop(0, shots // group, transform, 0)
    for partner_ref in partner_refs:
        for chip, out_ref in enumerate(out_refs):
            out_ref[1] = partner_ref[chip]


def step_kernel(
    meta_ref, delay_ref, est_ref, obs_ref, before_ref, after_ref, out_ref, energy_ref, est32, res32
):
    def store(shot, column, values):
        out_ref[shot, :, column * LANES : (column + 1) * LANES] = values

    blend_into(
        meta_ref, delay_ref, est_ref, obs_ref, before_ref, after_ref, energy_ref, est32, res32, store
    )


def shots_kernel(inputs, meta_ref, table_ref, level_ref, _, *refs):
    *refs, wide, back = refs
    _, held, rows, width = refs[0].shape
    pieces, size, _ = wide.shape
    shots = size // rows
    half = width // 2

    def place(slot):
        size = held * rows
        return pl.ds(pl.multiple_of(meta_ref[3 + slot] * size, size), size)

    for slot, ref in enumerate(views(refs[:inputs])):
        block = ref[...].reshape(held * rows, width).astype(jnp.float32)
        for piece in range(pieces):
            wide[piece, place(slot), :] = block[:, piece * LANES : (piece + 1) * LANES]
    level = level_ref[...]
    sign = jnp.where(
        lax.broadcasted_iota(jnp.int32, (1, width), 1) < half, jnp.float32(1.0), jnp.float32(-1.0)
    )

    def receiver(index, carry):
        pick = pl.ds(index, shots, stride=rows)
        block = jnp.concatenate([wide.at[piece][pick, :] for piece in range(pieces)], axis=1)
        both = jnp.dot(
            table_ref[...], block.astype(jnp.bfloat16), preferred_element_type=jnp.float32
        )
        wave = both[:shots] + sign * pltpu.roll(both[shots:], half, 1)
        power = wave * wave
        power = power + pltpu.roll(power, half, 1)
        factor = jnp.maximum(1.0 - level * lax.rsqrt(power), 0.0)
        kept = (wave * factor).astype(jnp.bfloat16)
        both = jnp.dot(table_ref[...], kept, preferred_element_type=jnp.float32)
        both = both[:shots] - sign * pltpu.roll(both[shots:], half, 1)
        for piece in range(pieces):
            back.at[piece][pick, :] = both[:, piece * LANES : (piece + 1) * LANES]
        return carry

    lax.fori_loop(0, rows, receiver, 0, unroll=2)
    for slot, ref in enumerate(views(refs[inputs:])):
        block = jnp.concatenate([back[piece, place(slot), :] for piece in range(pieces)], axis=1)
        ref[...] = block.astype(jnp.bfloat16).reshape(held, rows, width)


def update_kernel(inputs, passes, meta_ref, table_ref, _, *refs):
    restored_refs, whole_rows = refs[:inputs], refs[-1]
    outputs = refs[-4:-1] if passes else refs[-3:-1]
    own = [restored_refs[0].at[chip] for chip in range(restored_refs[0].shape[0])]
    if inputs > 1:
        own = [ref.at[0] for ref in restored_refs]
    held, rows, width = own[0].shape
    for chip, ref in enumerate(own):
        whole_rows[:, band(meta_ref, chip, width)] = ref[...].reshape(held * rows, width)
    outputs[0][...] = jnp.dot(
        whole_rows[...], table_ref[...], preferred_element_type=jnp.float32
    ).reshape(outputs[0].shape)
    outputs[1][...] = jnp.zeros_like(outputs[1])
    if passes:
        for chip, ref in enumerate(restored_refs):
            outputs[2][chip] = ref[1]


def whole(shape):
    return pl.BlockSpec(shape, lambda *_: (0,) * len(shape))


def blend_specs(shots, rows, samples, block, edge_block):
    at = lambda step, meta, delays: (0, block(meta), 0)
    edge = lambda step, meta, delays: (0, edge_block(meta), 0)
    return [
        pl.BlockSpec((shots, rows, samples), at),
        pl.BlockSpec((shots, rows, samples), at),
        pl.BlockSpec((HALO, rows, samples), edge),
        pl.BlockSpec((HALO, rows, samples), edge),
    ]


def blend_scratch(shots, rows, samples):
    columns = (samples + 2 * (FAR - NEAR)) // LANES
    return [
        pltpu.VMEM((shots + 4, columns, rows, LANES), jnp.float32),
        pltpu.VMEM((shots + 2, columns, rows, LANES), jnp.float32),
    ]


PARAMS = pltpu.CompilerParams(vmem_limit_bytes=60 * 1024 * 1024)
ANYWHERE = pl.BlockSpec(memory_space=pl.ANY)


def spectra_of(meta, delays, fields, table, block, edge_block, rows, peers, mode, partner, after):
    shots, _, samples = fields[0].shape
    chips = peers // 2
    block_shape = (shots, rows, 2 * F // chips)
    shapes = {
        "apart": [(1, *block_shape)] * chips,
        "packed": [(chips, *block_shape)],
        "joined": [(2, *block_shape)] * chips,
    }[mode]
    group = min(shots, max(1, 256 // rows))
    partners = [] if partner is None else [partner]
    start = lambda step: (0, 0, 0, 0)
    *spectra, energy = pl.pallas_call(
        functools.partial(spectra_kernel, len(shapes), mode == "packed"),
        grid_spec=pltpu.PrefetchScalarGridSpec(
            num_scalar_prefetch=2,
            grid=(1,),
            in_specs=blend_specs(shots, rows, samples, block, edge_block)
            + [whole(table.shape), ANYWHERE]
            + [read(item, (chips, *block_shape), start) for item in partners],
            out_specs=[whole(shape) for shape in shapes] + [whole((shots, LANES))],
            scratch_shapes=blend_scratch(shots, rows, samples)
            + [
                pltpu.VMEM((shots * rows, samples), jnp.bfloat16),
                pltpu.VMEM((group * rows, 2 * F), jnp.bfloat16),
            ],
        ),
        out_shape=[pltpu.HBM(shape, jnp.bfloat16) for shape in shapes]
        + [pltpu.HBM((shots, LANES), jnp.float32)],
        compiler_params=PARAMS,
        cost_estimate=pl.CostEstimate(
            flops=4 * F * shots * rows * samples,
            bytes_accessed=3 * 2 * shots * rows * samples + table.size * 2,
            transcendentals=0,
        ),
        name="spectra_" + mode,
    )(meta, delays, *fields, table, after, *[array for array, _ in partners])
    return spectra, energy


def stepped_of(meta, delays, fields, rows, index):
    shots, _, samples = fields[0].shape
    block = lambda meta: index
    return pl.pallas_call(
        step_kernel,
        grid_spec=pltpu.PrefetchScalarGridSpec(
            num_scalar_prefetch=2,
            grid=(1,),
            in_specs=blend_specs(shots, rows, samples, block, block),
            out_specs=[whole((shots, rows, samples)), whole((shots, LANES))],
            scratch_shapes=blend_scratch(shots, rows, samples),
        ),
        out_shape=[
            jax.ShapeDtypeStruct((shots, rows, samples), jnp.bfloat16),
            jax.ShapeDtypeStruct((shots, LANES), jnp.float32),
        ],
        compiler_params=PARAMS,
        name="stepped",
    )(meta, delays, *fields)


def shrunk_of(meta, spectra, table, level, joined, after):
    count, here, rows, width = spectra[0][0].shape[-4:]
    shots = table.shape[1]
    peers = shots // here
    size = shots * rows * width
    shapes = [(2, here, rows, width)] * (peers // 2) if joined else [(1, here, rows, width)] * peers
    start = lambda step: (0, 0, 0, 0)
    return pl.pallas_call(
        functools.partial(shots_kernel, len(spectra)),
        grid_spec=pltpu.PrefetchScalarGridSpec(
            num_scalar_prefetch=1,
            grid=(1,),
            in_specs=[whole(table.shape), whole(level.shape), ANYWHERE]
            + [read(item, (count, here, rows, width), start) for item in spectra],
            out_specs=[whole(shape) for shape in shapes],
            scratch_shapes=[pltpu.VMEM((width // LANES, shots * rows, LANES), jnp.float32)] * 2,
        ),
        out_shape=[pltpu.HBM(shape, jnp.bfloat16) for shape in shapes],
        compiler_params=PARAMS,
        cost_estimate=pl.CostEstimate(
            flops=8 * shots * size, bytes_accessed=4 * size + 2 * table.size, transcendentals=size
        ),
        name="shrink",
    )(meta, table, level, after, *[array for array, _ in spectra])


def updated_of(meta, restored, table, block, receivers, onto, passes, after):
    count, shots, rows, width = restored[0][0].shape[-4:]
    samples = table.shape[1]
    chips = table.shape[0] // width
    group = min(shots, max(1, 256 // rows))
    by_shots = lambda step, meta: (0, step, 0, 0)
    in_specs = [whole(table.shape), ANYWHERE]
    in_specs += [
        read(item, (count, group, rows, width), lambda step: (0, step, 0, 0)) for item in restored
    ]
    operands = [meta, table, after, *[array for array, _ in restored]]
    if onto is not None:
        in_specs.append(ANYWHERE)
        operands.append(onto)
    out_specs = [
        pl.BlockSpec((group, rows, samples), lambda step, meta: (step, block(meta), 0)),
        whole((8, LANES)),
    ]
    out_shape = [
        pltpu.HBM((shots, receivers, samples), jnp.float32),
        pltpu.HBM((8, LANES), jnp.float32),
    ]
    if passes:
        out_specs.append(pl.BlockSpec((chips, group, rows, width), by_shots))
        out_shape.append(pltpu.HBM((chips, shots, rows, width), jnp.bfloat16))
    return pl.pallas_call(
        functools.partial(update_kernel, len(restored), passes),
        grid_spec=pltpu.PrefetchScalarGridSpec(
            num_scalar_prefetch=1,
            grid=(shots // group,),
            in_specs=in_specs,
            out_specs=out_specs,
            scratch_shapes=[pltpu.VMEM((group * rows, 2 * F), jnp.bfloat16)],
        ),
        out_shape=out_shape,
        input_output_aliases={} if onto is None else {len(operands) - 1: 0},
        compiler_params=PARAMS,
        cost_estimate=pl.CostEstimate(
            flops=4 * F * shots * rows * samples,
            bytes_accessed=4 * F * shots * rows + 2 * table.size + 4 * shots * rows * samples,
            transcendentals=0,
        ),
        name="update",
    )(*operands)


def swapped(array):
    return lax.all_to_all(array, "shot", split_axis=0, concat_axis=0, tiled=True)


def sent(array, distance):
    peers = lax.axis_size("shot")
    if distance < peers // 2:
        groups = [[i, i ^ distance] for i in range(peers) if i < i ^ distance]
        return lax.all_gather(array, "shot", axis_index_groups=groups), distance
    return lax.ppermute(array, "shot", [(i, i ^ distance) for i in range(peers)]), 0


def held(array):
    return array, 0


def read(item, shape, where):
    _, distance = item
    if distance == 0:
        return pl.BlockSpec(shape, lambda step, meta, *_: where(step))
    return pl.BlockSpec(
        (None, *shape),
        lambda step, meta, *_: (jnp.where(meta[3] < meta[3 + distance], 1, 0), *where(step)),
    )


def edges(estimate, observed):
    peers = lax.axis_size("shot")
    up = [(i, i + 1) for i in range(peers - 1)]
    down = [(j, i) for i, j in up]
    tail = jnp.concatenate([estimate[-2:], observed[-1:]])
    head = jnp.concatenate([estimate[:2], observed[:1]])
    return lax.ppermute(tail, "shot", up), lax.ppermute(head, "shot", down)


def part_of_halves(array, start, stop):
    shots, receivers, samples = array.shape
    halves = array.reshape(shots, 2, receivers // 2, samples)[:, :, start:stop]
    return halves.reshape(shots, 2 * (stop - start), samples)


def turns(steps):
    for turn in range(steps + 4):
        if turn == 0:
            yield "own", 0
            yield "other", 0
        if turn + 1 < steps:
            yield "other", turn + 1
        if 0 < turn < steps:
            yield "own", turn
        for name, lag in (("shrink", 1), ("update own", 3), ("update other", 4)):
            if 0 <= turn - lag < steps:
                yield name, turn - lag


def in_pairs(estimate, observed, delays, thresholds, rows):
    shots, receivers, samples = estimate.shape
    peers = lax.axis_size("shot")
    rank = lax.axis_index("shot")
    total = delays.shape[0]
    chips = peers // 2
    share = F // chips
    steps = receivers // 2 // rows
    core = rank % 2
    meta = jnp.concatenate(
        [jnp.stack([rank * shots, core, 1 - core]), rank ^ jnp.arange(peers, dtype=jnp.int32)]
    ).astype(jnp.int32)
    forward, inverse = (jnp.asarray(table) for table in time_tables(samples, chips))
    table = jnp.asarray(shot_table(total))
    levels = jnp.tile(lax.dynamic_slice_in_dim(thresholds, rank // 2 * share, share), 2)[None, :]
    early = edges(part_of_halves(estimate, 0, rows), part_of_halves(observed, 0, rows))
    late = None
    last, updated, energy = levels, None, 0.0
    packed, ahead, behind, passed = {}, {}, {}, {}
    for name, step in turns(steps):
        side = 1 if name.endswith("own") else 2
        block = lambda meta, side=side, step=step: meta[side] * steps + step
        if name in ("own", "other"):
            edge_block = block
            if step == 0:
                edge_block = lambda meta, side=side: meta[side]
            else:
                edge_block = lambda meta, side=side, step=step: meta[side] * (steps - 1) + step - 1
            direct = step == 0
            mode = "apart" if direct else "joined" if name == "own" else "packed"
            spectra, power = spectra_of(
                meta,
                delays,
                (estimate, observed, *(late if step else early)),
                forward,
                block,
                edge_block,
                rows,
                peers,
                mode,
                packed.pop(step) if mode == "joined" else None,
                last,
            )
            last = power
            energy = energy + power
            if mode == "packed":
                packed[step] = sent(spectra[0], 1)
            elif mode == "joined":
                far = [sent(spectra[chip], 2 * chip) for chip in range(1, chips)]
                ahead[step] = [held(spectra[0]), *far]
            elif name == "own":
                far = [sent(spectra[chip], 2 * chip) for chip in range(1, chips)]
                ahead[step] = [held(spectra[0]), *far]
                held_estimate, held_observed, _ = lax.optimization_barrier(
                    (estimate, observed, power)
                )
                if steps > 1:
                    late = edges(
                        part_of_halves(held_estimate, rows, receivers // 2),
                        part_of_halves(held_observed, rows, receivers // 2),
                    )
            else:
                other = [sent(spectra[chip], 2 * chip + 1) for chip in range(chips)]
                ahead[step] = [array for pair in zip(ahead[step], other) for array in pair]
        elif name == "shrink":
            direct = step == steps - 1
            shrunk = shrunk_of(meta, ahead.pop(step), table, levels, not direct, last)
            last = shrunk[0]
            unit = 1 if direct else 2
            behind[step] = [
                sent(array, unit * index) if index else held(array)
                for index, array in enumerate(shrunk)
            ]
        elif name == "update own":
            direct = step == steps - 1
            restored = behind.pop(step)
            if direct:
                passed[step] = restored[1::2]
                restored = restored[::2]
            updated, last, *partner = updated_of(
                meta, restored, inverse, block, receivers, updated, not direct, last
            )
            if not direct:
                passed[step] = [sent(partner[0], 1)]
        else:
            updated, last = updated_of(
                meta, passed.pop(step), inverse, block, receivers, updated, False, last
            )
    return updated, energy


def spectral_by_einsum(stepped, forward, inverse, table, level, peers):
    shots, receivers, samples = stepped.shape
    total = table.shape[1]
    share = F // peers
    spectra = jnp.einsum(
        "srt,tdpf->dpfsr",
        stepped,
        forward.reshape(samples, peers, 2, share),
        preferred_element_type=jnp.float32,
    ).astype(jnp.bfloat16)
    mixed = swapped(spectra).transpose(1, 2, 0, 3, 4).reshape(2, share, total, receivers)
    cosine, sine = table[:total], table[total:]
    across = jnp.stack([jnp.stack([cosine, sine]), jnp.stack([-sine, cosine])])
    wave = jnp.einsum("pqks,qfsr->pfkr", across, mixed, preferred_element_type=jnp.float32)
    magnitude = jnp.sqrt(wave[0] * wave[0] + wave[1] * wave[1])
    bound = level[:, None, None]
    factor = jnp.maximum(magnitude - bound, 0.0) / jnp.maximum(magnitude, bound)
    shrunk = (wave * factor[None]).astype(jnp.bfloat16)
    back = jnp.stack([jnp.stack([cosine, -sine]), jnp.stack([sine, cosine])])
    restored = jnp.einsum(
        "pqks,qfkr->pfsr", back, shrunk, preferred_element_type=jnp.float32
    ).astype(jnp.bfloat16)
    restored = restored.reshape(2, share, peers, shots, receivers).transpose(2, 0, 1, 3, 4)
    return jnp.einsum(
        "dpft,dpfsr->srt",
        inverse.reshape(peers, 2, share, samples),
        swapped(restored),
        preferred_element_type=jnp.float32,
    )


def by_einsum(estimate, observed, delays, thresholds, rows):
    shots, receivers, samples = estimate.shape
    peers = lax.axis_size("shot")
    rank = lax.axis_index("shot")
    share = F // peers
    meta = jnp.reshape(rank * shots, (1,)).astype(jnp.int32)
    sides = edges(estimate, observed)
    energy = 0.0
    parts = []
    for index in range(receivers // rows):
        part, power = stepped_of(meta, delays, (estimate, observed, *sides), rows, index)
        energy = energy + power
        parts.append(part)
    forward, inverse = (jnp.asarray(table) for table in time_tables(samples, peers))
    table = jnp.asarray(shot_table(delays.shape[0]))
    level = lax.dynamic_slice_in_dim(thresholds, rank * share, share)
    stepped = jnp.concatenate(parts, axis=1)
    return spectral_by_einsum(stepped, forward, inverse, table, level, peers), energy


def local(estimate, observed, random_source_delays, thresholds):
    receivers, samples = estimate.shape[1:]
    peers = lax.axis_size("shot")
    rows = min(16, receivers)
    paired = (
        peers > 1
        and peers & (peers - 1) == 0
        and (4 * F // peers) % LANES == 0
        and receivers % (2 * rows) == 0
    )
    path = in_pairs if paired else by_einsum
    updated, energy = path(estimate, observed, random_source_delays, thresholds, rows)
    misfit = lax.psum(jnp.sum(energy, axis=1), "patch") / (
        receivers * lax.axis_size("patch") * samples
    )
    return updated, misfit


def solution(mesh):
    in_specs = (P("shot", "patch", None), P("shot", "patch", None), P(), P())
    out_specs = (P("shot", "patch", None), P("shot"))
    return jax.shard_map(local, mesh=mesh, in_specs=in_specs, out_specs=out_specs, check_vma=False)
```

```python
import functools

import jax
import jax.numpy as jnp
import ml_dtypes
import numpy as np
from jax import lax
from jax.experimental import pallas as pl
from jax.experimental.pallas import tpu as pltpu
from jax.sharding import PartitionSpec as P

F = 512
SOURCE_SPACING = 512
JITTER = 256
STEP = 0.5
LANES = 128
NEAR = SOURCE_SPACING - JITTER
FAR = SOURCE_SPACING + JITTER
HALO = 3


def time_tables(samples, blocks):
    freq = np.arange(F, dtype=np.int32)
    sample = np.arange(samples, dtype=np.int32)
    phase = (freq[:, None] * sample[None, :] % samples).astype(np.float32)
    angle = np.float32(2.0 * np.pi) * phase / np.float32(samples)
    root = np.sqrt(np.float32(samples))
    weight = np.where(freq == 0, 1.0, 2.0).astype(np.float32)[:, None] / root
    forward = np.stack([np.cos(angle) / root, -np.sin(angle) / root])
    inverse = np.stack([weight * np.cos(angle), -weight * np.sin(angle)])

    def ordered(table):
        table = table.astype(np.float32).astype(ml_dtypes.bfloat16)
        table = table.reshape(2, blocks, F // blocks, samples).transpose(1, 0, 2, 3)
        return table.reshape(2 * F, samples)

    return np.ascontiguousarray(ordered(forward).T), ordered(inverse)


def shot_table(shots):
    index = np.arange(shots, dtype=np.int32)
    phase = (index[:, None] * index[None, :] % shots).astype(np.float32)
    angle = np.float32(2.0 * np.pi) * phase / np.float32(shots)
    root = np.sqrt(np.float32(shots))
    table = np.concatenate([np.cos(angle) / root, np.sin(angle) / root])
    return table.astype(np.float32).astype(ml_dtypes.bfloat16)


def band(meta_ref, chip, width):
    return pl.ds(pl.multiple_of(meta_ref[3 + 2 * chip] // 2 * width, width), width)


def views(refs):
    return [ref.at[index] for ref in refs for index in range(ref.shape[0])]


def blend_into(
    meta_ref, delay_ref, est_ref, obs_ref, before_ref, after_ref, energy_ref, est32, res32, store
):
    shots, rows, samples = est_ref.shape
    columns = samples // LANES
    margin = (FAR - NEAR) // LANES
    inner = (samples - NEAR) // LANES
    skip = NEAR // LANES
    total = delay_ref.shape[0]
    first = meta_ref[0]
    lane = lax.broadcasted_iota(jnp.int32, (1, rows, LANES), 2)

    def ahead(shot):
        shot = jnp.clip(shot, 0, total - 2)
        return jnp.clip(SOURCE_SPACING + delay_ref[shot + 1] - delay_ref[shot], NEAR + 1, FAR - 1)

    def window(field, slot, start):
        column, rest = start // LANES, start % LANES
        wide = field[slot, pl.ds(column, inner + 1)]
        turned = pltpu.roll(
            wide.reshape((inner + 1) * rows, LANES), (LANES - rest) % LANES, 1
        ).reshape(inner + 1, rows, LANES)
        return jnp.where(lane < LANES - rest, turned[:-1], turned[1:])

    def blended(field, slot, shot):
        later = window(field, slot + 1, margin * LANES + NEAR - ahead(shot))
        earlier = window(field, slot - 1, margin * LANES + ahead(shot - 1))
        return later, earlier

    def fill(field, slot, values):
        blank = jnp.zeros((margin, rows, LANES), jnp.float32)
        field[slot, pl.ds(0, margin)] = blank
        field[slot, pl.ds(margin + columns, margin)] = blank
        for column in range(columns):
            field[slot, margin + column] = values(column)

    def cut(ref, shot):
        return lambda column: ref[shot, :, column * LANES : (column + 1) * LANES].astype(jnp.float32)

    for slot in range(2):
        fill(est32, slot, cut(before_ref, slot))
        fill(est32, shots + 2 + slot, cut(after_ref, slot))

    def load(shot, carry):
        fill(est32, shot + 2, cut(est_ref, shot))
        return carry

    lax.fori_loop(0, shots, load, 0, unroll=4)

    def residual(place, values):
        shot = first + place - 1
        inside = jnp.logical_and(shot >= 0, shot < total)
        later, earlier = blended(est32, place + 1, shot)
        power = jnp.zeros((rows, LANES), jnp.float32)
        cells = []
        for column in range(columns):
            cell = est32[place + 1, margin + column]
            if column >= skip:
                cell = cell + later[column - skip]
            if column < inner:
                cell = cell + earlier[column]
            cell = jnp.where(inside, values(column) - cell, 0.0)
            power = power + cell * cell
            cells.append(cell)
        fill(res32, place, lambda column: cells[column])
        return power

    residual(0, cut(before_ref, 2))
    residual(shots + 1, cut(after_ref, 2))

    def middle(shot, carry):
        power = residual(shot + 1, cut(obs_ref, shot))
        energy_ref[pl.ds(shot, 1), :] = jnp.sum(power, axis=0, keepdims=True)
        return carry

    lax.fori_loop(0, shots, middle, 0, unroll=4)

    def step(shot, carry):
        later, earlier = blended(res32, shot + 1, first + shot)
        for column in range(columns):
            cell = res32[shot + 1, margin + column]
            if column >= skip:
                cell = cell + later[column - skip]
            if column < inner:
                cell = cell + earlier[column]
            cell = est32[shot + 2, margin + column] + STEP * cell
            store(shot, column, cell.astype(jnp.bfloat16))
        return carry

    lax.fori_loop(0, shots, step, 0, unroll=4)


def spectra_kernel(outputs, packed, meta_ref, delay_ref, est_ref, obs_ref, before_ref, after_ref, table_ref, _, *refs):
    *refs, energy_ref, est32, res32, stepped, result = refs
    out_refs, partner_refs = refs[-outputs:], refs[:-outputs]
    shots, rows, samples = est_ref.shape
    width = out_refs[0].shape[3]

    def store(shot, column, values):
        start = pl.multiple_of(shot * rows, rows)
        stepped[pl.ds(start, rows), column * LANES : (column + 1) * LANES] = values

    blend_into(
        meta_ref, delay_ref, est_ref, obs_ref, before_ref, after_ref, energy_ref, est32, res32, store
    )
    held = result.shape[0]
    group = held // rows
    if packed:
        targets = [out_refs[0].at[chip] for chip in range(out_refs[0].shape[0])]
    else:
        targets = [ref.at[0] for ref in out_refs]

    def transform(part, carry):
        start = pl.multiple_of(part * held, held)
        result[...] = jnp.dot(
            stepped[pl.ds(start, held), :], table_ref[...], preferred_element_type=jnp.float32
        ).astype(jnp.bfloat16)
        for chip, target in enumerate(targets):
            target[pl.ds(part * group, group)] = result[:, band(meta_ref, chip, width)].reshape(
                group, rows, width
            )
        return carry

    lax.fori_loop(0, shots // group, transform, 0)
    for partner_ref in partner_refs:
        for chip, out_ref in enumerate(out_refs):
            out_ref[1] = partner_ref[chip]


def step_kernel(
    meta_ref, delay_ref, est_ref, obs_ref, before_ref, after_ref, out_ref, energy_ref, est32, res32
):
    def store(shot, column, values):
        out_ref[shot, :, column * LANES : (column + 1) * LANES] = values

    blend_into(
        meta_ref, delay_ref, est_ref, obs_ref, before_ref, after_ref, energy_ref, est32, res32, store
    )


def shots_kernel(inputs, meta_ref, table_ref, level_ref, _, *refs):
    *refs, wide, back = refs
    _, held, rows, width = refs[0].shape
    pieces, size, _ = wide.shape
    shots = size // rows
    half = width // 2

    def place(slot):
        size = held * rows
        return pl.ds(pl.multiple_of(meta_ref[3 + slot] * size, size), size)

    for slot, ref in enumerate(views(refs[:inputs])):
        block = ref[...].reshape(held * rows, width).astype(jnp.float32)
        for piece in range(pieces):
            wide[piece, place(slot), :] = block[:, piece * LANES : (piece + 1) * LANES]
    level = level_ref[...]
    sign = jnp.where(
        lax.broadcasted_iota(jnp.int32, (1, width), 1) < half, jnp.float32(1.0), jnp.float32(-1.0)
    )

    def receiver(index, carry):
        pick = pl.ds(index, shots, stride=rows)
        block = jnp.concatenate([wide.at[piece][pick, :] for piece in range(pieces)], axis=1)
        both = jnp.dot(
            table_ref[...], block.astype(jnp.bfloat16), preferred_element_type=jnp.float32
        )
        wave = both[:shots] + sign * pltpu.roll(both[shots:], half, 1)
        power = wave * wave
        power = power + pltpu.roll(power, half, 1)
        factor = jnp.maximum(1.0 - level * lax.rsqrt(power), 0.0)
        kept = (wave * factor).astype(jnp.bfloat16)
        both = jnp.dot(table_ref[...], kept, preferred_element_type=jnp.float32)
        both = both[:shots] - sign * pltpu.roll(both[shots:], half, 1)
        for piece in range(pieces):
            back.at[piece][pick, :] = both[:, piece * LANES : (piece + 1) * LANES]
        return carry

    lax.fori_loop(0, rows, receiver, 0, unroll=2)
    for slot, ref in enumerate(views(refs[inputs:])):
        block = jnp.concatenate([back[piece, place(slot), :] for piece in range(pieces)], axis=1)
        ref[...] = block.astype(jnp.bfloat16).reshape(held, rows, width)


def update_kernel(inputs, passes, meta_ref, table_ref, _, *refs):
    restored_refs, whole_rows = refs[:inputs], refs[-1]
    outputs = refs[-4:-1] if passes else refs[-3:-1]
    own = [restored_refs[0].at[chip] for chip in range(restored_refs[0].shape[0])]
    if inputs > 1:
        own = [ref.at[0] for ref in restored_refs]
    held, rows, width = own[0].shape
    for chip, ref in enumerate(own):
        whole_rows[:, band(meta_ref, chip, width)] = ref[...].reshape(held * rows, width)
    outputs[0][...] = jnp.dot(
        whole_rows[...], table_ref[...], preferred_element_type=jnp.float32
    ).reshape(outputs[0].shape)
    outputs[1][...] = jnp.zeros_like(outputs[1])
    if passes:
        for chip, ref in enumerate(restored_refs):
            outputs[2][chip] = ref[1]


def whole(shape):
    return pl.BlockSpec(shape, lambda *_: (0,) * len(shape))


def blend_specs(shots, rows, samples, block, edge_block):
    at = lambda step, meta, delays: (0, block(meta), 0)
    edge = lambda step, meta, delays: (0, edge_block(meta), 0)
    return [
        pl.BlockSpec((shots, rows, samples), at),
        pl.BlockSpec((shots, rows, samples), at),
        pl.BlockSpec((HALO, rows, samples), edge),
        pl.BlockSpec((HALO, rows, samples), edge),
    ]


def blend_scratch(shots, rows, samples):
    columns = (samples + 2 * (FAR - NEAR)) // LANES
    return [
        pltpu.VMEM((shots + 4, columns, rows, LANES), jnp.float32),
        pltpu.VMEM((shots + 2, columns, rows, LANES), jnp.float32),
    ]


PARAMS = pltpu.CompilerParams(vmem_limit_bytes=60 * 1024 * 1024)
SMALL = pl.CostEstimate(flops=1024, bytes_accessed=1024, transcendentals=0)
ANYWHERE = pl.BlockSpec(memory_space=pl.ANY)


def spectra_of(meta, delays, fields, table, block, edge_block, rows, peers, mode, partner, after):
    shots, _, samples = fields[0].shape
    chips = peers // 2
    block_shape = (shots, rows, 2 * F // chips)
    shapes = {
        "packed": [(chips, *block_shape)],
        "joined": [(2, *block_shape)] * chips,
    }[mode]
    group = min(shots, max(1, 256 // rows))
    partners = [] if partner is None else [partner]
    *spectra, energy = pl.pallas_call(
        functools.partial(spectra_kernel, len(shapes), mode == "packed"),
        grid_spec=pltpu.PrefetchScalarGridSpec(
            num_scalar_prefetch=2,
            grid=(1,),
            in_specs=blend_specs(shots, rows, samples, block, edge_block)
            + [whole(table.shape), ANYWHERE]
            + [whole(array.shape) for array in partners],
            out_specs=[whole(shape) for shape in shapes] + [whole((shots, LANES))],
            scratch_shapes=blend_scratch(shots, rows, samples)
            + [
                pltpu.VMEM((shots * rows, samples), jnp.bfloat16),
                pltpu.VMEM((group * rows, 2 * F), jnp.bfloat16),
            ],
        ),
        out_shape=[pltpu.HBM(shape, jnp.bfloat16) for shape in shapes]
        + [pltpu.HBM((shots, LANES), jnp.float32)],
        compiler_params=PARAMS,
        cost_estimate=SMALL,
        name="spectra_" + mode,
    )(meta, delays, *fields, table, after, *partners)
    return spectra, energy


def stepped_of(meta, delays, fields, rows, index):
    shots, _, samples = fields[0].shape
    block = lambda meta: index
    return pl.pallas_call(
        step_kernel,
        grid_spec=pltpu.PrefetchScalarGridSpec(
            num_scalar_prefetch=2,
            grid=(1,),
            in_specs=blend_specs(shots, rows, samples, block, block),
            out_specs=[whole((shots, rows, samples)), whole((shots, LANES))],
            scratch_shapes=blend_scratch(shots, rows, samples),
        ),
        out_shape=[
            jax.ShapeDtypeStruct((shots, rows, samples), jnp.bfloat16),
            jax.ShapeDtypeStruct((shots, LANES), jnp.float32),
        ],
        compiler_params=PARAMS,
        name="stepped",
    )(meta, delays, *fields)


def shrunk_of(meta, spectra, table, level, joined, after):
    _, held, rows, width = spectra[0].shape
    shots = table.shape[1]
    peers = shots // held
    size = shots * rows * width
    shapes = [(2, held, rows, width)] * (peers // 2) if joined else [(1, held, rows, width)] * peers
    return pl.pallas_call(
        functools.partial(shots_kernel, len(spectra)),
        grid_spec=pltpu.PrefetchScalarGridSpec(
            num_scalar_prefetch=1,
            grid=(1,),
            in_specs=[whole(table.shape), whole(level.shape), ANYWHERE]
            + [whole(block.shape) for block in spectra],
            out_specs=[whole(shape) for shape in shapes],
            scratch_shapes=[pltpu.VMEM((width // LANES, shots * rows, LANES), jnp.float32)] * 2,
        ),
        out_shape=[pltpu.HBM(shape, jnp.bfloat16) for shape in shapes],
        compiler_params=PARAMS,
        cost_estimate=SMALL,
        name="shrink",
    )(meta, table, level, after, *spectra)


def updated_of(meta, restored, table, block, receivers, onto, passes, after):
    _, shots, rows, width = restored[0].shape
    samples = table.shape[1]
    chips = table.shape[0] // width
    group = min(shots, max(1, 256 // rows))
    by_shots = lambda step, meta: (0, step, 0, 0)
    in_specs = [whole(table.shape), ANYWHERE]
    in_specs += [pl.BlockSpec((array.shape[0], group, rows, width), by_shots) for array in restored]
    operands = [meta, table, after, *restored]
    if onto is not None:
        in_specs.append(ANYWHERE)
        operands.append(onto)
    out_specs = [
        pl.BlockSpec((group, rows, samples), lambda step, meta: (step, block(meta), 0)),
        whole((8, LANES)),
    ]
    out_shape = [
        pltpu.HBM((shots, receivers, samples), jnp.float32),
        pltpu.HBM((8, LANES), jnp.float32),
    ]
    if passes:
        out_specs.append(pl.BlockSpec((chips, group, rows, width), by_shots))
        out_shape.append(pltpu.HBM((chips, shots, rows, width), jnp.bfloat16))
    return pl.pallas_call(
        functools.partial(update_kernel, len(restored), passes),
        grid_spec=pltpu.PrefetchScalarGridSpec(
            num_scalar_prefetch=1,
            grid=(shots // group,),
            in_specs=in_specs,
            out_specs=out_specs,
            scratch_shapes=[pltpu.VMEM((group * rows, 2 * F), jnp.bfloat16)],
        ),
        out_shape=out_shape,
        input_output_aliases={} if onto is None else {len(operands) - 1: 0},
        compiler_params=pltpu.CompilerParams(vmem_limit_bytes=24 * 1024 * 1024),
        cost_estimate=SMALL,
        name="update",
    )(*operands)


def swapped(array):
    return lax.all_to_all(array, "shot", split_axis=0, concat_axis=0, tiled=True)


def sent(array, distance):
    peers = lax.axis_size("shot")
    return lax.ppermute(array, "shot", [(i, i ^ distance) for i in range(peers)])


def edges(estimate, observed):
    peers = lax.axis_size("shot")
    up = [(i, i + 1) for i in range(peers - 1)]
    down = [(j, i) for i, j in up]
    tail = jnp.concatenate([estimate[-2:], observed[-1:]])
    head = jnp.concatenate([estimate[:2], observed[:1]])
    return lax.ppermute(tail, "shot", up), lax.ppermute(head, "shot", down)


def part_of_halves(array, start, stop):
    shots, receivers, samples = array.shape
    halves = array.reshape(shots, 2, receivers // 2, samples)[:, :, start:stop]
    return halves.reshape(shots, 2 * (stop - start), samples)


def turns(steps):
    lags = (("other", 0), ("own", 0), ("shrink", 1), ("update own", 2), ("update other", 3))
    for turn in range(steps + 3):
        for name, lag in lags:
            if 0 <= turn - lag < steps:
                yield name, turn - lag


def to_chips(arrays):
    far = {chip: sent(arrays[chip], 2 * chip) for chip in range(len(arrays) // 2, len(arrays))}
    near = {chip: sent(arrays[chip], 2 * chip) for chip in range(1, len(arrays) // 2)}
    return [arrays[0], *[{**near, **far}[chip] for chip in range(1, len(arrays))]]


def to_devices(arrays):
    count = len(arrays)
    order = [*range(count // 2, count, 2), *range(count // 2 + 1, count, 2)]
    order += [*range(2, count // 2, 2), *range(3, count // 2, 2), 1]
    moved = {slot: sent(arrays[slot], slot) for slot in order}
    return [arrays[0], *[moved[slot] for slot in range(1, count)]]


def in_pairs(estimate, observed, delays, thresholds, rows):
    shots, receivers, samples = estimate.shape
    peers = lax.axis_size("shot")
    rank = lax.axis_index("shot")
    total = delays.shape[0]
    chips = peers // 2
    share = F // chips
    steps = receivers // 2 // rows
    core = rank % 2
    meta = jnp.concatenate(
        [jnp.stack([rank * shots, core, 1 - core]), rank ^ jnp.arange(peers, dtype=jnp.int32)]
    ).astype(jnp.int32)
    forward, inverse = (jnp.asarray(table) for table in time_tables(samples, chips))
    table = jnp.asarray(shot_table(total))
    levels = jnp.tile(lax.dynamic_slice_in_dim(thresholds, rank // 2 * share, share), 2)[None, :]
    early = edges(part_of_halves(estimate, 0, rows), part_of_halves(observed, 0, rows))
    late = None
    last, updated, energy = levels, None, 0.0
    packed, ahead, behind, passed = {}, {}, {}, {}
    for name, step in turns(steps):
        side = 1 if name.endswith("own") else 2
        block = lambda meta, side=side, step=step: meta[side] * steps + step
        if name in ("own", "other"):
            edge_block = block
            if step == 0:
                edge_block = lambda meta, side=side: meta[side]
            else:
                edge_block = lambda meta, side=side, step=step: meta[side] * (steps - 1) + step - 1
            mode = "joined" if name == "own" else "packed"
            spectra, power = spectra_of(
                meta,
                delays,
                (estimate, observed, *(late if step else early)),
                forward,
                block,
                edge_block,
                rows,
                peers,
                mode,
                packed.pop(step) if mode == "joined" else None,
                last,
            )
            last = power
            energy = energy + power
            if mode == "joined":
                ahead[step] = to_chips(spectra)
            else:
                packed[step] = sent(spectra[0], 1)
            if late is None and steps > 1:
                later = lax.optimization_barrier((estimate, observed, power))
                late = edges(*[part_of_halves(array, rows, receivers // 2) for array in later[:2]])
        elif name == "shrink":
            direct = step == steps - 1
            shrunk = shrunk_of(meta, ahead.pop(step), table, levels, not direct, last)
            last = shrunk[0]
            behind[step] = to_devices(shrunk) if direct else to_chips(shrunk)
        elif name == "update own":
            direct = step == steps - 1
            restored = behind.pop(step)
            if direct:
                passed[step] = restored[1::2]
                restored = restored[::2]
            updated, last, *partner = updated_of(
                meta, restored, inverse, block, receivers, updated, not direct, last
            )
            if not direct:
                passed[step] = [sent(partner[0], 1)]
        else:
            updated, last = updated_of(
                meta, passed.pop(step), inverse, block, receivers, updated, False, last
            )
    return updated, energy


def spectral_by_einsum(stepped, forward, inverse, table, level, peers):
    shots, receivers, samples = stepped.shape
    total = table.shape[1]
    share = F // peers
    spectra = jnp.einsum(
        "srt,tdpf->dpfsr",
        stepped,
        forward.reshape(samples, peers, 2, share),
        preferred_element_type=jnp.float32,
    ).astype(jnp.bfloat16)
    mixed = swapped(spectra).transpose(1, 2, 0, 3, 4).reshape(2, share, total, receivers)
    cosine, sine = table[:total], table[total:]
    across = jnp.stack([jnp.stack([cosine, sine]), jnp.stack([-sine, cosine])])
    wave = jnp.einsum("pqks,qfsr->pfkr", across, mixed, preferred_element_type=jnp.float32)
    magnitude = jnp.sqrt(wave[0] * wave[0] + wave[1] * wave[1])
    bound = level[:, None, None]
    factor = jnp.maximum(magnitude - bound, 0.0) / jnp.maximum(magnitude, bound)
    shrunk = (wave * factor[None]).astype(jnp.bfloat16)
    back = jnp.stack([jnp.stack([cosine, -sine]), jnp.stack([sine, cosine])])
    restored = jnp.einsum(
        "pqks,qfkr->pfsr", back, shrunk, preferred_element_type=jnp.float32
    ).astype(jnp.bfloat16)
    restored = restored.reshape(2, share, peers, shots, receivers).transpose(2, 0, 1, 3, 4)
    return jnp.einsum(
        "dpft,dpfsr->srt",
        inverse.reshape(peers, 2, share, samples),
        swapped(restored),
        preferred_element_type=jnp.float32,
    )


def by_einsum(estimate, observed, delays, thresholds, rows):
    shots, receivers, samples = estimate.shape
    peers = lax.axis_size("shot")
    rank = lax.axis_index("shot")
    share = F // peers
    meta = jnp.reshape(rank * shots, (1,)).astype(jnp.int32)
    sides = edges(estimate, observed)
    energy = 0.0
    parts = []
    for index in range(receivers // rows):
        part, power = stepped_of(meta, delays, (estimate, observed, *sides), rows, index)
        energy = energy + power
        parts.append(part)
    forward, inverse = (jnp.asarray(table) for table in time_tables(samples, peers))
    table = jnp.asarray(shot_table(delays.shape[0]))
    level = lax.dynamic_slice_in_dim(thresholds, rank * share, share)
    stepped = jnp.concatenate(parts, axis=1)
    return spectral_by_einsum(stepped, forward, inverse, table, level, peers), energy


def local(estimate, observed, random_source_delays, thresholds):
    receivers, samples = estimate.shape[1:]
    peers = lax.axis_size("shot")
    rows = min(16, receivers)
    paired = (
        peers >= 4
        and peers & (peers - 1) == 0
        and (4 * F // peers) % LANES == 0
        and receivers % (2 * rows) == 0
    )
    path = in_pairs if paired else by_einsum
    updated, energy = path(estimate, observed, random_source_delays, thresholds, rows)
    misfit = lax.psum(jnp.sum(energy, axis=1), "patch") / (
        receivers * lax.axis_size("patch") * samples
    )
    return updated, misfit


def solution(mesh):
    in_specs = (P("shot", "patch", None), P("shot", "patch", None), P(), P())
    out_specs = (P("shot", "patch", None), P("shot"))
    return jax.shard_map(local, mesh=mesh, in_specs=in_specs, out_specs=out_specs, check_vma=False)
```

```python
import functools

import jax
import jax.numpy as jnp
import ml_dtypes
import numpy as np
from jax import lax
from jax.experimental import pallas as pl
from jax.experimental.pallas import tpu as pltpu
from jax.sharding import PartitionSpec as P

F = 512
SOURCE_SPACING = 512
JITTER = 256
STEP = 0.5
LANES = 128
NEAR = SOURCE_SPACING - JITTER
FAR = SOURCE_SPACING + JITTER
HALO = 3


def time_tables(samples, blocks):
    freq = np.arange(F, dtype=np.int32)
    sample = np.arange(samples, dtype=np.int32)
    phase = (freq[:, None] * sample[None, :] % samples).astype(np.float32)
    angle = np.float32(2.0 * np.pi) * phase / np.float32(samples)
    root = np.sqrt(np.float32(samples))
    weight = np.where(freq == 0, 1.0, 2.0).astype(np.float32)[:, None] / root
    forward = np.stack([np.cos(angle) / root, -np.sin(angle) / root])
    inverse = np.stack([weight * np.cos(angle), -weight * np.sin(angle)])

    def ordered(table):
        table = table.astype(np.float32).astype(ml_dtypes.bfloat16)
        table = table.reshape(2, blocks, F // blocks, samples).transpose(1, 0, 2, 3)
        return table.reshape(2 * F, samples)

    return np.ascontiguousarray(ordered(forward).T), ordered(inverse)


def shot_table(shots):
    index = np.arange(shots, dtype=np.int32)
    phase = (index[:, None] * index[None, :] % shots).astype(np.float32)
    angle = np.float32(2.0 * np.pi) * phase / np.float32(shots)
    root = np.sqrt(np.float32(shots))
    table = np.concatenate([np.cos(angle) / root, np.sin(angle) / root])
    return table.astype(np.float32).astype(ml_dtypes.bfloat16)


def band(meta_ref, slot, width):
    return pl.ds(pl.multiple_of(meta_ref[1 + slot] * width, width), width)


def blend_into(
    meta_ref, delay_ref, est_ref, obs_ref, before_ref, after_ref, energy_ref, est32, res32, store
):
    shots, rows, samples = est_ref.shape
    columns = samples // LANES
    margin = (FAR - NEAR) // LANES
    inner = (samples - NEAR) // LANES
    skip = NEAR // LANES
    total = delay_ref.shape[0]
    first = meta_ref[0]
    lane = lax.broadcasted_iota(jnp.int32, (1, rows, LANES), 2)

    def ahead(shot):
        shot = jnp.clip(shot, 0, total - 2)
        return jnp.clip(SOURCE_SPACING + delay_ref[shot + 1] - delay_ref[shot], NEAR + 1, FAR - 1)

    def window(field, slot, start):
        column, rest = start // LANES, start % LANES
        wide = field[slot, pl.ds(column, inner + 1)]
        turned = pltpu.roll(
            wide.reshape((inner + 1) * rows, LANES), (LANES - rest) % LANES, 1
        ).reshape(inner + 1, rows, LANES)
        return jnp.where(lane < LANES - rest, turned[:-1], turned[1:])

    def blended(field, slot, shot):
        later = window(field, slot + 1, margin * LANES + NEAR - ahead(shot))
        earlier = window(field, slot - 1, margin * LANES + ahead(shot - 1))
        return later, earlier

    def fill(field, slot, values):
        blank = jnp.zeros((margin, rows, LANES), jnp.float32)
        field[slot, pl.ds(0, margin)] = blank
        field[slot, pl.ds(margin + columns, margin)] = blank
        for column in range(columns):
            field[slot, margin + column] = values(column)

    def cut(ref, shot):
        return lambda column: ref[shot, :, column * LANES : (column + 1) * LANES].astype(jnp.float32)

    for slot in range(2):
        fill(est32, slot, cut(before_ref, slot))
        fill(est32, shots + 2 + slot, cut(after_ref, slot))

    def load(shot, carry):
        fill(est32, shot + 2, cut(est_ref, shot))
        return carry

    lax.fori_loop(0, shots, load, 0, unroll=2)

    def residual(place, values):
        shot = first + place - 1
        inside = jnp.logical_and(shot >= 0, shot < total)
        later, earlier = blended(est32, place + 1, shot)
        power = jnp.zeros((rows, LANES), jnp.float32)
        cells = []
        for column in range(columns):
            cell = est32[place + 1, margin + column]
            if column >= skip:
                cell = cell + later[column - skip]
            if column < inner:
                cell = cell + earlier[column]
            cell = jnp.where(inside, values(column) - cell, 0.0)
            power = power + cell * cell
            cells.append(cell)
        fill(res32, place, lambda column: cells[column])
        return power

    residual(0, cut(before_ref, 2))
    residual(shots + 1, cut(after_ref, 2))

    def middle(shot, carry):
        power = residual(shot + 1, cut(obs_ref, shot))
        energy_ref[pl.ds(shot, 1), :] = jnp.sum(power, axis=0, keepdims=True)
        return carry

    lax.fori_loop(0, shots, middle, 0, unroll=4)

    def step(shot, carry):
        later, earlier = blended(res32, shot + 1, first + shot)
        for column in range(columns):
            cell = res32[shot + 1, margin + column]
            if column >= skip:
                cell = cell + later[column - skip]
            if column < inner:
                cell = cell + earlier[column]
            cell = est32[shot + 2, margin + column] + STEP * cell
            store(shot, column, cell.astype(jnp.bfloat16))
        return carry

    lax.fori_loop(0, shots, step, 0, unroll=4)


def spectra_kernel(
    meta_ref, delay_ref, est_ref, obs_ref, before_ref, after_ref, table_ref, _, *refs
):
    *out_refs, energy_ref, est32, res32, stepped, result = refs
    shots, rows, samples = est_ref.shape
    width = out_refs[0].shape[2]

    def store(shot, column, values):
        start = pl.multiple_of(shot * rows, rows)
        stepped[pl.ds(start, rows), column * LANES : (column + 1) * LANES] = values

    blend_into(
        meta_ref, delay_ref, est_ref, obs_ref, before_ref, after_ref, energy_ref, est32, res32, store
    )
    held = result.shape[0]
    group = held // rows

    def transform(part, carry):
        start = pl.multiple_of(part * held, held)
        result[...] = jnp.dot(
            stepped[pl.ds(start, held), :], table_ref[...], preferred_element_type=jnp.float32
        ).astype(jnp.bfloat16)
        for slot, ref in enumerate(out_refs):
            ref[pl.ds(part * group, group)] = result[:, band(meta_ref, slot, width)].reshape(
                group, rows, width
            )
        return carry

    lax.fori_loop(0, shots // group, transform, 0)


def step_kernel(
    meta_ref, delay_ref, est_ref, obs_ref, before_ref, after_ref, out_ref, energy_ref, est32, res32
):
    def store(shot, column, values):
        out_ref[shot, :, column * LANES : (column + 1) * LANES] = values

    blend_into(
        meta_ref, delay_ref, est_ref, obs_ref, before_ref, after_ref, energy_ref, est32, res32, store
    )


def shots_kernel(meta_ref, table_ref, level_ref, _, *refs):
    *refs, wide, back = refs
    spectra_refs, out_refs = refs[: len(refs) // 2], refs[len(refs) // 2 :]
    held, rows, width = out_refs[0].shape
    shots = wide.shape[0] // rows
    half = width // 2

    def place(slot):
        size = held * rows
        return pl.ds(pl.multiple_of(meta_ref[1 + slot] * size, size), size)

    for slot, ref in zip(slots_of(len(spectra_refs)), spectra_refs):
        wide[place(slot), :] = ref[...].reshape(held * rows, width).astype(jnp.float32)
    level = level_ref[...]
    sign = jnp.where(
        lax.broadcasted_iota(jnp.int32, (1, width), 1) < half, jnp.float32(1.0), jnp.float32(-1.0)
    )

    def pair(index, carry):
        picks = [pl.ds(index * 2 + turn, shots, stride=rows) for turn in range(2)]
        block = jnp.concatenate([wide[pick, :] for pick in picks], axis=1).astype(jnp.bfloat16)
        both = jnp.dot(table_ref[...], block, preferred_element_type=jnp.float32)
        kept = []
        for turn in range(2):
            own = both[:, turn * width : (turn + 1) * width]
            wave = own[:shots] + sign * pltpu.roll(own[shots:], half, 1)
            power = wave * wave
            power = power + pltpu.roll(power, half, 1)
            factor = jnp.maximum(1.0 - level * lax.rsqrt(power), 0.0)
            kept.append((wave * factor).astype(jnp.bfloat16))
        both = jnp.dot(table_ref[...], jnp.concatenate(kept, axis=1), preferred_element_type=jnp.float32)
        for turn in range(2):
            own = both[:, turn * width : (turn + 1) * width]
            back[picks[turn], :] = own[:shots] - sign * pltpu.roll(own[shots:], half, 1)
        return carry

    lax.fori_loop(0, rows // 2, pair, 0, unroll=2)
    for slot, ref in enumerate(out_refs):
        ref[...] = back[place(slot), :].astype(jnp.bfloat16).reshape(held, rows, width)


def update_kernel(inputs, meta_ref, table_ref, _, *refs):
    restored_refs, (out_ref, turn_ref, whole_rows) = refs[:inputs], refs[-3:]
    held, rows, width = restored_refs[0].shape
    for slot, ref in zip(slots_of(inputs), restored_refs):
        whole_rows[:, band(meta_ref, slot, width)] = ref[...].reshape(held * rows, width)
    out_ref[...] = jnp.dot(
        whole_rows[...], table_ref[...], preferred_element_type=jnp.float32
    ).reshape(out_ref.shape)
    turn_ref[...] = jnp.zeros_like(turn_ref)


def whole(shape):
    return pl.BlockSpec(shape, lambda *_: (0,) * len(shape))


def blend_specs(shots, rows, samples, block, edge_block):
    at = lambda step, meta, delays: (0, block, 0)
    edge = lambda step, meta, delays: (0, edge_block, 0)
    return [
        pl.BlockSpec((shots, rows, samples), at),
        pl.BlockSpec((shots, rows, samples), at),
        pl.BlockSpec((HALO, rows, samples), edge),
        pl.BlockSpec((HALO, rows, samples), edge),
    ]


def blend_scratch(shots, rows, samples):
    columns = (samples + 2 * (FAR - NEAR)) // LANES
    return [
        pltpu.VMEM((shots + 4, columns, rows, LANES), jnp.float32),
        pltpu.VMEM((shots + 2, columns, rows, LANES), jnp.float32),
    ]


PARAMS = pltpu.CompilerParams(vmem_limit_bytes=60 * 1024 * 1024)
SMALL = pl.CostEstimate(flops=1024, bytes_accessed=1024, transcendentals=0)
ANYWHERE = pl.BlockSpec(memory_space=pl.ANY)


def spectra_of(meta, delays, fields, table, rows, block, edge_block, peers, after):
    shots, _, samples = fields[0].shape
    shape = (shots, rows, 2 * F // peers)
    group = min(shots, max(1, 256 // rows))
    *spectra, energy = pl.pallas_call(
        spectra_kernel,
        grid_spec=pltpu.PrefetchScalarGridSpec(
            num_scalar_prefetch=2,
            grid=(1,),
            in_specs=blend_specs(shots, rows, samples, block, edge_block)
            + [whole(table.shape), ANYWHERE],
            out_specs=[whole(shape)] * peers + [whole((shots, LANES))],
            scratch_shapes=blend_scratch(shots, rows, samples)
            + [
                pltpu.VMEM((shots * rows, samples), jnp.bfloat16),
                pltpu.VMEM((group * rows, 2 * F), jnp.bfloat16),
            ],
        ),
        out_shape=[pltpu.HBM(shape, jnp.bfloat16)] * peers + [pltpu.HBM((shots, LANES), jnp.float32)],
        compiler_params=PARAMS,
        cost_estimate=SMALL,
        name="spectra",
    )(meta, delays, *fields, table, after)
    return spectra, energy


def stepped_of(meta, delays, fields, rows, index):
    shots, _, samples = fields[0].shape
    return pl.pallas_call(
        step_kernel,
        grid_spec=pltpu.PrefetchScalarGridSpec(
            num_scalar_prefetch=2,
            grid=(1,),
            in_specs=blend_specs(shots, rows, samples, index, index),
            out_specs=[whole((shots, rows, samples)), whole((shots, LANES))],
            scratch_shapes=blend_scratch(shots, rows, samples),
        ),
        out_shape=[
            jax.ShapeDtypeStruct((shots, rows, samples), jnp.bfloat16),
            jax.ShapeDtypeStruct((shots, LANES), jnp.float32),
        ],
        compiler_params=PARAMS,
        name="stepped",
    )(meta, delays, *fields)


def shrunk_of(meta, spectra, table, level, after):
    shape = spectra[0][0].shape
    held, rows, width = shape
    peers = len(spectra)
    return pl.pallas_call(
        shots_kernel,
        grid_spec=pltpu.PrefetchScalarGridSpec(
            num_scalar_prefetch=1,
            grid=(1,),
            in_specs=[whole(table.shape), whole(level.shape), ANYWHERE]
            + [read(item, shape, lambda step: (0, 0, 0)) for item in spectra],
            out_specs=[whole(shape)] * peers,
            scratch_shapes=[pltpu.VMEM((peers * held * rows, width), jnp.float32)] * 2,
        ),
        out_shape=[pltpu.HBM(shape, jnp.bfloat16)] * peers,
        compiler_params=PARAMS,
        cost_estimate=SMALL,
        name="shrink",
    )(meta, table, level, after, *[array for array, _ in spectra])


def updated_of(meta, restored, table, block, receivers, onto, after):
    shots, rows, width = restored[0][0].shape
    samples = table.shape[1]
    group = min(shots, max(1, 256 // rows))
    in_specs = [whole(table.shape), ANYWHERE]
    in_specs += [read(item, (group, rows, width), lambda step: (step, 0, 0)) for item in restored]
    operands = [meta, table, after, *[array for array, _ in restored]]
    if onto is not None:
        in_specs.append(ANYWHERE)
        operands.append(onto)
    return pl.pallas_call(
        functools.partial(update_kernel, len(restored)),
        grid_spec=pltpu.PrefetchScalarGridSpec(
            num_scalar_prefetch=1,
            grid=(shots // group,),
            in_specs=in_specs,
            out_specs=[
                pl.BlockSpec((group, rows, samples), lambda step, meta: (step, block, 0)),
                whole((8, LANES)),
            ],
            scratch_shapes=[pltpu.VMEM((group * rows, 2 * F), jnp.bfloat16)],
        ),
        out_shape=[
            pltpu.HBM((shots, receivers, samples), jnp.float32),
            pltpu.HBM((8, LANES), jnp.float32),
        ],
        input_output_aliases={} if onto is None else {len(operands) - 1: 0},
        compiler_params=pltpu.CompilerParams(vmem_limit_bytes=24 * 1024 * 1024),
        cost_estimate=SMALL,
        name="update",
    )(*operands)


def swapped(array):
    return lax.all_to_all(array, "shot", split_axis=0, concat_axis=0, tiled=True)


def sent(array, distance):
    peers = lax.axis_size("shot")
    if distance == 1:
        groups = [[i, i ^ 1] for i in range(0, peers, 2)]
        return lax.all_gather(array, "shot", axis_index_groups=groups), distance
    return lax.ppermute(array, "shot", [(i, i ^ distance) for i in range(peers)]), 0


def held(array):
    return array, 0


def read(item, shape, where):
    _, distance = item
    if distance == 0:
        return pl.BlockSpec(shape, lambda step, meta, *_: where(step))
    return pl.BlockSpec(
        (None, *shape),
        lambda step, meta, *_: (jnp.where(meta[1] < meta[1 + distance], 1, 0), *where(step)),
    )


def slots_of(peers):
    far, near = list(range(peers // 2, peers)), list(range(2, peers // 2))
    order = [0, 1]
    while far or near:
        order += far[:2] + near[:1]
        far, near = far[2:], near[1:]
    return order


def exchanged(arrays):
    slots = slots_of(len(arrays))
    return [sent(arrays[slot], slot) if slot else held(arrays[slot]) for slot in slots]


def edges(estimate, observed):
    peers = lax.axis_size("shot")
    up = [(i, i + 1) for i in range(peers - 1)]
    down = [(j, i) for i, j in up]
    tail = jnp.concatenate([estimate[-2:], observed[-1:]])
    head = jnp.concatenate([estimate[:2], observed[:1]])
    return lax.ppermute(tail, "shot", up), lax.ppermute(head, "shot", down)


def chunks_of(receivers):
    if receivers == 128:
        return [(16, 7), (16, 6), (32, 2), (32, 1), (16, 1), (16, 0)]
    rows = min(16, receivers)
    return [(rows, index) for index in range(receivers // rows)][::-1]


def direct(estimate, observed, delays, thresholds):
    shots, receivers, samples = estimate.shape
    peers = lax.axis_size("shot")
    rank = lax.axis_index("shot")
    share = F // peers
    meta = jnp.concatenate(
        [jnp.reshape(rank * shots, (1,)), rank ^ jnp.arange(peers, dtype=jnp.int32)]
    ).astype(jnp.int32)
    forward, inverse = (jnp.asarray(table) for table in time_tables(samples, peers))
    table = jnp.asarray(shot_table(delays.shape[0]))
    levels = jnp.tile(lax.dynamic_slice_in_dim(thresholds, rank * share, share), 2)[None, :]
    chunks = chunks_of(receivers)
    rest = receivers - chunks[0][0]
    early = edges(estimate[:, rest:], observed[:, rest:])
    late = None
    last, updated, energy = levels, None, 0.0
    lag = 2
    ahead, behind = {}, {}
    for turn in range(len(chunks) + 2 * lag):
        if turn < len(chunks):
            rows, index = chunks[turn]
            spectra, power = spectra_of(
                meta,
                delays,
                (estimate, observed, *(late if turn else early)),
                forward,
                rows,
                index,
                index if turn else 0,
                peers,
                last,
            )
            last = power
            energy = energy + power
            ahead[turn] = exchanged(spectra)
            if turn == 0 and rest:
                later = lax.optimization_barrier((estimate, observed, power))
                late = edges(later[0][:, :rest], later[1][:, :rest])
        place = turn - lag
        if place in ahead:
            shrunk = shrunk_of(meta, ahead.pop(place), table, levels, last)
            last = shrunk[0]
            behind[place] = exchanged(shrunk)
        place = turn - 2 * lag
        if place in behind:
            updated, last = updated_of(
                meta, behind.pop(place), inverse, chunks[place][1], receivers, updated, last
            )
    return updated, energy


def spectral_by_einsum(stepped, forward, inverse, table, level, peers):
    shots, receivers, samples = stepped.shape
    total = table.shape[1]
    share = F // peers
    spectra = jnp.einsum(
        "srt,tdpf->dpfsr",
        stepped,
        forward.reshape(samples, peers, 2, share),
        preferred_element_type=jnp.float32,
    ).astype(jnp.bfloat16)
    mixed = swapped(spectra).transpose(1, 2, 0, 3, 4).reshape(2, share, total, receivers)
    cosine, sine = table[:total], table[total:]
    across = jnp.stack([jnp.stack([cosine, sine]), jnp.stack([-sine, cosine])])
    wave = jnp.einsum("pqks,qfsr->pfkr", across, mixed, preferred_element_type=jnp.float32)
    magnitude = jnp.sqrt(wave[0] * wave[0] + wave[1] * wave[1])
    bound = level[:, None, None]
    factor = jnp.maximum(magnitude - bound, 0.0) / jnp.maximum(magnitude, bound)
    shrunk = (wave * factor[None]).astype(jnp.bfloat16)
    back = jnp.stack([jnp.stack([cosine, -sine]), jnp.stack([sine, cosine])])
    restored = jnp.einsum(
        "pqks,qfkr->pfsr", back, shrunk, preferred_element_type=jnp.float32
    ).astype(jnp.bfloat16)
    restored = restored.reshape(2, share, peers, shots, receivers).transpose(2, 0, 1, 3, 4)
    return jnp.einsum(
        "dpft,dpfsr->srt",
        inverse.reshape(peers, 2, share, samples),
        swapped(restored),
        preferred_element_type=jnp.float32,
    )


def by_einsum(estimate, observed, delays, thresholds):
    shots, receivers, samples = estimate.shape
    peers = lax.axis_size("shot")
    rank = lax.axis_index("shot")
    share = F // peers
    rows = min(16, receivers)
    meta = jnp.reshape(rank * shots, (1,)).astype(jnp.int32)
    sides = edges(estimate, observed)
    energy = 0.0
    parts = []
    for index in range(receivers // rows):
        part, power = stepped_of(meta, delays, (estimate, observed, *sides), rows, index)
        energy = energy + power
        parts.append(part)
    forward, inverse = (jnp.asarray(table) for table in time_tables(samples, peers))
    table = jnp.asarray(shot_table(delays.shape[0]))
    level = lax.dynamic_slice_in_dim(thresholds, rank * share, share)
    stepped = jnp.concatenate(parts, axis=1)
    return spectral_by_einsum(stepped, forward, inverse, table, level, peers), energy


def local(estimate, observed, random_source_delays, thresholds):
    receivers, samples = estimate.shape[1:]
    peers = lax.axis_size("shot")
    filled = peers >= 4 and peers & (peers - 1) == 0 and (2 * F // peers) % LANES == 0
    path = direct if filled else by_einsum
    updated, energy = path(estimate, observed, random_source_delays, thresholds)
    misfit = lax.psum(jnp.sum(energy, axis=1), "patch") / (
        receivers * lax.axis_size("patch") * samples
    )
    return updated, misfit


def solution(mesh):
    in_specs = (P("shot", "patch", None), P("shot", "patch", None), P(), P())
    out_specs = (P("shot", "patch", None), P("shot"))
    return jax.shard_map(local, mesh=mesh, in_specs=in_specs, out_specs=out_specs, check_vma=False)
```

```python
import functools

import jax
import jax.numpy as jnp
import ml_dtypes
import numpy as np
from jax import lax
from jax.experimental import pallas as pl
from jax.experimental.pallas import tpu as pltpu
from jax.sharding import PartitionSpec as P

F = 512
SOURCE_SPACING = 512
JITTER = 256
STEP = 0.5
LANES = 128
NEAR = SOURCE_SPACING - JITTER
FAR = SOURCE_SPACING + JITTER
HALO = 3


def time_tables(samples, blocks):
    freq = np.arange(F, dtype=np.int32)
    sample = np.arange(samples, dtype=np.int32)
    phase = (freq[:, None] * sample[None, :] % samples).astype(np.float32)
    angle = np.float32(2.0 * np.pi) * phase / np.float32(samples)
    root = np.sqrt(np.float32(samples))
    weight = np.where(freq == 0, 1.0, 2.0).astype(np.float32)[:, None] / root
    forward = np.stack([np.cos(angle) / root, -np.sin(angle) / root])
    inverse = np.stack([weight * np.cos(angle), -weight * np.sin(angle)])

    def ordered(table):
        table = table.astype(np.float32).astype(ml_dtypes.bfloat16)
        table = table.reshape(2, blocks, F // blocks, samples).transpose(1, 0, 2, 3)
        return table.reshape(2 * F, samples)

    return np.ascontiguousarray(ordered(forward).T), ordered(inverse)


def shot_table(shots):
    index = np.arange(shots, dtype=np.int32)
    phase = (index[:, None] * index[None, :] % shots).astype(np.float32)
    angle = np.float32(2.0 * np.pi) * phase / np.float32(shots)
    root = np.sqrt(np.float32(shots))
    table = np.concatenate([np.cos(angle) / root, np.sin(angle) / root])
    return table.astype(np.float32).astype(ml_dtypes.bfloat16)


def band(meta_ref, slot, width):
    return pl.ds(pl.multiple_of(meta_ref[1 + slot] * width, width), width)


def blend_into(
    meta_ref, delay_ref, est_ref, obs_ref, before_ref, after_ref, energy_ref, est32, res32, store
):
    shots, rows, samples = est_ref.shape
    columns = samples // LANES
    margin = (FAR - NEAR) // LANES
    inner = (samples - NEAR) // LANES
    skip = NEAR // LANES
    total = delay_ref.shape[0]
    first = meta_ref[0]
    lane = lax.broadcasted_iota(jnp.int32, (1, rows, LANES), 2)

    def ahead(shot):
        shot = jnp.clip(shot, 0, total - 2)
        return jnp.clip(SOURCE_SPACING + delay_ref[shot + 1] - delay_ref[shot], NEAR + 1, FAR - 1)

    def window(field, slot, start):
        column, rest = start // LANES, start % LANES
        wide = field[slot, pl.ds(column, inner + 1)]
        turned = pltpu.roll(
            wide.reshape((inner + 1) * rows, LANES), (LANES - rest) % LANES, 1
        ).reshape(inner + 1, rows, LANES)
        return jnp.where(lane < LANES - rest, turned[:-1], turned[1:])

    def blended(field, slot, shot):
        later = window(field, slot + 1, margin * LANES + NEAR - ahead(shot))
        earlier = window(field, slot - 1, margin * LANES + ahead(shot - 1))
        return later, earlier

    def fill(field, slot, values):
        blank = jnp.zeros((margin, rows, LANES), jnp.float32)
        field[slot, pl.ds(0, margin)] = blank
        field[slot, pl.ds(margin + columns, margin)] = blank
        for column in range(columns):
            field[slot, margin + column] = values(column)

    def cut(ref, shot):
        return lambda column: ref[shot, :, column * LANES : (column + 1) * LANES].astype(jnp.float32)

    for slot in range(2):
        fill(est32, slot, cut(before_ref, slot))
        fill(est32, shots + 2 + slot, cut(after_ref, slot))

    def load(shot, carry):
        fill(est32, shot + 2, cut(est_ref, shot))
        return carry

    lax.fori_loop(0, shots, load, 0, unroll=2)

    def residual(place, values):
        shot = first + place - 1
        inside = jnp.logical_and(shot >= 0, shot < total)
        later, earlier = blended(est32, place + 1, shot)
        power = jnp.zeros((rows, LANES), jnp.float32)
        cells = []
        for column in range(columns):
            cell = est32[place + 1, margin + column]
            if column >= skip:
                cell = cell + later[column - skip]
            if column < inner:
                cell = cell + earlier[column]
            cell = jnp.where(inside, values(column) - cell, 0.0)
            power = power + cell * cell
            cells.append(cell)
        fill(res32, place, lambda column: cells[column])
        return power

    residual(0, cut(before_ref, 2))
    residual(shots + 1, cut(after_ref, 2))

    def middle(shot, carry):
        power = residual(shot + 1, cut(obs_ref, shot))
        energy_ref[pl.ds(shot, 1), :] = jnp.sum(power, axis=0, keepdims=True)
        return carry

    lax.fori_loop(0, shots, middle, 0, unroll=4)

    def step(shot, carry):
        later, earlier = blended(res32, shot + 1, first + shot)
        for column in range(columns):
            cell = res32[shot + 1, margin + column]
            if column >= skip:
                cell = cell + later[column - skip]
            if column < inner:
                cell = cell + earlier[column]
            cell = est32[shot + 2, margin + column] + STEP * cell
            store(shot, column, cell.astype(jnp.bfloat16))
        return carry

    lax.fori_loop(0, shots, step, 0, unroll=4)


def spectra_kernel(
    unused, meta_ref, delay_ref, est_ref, obs_ref, before_ref, after_ref, table_ref, *refs
):
    *out_refs, energy_ref, est32, res32, stepped, result = refs[unused:]
    shots, rows, samples = est_ref.shape
    width = out_refs[0].shape[2]

    def store(shot, column, values):
        start = pl.multiple_of(shot * rows, rows)
        stepped[pl.ds(start, rows), column * LANES : (column + 1) * LANES] = values

    blend_into(
        meta_ref, delay_ref, est_ref, obs_ref, before_ref, after_ref, energy_ref, est32, res32, store
    )
    held = result.shape[0]
    group = held // rows

    def transform(part, carry):
        start = pl.multiple_of(part * held, held)
        result[...] = jnp.dot(
            stepped[pl.ds(start, held), :], table_ref[...], preferred_element_type=jnp.float32
        ).astype(jnp.bfloat16)
        for slot, ref in enumerate(out_refs):
            ref[pl.ds(part * group, group)] = result[:, band(meta_ref, slot, width)].reshape(
                group, rows, width
            )
        return carry

    lax.fori_loop(0, shots // group, transform, 0)


def step_kernel(
    meta_ref, delay_ref, est_ref, obs_ref, before_ref, after_ref, out_ref, energy_ref, est32, res32
):
    def store(shot, column, values):
        out_ref[shot, :, column * LANES : (column + 1) * LANES] = values

    blend_into(
        meta_ref, delay_ref, est_ref, obs_ref, before_ref, after_ref, energy_ref, est32, res32, store
    )


def shots_kernel(unused, meta_ref, table_ref, level_ref, *refs):
    *refs, wide, back = refs[unused:]
    spectra_refs, out_refs = refs[: len(refs) // 2], refs[len(refs) // 2 :]
    held, rows, width = out_refs[0].shape
    shots = wide.shape[0] // rows
    half = width // 2

    def place(slot):
        size = held * rows
        return pl.ds(pl.multiple_of(meta_ref[1 + slot] * size, size), size)

    for slot, ref in zip(slots_of(len(spectra_refs)), spectra_refs):
        wide[place(slot), :] = ref[...].reshape(held * rows, width).astype(jnp.float32)
    level = level_ref[...]
    sign = jnp.where(
        lax.broadcasted_iota(jnp.int32, (1, width), 1) < half, jnp.float32(1.0), jnp.float32(-1.0)
    )

    def pair(index, carry):
        picks = [pl.ds(index * 2 + turn, shots, stride=rows) for turn in range(2)]
        block = jnp.concatenate([wide[pick, :] for pick in picks], axis=1).astype(jnp.bfloat16)
        both = jnp.dot(table_ref[...], block, preferred_element_type=jnp.float32)
        kept = []
        for turn in range(2):
            own = both[:, turn * width : (turn + 1) * width]
            wave = own[:shots] + sign * pltpu.roll(own[shots:], half, 1)
            power = wave * wave
            power = power + pltpu.roll(power, half, 1)
            factor = jnp.maximum(1.0 - level * lax.rsqrt(power), 0.0)
            kept.append((wave * factor).astype(jnp.bfloat16))
        both = jnp.dot(table_ref[...], jnp.concatenate(kept, axis=1), preferred_element_type=jnp.float32)
        for turn in range(2):
            own = both[:, turn * width : (turn + 1) * width]
            back[picks[turn], :] = own[:shots] - sign * pltpu.roll(own[shots:], half, 1)
        return carry

    lax.fori_loop(0, rows // 2, pair, 0, unroll=2)
    for slot, ref in enumerate(out_refs):
        ref[...] = back[place(slot), :].astype(jnp.bfloat16).reshape(held, rows, width)


def update_kernel(unused, inputs, meta_ref, table_ref, *refs):
    refs = refs[unused:]
    restored_refs, (out_ref, turn_ref, whole_rows) = refs[:inputs], refs[-3:]
    held, rows, width = restored_refs[0].shape
    for slot, ref in zip(slots_of(inputs), restored_refs):
        whole_rows[:, band(meta_ref, slot, width)] = ref[...].reshape(held * rows, width)
    out_ref[...] = jnp.dot(
        whole_rows[...], table_ref[...], preferred_element_type=jnp.float32
    ).reshape(out_ref.shape)
    turn_ref[...] = jnp.zeros_like(turn_ref)


def whole(shape):
    return pl.BlockSpec(shape, lambda *_: (0,) * len(shape))


def blend_specs(shots, rows, samples, block, edge_block):
    at = lambda step, meta, delays: (0, block, 0)
    edge = lambda step, meta, delays: (0, edge_block, 0)
    return [
        pl.BlockSpec((shots, rows, samples), at),
        pl.BlockSpec((shots, rows, samples), at),
        pl.BlockSpec((HALO, rows, samples), edge),
        pl.BlockSpec((HALO, rows, samples), edge),
    ]


def blend_scratch(shots, rows, samples):
    columns = (samples + 2 * (FAR - NEAR)) // LANES
    return [
        pltpu.VMEM((shots + 4, columns, rows, LANES), jnp.float32),
        pltpu.VMEM((shots + 2, columns, rows, LANES), jnp.float32),
    ]


PARAMS = pltpu.CompilerParams(vmem_limit_bytes=60 * 1024 * 1024)
SMALL = pl.CostEstimate(flops=1024, bytes_accessed=1024, transcendentals=0)
ANYWHERE = pl.BlockSpec(memory_space=pl.ANY)


def spectra_of(meta, delays, fields, table, rows, block, edge_block, peers, after):
    shots, _, samples = fields[0].shape
    shape = (shots, rows, 2 * F // peers)
    group = min(shots, max(1, 256 // rows))
    *spectra, energy = pl.pallas_call(
        functools.partial(spectra_kernel, len(after)),
        grid_spec=pltpu.PrefetchScalarGridSpec(
            num_scalar_prefetch=2,
            grid=(1,),
            in_specs=blend_specs(shots, rows, samples, block, edge_block)
            + [whole(table.shape)]
            + [ANYWHERE] * len(after),
            out_specs=[whole(shape)] * peers + [whole((shots, LANES))],
            scratch_shapes=blend_scratch(shots, rows, samples)
            + [
                pltpu.VMEM((shots * rows, samples), jnp.bfloat16),
                pltpu.VMEM((group * rows, 2 * F), jnp.bfloat16),
            ],
        ),
        out_shape=[pltpu.HBM(shape, jnp.bfloat16)] * peers + [pltpu.HBM((shots, LANES), jnp.float32)],
        compiler_params=PARAMS,
        cost_estimate=SMALL,
        name="spectra",
    )(meta, delays, *fields, table, *after)
    return spectra, energy


def stepped_of(meta, delays, fields, rows, index):
    shots, _, samples = fields[0].shape
    return pl.pallas_call(
        step_kernel,
        grid_spec=pltpu.PrefetchScalarGridSpec(
            num_scalar_prefetch=2,
            grid=(1,),
            in_specs=blend_specs(shots, rows, samples, index, index),
            out_specs=[whole((shots, rows, samples)), whole((shots, LANES))],
            scratch_shapes=blend_scratch(shots, rows, samples),
        ),
        out_shape=[
            jax.ShapeDtypeStruct((shots, rows, samples), jnp.bfloat16),
            jax.ShapeDtypeStruct((shots, LANES), jnp.float32),
        ],
        compiler_params=PARAMS,
        name="stepped",
    )(meta, delays, *fields)


def shrunk_of(meta, spectra, table, level, after):
    shape = spectra[0][0].shape
    held, rows, width = shape
    peers = len(spectra)
    return pl.pallas_call(
        functools.partial(shots_kernel, len(after)),
        grid_spec=pltpu.PrefetchScalarGridSpec(
            num_scalar_prefetch=1,
            grid=(1,),
            in_specs=[whole(table.shape), whole(level.shape)]
            + [ANYWHERE] * len(after)
            + [read(item, shape, lambda step: (0, 0, 0)) for item in spectra],
            out_specs=[whole(shape)] * peers,
            scratch_shapes=[pltpu.VMEM((peers * held * rows, width), jnp.float32)] * 2,
        ),
        out_shape=[pltpu.HBM(shape, jnp.bfloat16)] * peers,
        compiler_params=PARAMS,
        cost_estimate=SMALL,
        name="shrink",
    )(meta, table, level, *after, *[array for array, _ in spectra])


def updated_of(meta, restored, table, block, receivers, onto, after):
    shots, rows, width = restored[0][0].shape
    samples = table.shape[1]
    group = min(shots, max(1, 256 // rows))
    in_specs = [whole(table.shape)] + [ANYWHERE] * len(after)
    in_specs += [read(item, (group, rows, width), lambda step: (step, 0, 0)) for item in restored]
    operands = [meta, table, *after, *[array for array, _ in restored]]
    if onto is not None:
        in_specs.append(ANYWHERE)
        operands.append(onto)
    return pl.pallas_call(
        functools.partial(update_kernel, len(after), len(restored)),
        grid_spec=pltpu.PrefetchScalarGridSpec(
            num_scalar_prefetch=1,
            grid=(shots // group,),
            in_specs=in_specs,
            out_specs=[
                pl.BlockSpec((group, rows, samples), lambda step, meta: (step, block, 0)),
                whole((8, LANES)),
            ],
            scratch_shapes=[pltpu.VMEM((group * rows, 2 * F), jnp.bfloat16)],
        ),
        out_shape=[
            pltpu.HBM((shots, receivers, samples), jnp.float32),
            pltpu.HBM((8, LANES), jnp.float32),
        ],
        input_output_aliases={} if onto is None else {len(operands) - 1: 0},
        compiler_params=pltpu.CompilerParams(vmem_limit_bytes=24 * 1024 * 1024),
        cost_estimate=SMALL,
        name="update",
    )(*operands)


def swapped(array):
    return lax.all_to_all(array, "shot", split_axis=0, concat_axis=0, tiled=True)


def sent(array, distance):
    peers = lax.axis_size("shot")
    if distance == 1:
        groups = [[i, i ^ 1] for i in range(0, peers, 2)]
        return lax.all_gather(array, "shot", axis_index_groups=groups), distance
    return lax.ppermute(array, "shot", [(i, i ^ distance) for i in range(peers)]), 0


def held(array):
    return array, 0


def read(item, shape, where):
    _, distance = item
    if distance == 0:
        return pl.BlockSpec(shape, lambda step, meta, *_: where(step))
    return pl.BlockSpec(
        (None, *shape),
        lambda step, meta, *_: (jnp.where(meta[1] < meta[1 + distance], 1, 0), *where(step)),
    )


def slots_of(peers):
    return [0, 1, *range(2, min(3, peers // 2)), *range(peers // 2, peers), *range(3, peers // 2)]


def exchanged(arrays):
    slots = slots_of(len(arrays))
    return [sent(arrays[slot], slot) if slot else held(arrays[slot]) for slot in slots]


def edges(estimate, observed):
    peers = lax.axis_size("shot")
    up = [(i, i + 1) for i in range(peers - 1)]
    down = [(j, i) for i, j in up]
    tail = jnp.concatenate([estimate[-2:], observed[-1:]])
    head = jnp.concatenate([estimate[:2], observed[:1]])
    return lax.ppermute(tail, "shot", up), lax.ppermute(head, "shot", down)


def chunks_of(receivers):
    if receivers == 128:
        return [(16, 96), (32, 64), (32, 32), (32, 0), (16, 112)], 2
    rows = min(16, receivers)
    return [(rows, start) for start in range(0, receivers, rows)], 1


def edges_of(estimate, observed, chunks):
    order = sorted(chunks, key=lambda chunk: (-chunk[0], chunk[1]))
    cut = lambda array: jnp.concatenate([array[:, start : start + rows] for rows, start in order], axis=1)
    ends = [jnp.concatenate([array[:2], array[-2:]]) for array in (estimate, observed)]
    places, position = {}, 0
    for rows, start in order:
        places[start] = position // rows
        position += rows
    return edges(*[cut(array) for array in ends]), places


def direct(estimate, observed, delays, thresholds):
    shots, receivers, samples = estimate.shape
    peers = lax.axis_size("shot")
    rank = lax.axis_index("shot")
    share = F // peers
    meta = jnp.concatenate(
        [jnp.reshape(rank * shots, (1,)), rank ^ jnp.arange(peers, dtype=jnp.int32)]
    ).astype(jnp.int32)
    forward, inverse = (jnp.asarray(table) for table in time_tables(samples, peers))
    table = jnp.asarray(shot_table(delays.shape[0]))
    levels = jnp.tile(lax.dynamic_slice_in_dim(thresholds, rank * share, share), 2)[None, :]
    chunks, ahead = chunks_of(receivers)
    sides, places = edges_of(estimate, observed, chunks[:ahead])
    makers = [("spectra", 0)]
    for chunk in range(len(chunks)):
        makers += [("spectra", chunk + 1)] if chunk + 1 < len(chunks) and chunk == 0 else []
        makers += [("shrink", chunk)]
        makers += [("spectra", chunk + 2)] if chunk + 2 < len(chunks) else []
    last, updated, energy = levels, None, 0.0
    brought, exchanges = {}, []
    for place, (name, chunk) in enumerate(makers):
        rows, start = chunks[chunk]
        after = [last]
        if place >= 2:
            after += [array for array, _ in exchanges[place - 2][1:]]
        if name == "spectra":
            if chunk == ahead:
                later = lax.optimization_barrier((estimate, observed, energy))
                sides, places = edges_of(*later[:2], chunks[ahead:])
            blocks, power = spectra_of(
                meta,
                delays,
                (estimate, observed, *sides),
                forward,
                rows,
                start // rows,
                places[start],
                peers,
                after,
            )
            last = power
            energy = energy + power
        else:
            blocks = shrunk_of(meta, brought.pop(("spectra", chunk)), table, levels, after)
            last = blocks[0]
        exchanges.append(exchanged(blocks))
        brought[name, chunk] = exchanges[-1]
        ready = [chunk - 1] if name == "shrink" and chunk else []
        ready += [chunk] if place == len(makers) - 1 else []
        for done in ready:
            rows, start = chunks[done]
            updated, last = updated_of(
                meta, brought.pop(("shrink", done)), inverse, start // rows, receivers, updated, [last]
            )
    return updated, energy


def spectral_by_einsum(stepped, forward, inverse, table, level, peers):
    shots, receivers, samples = stepped.shape
    total = table.shape[1]
    share = F // peers
    spectra = jnp.einsum(
        "srt,tdpf->dpfsr",
        stepped,
        forward.reshape(samples, peers, 2, share),
        preferred_element_type=jnp.float32,
    ).astype(jnp.bfloat16)
    mixed = swapped(spectra).transpose(1, 2, 0, 3, 4).reshape(2, share, total, receivers)
    cosine, sine = table[:total], table[total:]
    across = jnp.stack([jnp.stack([cosine, sine]), jnp.stack([-sine, cosine])])
    wave = jnp.einsum("pqks,qfsr->pfkr", across, mixed, preferred_element_type=jnp.float32)
    magnitude = jnp.sqrt(wave[0] * wave[0] + wave[1] * wave[1])
    bound = level[:, None, None]
    factor = jnp.maximum(magnitude - bound, 0.0) / jnp.maximum(magnitude, bound)
    shrunk = (wave * factor[None]).astype(jnp.bfloat16)
    back = jnp.stack([jnp.stack([cosine, -sine]), jnp.stack([sine, cosine])])
    restored = jnp.einsum(
        "pqks,qfkr->pfsr", back, shrunk, preferred_element_type=jnp.float32
    ).astype(jnp.bfloat16)
    restored = restored.reshape(2, share, peers, shots, receivers).transpose(2, 0, 1, 3, 4)
    return jnp.einsum(
        "dpft,dpfsr->srt",
        inverse.reshape(peers, 2, share, samples),
        swapped(restored),
        preferred_element_type=jnp.float32,
    )


def by_einsum(estimate, observed, delays, thresholds):
    shots, receivers, samples = estimate.shape
    peers = lax.axis_size("shot")
    rank = lax.axis_index("shot")
    share = F // peers
    rows = min(16, receivers)
    meta = jnp.reshape(rank * shots, (1,)).astype(jnp.int32)
    sides = edges(estimate, observed)
    energy = 0.0
    parts = []
    for index in range(receivers // rows):
        part, power = stepped_of(meta, delays, (estimate, observed, *sides), rows, index)
        energy = energy + power
        parts.append(part)
    forward, inverse = (jnp.asarray(table) for table in time_tables(samples, peers))
    table = jnp.asarray(shot_table(delays.shape[0]))
    level = lax.dynamic_slice_in_dim(thresholds, rank * share, share)
    stepped = jnp.concatenate(parts, axis=1)
    return spectral_by_einsum(stepped, forward, inverse, table, level, peers), energy


def local(estimate, observed, random_source_delays, thresholds):
    receivers, samples = estimate.shape[1:]
    peers = lax.axis_size("shot")
    filled = peers >= 4 and peers & (peers - 1) == 0 and (2 * F // peers) % LANES == 0
    path = direct if filled else by_einsum
    updated, energy = path(estimate, observed, random_source_delays, thresholds)
    misfit = lax.psum(jnp.sum(energy, axis=1), "patch") / (
        receivers * lax.axis_size("patch") * samples
    )
    return updated, misfit


def solution(mesh):
    in_specs = (P("shot", "patch", None), P("shot", "patch", None), P(), P())
    out_specs = (P("shot", "patch", None), P("shot"))
    return jax.shard_map(local, mesh=mesh, in_specs=in_specs, out_specs=out_specs, check_vma=False)
```

```python
import functools

import jax
import jax.numpy as jnp
import ml_dtypes
import numpy as np
from jax import lax
from jax.experimental import pallas as pl
from jax.experimental.pallas import tpu as pltpu
from jax.sharding import PartitionSpec as P

F = 512
SOURCE_SPACING = 512
JITTER = 256
STEP = 0.5
LANES = 128
NEAR = SOURCE_SPACING - JITTER
FAR = SOURCE_SPACING + JITTER
HALO = 3


def time_tables(samples, blocks):
    freq = np.arange(F, dtype=np.int32)
    sample = np.arange(samples, dtype=np.int32)
    phase = (freq[:, None] * sample[None, :] % samples).astype(np.float32)
    angle = np.float32(2.0 * np.pi) * phase / np.float32(samples)
    root = np.sqrt(np.float32(samples))
    weight = np.where(freq == 0, 1.0, 2.0).astype(np.float32)[:, None] / root
    forward = np.stack([np.cos(angle) / root, -np.sin(angle) / root])
    inverse = np.stack([weight * np.cos(angle), -weight * np.sin(angle)])

    def ordered(table):
        table = table.astype(np.float32).astype(ml_dtypes.bfloat16)
        table = table.reshape(2, blocks, F // blocks, samples).transpose(1, 0, 2, 3)
        return table.reshape(2 * F, samples)

    return np.ascontiguousarray(ordered(forward).T), ordered(inverse)


def shot_table(shots):
    index = np.arange(shots, dtype=np.int32)
    phase = (index[:, None] * index[None, :] % shots).astype(np.float32)
    angle = np.float32(2.0 * np.pi) * phase / np.float32(shots)
    root = np.sqrt(np.float32(shots))
    table = np.concatenate([np.cos(angle) / root, np.sin(angle) / root])
    return table.astype(np.float32).astype(ml_dtypes.bfloat16)


def band(meta_ref, chip, width):
    return pl.ds(pl.multiple_of(meta_ref[3 + 2 * chip] // 2 * width, width), width)


def views(refs):
    return [ref.at[index] for ref in refs for index in range(ref.shape[0])]


def blend_into(
    meta_ref, delay_ref, est_ref, obs_ref, before_ref, after_ref, energy_ref, est32, res32, store
):
    shots, rows, samples = est_ref.shape
    columns = samples // LANES
    margin = (FAR - NEAR) // LANES
    inner = (samples - NEAR) // LANES
    skip = NEAR // LANES
    total = delay_ref.shape[0]
    first = meta_ref[0]
    lane = lax.broadcasted_iota(jnp.int32, (1, rows, LANES), 2)

    def ahead(shot):
        shot = jnp.clip(shot, 0, total - 2)
        return jnp.clip(SOURCE_SPACING + delay_ref[shot + 1] - delay_ref[shot], NEAR + 1, FAR - 1)

    def window(field, slot, start):
        column, rest = start // LANES, start % LANES
        wide = field[slot, pl.ds(column, inner + 1)]
        turned = pltpu.roll(
            wide.reshape((inner + 1) * rows, LANES), (LANES - rest) % LANES, 1
        ).reshape(inner + 1, rows, LANES)
        return jnp.where(lane < LANES - rest, turned[:-1], turned[1:])

    def blended(field, slot, shot):
        later = window(field, slot + 1, margin * LANES + NEAR - ahead(shot))
        earlier = window(field, slot - 1, margin * LANES + ahead(shot - 1))
        return later, earlier

    def fill(field, slot, values):
        blank = jnp.zeros((margin, rows, LANES), jnp.float32)
        field[slot, pl.ds(0, margin)] = blank
        field[slot, pl.ds(margin + columns, margin)] = blank
        for column in range(columns):
            field[slot, margin + column] = values(column)

    def cut(ref, shot):
        return lambda column: ref[shot, :, column * LANES : (column + 1) * LANES].astype(jnp.float32)

    for slot in range(2):
        fill(est32, slot, cut(before_ref, slot))
        fill(est32, shots + 2 + slot, cut(after_ref, slot))

    def load(shot, carry):
        fill(est32, shot + 2, cut(est_ref, shot))
        return carry

    lax.fori_loop(0, shots, load, 0, unroll=2)

    def residual(place, values):
        shot = first + place - 1
        inside = jnp.logical_and(shot >= 0, shot < total)
        later, earlier = blended(est32, place + 1, shot)
        power = jnp.zeros((rows, LANES), jnp.float32)
        cells = []
        for column in range(columns):
            cell = est32[place + 1, margin + column]
            if column >= skip:
                cell = cell + later[column - skip]
            if column < inner:
                cell = cell + earlier[column]
            cell = jnp.where(inside, values(column) - cell, 0.0)
            power = power + cell * cell
            cells.append(cell)
        fill(res32, place, lambda column: cells[column])
        return power

    residual(0, cut(before_ref, 2))
    residual(shots + 1, cut(after_ref, 2))

    def middle(shot, carry):
        power = residual(shot + 1, cut(obs_ref, shot))
        energy_ref[pl.ds(shot, 1), :] = jnp.sum(power, axis=0, keepdims=True)
        return carry

    lax.fori_loop(0, shots, middle, 0, unroll=4)

    def step(shot, carry):
        later, earlier = blended(res32, shot + 1, first + shot)
        for column in range(columns):
            cell = res32[shot + 1, margin + column]
            if column >= skip:
                cell = cell + later[column - skip]
            if column < inner:
                cell = cell + earlier[column]
            cell = est32[shot + 2, margin + column] + STEP * cell
            store(shot, column, cell.astype(jnp.bfloat16))
        return carry

    lax.fori_loop(0, shots, step, 0, unroll=4)


def spectra_kernel(outputs, packed, meta_ref, delay_ref, est_ref, obs_ref, before_ref, after_ref, table_ref, _, *refs):
    *refs, energy_ref, est32, res32, stepped, result = refs
    out_refs, partner_refs = refs[-outputs:], refs[:-outputs]
    shots, rows, samples = est_ref.shape
    width = out_refs[0].shape[3]

    def store(shot, column, values):
        start = pl.multiple_of(shot * rows, rows)
        stepped[pl.ds(start, rows), column * LANES : (column + 1) * LANES] = values

    blend_into(
        meta_ref, delay_ref, est_ref, obs_ref, before_ref, after_ref, energy_ref, est32, res32, store
    )
    held = result.shape[0]
    group = held // rows
    if packed:
        targets = [out_refs[0].at[chip] for chip in range(out_refs[0].shape[0])]
    else:
        targets = [ref.at[0] for ref in out_refs]

    def transform(part, carry):
        start = pl.multiple_of(part * held, held)
        result[...] = jnp.dot(
            stepped[pl.ds(start, held), :], table_ref[...], preferred_element_type=jnp.float32
        ).astype(jnp.bfloat16)
        for chip, target in enumerate(targets):
            target[pl.ds(part * group, group)] = result[:, band(meta_ref, chip, width)].reshape(
                group, rows, width
            )
        return carry

    lax.fori_loop(0, shots // group, transform, 0)
    for partner_ref in partner_refs:
        for chip, out_ref in enumerate(out_refs):
            out_ref[1] = partner_ref[chip]


def step_kernel(
    meta_ref, delay_ref, est_ref, obs_ref, before_ref, after_ref, out_ref, energy_ref, est32, res32
):
    def store(shot, column, values):
        out_ref[shot, :, column * LANES : (column + 1) * LANES] = values

    blend_into(
        meta_ref, delay_ref, est_ref, obs_ref, before_ref, after_ref, energy_ref, est32, res32, store
    )


def shots_kernel(inputs, meta_ref, table_ref, level_ref, _, *refs):
    *refs, wide, back = refs
    _, held, rows, width = refs[0].shape
    pieces, size, _ = wide.shape
    shots = size // rows
    half = width // 2

    def place(slot):
        size = held * rows
        return pl.ds(pl.multiple_of(meta_ref[3 + slot] * size, size), size)

    for slot, ref in enumerate(views(refs[:inputs])):
        block = ref[...].reshape(held * rows, width).astype(jnp.float32)
        for piece in range(pieces):
            wide[piece, place(slot), :] = block[:, piece * LANES : (piece + 1) * LANES]
    level = level_ref[...]
    sign = jnp.where(
        lax.broadcasted_iota(jnp.int32, (1, width), 1) < half, jnp.float32(1.0), jnp.float32(-1.0)
    )

    def receiver(index, carry):
        pick = pl.ds(index, shots, stride=rows)
        block = jnp.concatenate([wide.at[piece][pick, :] for piece in range(pieces)], axis=1)
        both = jnp.dot(
            table_ref[...], block.astype(jnp.bfloat16), preferred_element_type=jnp.float32
        )
        wave = both[:shots] + sign * pltpu.roll(both[shots:], half, 1)
        power = wave * wave
        power = power + pltpu.roll(power, half, 1)
        factor = jnp.maximum(1.0 - level * lax.rsqrt(power), 0.0)
        kept = (wave * factor).astype(jnp.bfloat16)
        both = jnp.dot(table_ref[...], kept, preferred_element_type=jnp.float32)
        both = both[:shots] - sign * pltpu.roll(both[shots:], half, 1)
        for piece in range(pieces):
            back.at[piece][pick, :] = both[:, piece * LANES : (piece + 1) * LANES]
        return carry

    lax.fori_loop(0, rows, receiver, 0, unroll=2)
    for slot, ref in enumerate(views(refs[inputs:])):
        block = jnp.concatenate([back[piece, place(slot), :] for piece in range(pieces)], axis=1)
        ref[...] = block.astype(jnp.bfloat16).reshape(held, rows, width)


def update_kernel(inputs, passes, meta_ref, table_ref, _, *refs):
    restored_refs, whole_rows = refs[:inputs], refs[-1]
    outputs = refs[-4:-1] if passes else refs[-3:-1]
    own = [restored_refs[0].at[chip] for chip in range(restored_refs[0].shape[0])]
    if inputs > 1:
        own = [ref.at[0] for ref in restored_refs]
    held, rows, width = own[0].shape
    for chip, ref in enumerate(own):
        whole_rows[:, band(meta_ref, chip, width)] = ref[...].reshape(held * rows, width)
    outputs[0][...] = jnp.dot(
        whole_rows[...], table_ref[...], preferred_element_type=jnp.float32
    ).reshape(outputs[0].shape)
    outputs[1][...] = jnp.zeros_like(outputs[1])
    if passes:
        for chip, ref in enumerate(restored_refs):
            outputs[2][chip] = ref[1]


def whole(shape):
    return pl.BlockSpec(shape, lambda *_: (0,) * len(shape))


def blend_specs(shots, rows, samples, block, edge_block):
    at = lambda step, meta, delays: (0, block(meta), 0)
    edge = lambda step, meta, delays: (0, edge_block(meta), 0)
    return [
        pl.BlockSpec((shots, rows, samples), at),
        pl.BlockSpec((shots, rows, samples), at),
        pl.BlockSpec((HALO, rows, samples), edge),
        pl.BlockSpec((HALO, rows, samples), edge),
    ]


def blend_scratch(shots, rows, samples):
    columns = (samples + 2 * (FAR - NEAR)) // LANES
    return [
        pltpu.VMEM((shots + 4, columns, rows, LANES), jnp.float32),
        pltpu.VMEM((shots + 2, columns, rows, LANES), jnp.float32),
    ]


PARAMS = pltpu.CompilerParams(vmem_limit_bytes=60 * 1024 * 1024)
SMALL = pl.CostEstimate(flops=1024, bytes_accessed=1024, transcendentals=0)
ANYWHERE = pl.BlockSpec(memory_space=pl.ANY)


def spectra_of(meta, delays, fields, table, block, edge_block, rows, peers, mode, partner, after):
    shots, _, samples = fields[0].shape
    chips = peers // 2
    block_shape = (shots, rows, 2 * F // chips)
    shapes = {
        "apart": [(1, *block_shape)] * chips,
        "packed": [(chips, *block_shape)],
        "joined": [(2, *block_shape)] * chips,
    }[mode]
    group = min(shots, max(1, 256 // rows))
    partners = [] if partner is None else [partner]
    start = lambda step: (0, 0, 0, 0)
    *spectra, energy = pl.pallas_call(
        functools.partial(spectra_kernel, len(shapes), mode == "packed"),
        grid_spec=pltpu.PrefetchScalarGridSpec(
            num_scalar_prefetch=2,
            grid=(1,),
            in_specs=blend_specs(shots, rows, samples, block, edge_block)
            + [whole(table.shape), ANYWHERE]
            + [read(item, (chips, *block_shape), start) for item in partners],
            out_specs=[whole(shape) for shape in shapes] + [whole((shots, LANES))],
            scratch_shapes=blend_scratch(shots, rows, samples)
            + [
                pltpu.VMEM((shots * rows, samples), jnp.bfloat16),
                pltpu.VMEM((group * rows, 2 * F), jnp.bfloat16),
            ],
        ),
        out_shape=[pltpu.HBM(shape, jnp.bfloat16) for shape in shapes]
        + [pltpu.HBM((shots, LANES), jnp.float32)],
        compiler_params=PARAMS,
        cost_estimate=SMALL,
        name="spectra_" + mode,
    )(meta, delays, *fields, table, after, *[array for array, _ in partners])
    return spectra, energy


def stepped_of(meta, delays, fields, rows, index):
    shots, _, samples = fields[0].shape
    block = lambda meta: index
    return pl.pallas_call(
        step_kernel,
        grid_spec=pltpu.PrefetchScalarGridSpec(
            num_scalar_prefetch=2,
            grid=(1,),
            in_specs=blend_specs(shots, rows, samples, block, block),
            out_specs=[whole((shots, rows, samples)), whole((shots, LANES))],
            scratch_shapes=blend_scratch(shots, rows, samples),
        ),
        out_shape=[
            jax.ShapeDtypeStruct((shots, rows, samples), jnp.bfloat16),
            jax.ShapeDtypeStruct((shots, LANES), jnp.float32),
        ],
        compiler_params=PARAMS,
        name="stepped",
    )(meta, delays, *fields)


def shrunk_of(meta, spectra, table, level, joined, after):
    count, here, rows, width = spectra[0][0].shape[-4:]
    shots = table.shape[1]
    peers = shots // here
    size = shots * rows * width
    shapes = [(2, here, rows, width)] * (peers // 2) if joined else [(1, here, rows, width)] * peers
    start = lambda step: (0, 0, 0, 0)
    return pl.pallas_call(
        functools.partial(shots_kernel, len(spectra)),
        grid_spec=pltpu.PrefetchScalarGridSpec(
            num_scalar_prefetch=1,
            grid=(1,),
            in_specs=[whole(table.shape), whole(level.shape), ANYWHERE]
            + [read(item, (count, here, rows, width), start) for item in spectra],
            out_specs=[whole(shape) for shape in shapes],
            scratch_shapes=[pltpu.VMEM((width // LANES, shots * rows, LANES), jnp.float32)] * 2,
        ),
        out_shape=[pltpu.HBM(shape, jnp.bfloat16) for shape in shapes],
        compiler_params=PARAMS,
        cost_estimate=SMALL,
        name="shrink",
    )(meta, table, level, after, *[array for array, _ in spectra])


def updated_of(meta, restored, table, block, receivers, onto, passes, after):
    count, shots, rows, width = restored[0][0].shape[-4:]
    samples = table.shape[1]
    chips = table.shape[0] // width
    group = min(shots, max(1, 256 // rows))
    by_shots = lambda step, meta: (0, step, 0, 0)
    in_specs = [whole(table.shape), ANYWHERE]
    in_specs += [
        read(item, (count, group, rows, width), lambda step: (0, step, 0, 0)) for item in restored
    ]
    operands = [meta, table, after, *[array for array, _ in restored]]
    if onto is not None:
        in_specs.append(ANYWHERE)
        operands.append(onto)
    out_specs = [
        pl.BlockSpec((group, rows, samples), lambda step, meta: (step, block(meta), 0)),
        whole((8, LANES)),
    ]
    out_shape = [
        pltpu.HBM((shots, receivers, samples), jnp.float32),
        pltpu.HBM((8, LANES), jnp.float32),
    ]
    if passes:
        out_specs.append(pl.BlockSpec((chips, group, rows, width), by_shots))
        out_shape.append(pltpu.HBM((chips, shots, rows, width), jnp.bfloat16))
    return pl.pallas_call(
        functools.partial(update_kernel, len(restored), passes),
        grid_spec=pltpu.PrefetchScalarGridSpec(
            num_scalar_prefetch=1,
            grid=(shots // group,),
            in_specs=in_specs,
            out_specs=out_specs,
            scratch_shapes=[pltpu.VMEM((group * rows, 2 * F), jnp.bfloat16)],
        ),
        out_shape=out_shape,
        input_output_aliases={} if onto is None else {len(operands) - 1: 0},
        compiler_params=PARAMS,
        cost_estimate=SMALL,
        name="update",
    )(*operands)


def swapped(array):
    return lax.all_to_all(array, "shot", split_axis=0, concat_axis=0, tiled=True)


def sent(array, distance):
    peers = lax.axis_size("shot")
    if distance == 1:
        groups = [[i, i ^ 1] for i in range(0, peers, 2)]
        return lax.all_gather(array, "shot", axis_index_groups=groups), distance
    return lax.ppermute(array, "shot", [(i, i ^ distance) for i in range(peers)]), 0


def sent_all(arrays, distances):
    half = lax.axis_size("shot") // 2
    order = sorted(range(len(arrays)), key=lambda index: distances[index] < half)
    moved = {i: sent(arrays[i], distances[i]) if distances[i] else held(arrays[i]) for i in order}
    return [moved[index] for index in range(len(arrays))]


def held(array):
    return array, 0


def read(item, shape, where):
    _, distance = item
    if distance == 0:
        return pl.BlockSpec(shape, lambda step, meta, *_: where(step))
    return pl.BlockSpec(
        (None, *shape),
        lambda step, meta, *_: (jnp.where(meta[3] < meta[3 + distance], 1, 0), *where(step)),
    )


def edges(estimate, observed):
    peers = lax.axis_size("shot")
    up = [(i, i + 1) for i in range(peers - 1)]
    down = [(j, i) for i, j in up]
    tail = jnp.concatenate([estimate[-2:], observed[-1:]])
    head = jnp.concatenate([estimate[:2], observed[:1]])
    return lax.ppermute(tail, "shot", up), lax.ppermute(head, "shot", down)


def part_of_halves(array, start, stop):
    shots, receivers, samples = array.shape
    halves = array.reshape(shots, 2, receivers // 2, samples)[:, :, start:stop]
    return halves.reshape(shots, 2 * (stop - start), samples)


def turns(steps):
    work = [("own", 0), ("other", 0)]
    work += [("other", 1), ("own", 1)] if steps > 1 else []
    work += [("shrink", 0)]
    work += [("other", step) for step in range(2, min(4, steps))]
    for step in range(2, steps + 1):
        work += [("own", step)] if step < steps else []
        work += [("shrink", step - 1)]
        work += [("update own", step - 2)]
        work += [("update other", step - 3)] if step > 2 else []
        work += [("other", step + 2)] if step + 2 < steps else []
    for step in range(max(0, steps - 1), steps):
        work += [("update other", step - 1)] if step > 1 else []
        work += [("update own", step), ("update other", step)]
    done = {step for name, step in work if name == "update other"}
    return work + [("update other", step) for step in range(steps) if step not in done]


def in_pairs(estimate, observed, delays, thresholds, rows):
    shots, receivers, samples = estimate.shape
    peers = lax.axis_size("shot")
    rank = lax.axis_index("shot")
    total = delays.shape[0]
    chips = peers // 2
    share = F // chips
    steps = receivers // 2 // rows
    core = rank % 2
    meta = jnp.concatenate(
        [jnp.stack([rank * shots, core, 1 - core]), rank ^ jnp.arange(peers, dtype=jnp.int32)]
    ).astype(jnp.int32)
    forward, inverse = (jnp.asarray(table) for table in time_tables(samples, chips))
    table = jnp.asarray(shot_table(total))
    levels = jnp.tile(lax.dynamic_slice_in_dim(thresholds, rank // 2 * share, share), 2)[None, :]
    ahead_steps = min(2, steps)
    early = edges(*[part_of_halves(array, 0, ahead_steps * rows) for array in (estimate, observed)])
    late = None
    last, updated, energy = levels, None, 0.0
    packed, ahead, behind, passed = {}, {}, {}, {}
    for name, step in turns(steps):
        side = 1 if name.endswith("own") else 2
        block = lambda meta, side=side, step=step: meta[side] * steps + step
        if name in ("own", "other"):
            first, count = (0, ahead_steps) if step < ahead_steps else (ahead_steps, steps - ahead_steps)
            place = step - first
            edge_block = lambda meta, side=side, count=count, place=place: meta[side] * count + place
            mode = "apart" if step == 0 else "joined" if name == "own" else "packed"
            spectra, power = spectra_of(
                meta,
                delays,
                (estimate, observed, *(late if step >= ahead_steps else early)),
                forward,
                block,
                edge_block,
                rows,
                peers,
                mode,
                packed.pop(step) if mode == "joined" else None,
                last,
            )
            last = power
            energy = energy + power
            if mode == "packed":
                packed[step] = sent(spectra[0], 1)
            elif name == "own":
                ahead[step] = sent_all(spectra, range(0, peers, 2))
            else:
                other = sent_all(spectra, range(1, peers, 2))
                ahead[step] = [item for pair in zip(ahead[step], other) for item in pair]
            if late is None and step == 1 and steps > ahead_steps:
                later = lax.optimization_barrier((estimate, observed, power))
                late = edges(*[part_of_halves(a, ahead_steps * rows, receivers // 2) for a in later[:2]])
        elif name == "shrink":
            direct = step == steps - 1
            shrunk = shrunk_of(meta, ahead.pop(step), table, levels, not direct, last)
            last = shrunk[0]
            behind[step] = sent_all(shrunk, range(0, peers, 1 if direct else 2))
        elif name == "update own":
            direct = step == steps - 1
            restored = behind.pop(step)
            if direct:
                passed[step] = restored[1::2]
                restored = restored[::2]
            updated, last, *partner = updated_of(
                meta, restored, inverse, block, receivers, updated, not direct, last
            )
            if not direct:
                passed[step] = [sent(partner[0], 1)]
        else:
            updated, last = updated_of(
                meta, passed.pop(step), inverse, block, receivers, updated, False, last
            )
    return updated, energy


def spectral_by_einsum(stepped, forward, inverse, table, level, peers):
    shots, receivers, samples = stepped.shape
    total = table.shape[1]
    share = F // peers
    spectra = jnp.einsum(
        "srt,tdpf->dpfsr",
        stepped,
        forward.reshape(samples, peers, 2, share),
        preferred_element_type=jnp.float32,
    ).astype(jnp.bfloat16)
    mixed = swapped(spectra).transpose(1, 2, 0, 3, 4).reshape(2, share, total, receivers)
    cosine, sine = table[:total], table[total:]
    across = jnp.stack([jnp.stack([cosine, sine]), jnp.stack([-sine, cosine])])
    wave = jnp.einsum("pqks,qfsr->pfkr", across, mixed, preferred_element_type=jnp.float32)
    magnitude = jnp.sqrt(wave[0] * wave[0] + wave[1] * wave[1])
    bound = level[:, None, None]
    factor = jnp.maximum(magnitude - bound, 0.0) / jnp.maximum(magnitude, bound)
    shrunk = (wave * factor[None]).astype(jnp.bfloat16)
    back = jnp.stack([jnp.stack([cosine, -sine]), jnp.stack([sine, cosine])])
    restored = jnp.einsum(
        "pqks,qfkr->pfsr", back, shrunk, preferred_element_type=jnp.float32
    ).astype(jnp.bfloat16)
    restored = restored.reshape(2, share, peers, shots, receivers).transpose(2, 0, 1, 3, 4)
    return jnp.einsum(
        "dpft,dpfsr->srt",
        inverse.reshape(peers, 2, share, samples),
        swapped(restored),
        preferred_element_type=jnp.float32,
    )


def by_einsum(estimate, observed, delays, thresholds, rows):
    shots, receivers, samples = estimate.shape
    peers = lax.axis_size("shot")
    rank = lax.axis_index("shot")
    share = F // peers
    meta = jnp.reshape(rank * shots, (1,)).astype(jnp.int32)
    sides = edges(estimate, observed)
    energy = 0.0
    parts = []
    for index in range(receivers // rows):
        part, power = stepped_of(meta, delays, (estimate, observed, *sides), rows, index)
        energy = energy + power
        parts.append(part)
    forward, inverse = (jnp.asarray(table) for table in time_tables(samples, peers))
    table = jnp.asarray(shot_table(delays.shape[0]))
    level = lax.dynamic_slice_in_dim(thresholds, rank * share, share)
    stepped = jnp.concatenate(parts, axis=1)
    return spectral_by_einsum(stepped, forward, inverse, table, level, peers), energy


def local(estimate, observed, random_source_delays, thresholds):
    receivers, samples = estimate.shape[1:]
    peers = lax.axis_size("shot")
    rows = min(16, receivers)
    paired = (
        peers >= 4
        and peers & (peers - 1) == 0
        and (4 * F // peers) % LANES == 0
        and receivers % (2 * rows) == 0
    )
    path = in_pairs if paired else by_einsum
    updated, energy = path(estimate, observed, random_source_delays, thresholds, rows)
    misfit = lax.psum(jnp.sum(energy, axis=1), "patch") / (
        receivers * lax.axis_size("patch") * samples
    )
    return updated, misfit


def solution(mesh):
    in_specs = (P("shot", "patch", None), P("shot", "patch", None), P(), P())
    out_specs = (P("shot", "patch", None), P("shot"))
    return jax.shard_map(local, mesh=mesh, in_specs=in_specs, out_specs=out_specs, check_vma=False)
```

```python
import functools

import jax
import jax.numpy as jnp
import ml_dtypes
import numpy as np
from jax import lax
from jax.experimental import pallas as pl
from jax.experimental.pallas import tpu as pltpu
from jax.sharding import PartitionSpec as P

F = 512
SOURCE_SPACING = 512
JITTER = 256
STEP = 0.5
LANES = 128
NEAR = SOURCE_SPACING - JITTER
FAR = SOURCE_SPACING + JITTER
HALO = 3


def time_tables(samples, blocks):
    freq = np.arange(F, dtype=np.int32)
    sample = np.arange(samples, dtype=np.int32)
    phase = (freq[:, None] * sample[None, :] % samples).astype(np.float32)
    angle = np.float32(2.0 * np.pi) * phase / np.float32(samples)
    root = np.sqrt(np.float32(samples))
    weight = np.where(freq == 0, 1.0, 2.0).astype(np.float32)[:, None] / root
    forward = np.stack([np.cos(angle) / root, -np.sin(angle) / root])
    inverse = np.stack([weight * np.cos(angle), -weight * np.sin(angle)])

    def ordered(table):
        table = table.astype(np.float32).astype(ml_dtypes.bfloat16)
        table = table.reshape(2, blocks, F // blocks, samples).transpose(1, 0, 2, 3)
        return table.reshape(2 * F, samples)

    return np.ascontiguousarray(ordered(forward).T), ordered(inverse)


def shot_table(shots):
    index = np.arange(shots, dtype=np.int32)
    phase = (index[:, None] * index[None, :] % shots).astype(np.float32)
    angle = np.float32(2.0 * np.pi) * phase / np.float32(shots)
    root = np.sqrt(np.float32(shots))
    table = np.concatenate([np.cos(angle) / root, np.sin(angle) / root])
    return table.astype(np.float32).astype(ml_dtypes.bfloat16)


def band(meta_ref, slot, width):
    return pl.ds(pl.multiple_of(meta_ref[1 + slot] * width, width), width)


def blend_into(
    meta_ref, delay_ref, est_ref, obs_ref, before_ref, after_ref, energy_ref, est32, res32, store
):
    shots, rows, samples = est_ref.shape
    columns = samples // LANES
    margin = (FAR - NEAR) // LANES
    inner = (samples - NEAR) // LANES
    skip = NEAR // LANES
    total = delay_ref.shape[0]
    first = meta_ref[0]
    lane = lax.broadcasted_iota(jnp.int32, (1, rows, LANES), 2)

    def ahead(shot):
        shot = jnp.clip(shot, 0, total - 2)
        return jnp.clip(SOURCE_SPACING + delay_ref[shot + 1] - delay_ref[shot], NEAR + 1, FAR - 1)

    def window(field, slot, start):
        column, rest = start // LANES, start % LANES
        wide = field[slot, pl.ds(column, inner + 1)]
        turned = pltpu.roll(
            wide.reshape((inner + 1) * rows, LANES), (LANES - rest) % LANES, 1
        ).reshape(inner + 1, rows, LANES)
        return jnp.where(lane < LANES - rest, turned[:-1], turned[1:])

    def blended(field, slot, shot):
        later = window(field, slot + 1, margin * LANES + NEAR - ahead(shot))
        earlier = window(field, slot - 1, margin * LANES + ahead(shot - 1))
        return later, earlier

    def fill(field, slot, values):
        blank = jnp.zeros((margin, rows, LANES), jnp.float32)
        field[slot, pl.ds(0, margin)] = blank
        field[slot, pl.ds(margin + columns, margin)] = blank
        for column in range(columns):
            field[slot, margin + column] = values(column)

    def cut(ref, shot):
        return lambda column: ref[shot, :, column * LANES : (column + 1) * LANES].astype(jnp.float32)

    for slot in range(2):
        fill(est32, slot, cut(before_ref, slot))
        fill(est32, shots + 2 + slot, cut(after_ref, slot))

    def load(shot, carry):
        fill(est32, shot + 2, cut(est_ref, shot))
        return carry

    lax.fori_loop(0, shots, load, 0, unroll=2)

    def residual(place, values):
        shot = first + place - 1
        inside = jnp.logical_and(shot >= 0, shot < total)
        later, earlier = blended(est32, place + 1, shot)
        power = jnp.zeros((rows, LANES), jnp.float32)
        cells = []
        for column in range(columns):
            cell = est32[place + 1, margin + column]
            if column >= skip:
                cell = cell + later[column - skip]
            if column < inner:
                cell = cell + earlier[column]
            cell = jnp.where(inside, values(column) - cell, 0.0)
            power = power + cell * cell
            cells.append(cell)
        fill(res32, place, lambda column: cells[column])
        return power

    residual(0, cut(before_ref, 2))
    residual(shots + 1, cut(after_ref, 2))

    def middle(shot, carry):
        power = residual(shot + 1, cut(obs_ref, shot))
        energy_ref[pl.ds(shot, 1), :] = jnp.sum(power, axis=0, keepdims=True)
        return carry

    lax.fori_loop(0, shots, middle, 0, unroll=4)

    def step(shot, carry):
        later, earlier = blended(res32, shot + 1, first + shot)
        for column in range(columns):
            cell = res32[shot + 1, margin + column]
            if column >= skip:
                cell = cell + later[column - skip]
            if column < inner:
                cell = cell + earlier[column]
            cell = est32[shot + 2, margin + column] + STEP * cell
            store(shot, column, cell.astype(jnp.bfloat16))
        return carry

    lax.fori_loop(0, shots, step, 0, unroll=4)


def spectra_kernel(
    meta_ref, delay_ref, est_ref, obs_ref, before_ref, after_ref, table_ref, _, *refs
):
    *out_refs, energy_ref, est32, res32, stepped, result = refs
    shots, rows, samples = est_ref.shape
    width = out_refs[0].shape[2]

    def store(shot, column, values):
        start = pl.multiple_of(shot * rows, rows)
        stepped[pl.ds(start, rows), column * LANES : (column + 1) * LANES] = values

    blend_into(
        meta_ref, delay_ref, est_ref, obs_ref, before_ref, after_ref, energy_ref, est32, res32, store
    )
    held = result.shape[0]
    group = held // rows

    def transform(part, carry):
        start = pl.multiple_of(part * held, held)
        result[...] = jnp.dot(
            stepped[pl.ds(start, held), :], table_ref[...], preferred_element_type=jnp.float32
        ).astype(jnp.bfloat16)
        for slot, ref in enumerate(out_refs):
            ref[pl.ds(part * group, group)] = result[:, band(meta_ref, slot, width)].reshape(
                group, rows, width
            )
        return carry

    lax.fori_loop(0, shots // group, transform, 0)


def step_kernel(
    meta_ref, delay_ref, est_ref, obs_ref, before_ref, after_ref, out_ref, energy_ref, est32, res32
):
    def store(shot, column, values):
        out_ref[shot, :, column * LANES : (column + 1) * LANES] = values

    blend_into(
        meta_ref, delay_ref, est_ref, obs_ref, before_ref, after_ref, energy_ref, est32, res32, store
    )


def shots_kernel(meta_ref, table_ref, level_ref, _, *refs):
    *refs, wide, back = refs
    spectra_refs, out_refs = refs[: len(refs) // 2], refs[len(refs) // 2 :]
    held, rows, width = out_refs[0].shape
    shots = wide.shape[0] // rows
    half = width // 2

    def place(slot):
        size = held * rows
        return pl.ds(pl.multiple_of(meta_ref[1 + slot] * size, size), size)

    for slot, ref in enumerate(spectra_refs):
        wide[place(slot), :] = ref[...].reshape(held * rows, width).astype(jnp.float32)
    level = level_ref[...]
    sign = jnp.where(
        lax.broadcasted_iota(jnp.int32, (1, width), 1) < half, jnp.float32(1.0), jnp.float32(-1.0)
    )

    def pair(index, carry):
        picks = [pl.ds(index * 2 + turn, shots, stride=rows) for turn in range(2)]
        block = jnp.concatenate([wide[pick, :] for pick in picks], axis=1).astype(jnp.bfloat16)
        both = jnp.dot(table_ref[...], block, preferred_element_type=jnp.float32)
        kept = []
        for turn in range(2):
            own = both[:, turn * width : (turn + 1) * width]
            wave = own[:shots] + sign * pltpu.roll(own[shots:], half, 1)
            power = wave * wave
            power = power + pltpu.roll(power, half, 1)
            factor = jnp.maximum(1.0 - level * lax.rsqrt(power), 0.0)
            kept.append((wave * factor).astype(jnp.bfloat16))
        both = jnp.dot(table_ref[...], jnp.concatenate(kept, axis=1), preferred_element_type=jnp.float32)
        for turn in range(2):
            own = both[:, turn * width : (turn + 1) * width]
            back[picks[turn], :] = own[:shots] - sign * pltpu.roll(own[shots:], half, 1)
        return carry

    lax.fori_loop(0, rows // 2, pair, 0, unroll=2)
    for slot, ref in enumerate(out_refs):
        ref[...] = back[place(slot), :].astype(jnp.bfloat16).reshape(held, rows, width)


def update_kernel(inputs, meta_ref, table_ref, _, *refs):
    restored_refs, (out_ref, turn_ref, whole_rows) = refs[:inputs], refs[-3:]
    held, rows, width = restored_refs[0].shape
    for slot, ref in enumerate(restored_refs):
        whole_rows[:, band(meta_ref, slot, width)] = ref[...].reshape(held * rows, width)
    out_ref[...] = jnp.dot(
        whole_rows[...], table_ref[...], preferred_element_type=jnp.float32
    ).reshape(out_ref.shape)
    turn_ref[...] = jnp.zeros_like(turn_ref)


def whole(shape):
    return pl.BlockSpec(shape, lambda *_: (0,) * len(shape))


def blend_specs(shots, rows, samples, block, edge_block):
    at = lambda step, meta, delays: (0, block, 0)
    edge = lambda step, meta, delays: (0, edge_block, 0)
    return [
        pl.BlockSpec((shots, rows, samples), at),
        pl.BlockSpec((shots, rows, samples), at),
        pl.BlockSpec((HALO, rows, samples), edge),
        pl.BlockSpec((HALO, rows, samples), edge),
    ]


def blend_scratch(shots, rows, samples):
    columns = (samples + 2 * (FAR - NEAR)) // LANES
    return [
        pltpu.VMEM((shots + 4, columns, rows, LANES), jnp.float32),
        pltpu.VMEM((shots + 2, columns, rows, LANES), jnp.float32),
    ]


PARAMS = pltpu.CompilerParams(vmem_limit_bytes=60 * 1024 * 1024)
ANYWHERE = pl.BlockSpec(memory_space=pl.ANY)


def spectra_of(meta, delays, fields, table, rows, block, edge_block, peers, after):
    shots, _, samples = fields[0].shape
    shape = (shots, rows, 2 * F // peers)
    group = min(shots, max(1, 256 // rows))
    *spectra, energy = pl.pallas_call(
        spectra_kernel,
        grid_spec=pltpu.PrefetchScalarGridSpec(
            num_scalar_prefetch=2,
            grid=(1,),
            in_specs=blend_specs(shots, rows, samples, block, edge_block)
            + [whole(table.shape), ANYWHERE],
            out_specs=[whole(shape)] * peers + [whole((shots, LANES))],
            scratch_shapes=blend_scratch(shots, rows, samples)
            + [
                pltpu.VMEM((shots * rows, samples), jnp.bfloat16),
                pltpu.VMEM((group * rows, 2 * F), jnp.bfloat16),
            ],
        ),
        out_shape=[pltpu.HBM(shape, jnp.bfloat16)] * peers + [pltpu.HBM((shots, LANES), jnp.float32)],
        compiler_params=PARAMS,
        cost_estimate=pl.CostEstimate(
            flops=4 * F * shots * rows * samples,
            bytes_accessed=3 * 2 * shots * rows * samples + table.size * 2,
            transcendentals=0,
        ),
        name="spectra",
    )(meta, delays, *fields, table, after)
    return spectra, energy


def stepped_of(meta, delays, fields, rows, index):
    shots, _, samples = fields[0].shape
    return pl.pallas_call(
        step_kernel,
        grid_spec=pltpu.PrefetchScalarGridSpec(
            num_scalar_prefetch=2,
            grid=(1,),
            in_specs=blend_specs(shots, rows, samples, index, index),
            out_specs=[whole((shots, rows, samples)), whole((shots, LANES))],
            scratch_shapes=blend_scratch(shots, rows, samples),
        ),
        out_shape=[
            jax.ShapeDtypeStruct((shots, rows, samples), jnp.bfloat16),
            jax.ShapeDtypeStruct((shots, LANES), jnp.float32),
        ],
        compiler_params=PARAMS,
        name="stepped",
    )(meta, delays, *fields)


def shrunk_of(meta, spectra, table, level, after):
    shape = spectra[0].shape
    held, rows, width = shape
    peers = len(spectra)
    return pl.pallas_call(
        shots_kernel,
        grid_spec=pltpu.PrefetchScalarGridSpec(
            num_scalar_prefetch=1,
            grid=(1,),
            in_specs=[whole(table.shape), whole(level.shape), ANYWHERE]
            + [whole(shape)] * peers,
            out_specs=[whole(shape)] * peers,
            scratch_shapes=[pltpu.VMEM((peers * held * rows, width), jnp.float32)] * 2,
        ),
        out_shape=[pltpu.HBM(shape, jnp.bfloat16)] * peers,
        compiler_params=PARAMS,
        cost_estimate=pl.CostEstimate(
            flops=8 * (peers * held) ** 2 * rows * width,
            bytes_accessed=4 * peers * held * rows * width + 2 * table.size,
            transcendentals=peers * held * rows * width,
        ),
        name="shrink",
    )(meta, table, level, after, *spectra)


def updated_of(meta, restored, table, block, receivers, onto, after):
    shots, rows, width = restored[0].shape
    samples = table.shape[1]
    group = min(shots, max(1, 256 // rows))
    in_specs = [whole(table.shape), ANYWHERE]
    in_specs += [pl.BlockSpec((group, rows, width), lambda step, meta: (step, 0, 0))] * len(restored)
    operands = [meta, table, after, *restored]
    if onto is not None:
        in_specs.append(ANYWHERE)
        operands.append(onto)
    return pl.pallas_call(
        functools.partial(update_kernel, len(restored)),
        grid_spec=pltpu.PrefetchScalarGridSpec(
            num_scalar_prefetch=1,
            grid=(shots // group,),
            in_specs=in_specs,
            out_specs=[
                pl.BlockSpec((group, rows, samples), lambda step, meta: (step, block, 0)),
                whole((8, LANES)),
            ],
            scratch_shapes=[pltpu.VMEM((group * rows, 2 * F), jnp.bfloat16)],
        ),
        out_shape=[
            pltpu.HBM((shots, receivers, samples), jnp.float32),
            pltpu.HBM((8, LANES), jnp.float32),
        ],
        input_output_aliases={} if onto is None else {len(operands) - 1: 0},
        compiler_params=PARAMS,
        cost_estimate=pl.CostEstimate(
            flops=4 * F * shots * rows * samples,
            bytes_accessed=4 * F * shots * rows + 2 * table.size + 4 * shots * rows * samples,
            transcendentals=0,
        ),
        name="update",
    )(*operands)


def swapped(array):
    return lax.all_to_all(array, "shot", split_axis=0, concat_axis=0, tiled=True)


def exchanged(arrays):
    peers = len(arrays)
    return [
        lax.ppermute(array, "shot", [(i, i ^ slot) for i in range(peers)]) if slot else array
        for slot, array in enumerate(arrays)
    ]


def edges(estimate, observed):
    peers = lax.axis_size("shot")
    up = [(i, i + 1) for i in range(peers - 1)]
    down = [(j, i) for i, j in up]
    tail = jnp.concatenate([estimate[-2:], observed[-1:]])
    head = jnp.concatenate([estimate[:2], observed[:1]])
    return lax.ppermute(tail, "shot", up), lax.ppermute(head, "shot", down)


def chunks_of(receivers):
    if receivers == 128:
        return [(16, 0), (16, 1), (32, 1), (32, 2), (16, 6), (16, 7)]
    rows = min(16, receivers)
    return [(rows, index) for index in range(receivers // rows)]


def direct(estimate, observed, delays, thresholds):
    shots, receivers, samples = estimate.shape
    peers = lax.axis_size("shot")
    rank = lax.axis_index("shot")
    share = F // peers
    meta = jnp.concatenate(
        [jnp.reshape(rank * shots, (1,)), rank ^ jnp.arange(peers, dtype=jnp.int32)]
    ).astype(jnp.int32)
    forward, inverse = (jnp.asarray(table) for table in time_tables(samples, peers))
    table = jnp.asarray(shot_table(delays.shape[0]))
    levels = jnp.tile(lax.dynamic_slice_in_dim(thresholds, rank * share, share), 2)[None, :]
    chunks = chunks_of(receivers)
    sides = edges(estimate, observed)
    last, updated, energy = levels, None, 0.0
    lag = 2
    ahead, behind = {}, {}
    for turn in range(len(chunks) + 2 * lag):
        if turn < len(chunks):
            rows, index = chunks[turn]
            spectra, power = spectra_of(
                meta,
                delays,
                (estimate, observed, *sides),
                forward,
                rows,
                index,
                index,
                peers,
                last,
            )
            last = power
            energy = energy + power
            ahead[turn] = exchanged(spectra)
        place = turn - lag
        if place in ahead:
            shrunk = shrunk_of(meta, ahead.pop(place), table, levels, last)
            last = shrunk[0]
            behind[place] = exchanged(shrunk)
        place = turn - 2 * lag
        if place in behind:
            updated, last = updated_of(
                meta, behind.pop(place), inverse, chunks[place][1], receivers, updated, last
            )
    return updated, energy


def spectral_by_einsum(stepped, forward, inverse, table, level, peers):
    shots, receivers, samples = stepped.shape
    total = table.shape[1]
    share = F // peers
    spectra = jnp.einsum(
        "srt,tdpf->dpfsr",
        stepped,
        forward.reshape(samples, peers, 2, share),
        preferred_element_type=jnp.float32,
    ).astype(jnp.bfloat16)
    mixed = swapped(spectra).transpose(1, 2, 0, 3, 4).reshape(2, share, total, receivers)
    cosine, sine = table[:total], table[total:]
    across = jnp.stack([jnp.stack([cosine, sine]), jnp.stack([-sine, cosine])])
    wave = jnp.einsum("pqks,qfsr->pfkr", across, mixed, preferred_element_type=jnp.float32)
    magnitude = jnp.sqrt(wave[0] * wave[0] + wave[1] * wave[1])
    bound = level[:, None, None]
    factor = jnp.maximum(magnitude - bound, 0.0) / jnp.maximum(magnitude, bound)
    shrunk = (wave * factor[None]).astype(jnp.bfloat16)
    back = jnp.stack([jnp.stack([cosine, -sine]), jnp.stack([sine, cosine])])
    restored = jnp.einsum(
        "pqks,qfkr->pfsr", back, shrunk, preferred_element_type=jnp.float32
    ).astype(jnp.bfloat16)
    restored = restored.reshape(2, share, peers, shots, receivers).transpose(2, 0, 1, 3, 4)
    return jnp.einsum(
        "dpft,dpfsr->srt",
        inverse.reshape(peers, 2, share, samples),
        swapped(restored),
        preferred_element_type=jnp.float32,
    )


def by_einsum(estimate, observed, delays, thresholds):
    shots, receivers, samples = estimate.shape
    peers = lax.axis_size("shot")
    rank = lax.axis_index("shot")
    share = F // peers
    rows = min(16, receivers)
    meta = jnp.reshape(rank * shots, (1,)).astype(jnp.int32)
    sides = edges(estimate, observed)
    energy = 0.0
    parts = []
    for index in range(receivers // rows):
        part, power = stepped_of(meta, delays, (estimate, observed, *sides), rows, index)
        energy = energy + power
        parts.append(part)
    forward, inverse = (jnp.asarray(table) for table in time_tables(samples, peers))
    table = jnp.asarray(shot_table(delays.shape[0]))
    level = lax.dynamic_slice_in_dim(thresholds, rank * share, share)
    stepped = jnp.concatenate(parts, axis=1)
    return spectral_by_einsum(stepped, forward, inverse, table, level, peers), energy


def local(estimate, observed, random_source_delays, thresholds):
    receivers, samples = estimate.shape[1:]
    peers = lax.axis_size("shot")
    filled = peers >= 4 and peers & (peers - 1) == 0 and (2 * F // peers) % LANES == 0
    path = direct if filled else by_einsum
    updated, energy = path(estimate, observed, random_source_delays, thresholds)
    misfit = lax.psum(jnp.sum(energy, axis=1), "patch") / (
        receivers * lax.axis_size("patch") * samples
    )
    return updated, misfit


def solution(mesh):
    in_specs = (P("shot", "patch", None), P("shot", "patch", None), P(), P())
    out_specs = (P("shot", "patch", None), P("shot"))
    return jax.shard_map(local, mesh=mesh, in_specs=in_specs, out_specs=out_specs, check_vma=False)
```

```python
import functools

import jax
import jax.numpy as jnp
import ml_dtypes
import numpy as np
from jax import lax
from jax.experimental import pallas as pl
from jax.experimental.pallas import tpu as pltpu
from jax.sharding import PartitionSpec as P

F = 512
SOURCE_SPACING = 512
JITTER = 256
STEP = 0.5
LANES = 128
NEAR = SOURCE_SPACING - JITTER
FAR = SOURCE_SPACING + JITTER
HALO = 3


def time_tables(samples, blocks):
    freq = np.arange(F, dtype=np.int32)
    sample = np.arange(samples, dtype=np.int32)
    phase = (freq[:, None] * sample[None, :] % samples).astype(np.float32)
    angle = np.float32(2.0 * np.pi) * phase / np.float32(samples)
    root = np.sqrt(np.float32(samples))
    weight = np.where(freq == 0, 1.0, 2.0).astype(np.float32)[:, None] / root
    forward = np.stack([np.cos(angle) / root, -np.sin(angle) / root])
    inverse = np.stack([weight * np.cos(angle), -weight * np.sin(angle)])

    def ordered(table):
        table = table.astype(np.float32).astype(ml_dtypes.bfloat16)
        table = table.reshape(2, blocks, F // blocks, samples).transpose(1, 0, 2, 3)
        return table.reshape(2 * F, samples)

    return np.ascontiguousarray(ordered(forward).T), ordered(inverse)


def shot_table(shots):
    index = np.arange(shots, dtype=np.int32)
    phase = (index[:, None] * index[None, :] % shots).astype(np.float32)
    angle = np.float32(2.0 * np.pi) * phase / np.float32(shots)
    root = np.sqrt(np.float32(shots))
    table = np.concatenate([np.cos(angle) / root, np.sin(angle) / root])
    return table.astype(np.float32).astype(ml_dtypes.bfloat16)


def band(meta_ref, slot, width):
    return pl.ds(pl.multiple_of(meta_ref[1 + slot] * width, width), width)


def blend_into(
    meta_ref, delay_ref, est_ref, obs_ref, before_ref, after_ref, energy_ref, est32, res32, store
):
    shots, rows, samples = est_ref.shape
    columns = samples // LANES
    margin = (FAR - NEAR) // LANES
    inner = (samples - NEAR) // LANES
    skip = NEAR // LANES
    total = delay_ref.shape[0]
    first = meta_ref[0]
    lane = lax.broadcasted_iota(jnp.int32, (1, rows, LANES), 2)

    def ahead(shot):
        shot = jnp.clip(shot, 0, total - 2)
        return jnp.clip(SOURCE_SPACING + delay_ref[shot + 1] - delay_ref[shot], NEAR + 1, FAR - 1)

    def window(field, slot, start):
        column, rest = start // LANES, start % LANES
        wide = field[slot, pl.ds(column, inner + 1)]
        turned = pltpu.roll(
            wide.reshape((inner + 1) * rows, LANES), (LANES - rest) % LANES, 1
        ).reshape(inner + 1, rows, LANES)
        return jnp.where(lane < LANES - rest, turned[:-1], turned[1:])

    def blended(field, slot, shot):
        later = window(field, slot + 1, margin * LANES + NEAR - ahead(shot))
        earlier = window(field, slot - 1, margin * LANES + ahead(shot - 1))
        return later, earlier

    def fill(field, slot, values):
        blank = jnp.zeros((margin, rows, LANES), jnp.float32)
        field[slot, pl.ds(0, margin)] = blank
        field[slot, pl.ds(margin + columns, margin)] = blank
        for column in range(columns):
            field[slot, margin + column] = values(column)

    def cut(ref, shot):
        return lambda column: ref[shot, :, column * LANES : (column + 1) * LANES].astype(jnp.float32)

    for slot in range(2):
        fill(est32, slot, cut(before_ref, slot))
        fill(est32, shots + 2 + slot, cut(after_ref, slot))

    def load(shot, carry):
        fill(est32, shot + 2, cut(est_ref, shot))
        return carry

    lax.fori_loop(0, shots, load, 0, unroll=2)

    def residual(place, values):
        shot = first + place - 1
        inside = jnp.logical_and(shot >= 0, shot < total)
        later, earlier = blended(est32, place + 1, shot)
        power = jnp.zeros((rows, LANES), jnp.float32)
        cells = []
        for column in range(columns):
            cell = est32[place + 1, margin + column]
            if column >= skip:
                cell = cell + later[column - skip]
            if column < inner:
                cell = cell + earlier[column]
            cell = jnp.where(inside, values(column) - cell, 0.0)
            power = power + cell * cell
            cells.append(cell)
        fill(res32, place, lambda column: cells[column])
        return power

    residual(0, cut(before_ref, 2))
    residual(shots + 1, cut(after_ref, 2))

    def middle(shot, carry):
        power = residual(shot + 1, cut(obs_ref, shot))
        energy_ref[pl.ds(shot, 1), :] = jnp.sum(power, axis=0, keepdims=True)
        return carry

    lax.fori_loop(0, shots, middle, 0, unroll=4)

    def step(shot, carry):
        later, earlier = blended(res32, shot + 1, first + shot)
        for column in range(columns):
            cell = res32[shot + 1, margin + column]
            if column >= skip:
                cell = cell + later[column - skip]
            if column < inner:
                cell = cell + earlier[column]
            cell = est32[shot + 2, margin + column] + STEP * cell
            store(shot, column, cell.astype(jnp.bfloat16))
        return carry

    lax.fori_loop(0, shots, step, 0, unroll=4)


def spectra_kernel(
    meta_ref, delay_ref, est_ref, obs_ref, before_ref, after_ref, table_ref, _, *refs
):
    *out_refs, energy_ref, est32, res32, stepped, result = refs
    shots, rows, samples = est_ref.shape
    width = out_refs[0].shape[2]

    def store(shot, column, values):
        start = pl.multiple_of(shot * rows, rows)
        stepped[pl.ds(start, rows), column * LANES : (column + 1) * LANES] = values

    blend_into(
        meta_ref, delay_ref, est_ref, obs_ref, before_ref, after_ref, energy_ref, est32, res32, store
    )
    held = result.shape[0]
    group = held // rows

    def transform(part, carry):
        start = pl.multiple_of(part * held, held)
        result[...] = jnp.dot(
            stepped[pl.ds(start, held), :], table_ref[...], preferred_element_type=jnp.float32
        ).astype(jnp.bfloat16)
        for slot, ref in enumerate(out_refs):
            ref[pl.ds(part * group, group)] = result[:, band(meta_ref, slot, width)].reshape(
                group, rows, width
            )
        return carry

    lax.fori_loop(0, shots // group, transform, 0)


def step_kernel(
    meta_ref, delay_ref, est_ref, obs_ref, before_ref, after_ref, out_ref, energy_ref, est32, res32
):
    def store(shot, column, values):
        out_ref[shot, :, column * LANES : (column + 1) * LANES] = values

    blend_into(
        meta_ref, delay_ref, est_ref, obs_ref, before_ref, after_ref, energy_ref, est32, res32, store
    )


def shots_kernel(meta_ref, table_ref, level_ref, _, *refs):
    *refs, wide, back = refs
    spectra_refs, out_refs = refs[: len(refs) // 2], refs[len(refs) // 2 :]
    held, rows, width = out_refs[0].shape
    shots = wide.shape[0] // rows
    half = width // 2

    def place(slot):
        size = held * rows
        return pl.ds(pl.multiple_of(meta_ref[1 + slot] * size, size), size)

    for slot, ref in zip(slots_of(len(spectra_refs)), spectra_refs):
        wide[place(slot), :] = ref[...].reshape(held * rows, width).astype(jnp.float32)
    level = level_ref[...]
    sign = jnp.where(
        lax.broadcasted_iota(jnp.int32, (1, width), 1) < half, jnp.float32(1.0), jnp.float32(-1.0)
    )

    def pair(index, carry):
        picks = [pl.ds(index * 2 + turn, shots, stride=rows) for turn in range(2)]
        block = jnp.concatenate([wide[pick, :] for pick in picks], axis=1).astype(jnp.bfloat16)
        both = jnp.dot(table_ref[...], block, preferred_element_type=jnp.float32)
        kept = []
        for turn in range(2):
            own = both[:, turn * width : (turn + 1) * width]
            wave = own[:shots] + sign * pltpu.roll(own[shots:], half, 1)
            power = wave * wave
            power = power + pltpu.roll(power, half, 1)
            factor = jnp.maximum(1.0 - level * lax.rsqrt(power), 0.0)
            kept.append((wave * factor).astype(jnp.bfloat16))
        both = jnp.dot(table_ref[...], jnp.concatenate(kept, axis=1), preferred_element_type=jnp.float32)
        for turn in range(2):
            own = both[:, turn * width : (turn + 1) * width]
            back[picks[turn], :] = own[:shots] - sign * pltpu.roll(own[shots:], half, 1)
        return carry

    lax.fori_loop(0, rows // 2, pair, 0, unroll=2)
    for slot, ref in enumerate(out_refs):
        ref[...] = back[place(slot), :].astype(jnp.bfloat16).reshape(held, rows, width)


def update_kernel(inputs, meta_ref, table_ref, _, *refs):
    restored_refs, (out_ref, turn_ref, whole_rows) = refs[:inputs], refs[-3:]
    held, rows, width = restored_refs[0].shape
    for slot, ref in zip(slots_of(inputs), restored_refs):
        whole_rows[:, band(meta_ref, slot, width)] = ref[...].reshape(held * rows, width)
    out_ref[...] = jnp.dot(
        whole_rows[...], table_ref[...], preferred_element_type=jnp.float32
    ).reshape(out_ref.shape)
    turn_ref[...] = jnp.zeros_like(turn_ref)


def whole(shape):
    return pl.BlockSpec(shape, lambda *_: (0,) * len(shape))


def blend_specs(shots, rows, samples, block, edge_block):
    at = lambda step, meta, delays: (0, block, 0)
    edge = lambda step, meta, delays: (0, edge_block, 0)
    return [
        pl.BlockSpec((shots, rows, samples), at),
        pl.BlockSpec((shots, rows, samples), at),
        pl.BlockSpec((HALO, rows, samples), edge),
        pl.BlockSpec((HALO, rows, samples), edge),
    ]


def blend_scratch(shots, rows, samples):
    columns = (samples + 2 * (FAR - NEAR)) // LANES
    return [
        pltpu.VMEM((shots + 4, columns, rows, LANES), jnp.float32),
        pltpu.VMEM((shots + 2, columns, rows, LANES), jnp.float32),
    ]


PARAMS = pltpu.CompilerParams(vmem_limit_bytes=60 * 1024 * 1024)
ANYWHERE = pl.BlockSpec(memory_space=pl.ANY)


def spectra_of(meta, delays, fields, table, rows, block, edge_block, peers, after):
    shots, _, samples = fields[0].shape
    shape = (shots, rows, 2 * F // peers)
    group = min(shots, max(1, 256 // rows))
    *spectra, energy = pl.pallas_call(
        spectra_kernel,
        grid_spec=pltpu.PrefetchScalarGridSpec(
            num_scalar_prefetch=2,
            grid=(1,),
            in_specs=blend_specs(shots, rows, samples, block, edge_block)
            + [whole(table.shape), ANYWHERE],
            out_specs=[whole(shape)] * peers + [whole((shots, LANES))],
            scratch_shapes=blend_scratch(shots, rows, samples)
            + [
                pltpu.VMEM((shots * rows, samples), jnp.bfloat16),
                pltpu.VMEM((group * rows, 2 * F), jnp.bfloat16),
            ],
        ),
        out_shape=[pltpu.HBM(shape, jnp.bfloat16)] * peers + [pltpu.HBM((shots, LANES), jnp.float32)],
        compiler_params=PARAMS,
        cost_estimate=pl.CostEstimate(
            flops=4 * F * shots * rows * samples,
            bytes_accessed=3 * 2 * shots * rows * samples + table.size * 2,
            transcendentals=0,
        ),
        name="spectra",
    )(meta, delays, *fields, table, after)
    return spectra, energy


def stepped_of(meta, delays, fields, rows, index):
    shots, _, samples = fields[0].shape
    return pl.pallas_call(
        step_kernel,
        grid_spec=pltpu.PrefetchScalarGridSpec(
            num_scalar_prefetch=2,
            grid=(1,),
            in_specs=blend_specs(shots, rows, samples, index, index),
            out_specs=[whole((shots, rows, samples)), whole((shots, LANES))],
            scratch_shapes=blend_scratch(shots, rows, samples),
        ),
        out_shape=[
            jax.ShapeDtypeStruct((shots, rows, samples), jnp.bfloat16),
            jax.ShapeDtypeStruct((shots, LANES), jnp.float32),
        ],
        compiler_params=PARAMS,
        name="stepped",
    )(meta, delays, *fields)


def shrunk_of(meta, spectra, table, level, after):
    shape = spectra[0].shape
    held, rows, width = shape
    peers = len(spectra)
    return pl.pallas_call(
        shots_kernel,
        grid_spec=pltpu.PrefetchScalarGridSpec(
            num_scalar_prefetch=1,
            grid=(1,),
            in_specs=[whole(table.shape), whole(level.shape), ANYWHERE]
            + [whole(shape)] * peers,
            out_specs=[whole(shape)] * peers,
            scratch_shapes=[pltpu.VMEM((peers * held * rows, width), jnp.float32)] * 2,
        ),
        out_shape=[pltpu.HBM(shape, jnp.bfloat16)] * peers,
        compiler_params=PARAMS,
        cost_estimate=pl.CostEstimate(
            flops=8 * (peers * held) ** 2 * rows * width,
            bytes_accessed=4 * peers * held * rows * width + 2 * table.size,
            transcendentals=peers * held * rows * width,
        ),
        name="shrink",
    )(meta, table, level, after, *spectra)


def updated_of(meta, restored, table, block, receivers, onto, after):
    shots, rows, width = restored[0].shape
    samples = table.shape[1]
    group = min(shots, max(1, 256 // rows))
    in_specs = [whole(table.shape), ANYWHERE]
    in_specs += [pl.BlockSpec((group, rows, width), lambda step, meta: (step, 0, 0))] * len(restored)
    operands = [meta, table, after, *restored]
    if onto is not None:
        in_specs.append(ANYWHERE)
        operands.append(onto)
    return pl.pallas_call(
        functools.partial(update_kernel, len(restored)),
        grid_spec=pltpu.PrefetchScalarGridSpec(
            num_scalar_prefetch=1,
            grid=(shots // group,),
            in_specs=in_specs,
            out_specs=[
                pl.BlockSpec((group, rows, samples), lambda step, meta: (step, block, 0)),
                whole((8, LANES)),
            ],
            scratch_shapes=[pltpu.VMEM((group * rows, 2 * F), jnp.bfloat16)],
        ),
        out_shape=[
            jax.ShapeDtypeStruct((shots, receivers, samples), jnp.float32),
            jax.ShapeDtypeStruct((8, LANES), jnp.float32),
        ],
        input_output_aliases={} if onto is None else {len(operands) - 1: 0},
        compiler_params=pltpu.CompilerParams(vmem_limit_bytes=48 * 1024 * 1024),
        cost_estimate=pl.CostEstimate(
            flops=4 * F * shots * rows * samples,
            bytes_accessed=4 * F * shots * rows + 2 * table.size + 4 * shots * rows * samples,
            transcendentals=0,
        ),
        name="update",
    )(*operands)


def swapped(array):
    return lax.all_to_all(array, "shot", split_axis=0, concat_axis=0, tiled=True)


def slots_of(peers):
    order = [0]
    for slot in range(peers // 2):
        order += [peers // 2 + slot] + ([slot + 1] if slot + 1 < peers // 2 else [])
    return order


def exchanged(arrays):
    peers = len(arrays)
    return [
        lax.ppermute(arrays[slot], "shot", [(i, i ^ slot) for i in range(peers)]) if slot else arrays[0]
        for slot in slots_of(peers)
    ]


def edges(estimate, observed):
    peers = lax.axis_size("shot")
    up = [(i, i + 1) for i in range(peers - 1)]
    down = [(j, i) for i, j in up]
    tail = jnp.concatenate([estimate[-2:], observed[-1:]])
    head = jnp.concatenate([estimate[:2], observed[:1]])
    return lax.ppermute(tail, "shot", up), lax.ppermute(head, "shot", down)


def chunks_of(receivers):
    if receivers == 128:
        return [(16, 0), (16, 1), (32, 1), (32, 2), (16, 6), (16, 7)]
    rows = min(16, receivers)
    return [(rows, index) for index in range(receivers // rows)]


def direct(estimate, observed, delays, thresholds):
    shots, receivers, samples = estimate.shape
    peers = lax.axis_size("shot")
    rank = lax.axis_index("shot")
    share = F // peers
    meta = jnp.concatenate(
        [jnp.reshape(rank * shots, (1,)), rank ^ jnp.arange(peers, dtype=jnp.int32)]
    ).astype(jnp.int32)
    forward, inverse = (jnp.asarray(table) for table in time_tables(samples, peers))
    table = jnp.asarray(shot_table(delays.shape[0]))
    levels = jnp.tile(lax.dynamic_slice_in_dim(thresholds, rank * share, share), 2)[None, :]
    chunks = chunks_of(receivers)
    sides = edges(estimate, observed)
    last, updated, energy = levels, None, 0.0
    lag = 2
    ahead, behind = {}, {}
    for turn in range(len(chunks) + 2 * lag):
        if turn < len(chunks):
            rows, index = chunks[turn]
            spectra, power = spectra_of(
                meta,
                delays,
                (estimate, observed, *sides),
                forward,
                rows,
                index,
                index,
                peers,
                last,
            )
            last = power
            energy = energy + power
            ahead[turn] = exchanged(spectra)
        place = turn - lag
        if place in ahead:
            shrunk = shrunk_of(meta, ahead.pop(place), table, levels, last)
            last = shrunk[0]
            behind[place] = exchanged(shrunk)
        place = turn - 2 * lag
        if place in behind:
            updated, last = updated_of(
                meta, behind.pop(place), inverse, chunks[place][1], receivers, updated, last
            )
    return updated, energy


def spectral_by_einsum(stepped, forward, inverse, table, level, peers):
    shots, receivers, samples = stepped.shape
    total = table.shape[1]
    share = F // peers
    spectra = jnp.einsum(
        "srt,tdpf->dpfsr",
        stepped,
        forward.reshape(samples, peers, 2, share),
        preferred_element_type=jnp.float32,
    ).astype(jnp.bfloat16)
    mixed = swapped(spectra).transpose(1, 2, 0, 3, 4).reshape(2, share, total, receivers)
    cosine, sine = table[:total], table[total:]
    across = jnp.stack([jnp.stack([cosine, sine]), jnp.stack([-sine, cosine])])
    wave = jnp.einsum("pqks,qfsr->pfkr", across, mixed, preferred_element_type=jnp.float32)
    magnitude = jnp.sqrt(wave[0] * wave[0] + wave[1] * wave[1])
    bound = level[:, None, None]
    factor = jnp.maximum(magnitude - bound, 0.0) / jnp.maximum(magnitude, bound)
    shrunk = (wave * factor[None]).astype(jnp.bfloat16)
    back = jnp.stack([jnp.stack([cosine, -sine]), jnp.stack([sine, cosine])])
    restored = jnp.einsum(
        "pqks,qfkr->pfsr", back, shrunk, preferred_element_type=jnp.float32
    ).astype(jnp.bfloat16)
    restored = restored.reshape(2, share, peers, shots, receivers).transpose(2, 0, 1, 3, 4)
    return jnp.einsum(
        "dpft,dpfsr->srt",
        inverse.reshape(peers, 2, share, samples),
        swapped(restored),
        preferred_element_type=jnp.float32,
    )


def by_einsum(estimate, observed, delays, thresholds):
    shots, receivers, samples = estimate.shape
    peers = lax.axis_size("shot")
    rank = lax.axis_index("shot")
    share = F // peers
    rows = min(16, receivers)
    meta = jnp.reshape(rank * shots, (1,)).astype(jnp.int32)
    sides = edges(estimate, observed)
    energy = 0.0
    parts = []
    for index in range(receivers // rows):
        part, power = stepped_of(meta, delays, (estimate, observed, *sides), rows, index)
        energy = energy + power
        parts.append(part)
    forward, inverse = (jnp.asarray(table) for table in time_tables(samples, peers))
    table = jnp.asarray(shot_table(delays.shape[0]))
    level = lax.dynamic_slice_in_dim(thresholds, rank * share, share)
    stepped = jnp.concatenate(parts, axis=1)
    return spectral_by_einsum(stepped, forward, inverse, table, level, peers), energy


def local(estimate, observed, random_source_delays, thresholds):
    receivers, samples = estimate.shape[1:]
    peers = lax.axis_size("shot")
    filled = peers >= 4 and peers & (peers - 1) == 0 and (2 * F // peers) % LANES == 0
    path = direct if filled else by_einsum
    updated, energy = path(estimate, observed, random_source_delays, thresholds)
    misfit = lax.psum(jnp.sum(energy, axis=1), "patch") / (
        receivers * lax.axis_size("patch") * samples
    )
    return updated, misfit


def solution(mesh):
    in_specs = (P("shot", "patch", None), P("shot", "patch", None), P(), P())
    out_specs = (P("shot", "patch", None), P("shot"))
    return jax.shard_map(local, mesh=mesh, in_specs=in_specs, out_specs=out_specs, check_vma=False)
```

```python
import functools

import jax
import jax.numpy as jnp
import ml_dtypes
import numpy as np
from jax import lax
from jax.experimental import pallas as pl
from jax.experimental.pallas import tpu as pltpu
from jax.sharding import PartitionSpec as P

F = 512
SOURCE_SPACING = 512
JITTER = 256
STEP = 0.5
LANES = 128
NEAR = SOURCE_SPACING - JITTER
FAR = SOURCE_SPACING + JITTER
HALO = 3


def time_tables(samples, blocks):
    freq = np.arange(F, dtype=np.int32)
    sample = np.arange(samples, dtype=np.int32)
    phase = (freq[:, None] * sample[None, :] % samples).astype(np.float32)
    angle = np.float32(2.0 * np.pi) * phase / np.float32(samples)
    root = np.sqrt(np.float32(samples))
    weight = np.where(freq == 0, 1.0, 2.0).astype(np.float32)[:, None] / root
    forward = np.stack([np.cos(angle) / root, -np.sin(angle) / root])
    inverse = np.stack([weight * np.cos(angle), -weight * np.sin(angle)])

    def ordered(table):
        table = table.astype(np.float32).astype(ml_dtypes.bfloat16)
        table = table.reshape(2, blocks, F // blocks, samples).transpose(1, 0, 2, 3)
        return table.reshape(2 * F, samples)

    return np.ascontiguousarray(ordered(forward).T), ordered(inverse)


def shot_table(shots):
    index = np.arange(shots, dtype=np.int32)
    phase = (index[:, None] * index[None, :] % shots).astype(np.float32)
    angle = np.float32(2.0 * np.pi) * phase / np.float32(shots)
    root = np.sqrt(np.float32(shots))
    table = np.concatenate([np.cos(angle) / root, np.sin(angle) / root])
    return table.astype(np.float32).astype(ml_dtypes.bfloat16)


def band(meta_ref, slot, width):
    return pl.ds(pl.multiple_of(meta_ref[1 + slot] * width, width), width)


def blend_into(
    meta_ref, delay_ref, est_ref, obs_ref, before_ref, after_ref, energy_ref, est32, res32, store
):
    shots, rows, samples = est_ref.shape
    columns = samples // LANES
    margin = (FAR - NEAR) // LANES
    inner = (samples - NEAR) // LANES
    skip = NEAR // LANES
    total = delay_ref.shape[0]
    first = meta_ref[0]
    lane = lax.broadcasted_iota(jnp.int32, (1, rows, LANES), 2)

    def ahead(shot):
        shot = jnp.clip(shot, 0, total - 2)
        return jnp.clip(SOURCE_SPACING + delay_ref[shot + 1] - delay_ref[shot], NEAR + 1, FAR - 1)

    def window(field, slot, start):
        column, rest = start // LANES, start % LANES
        wide = field[slot, pl.ds(column, inner + 1)]
        turned = pltpu.roll(
            wide.reshape((inner + 1) * rows, LANES), (LANES - rest) % LANES, 1
        ).reshape(inner + 1, rows, LANES)
        return jnp.where(lane < LANES - rest, turned[:-1], turned[1:])

    def blended(field, slot, shot):
        later = window(field, slot + 1, margin * LANES + NEAR - ahead(shot))
        earlier = window(field, slot - 1, margin * LANES + ahead(shot - 1))
        return later, earlier

    def fill(field, slot, values):
        blank = jnp.zeros((margin, rows, LANES), jnp.float32)
        field[slot, pl.ds(0, margin)] = blank
        field[slot, pl.ds(margin + columns, margin)] = blank
        for column in range(columns):
            field[slot, margin + column] = values(column)

    def cut(ref, shot):
        return lambda column: ref[shot, :, column * LANES : (column + 1) * LANES].astype(jnp.float32)

    for slot in range(2):
        fill(est32, slot, cut(before_ref, slot))
        fill(est32, shots + 2 + slot, cut(after_ref, slot))

    def load(shot, carry):
        fill(est32, shot + 2, cut(est_ref, shot))
        return carry

    lax.fori_loop(0, shots, load, 0, unroll=2)

    def residual(place, values):
        shot = first + place - 1
        inside = jnp.logical_and(shot >= 0, shot < total)
        later, earlier = blended(est32, place + 1, shot)
        power = jnp.zeros((rows, LANES), jnp.float32)
        cells = []
        for column in range(columns):
            cell = est32[place + 1, margin + column]
            if column >= skip:
                cell = cell + later[column - skip]
            if column < inner:
                cell = cell + earlier[column]
            cell = jnp.where(inside, values(column) - cell, 0.0)
            power = power + cell * cell
            cells.append(cell)
        fill(res32, place, lambda column: cells[column])
        return power

    residual(0, cut(before_ref, 2))
    residual(shots + 1, cut(after_ref, 2))

    def middle(shot, carry):
        power = residual(shot + 1, cut(obs_ref, shot))
        energy_ref[pl.ds(shot, 1), :] = jnp.sum(power, axis=0, keepdims=True)
        return carry

    lax.fori_loop(0, shots, middle, 0, unroll=4)

    def step(shot, carry):
        later, earlier = blended(res32, shot + 1, first + shot)
        for column in range(columns):
            cell = res32[shot + 1, margin + column]
            if column >= skip:
                cell = cell + later[column - skip]
            if column < inner:
                cell = cell + earlier[column]
            cell = est32[shot + 2, margin + column] + STEP * cell
            store(shot, column, cell.astype(jnp.bfloat16))
        return carry

    lax.fori_loop(0, shots, step, 0, unroll=4)


def spectra_kernel(
    meta_ref, delay_ref, est_ref, obs_ref, before_ref, after_ref, table_ref, _, *refs
):
    *out_refs, energy_ref, est32, res32, stepped, result = refs
    shots, rows, samples = est_ref.shape
    width = out_refs[0].shape[2]

    def store(shot, column, values):
        start = pl.multiple_of(shot * rows, rows)
        stepped[pl.ds(start, rows), column * LANES : (column + 1) * LANES] = values

    blend_into(
        meta_ref, delay_ref, est_ref, obs_ref, before_ref, after_ref, energy_ref, est32, res32, store
    )
    held = result.shape[0]
    group = held // rows

    def transform(part, carry):
        start = pl.multiple_of(part * held, held)
        result[...] = jnp.dot(
            stepped[pl.ds(start, held), :], table_ref[...], preferred_element_type=jnp.float32
        ).astype(jnp.bfloat16)
        for slot, ref in enumerate(out_refs):
            ref[pl.ds(part * group, group)] = result[:, band(meta_ref, slot, width)].reshape(
                group, rows, width
            )
        return carry

    lax.fori_loop(0, shots // group, transform, 0)


def step_kernel(
    meta_ref, delay_ref, est_ref, obs_ref, before_ref, after_ref, out_ref, energy_ref, est32, res32
):
    def store(shot, column, values):
        out_ref[shot, :, column * LANES : (column + 1) * LANES] = values

    blend_into(
        meta_ref, delay_ref, est_ref, obs_ref, before_ref, after_ref, energy_ref, est32, res32, store
    )


def shots_kernel(meta_ref, table_ref, level_ref, _, *refs):
    *refs, wide, back = refs
    spectra_refs, out_refs = refs[: len(refs) // 2], refs[len(refs) // 2 :]
    held, rows, width = out_refs[0].shape
    shots = wide.shape[0] // rows
    half = width // 2

    def place(slot):
        size = held * rows
        return pl.ds(pl.multiple_of(meta_ref[1 + slot] * size, size), size)

    for slot, ref in zip(slots_of(len(spectra_refs)), spectra_refs):
        wide[place(slot), :] = ref[...].reshape(held * rows, width).astype(jnp.float32)
    level = level_ref[...]
    sign = jnp.where(
        lax.broadcasted_iota(jnp.int32, (1, width), 1) < half, jnp.float32(1.0), jnp.float32(-1.0)
    )

    def pair(index, carry):
        picks = [pl.ds(index * 2 + turn, shots, stride=rows) for turn in range(2)]
        block = jnp.concatenate([wide[pick, :] for pick in picks], axis=1).astype(jnp.bfloat16)
        both = jnp.dot(table_ref[...], block, preferred_element_type=jnp.float32)
        kept = []
        for turn in range(2):
            own = both[:, turn * width : (turn + 1) * width]
            wave = own[:shots] + sign * pltpu.roll(own[shots:], half, 1)
            power = wave * wave
            power = power + pltpu.roll(power, half, 1)
            factor = jnp.maximum(1.0 - level * lax.rsqrt(power), 0.0)
            kept.append((wave * factor).astype(jnp.bfloat16))
        both = jnp.dot(table_ref[...], jnp.concatenate(kept, axis=1), preferred_element_type=jnp.float32)
        for turn in range(2):
            own = both[:, turn * width : (turn + 1) * width]
            back[picks[turn], :] = own[:shots] - sign * pltpu.roll(own[shots:], half, 1)
        return carry

    lax.fori_loop(0, rows // 2, pair, 0, unroll=2)
    for slot, ref in enumerate(out_refs):
        ref[...] = back[place(slot), :].astype(jnp.bfloat16).reshape(held, rows, width)


def update_kernel(inputs, meta_ref, table_ref, _, *refs):
    restored_refs, (out_ref, turn_ref, whole_rows) = refs[:inputs], refs[-3:]
    held, rows, width = restored_refs[0].shape
    for slot, ref in zip(slots_of(inputs), restored_refs):
        whole_rows[:, band(meta_ref, slot, width)] = ref[...].reshape(held * rows, width)
    out_ref[...] = jnp.dot(
        whole_rows[...], table_ref[...], preferred_element_type=jnp.float32
    ).reshape(out_ref.shape)
    turn_ref[...] = jnp.zeros_like(turn_ref)


def whole(shape):
    return pl.BlockSpec(shape, lambda *_: (0,) * len(shape))


def blend_specs(shots, rows, samples, block, edge_block):
    at = lambda step, meta, delays: (0, block, 0)
    edge = lambda step, meta, delays: (0, edge_block, 0)
    return [
        pl.BlockSpec((shots, rows, samples), at),
        pl.BlockSpec((shots, rows, samples), at),
        pl.BlockSpec((HALO, rows, samples), edge),
        pl.BlockSpec((HALO, rows, samples), edge),
    ]


def blend_scratch(shots, rows, samples):
    columns = (samples + 2 * (FAR - NEAR)) // LANES
    return [
        pltpu.VMEM((shots + 4, columns, rows, LANES), jnp.float32),
        pltpu.VMEM((shots + 2, columns, rows, LANES), jnp.float32),
    ]


PARAMS = pltpu.CompilerParams(vmem_limit_bytes=60 * 1024 * 1024)
ANYWHERE = pl.BlockSpec(memory_space=pl.ANY)


def spectra_of(meta, delays, fields, table, rows, block, edge_block, peers, after):
    shots, _, samples = fields[0].shape
    shape = (shots, rows, 2 * F // peers)
    group = min(shots, max(1, 256 // rows))
    *spectra, energy = pl.pallas_call(
        spectra_kernel,
        grid_spec=pltpu.PrefetchScalarGridSpec(
            num_scalar_prefetch=2,
            grid=(1,),
            in_specs=blend_specs(shots, rows, samples, block, edge_block)
            + [whole(table.shape), ANYWHERE],
            out_specs=[whole(shape)] * peers + [whole((shots, LANES))],
            scratch_shapes=blend_scratch(shots, rows, samples)
            + [
                pltpu.VMEM((shots * rows, samples), jnp.bfloat16),
                pltpu.VMEM((group * rows, 2 * F), jnp.bfloat16),
            ],
        ),
        out_shape=[pltpu.HBM(shape, jnp.bfloat16)] * peers + [pltpu.HBM((shots, LANES), jnp.float32)],
        compiler_params=PARAMS,
        cost_estimate=pl.CostEstimate(
            flops=4 * F * shots * rows * samples,
            bytes_accessed=3 * 2 * shots * rows * samples + table.size * 2,
            transcendentals=0,
        ),
        name="spectra",
    )(meta, delays, *fields, table, after)
    return spectra, energy


def stepped_of(meta, delays, fields, rows, index):
    shots, _, samples = fields[0].shape
    return pl.pallas_call(
        step_kernel,
        grid_spec=pltpu.PrefetchScalarGridSpec(
            num_scalar_prefetch=2,
            grid=(1,),
            in_specs=blend_specs(shots, rows, samples, index, index),
            out_specs=[whole((shots, rows, samples)), whole((shots, LANES))],
            scratch_shapes=blend_scratch(shots, rows, samples),
        ),
        out_shape=[
            jax.ShapeDtypeStruct((shots, rows, samples), jnp.bfloat16),
            jax.ShapeDtypeStruct((shots, LANES), jnp.float32),
        ],
        compiler_params=PARAMS,
        name="stepped",
    )(meta, delays, *fields)


def shrunk_of(meta, spectra, table, level, after):
    shape = spectra[0].shape
    held, rows, width = shape
    peers = len(spectra)
    return pl.pallas_call(
        shots_kernel,
        grid_spec=pltpu.PrefetchScalarGridSpec(
            num_scalar_prefetch=1,
            grid=(1,),
            in_specs=[whole(table.shape), whole(level.shape), ANYWHERE]
            + [whole(shape)] * peers,
            out_specs=[whole(shape)] * peers,
            scratch_shapes=[pltpu.VMEM((peers * held * rows, width), jnp.float32)] * 2,
        ),
        out_shape=[pltpu.HBM(shape, jnp.bfloat16)] * peers,
        compiler_params=PARAMS,
        cost_estimate=pl.CostEstimate(
            flops=8 * (peers * held) ** 2 * rows * width,
            bytes_accessed=4 * peers * held * rows * width + 2 * table.size,
            transcendentals=peers * held * rows * width,
        ),
        name="shrink",
    )(meta, table, level, after, *spectra)


def updated_of(meta, restored, table, block, receivers, onto, after):
    shots, rows, width = restored[0].shape
    samples = table.shape[1]
    group = min(shots, max(1, 256 // rows))
    in_specs = [whole(table.shape), ANYWHERE]
    in_specs += [pl.BlockSpec((group, rows, width), lambda step, meta: (step, 0, 0))] * len(restored)
    operands = [meta, table, after, *restored]
    if onto is not None:
        in_specs.append(ANYWHERE)
        operands.append(onto)
    return pl.pallas_call(
        functools.partial(update_kernel, len(restored)),
        grid_spec=pltpu.PrefetchScalarGridSpec(
            num_scalar_prefetch=1,
            grid=(shots // group,),
            in_specs=in_specs,
            out_specs=[
                pl.BlockSpec((group, rows, samples), lambda step, meta: (step, block, 0)),
                whole((8, LANES)),
            ],
            scratch_shapes=[pltpu.VMEM((group * rows, 2 * F), jnp.bfloat16)],
        ),
        out_shape=[
            jax.ShapeDtypeStruct((shots, receivers, samples), jnp.float32),
            jax.ShapeDtypeStruct((8, LANES), jnp.float32),
        ],
        input_output_aliases={} if onto is None else {len(operands) - 1: 0},
        compiler_params=pltpu.CompilerParams(vmem_limit_bytes=48 * 1024 * 1024),
        cost_estimate=pl.CostEstimate(
            flops=4 * F * shots * rows * samples,
            bytes_accessed=4 * F * shots * rows + 2 * table.size + 4 * shots * rows * samples,
            transcendentals=0,
        ),
        name="update",
    )(*operands)


def swapped(array):
    return lax.all_to_all(array, "shot", split_axis=0, concat_axis=0, tiled=True)


def slots_of(peers):
    order = [0]
    for slot in range(peers // 2):
        order += [peers // 2 + slot] + ([slot + 1] if slot + 1 < peers // 2 else [])
    return order


def exchanged(arrays):
    peers = len(arrays)
    return [
        lax.ppermute(arrays[slot], "shot", [(i, i ^ slot) for i in range(peers)]) if slot else arrays[0]
        for slot in slots_of(peers)
    ]


def edges(estimate, observed):
    peers = lax.axis_size("shot")
    up = [(i, i + 1) for i in range(peers - 1)]
    down = [(j, i) for i, j in up]
    tail = jnp.concatenate([estimate[-2:], observed[-1:]])
    head = jnp.concatenate([estimate[:2], observed[:1]])
    return lax.ppermute(tail, "shot", up), lax.ppermute(head, "shot", down)


def chunks_of(receivers):
    if receivers == 128:
        return [(16, 0), (32, 1), (32, 2), (32, 3), (16, 1)]
    rows = min(16, receivers)
    return [(rows, index) for index in range(receivers // rows)]


def direct(estimate, observed, delays, thresholds):
    shots, receivers, samples = estimate.shape
    peers = lax.axis_size("shot")
    rank = lax.axis_index("shot")
    share = F // peers
    meta = jnp.concatenate(
        [jnp.reshape(rank * shots, (1,)), rank ^ jnp.arange(peers, dtype=jnp.int32)]
    ).astype(jnp.int32)
    forward, inverse = (jnp.asarray(table) for table in time_tables(samples, peers))
    table = jnp.asarray(shot_table(delays.shape[0]))
    levels = jnp.tile(lax.dynamic_slice_in_dim(thresholds, rank * share, share), 2)[None, :]
    chunks = chunks_of(receivers)
    sides = edges(estimate, observed)
    last, updated, energy = levels, None, 0.0
    lag = 1
    ahead, behind = {}, {}
    for turn in range(len(chunks) + 2 * lag):
        if turn < len(chunks):
            rows, index = chunks[turn]
            spectra, power = spectra_of(
                meta,
                delays,
                (estimate, observed, *sides),
                forward,
                rows,
                index,
                index,
                peers,
                last,
            )
            last = power
            energy = energy + power
            ahead[turn] = exchanged(spectra)
        place = turn - lag
        if place in ahead:
            shrunk = shrunk_of(meta, ahead.pop(place), table, levels, last)
            last = shrunk[0]
            behind[place] = exchanged(shrunk)
        place = turn - 2 * lag
        if place in behind:
            updated, last = updated_of(
                meta, behind.pop(place), inverse, chunks[place][1], receivers, updated, last
            )
    return updated, energy


def spectral_by_einsum(stepped, forward, inverse, table, level, peers):
    shots, receivers, samples = stepped.shape
    total = table.shape[1]
    share = F // peers
    spectra = jnp.einsum(
        "srt,tdpf->dpfsr",
        stepped,
        forward.reshape(samples, peers, 2, share),
        preferred_element_type=jnp.float32,
    ).astype(jnp.bfloat16)
    mixed = swapped(spectra).transpose(1, 2, 0, 3, 4).reshape(2, share, total, receivers)
    cosine, sine = table[:total], table[total:]
    across = jnp.stack([jnp.stack([cosine, sine]), jnp.stack([-sine, cosine])])
    wave = jnp.einsum("pqks,qfsr->pfkr", across, mixed, preferred_element_type=jnp.float32)
    magnitude = jnp.sqrt(wave[0] * wave[0] + wave[1] * wave[1])
    bound = level[:, None, None]
    factor = jnp.maximum(magnitude - bound, 0.0) / jnp.maximum(magnitude, bound)
    shrunk = (wave * factor[None]).astype(jnp.bfloat16)
    back = jnp.stack([jnp.stack([cosine, -sine]), jnp.stack([sine, cosine])])
    restored = jnp.einsum(
        "pqks,qfkr->pfsr", back, shrunk, preferred_element_type=jnp.float32
    ).astype(jnp.bfloat16)
    restored = restored.reshape(2, share, peers, shots, receivers).transpose(2, 0, 1, 3, 4)
    return jnp.einsum(
        "dpft,dpfsr->srt",
        inverse.reshape(peers, 2, share, samples),
        swapped(restored),
        preferred_element_type=jnp.float32,
    )


def by_einsum(estimate, observed, delays, thresholds):
    shots, receivers, samples = estimate.shape
    peers = lax.axis_size("shot")
    rank = lax.axis_index("shot")
    share = F // peers
    rows = min(16, receivers)
    meta = jnp.reshape(rank * shots, (1,)).astype(jnp.int32)
    sides = edges(estimate, observed)
    energy = 0.0
    parts = []
    for index in range(receivers // rows):
        part, power = stepped_of(meta, delays, (estimate, observed, *sides), rows, index)
        energy = energy + power
        parts.append(part)
    forward, inverse = (jnp.asarray(table) for table in time_tables(samples, peers))
    table = jnp.asarray(shot_table(delays.shape[0]))
    level = lax.dynamic_slice_in_dim(thresholds, rank * share, share)
    stepped = jnp.concatenate(parts, axis=1)
    return spectral_by_einsum(stepped, forward, inverse, table, level, peers), energy


def local(estimate, observed, random_source_delays, thresholds):
    receivers, samples = estimate.shape[1:]
    peers = lax.axis_size("shot")
    filled = peers >= 4 and peers & (peers - 1) == 0 and (2 * F // peers) % LANES == 0
    path = direct if filled else by_einsum
    updated, energy = path(estimate, observed, random_source_delays, thresholds)
    misfit = lax.psum(jnp.sum(energy, axis=1), "patch") / (
        receivers * lax.axis_size("patch") * samples
    )
    return updated, misfit


def solution(mesh):
    in_specs = (P("shot", "patch", None), P("shot", "patch", None), P(), P())
    out_specs = (P("shot", "patch", None), P("shot"))
    return jax.shard_map(local, mesh=mesh, in_specs=in_specs, out_specs=out_specs, check_vma=False)
```

```python
import functools

import jax
import jax.numpy as jnp
import ml_dtypes
import numpy as np
from jax import lax
from jax.experimental import pallas as pl
from jax.experimental.pallas import tpu as pltpu
from jax.sharding import PartitionSpec as P

F = 512
SOURCE_SPACING = 512
JITTER = 256
STEP = 0.5
LANES = 128
NEAR = SOURCE_SPACING - JITTER
FAR = SOURCE_SPACING + JITTER
HALO = 3


def time_tables(samples, blocks):
    freq = np.arange(F, dtype=np.int32)
    sample = np.arange(samples, dtype=np.int32)
    phase = (freq[:, None] * sample[None, :] % samples).astype(np.float32)
    angle = np.float32(2.0 * np.pi) * phase / np.float32(samples)
    root = np.sqrt(np.float32(samples))
    weight = np.where(freq == 0, 1.0, 2.0).astype(np.float32)[:, None] / root
    forward = np.stack([np.cos(angle) / root, -np.sin(angle) / root])
    inverse = np.stack([weight * np.cos(angle), -weight * np.sin(angle)])

    def ordered(table):
        table = table.astype(np.float32).astype(ml_dtypes.bfloat16)
        table = table.reshape(2, blocks, F // blocks, samples).transpose(1, 0, 2, 3)
        return table.reshape(2 * F, samples)

    return np.ascontiguousarray(ordered(forward).T), ordered(inverse)


def shot_table(shots):
    index = np.arange(shots, dtype=np.int32)
    phase = (index[:, None] * index[None, :] % shots).astype(np.float32)
    angle = np.float32(2.0 * np.pi) * phase / np.float32(shots)
    root = np.sqrt(np.float32(shots))
    table = np.concatenate([np.cos(angle) / root, np.sin(angle) / root])
    return table.astype(np.float32).astype(ml_dtypes.bfloat16)


def band(meta_ref, slot, width):
    return pl.ds(pl.multiple_of(meta_ref[1 + slot] * width, width), width)


def blend_into(
    meta_ref, delay_ref, est_ref, obs_ref, before_ref, after_ref, energy_ref, est32, res32, store
):
    shots, rows, samples = est_ref.shape
    columns = samples // LANES
    margin = (FAR - NEAR) // LANES
    inner = (samples - NEAR) // LANES
    skip = NEAR // LANES
    total = delay_ref.shape[0]
    first = meta_ref[0]
    lane = lax.broadcasted_iota(jnp.int32, (1, rows, LANES), 2)

    def ahead(shot):
        shot = jnp.clip(shot, 0, total - 2)
        return jnp.clip(SOURCE_SPACING + delay_ref[shot + 1] - delay_ref[shot], NEAR + 1, FAR - 1)

    def window(field, slot, start):
        column, rest = start // LANES, start % LANES
        wide = field[slot, pl.ds(column, inner + 1)]
        turned = pltpu.roll(
            wide.reshape((inner + 1) * rows, LANES), (LANES - rest) % LANES, 1
        ).reshape(inner + 1, rows, LANES)
        return jnp.where(lane < LANES - rest, turned[:-1], turned[1:])

    def blended(field, slot, shot):
        later = window(field, slot + 1, margin * LANES + NEAR - ahead(shot))
        earlier = window(field, slot - 1, margin * LANES + ahead(shot - 1))
        return later, earlier

    def fill(field, slot, values):
        blank = jnp.zeros((margin, rows, LANES), jnp.float32)
        field[slot, pl.ds(0, margin)] = blank
        field[slot, pl.ds(margin + columns, margin)] = blank
        for column in range(columns):
            field[slot, margin + column] = values(column)

    def cut(ref, shot):
        return lambda column: ref[shot, :, column * LANES : (column + 1) * LANES].astype(jnp.float32)

    for slot in range(2):
        fill(est32, slot, cut(before_ref, slot))
        fill(est32, shots + 2 + slot, cut(after_ref, slot))

    def load(shot, carry):
        fill(est32, shot + 2, cut(est_ref, shot))
        return carry

    lax.fori_loop(0, shots, load, 0, unroll=2)

    def residual(place, values):
        shot = first + place - 1
        inside = jnp.logical_and(shot >= 0, shot < total)
        later, earlier = blended(est32, place + 1, shot)
        power = jnp.zeros((rows, LANES), jnp.float32)
        cells = []
        for column in range(columns):
            cell = est32[place + 1, margin + column]
            if column >= skip:
                cell = cell + later[column - skip]
            if column < inner:
                cell = cell + earlier[column]
            cell = jnp.where(inside, values(column) - cell, 0.0)
            power = power + cell * cell
            cells.append(cell)
        fill(res32, place, lambda column: cells[column])
        return power

    residual(0, cut(before_ref, 2))
    residual(shots + 1, cut(after_ref, 2))

    def middle(shot, carry):
        power = residual(shot + 1, cut(obs_ref, shot))
        energy_ref[pl.ds(shot, 1), :] = jnp.sum(power, axis=0, keepdims=True)
        return carry

    lax.fori_loop(0, shots, middle, 0, unroll=4)

    def step(shot, carry):
        later, earlier = blended(res32, shot + 1, first + shot)
        for column in range(columns):
            cell = res32[shot + 1, margin + column]
            if column >= skip:
                cell = cell + later[column - skip]
            if column < inner:
                cell = cell + earlier[column]
            cell = est32[shot + 2, margin + column] + STEP * cell
            store(shot, column, cell.astype(jnp.bfloat16))
        return carry

    lax.fori_loop(0, shots, step, 0, unroll=4)


def spectra_kernel(
    meta_ref, delay_ref, est_ref, obs_ref, before_ref, after_ref, table_ref, _, *refs
):
    out_ref, energy_ref, est32, res32, stepped = refs
    shots, rows, samples = est_ref.shape
    peers, _, _, width = out_ref.shape

    def store(shot, column, values):
        start = pl.multiple_of(shot * rows, rows)
        stepped[pl.ds(start, rows), column * LANES : (column + 1) * LANES] = values

    blend_into(
        meta_ref, delay_ref, est_ref, obs_ref, before_ref, after_ref, energy_ref, est32, res32, store
    )
    group = min(shots, max(1, 256 // rows))

    def transform(part, carry):
        start = pl.multiple_of(part * (group * rows), group * rows)
        result = jnp.dot(
            stepped[pl.ds(start, group * rows), :], table_ref[...], preferred_element_type=jnp.float32
        ).astype(jnp.bfloat16)
        for peer in range(peers):
            out_ref[peer, pl.ds(part * group, group)] = result[
                :, peer * width : (peer + 1) * width
            ].reshape(group, rows, width)
        return carry

    lax.fori_loop(0, shots // group, transform, 0)


def step_kernel(
    meta_ref, delay_ref, est_ref, obs_ref, before_ref, after_ref, out_ref, energy_ref, est32, res32
):
    def store(shot, column, values):
        out_ref[shot, :, column * LANES : (column + 1) * LANES] = values

    blend_into(
        meta_ref, delay_ref, est_ref, obs_ref, before_ref, after_ref, energy_ref, est32, res32, store
    )


def shots_kernel(meta_ref, table_ref, level_ref, _, *refs):
    *refs, wide, back = refs
    spectra_ref, *out_refs = refs
    held, rows, width = out_refs[0].shape
    shots = wide.shape[0] // rows
    half = width // 2

    def place(slot):
        size = held * rows
        return pl.ds(pl.multiple_of(meta_ref[1 + slot] * size, size), size)

    wide[...] = spectra_ref[...].reshape(shots * rows, width).astype(jnp.float32)
    level = level_ref[...]
    sign = jnp.where(
        lax.broadcasted_iota(jnp.int32, (1, width), 1) < half, jnp.float32(1.0), jnp.float32(-1.0)
    )

    def pair(index, carry):
        picks = [pl.ds(index * 2 + turn, shots, stride=rows) for turn in range(2)]
        block = jnp.concatenate([wide[pick, :] for pick in picks], axis=1).astype(jnp.bfloat16)
        both = jnp.dot(table_ref[...], block, preferred_element_type=jnp.float32)
        kept = []
        for turn in range(2):
            own = both[:, turn * width : (turn + 1) * width]
            wave = own[:shots] + sign * pltpu.roll(own[shots:], half, 1)
            power = wave * wave
            power = power + pltpu.roll(power, half, 1)
            factor = jnp.maximum(1.0 - level * lax.rsqrt(power), 0.0)
            kept.append((wave * factor).astype(jnp.bfloat16))
        both = jnp.dot(table_ref[...], jnp.concatenate(kept, axis=1), preferred_element_type=jnp.float32)
        for turn in range(2):
            own = both[:, turn * width : (turn + 1) * width]
            back[picks[turn], :] = own[:shots] - sign * pltpu.roll(own[shots:], half, 1)
        return carry

    lax.fori_loop(0, rows // 2, pair, 0, unroll=2)
    for slot, ref in enumerate(out_refs):
        ref[...] = back[place(slot), :].astype(jnp.bfloat16).reshape(held, rows, width)


def update_kernel(inputs, meta_ref, table_ref, _, *refs):
    restored_refs, (out_ref, turn_ref, whole_rows) = refs[:inputs], refs[-3:]
    held, rows, width = restored_refs[0].shape
    for slot, ref in zip(slots_of(inputs), restored_refs):
        whole_rows[:, band(meta_ref, slot, width)] = ref[...].reshape(held * rows, width)
    out_ref[...] = jnp.dot(
        whole_rows[...], table_ref[...], preferred_element_type=jnp.float32
    ).reshape(out_ref.shape)
    turn_ref[...] = jnp.zeros_like(turn_ref)


def whole(shape):
    return pl.BlockSpec(shape, lambda *_: (0,) * len(shape))


def blend_specs(shots, rows, samples, block, edge_block):
    at = lambda step, meta, delays: (0, block, 0)
    edge = lambda step, meta, delays: (0, edge_block, 0)
    return [
        pl.BlockSpec((shots, rows, samples), at),
        pl.BlockSpec((shots, rows, samples), at),
        pl.BlockSpec((HALO, rows, samples), edge),
        pl.BlockSpec((HALO, rows, samples), edge),
    ]


def blend_scratch(shots, rows, samples):
    columns = (samples + 2 * (FAR - NEAR)) // LANES
    return [
        pltpu.VMEM((shots + 4, columns, rows, LANES), jnp.float32),
        pltpu.VMEM((shots + 2, columns, rows, LANES), jnp.float32),
    ]


PARAMS = pltpu.CompilerParams(vmem_limit_bytes=60 * 1024 * 1024)
ANYWHERE = pl.BlockSpec(memory_space=pl.ANY)


def spectra_of(meta, delays, fields, table, rows, block, edge_block, peers, after):
    shots, _, samples = fields[0].shape
    shape = (peers, shots, rows, 2 * F // peers)
    return pl.pallas_call(
        spectra_kernel,
        grid_spec=pltpu.PrefetchScalarGridSpec(
            num_scalar_prefetch=2,
            grid=(1,),
            in_specs=blend_specs(shots, rows, samples, block, edge_block)
            + [whole(table.shape), ANYWHERE],
            out_specs=[whole(shape), whole((shots, LANES))],
            scratch_shapes=blend_scratch(shots, rows, samples)
            + [pltpu.VMEM((shots * rows, samples), jnp.bfloat16)],
        ),
        out_shape=[pltpu.HBM(shape, jnp.bfloat16), pltpu.HBM((shots, LANES), jnp.float32)],
        compiler_params=PARAMS,
        cost_estimate=pl.CostEstimate(
            flops=4 * F * shots * rows * samples,
            bytes_accessed=3 * 2 * shots * rows * samples + table.size * 2,
            transcendentals=0,
        ),
        name="spectra",
    )(meta, delays, *fields, table, after)


def stepped_of(meta, delays, fields, rows, index):
    shots, _, samples = fields[0].shape
    return pl.pallas_call(
        step_kernel,
        grid_spec=pltpu.PrefetchScalarGridSpec(
            num_scalar_prefetch=2,
            grid=(1,),
            in_specs=blend_specs(shots, rows, samples, index, index),
            out_specs=[whole((shots, rows, samples)), whole((shots, LANES))],
            scratch_shapes=blend_scratch(shots, rows, samples),
        ),
        out_shape=[
            jax.ShapeDtypeStruct((shots, rows, samples), jnp.bfloat16),
            jax.ShapeDtypeStruct((shots, LANES), jnp.float32),
        ],
        compiler_params=PARAMS,
        name="stepped",
    )(meta, delays, *fields)


def shrunk_of(meta, spectra, table, level, after):
    peers, held, rows, width = spectra.shape
    shape = (held, rows, width)
    return pl.pallas_call(
        shots_kernel,
        grid_spec=pltpu.PrefetchScalarGridSpec(
            num_scalar_prefetch=1,
            grid=(1,),
            in_specs=[whole(table.shape), whole(level.shape), ANYWHERE]
            + [whole(spectra.shape)],
            out_specs=[whole(shape)] * peers,
            scratch_shapes=[pltpu.VMEM((peers * held * rows, width), jnp.float32)] * 2,
        ),
        out_shape=[pltpu.HBM(shape, jnp.bfloat16)] * peers,
        compiler_params=PARAMS,
        cost_estimate=pl.CostEstimate(
            flops=8 * (peers * held) ** 2 * rows * width,
            bytes_accessed=4 * peers * held * rows * width + 2 * table.size,
            transcendentals=peers * held * rows * width,
        ),
        name="shrink",
    )(meta, table, level, after, spectra)


def updated_of(meta, restored, table, block, receivers, onto, after):
    shots, rows, width = restored[0].shape
    samples = table.shape[1]
    group = min(shots, max(1, 256 // rows))
    in_specs = [whole(table.shape), ANYWHERE]
    in_specs += [pl.BlockSpec((group, rows, width), lambda step, meta: (step, 0, 0))] * len(restored)
    operands = [meta, table, after, *restored]
    if onto is not None:
        in_specs.append(ANYWHERE)
        operands.append(onto)
    return pl.pallas_call(
        functools.partial(update_kernel, len(restored)),
        grid_spec=pltpu.PrefetchScalarGridSpec(
            num_scalar_prefetch=1,
            grid=(shots // group,),
            in_specs=in_specs,
            out_specs=[
                pl.BlockSpec((group, rows, samples), lambda step, meta: (step, block, 0)),
                whole((8, LANES)),
            ],
            scratch_shapes=[pltpu.VMEM((group * rows, 2 * F), jnp.bfloat16)],
        ),
        out_shape=[
            jax.ShapeDtypeStruct((shots, receivers, samples), jnp.float32),
            jax.ShapeDtypeStruct((8, LANES), jnp.float32),
        ],
        input_output_aliases={} if onto is None else {len(operands) - 1: 0},
        compiler_params=pltpu.CompilerParams(vmem_limit_bytes=48 * 1024 * 1024),
        cost_estimate=pl.CostEstimate(
            flops=4 * F * shots * rows * samples,
            bytes_accessed=4 * F * shots * rows + 2 * table.size + 4 * shots * rows * samples,
            transcendentals=0,
        ),
        name="update",
    )(*operands)


def swapped(array):
    return lax.all_to_all(array, "shot", split_axis=0, concat_axis=0, tiled=True)


def slots_of(peers):
    order = [0]
    for slot in range(peers // 2):
        order += [peers // 2 + slot] + ([slot + 1] if slot + 1 < peers // 2 else [])
    return order


def exchanged(arrays):
    peers = len(arrays)
    return [
        lax.ppermute(arrays[slot], "shot", [(i, i ^ slot) for i in range(peers)]) if slot else arrays[0]
        for slot in slots_of(peers)
    ]


def edges(estimate, observed):
    peers = lax.axis_size("shot")
    up = [(i, i + 1) for i in range(peers - 1)]
    down = [(j, i) for i, j in up]
    tail = jnp.concatenate([estimate[-2:], observed[-1:]])
    head = jnp.concatenate([estimate[:2], observed[:1]])
    return lax.ppermute(tail, "shot", up), lax.ppermute(head, "shot", down)


def chunks_of(receivers):
    if receivers == 128:
        return [(16, 0), (32, 1), (32, 2), (32, 3), (16, 1)]
    rows = min(16, receivers)
    return [(rows, index) for index in range(receivers // rows)]


def direct(estimate, observed, delays, thresholds):
    shots, receivers, samples = estimate.shape
    peers = lax.axis_size("shot")
    rank = lax.axis_index("shot")
    share = F // peers
    meta = jnp.concatenate(
        [jnp.reshape(rank * shots, (1,)), rank ^ jnp.arange(peers, dtype=jnp.int32)]
    ).astype(jnp.int32)
    forward, inverse = (jnp.asarray(table) for table in time_tables(samples, peers))
    table = jnp.asarray(shot_table(delays.shape[0]))
    levels = jnp.tile(lax.dynamic_slice_in_dim(thresholds, rank * share, share), 2)[None, :]
    chunks = chunks_of(receivers)
    sides = edges(estimate, observed)
    last, updated, energy = levels, None, 0.0
    lag = 1
    ahead, behind = {}, {}
    for turn in range(len(chunks) + 2 * lag):
        if turn < len(chunks):
            rows, index = chunks[turn]
            spectra, power = spectra_of(
                meta,
                delays,
                (estimate, observed, *sides),
                forward,
                rows,
                index,
                index,
                peers,
                last,
            )
            last = power
            energy = energy + power
            ahead[turn] = swapped(spectra)
        place = turn - lag
        if place in ahead:
            shrunk = shrunk_of(meta, ahead.pop(place), table, levels, last)
            last = shrunk[0]
            behind[place] = exchanged(shrunk)
        place = turn - 2 * lag
        if place in behind:
            updated, last = updated_of(
                meta, behind.pop(place), inverse, chunks[place][1], receivers, updated, last
            )
    return updated, energy


def spectral_by_einsum(stepped, forward, inverse, table, level, peers):
    shots, receivers, samples = stepped.shape
    total = table.shape[1]
    share = F // peers
    spectra = jnp.einsum(
        "srt,tdpf->dpfsr",
        stepped,
        forward.reshape(samples, peers, 2, share),
        preferred_element_type=jnp.float32,
    ).astype(jnp.bfloat16)
    mixed = swapped(spectra).transpose(1, 2, 0, 3, 4).reshape(2, share, total, receivers)
    cosine, sine = table[:total], table[total:]
    across = jnp.stack([jnp.stack([cosine, sine]), jnp.stack([-sine, cosine])])
    wave = jnp.einsum("pqks,qfsr->pfkr", across, mixed, preferred_element_type=jnp.float32)
    magnitude = jnp.sqrt(wave[0] * wave[0] + wave[1] * wave[1])
    bound = level[:, None, None]
    factor = jnp.maximum(magnitude - bound, 0.0) / jnp.maximum(magnitude, bound)
    shrunk = (wave * factor[None]).astype(jnp.bfloat16)
    back = jnp.stack([jnp.stack([cosine, -sine]), jnp.stack([sine, cosine])])
    restored = jnp.einsum(
        "pqks,qfkr->pfsr", back, shrunk, preferred_element_type=jnp.float32
    ).astype(jnp.bfloat16)
    restored = restored.reshape(2, share, peers, shots, receivers).transpose(2, 0, 1, 3, 4)
    return jnp.einsum(
        "dpft,dpfsr->srt",
        inverse.reshape(peers, 2, share, samples),
        swapped(restored),
        preferred_element_type=jnp.float32,
    )


def by_einsum(estimate, observed, delays, thresholds):
    shots, receivers, samples = estimate.shape
    peers = lax.axis_size("shot")
    rank = lax.axis_index("shot")
    share = F // peers
    rows = min(16, receivers)
    meta = jnp.reshape(rank * shots, (1,)).astype(jnp.int32)
    sides = edges(estimate, observed)
    energy = 0.0
    parts = []
    for index in range(receivers // rows):
        part, power = stepped_of(meta, delays, (estimate, observed, *sides), rows, index)
        energy = energy + power
        parts.append(part)
    forward, inverse = (jnp.asarray(table) for table in time_tables(samples, peers))
    table = jnp.asarray(shot_table(delays.shape[0]))
    level = lax.dynamic_slice_in_dim(thresholds, rank * share, share)
    stepped = jnp.concatenate(parts, axis=1)
    return spectral_by_einsum(stepped, forward, inverse, table, level, peers), energy


def local(estimate, observed, random_source_delays, thresholds):
    receivers, samples = estimate.shape[1:]
    peers = lax.axis_size("shot")
    filled = peers >= 4 and peers & (peers - 1) == 0 and (2 * F // peers) % LANES == 0
    path = direct if filled else by_einsum
    updated, energy = path(estimate, observed, random_source_delays, thresholds)
    misfit = lax.psum(jnp.sum(energy, axis=1), "patch") / (
        receivers * lax.axis_size("patch") * samples
    )
    return updated, misfit


def solution(mesh):
    in_specs = (P("shot", "patch", None), P("shot", "patch", None), P(), P())
    out_specs = (P("shot", "patch", None), P("shot"))
    return jax.shard_map(local, mesh=mesh, in_specs=in_specs, out_specs=out_specs, check_vma=False)
```

```python
import functools

import jax
import jax.numpy as jnp
import ml_dtypes
import numpy as np
from jax import lax
from jax.experimental import pallas as pl
from jax.experimental.pallas import tpu as pltpu
from jax.sharding import PartitionSpec as P

F = 512
SOURCE_SPACING = 512
JITTER = 256
STEP = 0.5
LANES = 128
NEAR = SOURCE_SPACING - JITTER
FAR = SOURCE_SPACING + JITTER
HALO = 3


def time_tables(samples, blocks):
    freq = np.arange(F, dtype=np.int32)
    sample = np.arange(samples, dtype=np.int32)
    phase = (freq[:, None] * sample[None, :] % samples).astype(np.float32)
    angle = np.float32(2.0 * np.pi) * phase / np.float32(samples)
    root = np.sqrt(np.float32(samples))
    weight = np.where(freq == 0, 1.0, 2.0).astype(np.float32)[:, None] / root
    forward = np.stack([np.cos(angle) / root, -np.sin(angle) / root])
    inverse = np.stack([weight * np.cos(angle), -weight * np.sin(angle)])

    def ordered(table):
        table = table.astype(np.float32).astype(ml_dtypes.bfloat16)
        table = table.reshape(2, blocks, F // blocks, samples).transpose(1, 0, 2, 3)
        return table.reshape(2 * F, samples)

    return np.ascontiguousarray(ordered(forward).T), ordered(inverse)


def shot_table(shots):
    index = np.arange(shots, dtype=np.int32)
    phase = (index[:, None] * index[None, :] % shots).astype(np.float32)
    angle = np.float32(2.0 * np.pi) * phase / np.float32(shots)
    root = np.sqrt(np.float32(shots))
    table = np.concatenate([np.cos(angle) / root, np.sin(angle) / root])
    return table.astype(np.float32).astype(ml_dtypes.bfloat16)


def band(meta_ref, slot, width):
    return pl.ds(pl.multiple_of(meta_ref[1 + slot] * width, width), width)


def blend_into(
    meta_ref, delay_ref, est_ref, obs_ref, before_ref, after_ref, energy_ref, est32, res32, store
):
    shots, rows, samples = est_ref.shape
    columns = samples // LANES
    margin = (FAR - NEAR) // LANES
    inner = (samples - NEAR) // LANES
    skip = NEAR // LANES
    total = delay_ref.shape[0]
    first = meta_ref[0]
    lane = lax.broadcasted_iota(jnp.int32, (1, rows, LANES), 2)

    def ahead(shot):
        shot = jnp.clip(shot, 0, total - 2)
        return jnp.clip(SOURCE_SPACING + delay_ref[shot + 1] - delay_ref[shot], NEAR + 1, FAR - 1)

    def window(field, slot, start):
        column, rest = start // LANES, start % LANES
        wide = field[slot, pl.ds(column, inner + 1)]
        turned = pltpu.roll(
            wide.reshape((inner + 1) * rows, LANES), (LANES - rest) % LANES, 1
        ).reshape(inner + 1, rows, LANES)
        return jnp.where(lane < LANES - rest, turned[:-1], turned[1:])

    def blended(field, slot, shot):
        later = window(field, slot + 1, margin * LANES + NEAR - ahead(shot))
        earlier = window(field, slot - 1, margin * LANES + ahead(shot - 1))
        return later, earlier

    def fill(field, slot, values):
        blank = jnp.zeros((margin, rows, LANES), jnp.float32)
        field[slot, pl.ds(0, margin)] = blank
        field[slot, pl.ds(margin + columns, margin)] = blank
        for column in range(columns):
            field[slot, margin + column] = values(column)

    def cut(ref, shot):
        return lambda column: ref[shot, :, column * LANES : (column + 1) * LANES].astype(jnp.float32)

    for slot in range(2):
        fill(est32, slot, cut(before_ref, slot))
        fill(est32, shots + 2 + slot, cut(after_ref, slot))

    def load(shot, carry):
        fill(est32, shot + 2, cut(est_ref, shot))
        return carry

    lax.fori_loop(0, shots, load, 0, unroll=2)

    def residual(place, values):
        shot = first + place - 1
        inside = jnp.logical_and(shot >= 0, shot < total)
        later, earlier = blended(est32, place + 1, shot)
        power = jnp.zeros((rows, LANES), jnp.float32)
        cells = []
        for column in range(columns):
            cell = est32[place + 1, margin + column]
            if column >= skip:
                cell = cell + later[column - skip]
            if column < inner:
                cell = cell + earlier[column]
            cell = jnp.where(inside, values(column) - cell, 0.0)
            power = power + cell * cell
            cells.append(cell)
        fill(res32, place, lambda column: cells[column])
        return power

    residual(0, cut(before_ref, 2))
    residual(shots + 1, cut(after_ref, 2))

    def middle(shot, carry):
        power = residual(shot + 1, cut(obs_ref, shot))
        energy_ref[pl.ds(shot, 1), :] = jnp.sum(power, axis=0, keepdims=True)
        return carry

    lax.fori_loop(0, shots, middle, 0, unroll=4)

    def step(shot, carry):
        later, earlier = blended(res32, shot + 1, first + shot)
        for column in range(columns):
            cell = res32[shot + 1, margin + column]
            if column >= skip:
                cell = cell + later[column - skip]
            if column < inner:
                cell = cell + earlier[column]
            cell = est32[shot + 2, margin + column] + STEP * cell
            store(shot, column, cell.astype(jnp.bfloat16))
        return carry

    lax.fori_loop(0, shots, step, 0, unroll=4)


def spectra_kernel(
    meta_ref, delay_ref, est_ref, obs_ref, before_ref, after_ref, table_ref, _, *refs
):
    *out_refs, energy_ref, est32, res32, stepped, result = refs
    shots, rows, samples = est_ref.shape
    width = out_refs[0].shape[2]

    def store(shot, column, values):
        start = pl.multiple_of(shot * rows, rows)
        stepped[pl.ds(start, rows), column * LANES : (column + 1) * LANES] = values

    blend_into(
        meta_ref, delay_ref, est_ref, obs_ref, before_ref, after_ref, energy_ref, est32, res32, store
    )
    held = result.shape[0]
    group = held // rows

    def transform(part, carry):
        start = pl.multiple_of(part * held, held)
        result[...] = jnp.dot(
            stepped[pl.ds(start, held), :], table_ref[...], preferred_element_type=jnp.float32
        ).astype(jnp.bfloat16)
        for slot, ref in enumerate(out_refs):
            ref[pl.ds(part * group, group)] = result[:, band(meta_ref, slot, width)].reshape(
                group, rows, width
            )
        return carry

    lax.fori_loop(0, shots // group, transform, 0)


def step_kernel(
    meta_ref, delay_ref, est_ref, obs_ref, before_ref, after_ref, out_ref, energy_ref, est32, res32
):
    def store(shot, column, values):
        out_ref[shot, :, column * LANES : (column + 1) * LANES] = values

    blend_into(
        meta_ref, delay_ref, est_ref, obs_ref, before_ref, after_ref, energy_ref, est32, res32, store
    )


def shots_kernel(meta_ref, table_ref, level_ref, _, *refs):
    *refs, wide, back = refs
    spectra_refs, out_refs = refs[: len(refs) // 2], refs[len(refs) // 2 :]
    held, rows, width = out_refs[0].shape
    shots = wide.shape[0] // rows
    half = width // 2

    def place(slot):
        size = held * rows
        return pl.ds(pl.multiple_of(meta_ref[1 + slot] * size, size), size)

    for slot, ref in zip(slots_of(len(spectra_refs)), spectra_refs):
        wide[place(slot), :] = ref[...].reshape(held * rows, width).astype(jnp.float32)
    level = level_ref[...]
    sign = jnp.where(
        lax.broadcasted_iota(jnp.int32, (1, width), 1) < half, jnp.float32(1.0), jnp.float32(-1.0)
    )

    def pair(index, carry):
        picks = [pl.ds(index * 2 + turn, shots, stride=rows) for turn in range(2)]
        block = jnp.concatenate([wide[pick, :] for pick in picks], axis=1).astype(jnp.bfloat16)
        both = jnp.dot(table_ref[...], block, preferred_element_type=jnp.float32)
        kept = []
        for turn in range(2):
            own = both[:, turn * width : (turn + 1) * width]
            wave = own[:shots] + sign * pltpu.roll(own[shots:], half, 1)
            power = wave * wave
            power = power + pltpu.roll(power, half, 1)
            factor = jnp.maximum(1.0 - level * lax.rsqrt(power), 0.0)
            kept.append((wave * factor).astype(jnp.bfloat16))
        both = jnp.dot(table_ref[...], jnp.concatenate(kept, axis=1), preferred_element_type=jnp.float32)
        for turn in range(2):
            own = both[:, turn * width : (turn + 1) * width]
            back[picks[turn], :] = own[:shots] - sign * pltpu.roll(own[shots:], half, 1)
        return carry

    lax.fori_loop(0, rows // 2, pair, 0, unroll=2)
    for slot, ref in enumerate(out_refs):
        ref[...] = back[place(slot), :].astype(jnp.bfloat16).reshape(held, rows, width)


def update_kernel(inputs, meta_ref, table_ref, _, *refs):
    restored_refs, (out_ref, turn_ref, whole_rows) = refs[:inputs], refs[-3:]
    held, rows, width = restored_refs[0].shape
    for slot, ref in zip(slots_of(inputs), restored_refs):
        whole_rows[:, band(meta_ref, slot, width)] = ref[...].reshape(held * rows, width)
    out_ref[...] = jnp.dot(
        whole_rows[...], table_ref[...], preferred_element_type=jnp.float32
    ).reshape(out_ref.shape)
    turn_ref[...] = jnp.zeros_like(turn_ref)


def whole(shape):
    return pl.BlockSpec(shape, lambda *_: (0,) * len(shape))


def blend_specs(shots, rows, samples, block, edge_block):
    at = lambda step, meta, delays: (0, block, 0)
    edge = lambda step, meta, delays: (0, edge_block, 0)
    return [
        pl.BlockSpec((shots, rows, samples), at),
        pl.BlockSpec((shots, rows, samples), at),
        pl.BlockSpec((HALO, rows, samples), edge),
        pl.BlockSpec((HALO, rows, samples), edge),
    ]


def blend_scratch(shots, rows, samples):
    columns = (samples + 2 * (FAR - NEAR)) // LANES
    return [
        pltpu.VMEM((shots + 4, columns, rows, LANES), jnp.float32),
        pltpu.VMEM((shots + 2, columns, rows, LANES), jnp.float32),
    ]


PARAMS = pltpu.CompilerParams(vmem_limit_bytes=60 * 1024 * 1024)
ANYWHERE = pl.BlockSpec(memory_space=pl.ANY)


def spectra_of(meta, delays, fields, table, rows, block, edge_block, peers, after):
    shots, _, samples = fields[0].shape
    shape = (shots, rows, 2 * F // peers)
    group = min(shots, max(1, 256 // rows))
    *spectra, energy = pl.pallas_call(
        spectra_kernel,
        grid_spec=pltpu.PrefetchScalarGridSpec(
            num_scalar_prefetch=2,
            grid=(1,),
            in_specs=blend_specs(shots, rows, samples, block, edge_block)
            + [whole(table.shape), ANYWHERE],
            out_specs=[whole(shape)] * peers + [whole((shots, LANES))],
            scratch_shapes=blend_scratch(shots, rows, samples)
            + [
                pltpu.VMEM((shots * rows, samples), jnp.bfloat16),
                pltpu.VMEM((group * rows, 2 * F), jnp.bfloat16),
            ],
        ),
        out_shape=[pltpu.HBM(shape, jnp.bfloat16)] * peers + [pltpu.HBM((shots, LANES), jnp.float32)],
        compiler_params=PARAMS,
        cost_estimate=pl.CostEstimate(
            flops=4 * F * shots * rows * samples,
            bytes_accessed=3 * 2 * shots * rows * samples + table.size * 2,
            transcendentals=0,
        ),
        name="spectra",
    )(meta, delays, *fields, table, after)
    return spectra, energy


def stepped_of(meta, delays, fields, rows, index):
    shots, _, samples = fields[0].shape
    return pl.pallas_call(
        step_kernel,
        grid_spec=pltpu.PrefetchScalarGridSpec(
            num_scalar_prefetch=2,
            grid=(1,),
            in_specs=blend_specs(shots, rows, samples, index, index),
            out_specs=[whole((shots, rows, samples)), whole((shots, LANES))],
            scratch_shapes=blend_scratch(shots, rows, samples),
        ),
        out_shape=[
            jax.ShapeDtypeStruct((shots, rows, samples), jnp.bfloat16),
            jax.ShapeDtypeStruct((shots, LANES), jnp.float32),
        ],
        compiler_params=PARAMS,
        name="stepped",
    )(meta, delays, *fields)


def shrunk_of(meta, spectra, table, level, after):
    shape = spectra[0].shape
    held, rows, width = shape
    peers = len(spectra)
    return pl.pallas_call(
        shots_kernel,
        grid_spec=pltpu.PrefetchScalarGridSpec(
            num_scalar_prefetch=1,
            grid=(1,),
            in_specs=[whole(table.shape), whole(level.shape), ANYWHERE]
            + [whole(shape)] * peers,
            out_specs=[whole(shape)] * peers,
            scratch_shapes=[pltpu.VMEM((peers * held * rows, width), jnp.float32)] * 2,
        ),
        out_shape=[pltpu.HBM(shape, jnp.bfloat16)] * peers,
        compiler_params=PARAMS,
        cost_estimate=pl.CostEstimate(
            flops=8 * (peers * held) ** 2 * rows * width,
            bytes_accessed=4 * peers * held * rows * width + 2 * table.size,
            transcendentals=peers * held * rows * width,
        ),
        name="shrink",
    )(meta, table, level, after, *spectra)


def updated_of(meta, restored, table, block, receivers, onto, after):
    shots, rows, width = restored[0].shape
    samples = table.shape[1]
    group = min(shots, max(1, 256 // rows))
    in_specs = [whole(table.shape), ANYWHERE]
    in_specs += [pl.BlockSpec((group, rows, width), lambda step, meta: (step, 0, 0))] * len(restored)
    operands = [meta, table, after, *restored]
    if onto is not None:
        in_specs.append(ANYWHERE)
        operands.append(onto)
    return pl.pallas_call(
        functools.partial(update_kernel, len(restored)),
        grid_spec=pltpu.PrefetchScalarGridSpec(
            num_scalar_prefetch=1,
            grid=(shots // group,),
            in_specs=in_specs,
            out_specs=[
                pl.BlockSpec((group, rows, samples), lambda step, meta: (step, block, 0)),
                whole((8, LANES)),
            ],
            scratch_shapes=[pltpu.VMEM((group * rows, 2 * F), jnp.bfloat16)],
        ),
        out_shape=[
            jax.ShapeDtypeStruct((shots, receivers, samples), jnp.float32),
            jax.ShapeDtypeStruct((8, LANES), jnp.float32),
        ],
        input_output_aliases={} if onto is None else {len(operands) - 1: 0},
        compiler_params=pltpu.CompilerParams(vmem_limit_bytes=48 * 1024 * 1024),
        cost_estimate=pl.CostEstimate(
            flops=4 * F * shots * rows * samples,
            bytes_accessed=4 * F * shots * rows + 2 * table.size + 4 * shots * rows * samples,
            transcendentals=0,
        ),
        name="update",
    )(*operands)


def swapped(array):
    return lax.all_to_all(array, "shot", split_axis=0, concat_axis=0, tiled=True)


def slots_of(peers):
    order = [0]
    for slot in range(peers // 2):
        order += [peers // 2 + slot] + ([slot + 1] if slot + 1 < peers // 2 else [])
    return order


def exchanged(arrays):
    peers = len(arrays)
    return [
        lax.ppermute(arrays[slot], "shot", [(i, i ^ slot) for i in range(peers)]) if slot else arrays[0]
        for slot in slots_of(peers)
    ]


def edges(estimate, observed):
    peers = lax.axis_size("shot")
    up = [(i, i + 1) for i in range(peers - 1)]
    down = [(j, i) for i, j in up]
    tail = jnp.concatenate([estimate[-2:], observed[-1:]])
    head = jnp.concatenate([estimate[:2], observed[:1]])
    return lax.ppermute(tail, "shot", up), lax.ppermute(head, "shot", down)


def chunks_of(receivers):
    if receivers == 128:
        return [(16, 0), (16, 1), (32, 1), (32, 2), (16, 6), (16, 7)]
    rows = min(16, receivers)
    return [(rows, index) for index in range(receivers // rows)]


def summed(energy):
    return lax.psum(jnp.sum(energy, axis=1), "patch")


def direct(estimate, observed, delays, thresholds):
    shots, receivers, samples = estimate.shape
    peers = lax.axis_size("shot")
    rank = lax.axis_index("shot")
    share = F // peers
    meta = jnp.concatenate(
        [jnp.reshape(rank * shots, (1,)), rank ^ jnp.arange(peers, dtype=jnp.int32)]
    ).astype(jnp.int32)
    forward, inverse = (jnp.asarray(table) for table in time_tables(samples, peers))
    table = jnp.asarray(shot_table(delays.shape[0]))
    levels = jnp.tile(lax.dynamic_slice_in_dim(thresholds, rank * share, share), 2)[None, :]
    chunks = chunks_of(receivers)
    sides = edges(estimate, observed)
    last, updated, energy = levels, None, 0.0
    lag = 1
    ahead, behind = {}, {}
    for turn in range(len(chunks) + 2 * lag):
        if turn < len(chunks):
            rows, index = chunks[turn]
            spectra, power = spectra_of(
                meta,
                delays,
                (estimate, observed, *sides),
                forward,
                rows,
                index,
                index,
                peers,
                last,
            )
            last = power
            energy = energy + power
            ahead[turn] = exchanged(spectra)
            if turn == len(chunks) - 1:
                energy = last = summed(energy)
        place = turn - lag
        if place in ahead:
            shrunk = shrunk_of(meta, ahead.pop(place), table, levels, last)
            last = shrunk[0]
            behind[place] = exchanged(shrunk)
        place = turn - 2 * lag
        if place in behind:
            updated, last = updated_of(
                meta, behind.pop(place), inverse, chunks[place][1], receivers, updated, last
            )
    return updated, energy


def spectral_by_einsum(stepped, forward, inverse, table, level, peers):
    shots, receivers, samples = stepped.shape
    total = table.shape[1]
    share = F // peers
    spectra = jnp.einsum(
        "srt,tdpf->dpfsr",
        stepped,
        forward.reshape(samples, peers, 2, share),
        preferred_element_type=jnp.float32,
    ).astype(jnp.bfloat16)
    mixed = swapped(spectra).transpose(1, 2, 0, 3, 4).reshape(2, share, total, receivers)
    cosine, sine = table[:total], table[total:]
    across = jnp.stack([jnp.stack([cosine, sine]), jnp.stack([-sine, cosine])])
    wave = jnp.einsum("pqks,qfsr->pfkr", across, mixed, preferred_element_type=jnp.float32)
    magnitude = jnp.sqrt(wave[0] * wave[0] + wave[1] * wave[1])
    bound = level[:, None, None]
    factor = jnp.maximum(magnitude - bound, 0.0) / jnp.maximum(magnitude, bound)
    shrunk = (wave * factor[None]).astype(jnp.bfloat16)
    back = jnp.stack([jnp.stack([cosine, -sine]), jnp.stack([sine, cosine])])
    restored = jnp.einsum(
        "pqks,qfkr->pfsr", back, shrunk, preferred_element_type=jnp.float32
    ).astype(jnp.bfloat16)
    restored = restored.reshape(2, share, peers, shots, receivers).transpose(2, 0, 1, 3, 4)
    return jnp.einsum(
        "dpft,dpfsr->srt",
        inverse.reshape(peers, 2, share, samples),
        swapped(restored),
        preferred_element_type=jnp.float32,
    )


def by_einsum(estimate, observed, delays, thresholds):
    shots, receivers, samples = estimate.shape
    peers = lax.axis_size("shot")
    rank = lax.axis_index("shot")
    share = F // peers
    rows = min(16, receivers)
    meta = jnp.reshape(rank * shots, (1,)).astype(jnp.int32)
    sides = edges(estimate, observed)
    energy = 0.0
    parts = []
    for index in range(receivers // rows):
        part, power = stepped_of(meta, delays, (estimate, observed, *sides), rows, index)
        energy = energy + power
        parts.append(part)
    forward, inverse = (jnp.asarray(table) for table in time_tables(samples, peers))
    table = jnp.asarray(shot_table(delays.shape[0]))
    level = lax.dynamic_slice_in_dim(thresholds, rank * share, share)
    stepped = jnp.concatenate(parts, axis=1)
    return spectral_by_einsum(stepped, forward, inverse, table, level, peers), summed(energy)


def local(estimate, observed, random_source_delays, thresholds):
    receivers, samples = estimate.shape[1:]
    peers = lax.axis_size("shot")
    filled = peers >= 4 and peers & (peers - 1) == 0 and (2 * F // peers) % LANES == 0
    path = direct if filled else by_einsum
    updated, energy = path(estimate, observed, random_source_delays, thresholds)
    return updated, energy / (receivers * lax.axis_size("patch") * samples)


def solution(mesh):
    in_specs = (P("shot", "patch", None), P("shot", "patch", None), P(), P())
    out_specs = (P("shot", "patch", None), P("shot"))
    return jax.shard_map(local, mesh=mesh, in_specs=in_specs, out_specs=out_specs, check_vma=False)
```

```python
import functools

import jax
import jax.numpy as jnp
import ml_dtypes
import numpy as np
from jax import lax
from jax.experimental import pallas as pl
from jax.experimental.pallas import tpu as pltpu
from jax.sharding import PartitionSpec as P

F = 512
SOURCE_SPACING = 512
JITTER = 256
STEP = 0.5
LANES = 128
NEAR = SOURCE_SPACING - JITTER
FAR = SOURCE_SPACING + JITTER
HALO = 3


def time_tables(samples, blocks):
    freq = np.arange(F, dtype=np.int32)
    sample = np.arange(samples, dtype=np.int32)
    phase = (freq[:, None] * sample[None, :] % samples).astype(np.float32)
    angle = np.float32(2.0 * np.pi) * phase / np.float32(samples)
    root = np.sqrt(np.float32(samples))
    weight = np.where(freq == 0, 1.0, 2.0).astype(np.float32)[:, None] / root
    forward = np.stack([np.cos(angle) / root, -np.sin(angle) / root])
    inverse = np.stack([weight * np.cos(angle), -weight * np.sin(angle)])

    def ordered(table):
        table = table.astype(np.float32).astype(ml_dtypes.bfloat16)
        table = table.reshape(2, blocks, F // blocks, samples).transpose(1, 0, 2, 3)
        return table.reshape(2 * F, samples)

    return np.ascontiguousarray(ordered(forward).T), ordered(inverse)


def shot_table(shots):
    index = np.arange(shots, dtype=np.int32)
    phase = (index[:, None] * index[None, :] % shots).astype(np.float32)
    angle = np.float32(2.0 * np.pi) * phase / np.float32(shots)
    root = np.sqrt(np.float32(shots))
    table = np.concatenate([np.cos(angle) / root, np.sin(angle) / root])
    return table.astype(np.float32).astype(ml_dtypes.bfloat16)


def band(meta_ref, slot, width):
    return pl.ds(pl.multiple_of(meta_ref[1 + slot] * width, width), width)


def blend_into(
    meta_ref, delay_ref, est_ref, obs_ref, before_ref, after_ref, energy_ref, est32, res32, store
):
    shots, rows, samples = est_ref.shape
    columns = samples // LANES
    margin = (FAR - NEAR) // LANES
    inner = (samples - NEAR) // LANES
    skip = NEAR // LANES
    total = delay_ref.shape[0]
    first = meta_ref[0]
    lane = lax.broadcasted_iota(jnp.int32, (1, rows, LANES), 2)

    def ahead(shot):
        shot = jnp.clip(shot, 0, total - 2)
        return jnp.clip(SOURCE_SPACING + delay_ref[shot + 1] - delay_ref[shot], NEAR + 1, FAR - 1)

    def window(field, slot, start):
        column, rest = start // LANES, start % LANES
        wide = field[slot, pl.ds(column, inner + 1)]
        turned = pltpu.roll(
            wide.reshape((inner + 1) * rows, LANES), (LANES - rest) % LANES, 1
        ).reshape(inner + 1, rows, LANES)
        return jnp.where(lane < LANES - rest, turned[:-1], turned[1:])

    def blended(field, slot, shot):
        later = window(field, slot + 1, margin * LANES + NEAR - ahead(shot))
        earlier = window(field, slot - 1, margin * LANES + ahead(shot - 1))
        return later, earlier

    def fill(field, slot, values):
        blank = jnp.zeros((margin, rows, LANES), jnp.float32)
        field[slot, pl.ds(0, margin)] = blank
        field[slot, pl.ds(margin + columns, margin)] = blank
        for column in range(columns):
            field[slot, margin + column] = values(column)

    def cut(ref, shot):
        return lambda column: ref[shot, :, column * LANES : (column + 1) * LANES].astype(jnp.float32)

    for slot in range(2):
        fill(est32, slot, cut(before_ref, slot))
        fill(est32, shots + 2 + slot, cut(after_ref, slot))

    def load(shot, carry):
        fill(est32, shot + 2, cut(est_ref, shot))
        return carry

    lax.fori_loop(0, shots, load, 0, unroll=2)

    def residual(place, values):
        shot = first + place - 1
        inside = jnp.logical_and(shot >= 0, shot < total)
        later, earlier = blended(est32, place + 1, shot)
        power = jnp.zeros((rows, LANES), jnp.float32)
        cells = []
        for column in range(columns):
            cell = est32[place + 1, margin + column]
            if column >= skip:
                cell = cell + later[column - skip]
            if column < inner:
                cell = cell + earlier[column]
            cell = jnp.where(inside, values(column) - cell, 0.0)
            power = power + cell * cell
            cells.append(cell)
        fill(res32, place, lambda column: cells[column])
        return power

    residual(0, cut(before_ref, 2))
    residual(shots + 1, cut(after_ref, 2))

    def middle(shot, carry):
        power = residual(shot + 1, cut(obs_ref, shot))
        energy_ref[pl.ds(shot, 1), :] = jnp.sum(power, axis=0, keepdims=True)
        return carry

    lax.fori_loop(0, shots, middle, 0, unroll=4)

    def step(shot, carry):
        later, earlier = blended(res32, shot + 1, first + shot)
        for column in range(columns):
            cell = res32[shot + 1, margin + column]
            if column >= skip:
                cell = cell + later[column - skip]
            if column < inner:
                cell = cell + earlier[column]
            cell = est32[shot + 2, margin + column] + STEP * cell
            store(shot, column, cell.astype(jnp.bfloat16))
        return carry

    lax.fori_loop(0, shots, step, 0, unroll=4)


def spectra_kernel(
    meta_ref, delay_ref, est_ref, obs_ref, before_ref, after_ref, table_ref, _, *refs
):
    *out_refs, energy_ref, est32, res32, stepped, result = refs
    shots, rows, samples = est_ref.shape
    width = out_refs[0].shape[2]

    def store(shot, column, values):
        start = pl.multiple_of(shot * rows, rows)
        stepped[pl.ds(start, rows), column * LANES : (column + 1) * LANES] = values

    blend_into(
        meta_ref, delay_ref, est_ref, obs_ref, before_ref, after_ref, energy_ref, est32, res32, store
    )
    held = result.shape[0]
    group = held // rows

    def transform(part, carry):
        start = pl.multiple_of(part * held, held)
        result[...] = jnp.dot(
            stepped[pl.ds(start, held), :], table_ref[...], preferred_element_type=jnp.float32
        ).astype(jnp.bfloat16)
        for slot, ref in enumerate(out_refs):
            ref[pl.ds(part * group, group)] = result[:, band(meta_ref, slot, width)].reshape(
                group, rows, width
            )
        return carry

    lax.fori_loop(0, shots // group, transform, 0)


def step_kernel(
    meta_ref, delay_ref, est_ref, obs_ref, before_ref, after_ref, out_ref, energy_ref, est32, res32
):
    def store(shot, column, values):
        out_ref[shot, :, column * LANES : (column + 1) * LANES] = values

    blend_into(
        meta_ref, delay_ref, est_ref, obs_ref, before_ref, after_ref, energy_ref, est32, res32, store
    )


def shots_kernel(meta_ref, table_ref, level_ref, _, *refs):
    *refs, wide, back = refs
    spectra_refs, out_refs = refs[: len(refs) // 2], refs[len(refs) // 2 :]
    held, rows, width = out_refs[0].shape
    shots = wide.shape[0] // rows
    half = width // 2

    def place(slot):
        size = held * rows
        return pl.ds(pl.multiple_of(meta_ref[1 + slot] * size, size), size)

    for slot, ref in zip(slots_of(len(spectra_refs)), spectra_refs):
        wide[place(slot), :] = ref[...].reshape(held * rows, width).astype(jnp.float32)
    level = level_ref[...]
    sign = jnp.where(
        lax.broadcasted_iota(jnp.int32, (1, width), 1) < half, jnp.float32(1.0), jnp.float32(-1.0)
    )

    def pair(index, carry):
        picks = [pl.ds(index * 2 + turn, shots, stride=rows) for turn in range(2)]
        block = jnp.concatenate([wide[pick, :] for pick in picks], axis=1).astype(jnp.bfloat16)
        both = jnp.dot(table_ref[...], block, preferred_element_type=jnp.float32)
        kept = []
        for turn in range(2):
            own = both[:, turn * width : (turn + 1) * width]
            wave = own[:shots] + sign * pltpu.roll(own[shots:], half, 1)
            power = wave * wave
            power = power + pltpu.roll(power, half, 1)
            factor = jnp.maximum(1.0 - level * lax.rsqrt(power), 0.0)
            kept.append((wave * factor).astype(jnp.bfloat16))
        both = jnp.dot(table_ref[...], jnp.concatenate(kept, axis=1), preferred_element_type=jnp.float32)
        for turn in range(2):
            own = both[:, turn * width : (turn + 1) * width]
            back[picks[turn], :] = own[:shots] - sign * pltpu.roll(own[shots:], half, 1)
        return carry

    lax.fori_loop(0, rows // 2, pair, 0, unroll=2)
    for slot, ref in enumerate(out_refs):
        ref[...] = back[place(slot), :].astype(jnp.bfloat16).reshape(held, rows, width)


def update_kernel(inputs, meta_ref, table_ref, _, *refs):
    restored_refs, (out_ref, turn_ref, whole_rows) = refs[:inputs], refs[-3:]
    held, rows, width = restored_refs[0].shape
    for slot, ref in zip(slots_of(inputs), restored_refs):
        whole_rows[:, band(meta_ref, slot, width)] = ref[...].reshape(held * rows, width)
    out_ref[...] = jnp.dot(
        whole_rows[...], table_ref[...], preferred_element_type=jnp.float32
    ).reshape(out_ref.shape)
    turn_ref[...] = jnp.zeros_like(turn_ref)


def whole(shape):
    return pl.BlockSpec(shape, lambda *_: (0,) * len(shape))


def blend_specs(shots, rows, samples, block, edge_block):
    at = lambda step, meta, delays: (0, block, 0)
    edge = lambda step, meta, delays: (0, edge_block, 0)
    return [
        pl.BlockSpec((shots, rows, samples), at),
        pl.BlockSpec((shots, rows, samples), at),
        pl.BlockSpec((HALO, rows, samples), edge),
        pl.BlockSpec((HALO, rows, samples), edge),
    ]


def blend_scratch(shots, rows, samples):
    columns = (samples + 2 * (FAR - NEAR)) // LANES
    return [
        pltpu.VMEM((shots + 4, columns, rows, LANES), jnp.float32),
        pltpu.VMEM((shots + 2, columns, rows, LANES), jnp.float32),
    ]


PARAMS = pltpu.CompilerParams(vmem_limit_bytes=60 * 1024 * 1024)
ANYWHERE = pl.BlockSpec(memory_space=pl.ANY)


def spectra_of(meta, delays, fields, table, rows, block, edge_block, peers, after):
    shots, _, samples = fields[0].shape
    shape = (shots, rows, 2 * F // peers)
    group = min(shots, max(1, 256 // rows))
    *spectra, energy = pl.pallas_call(
        spectra_kernel,
        grid_spec=pltpu.PrefetchScalarGridSpec(
            num_scalar_prefetch=2,
            grid=(1,),
            in_specs=blend_specs(shots, rows, samples, block, edge_block)
            + [whole(table.shape), ANYWHERE],
            out_specs=[whole(shape)] * peers + [whole((shots, LANES))],
            scratch_shapes=blend_scratch(shots, rows, samples)
            + [
                pltpu.VMEM((shots * rows, samples), jnp.bfloat16),
                pltpu.VMEM((group * rows, 2 * F), jnp.bfloat16),
            ],
        ),
        out_shape=[pltpu.HBM(shape, jnp.bfloat16)] * peers + [pltpu.HBM((shots, LANES), jnp.float32)],
        compiler_params=PARAMS,
        cost_estimate=pl.CostEstimate(
            flops=4 * F * shots * rows * samples,
            bytes_accessed=3 * 2 * shots * rows * samples + table.size * 2,
            transcendentals=0,
        ),
        name="spectra",
    )(meta, delays, *fields, table, after)
    return spectra, energy


def stepped_of(meta, delays, fields, rows, index):
    shots, _, samples = fields[0].shape
    return pl.pallas_call(
        step_kernel,
        grid_spec=pltpu.PrefetchScalarGridSpec(
            num_scalar_prefetch=2,
            grid=(1,),
            in_specs=blend_specs(shots, rows, samples, index, index),
            out_specs=[whole((shots, rows, samples)), whole((shots, LANES))],
            scratch_shapes=blend_scratch(shots, rows, samples),
        ),
        out_shape=[
            jax.ShapeDtypeStruct((shots, rows, samples), jnp.bfloat16),
            jax.ShapeDtypeStruct((shots, LANES), jnp.float32),
        ],
        compiler_params=PARAMS,
        name="stepped",
    )(meta, delays, *fields)


def shrunk_of(meta, spectra, table, level, after):
    shape = spectra[0].shape
    held, rows, width = shape
    peers = len(spectra)
    return pl.pallas_call(
        shots_kernel,
        grid_spec=pltpu.PrefetchScalarGridSpec(
            num_scalar_prefetch=1,
            grid=(1,),
            in_specs=[whole(table.shape), whole(level.shape), ANYWHERE]
            + [whole(shape)] * peers,
            out_specs=[whole(shape)] * peers,
            scratch_shapes=[pltpu.VMEM((peers * held * rows, width), jnp.float32)] * 2,
        ),
        out_shape=[pltpu.HBM(shape, jnp.bfloat16)] * peers,
        compiler_params=PARAMS,
        cost_estimate=pl.CostEstimate(
            flops=8 * (peers * held) ** 2 * rows * width,
            bytes_accessed=4 * peers * held * rows * width + 2 * table.size,
            transcendentals=peers * held * rows * width,
        ),
        name="shrink",
    )(meta, table, level, after, *spectra)


def updated_of(meta, restored, table, block, receivers, onto, after):
    shots, rows, width = restored[0].shape
    samples = table.shape[1]
    group = min(shots, max(1, 256 // rows))
    in_specs = [whole(table.shape), ANYWHERE]
    in_specs += [pl.BlockSpec((group, rows, width), lambda step, meta: (step, 0, 0))] * len(restored)
    operands = [meta, table, after, *restored]
    if onto is not None:
        in_specs.append(ANYWHERE)
        operands.append(onto)
    return pl.pallas_call(
        functools.partial(update_kernel, len(restored)),
        grid_spec=pltpu.PrefetchScalarGridSpec(
            num_scalar_prefetch=1,
            grid=(shots // group,),
            in_specs=in_specs,
            out_specs=[
                pl.BlockSpec((group, rows, samples), lambda step, meta: (step, block, 0)),
                whole((8, LANES)),
            ],
            scratch_shapes=[pltpu.VMEM((group * rows, 2 * F), jnp.bfloat16)],
        ),
        out_shape=[
            jax.ShapeDtypeStruct((shots, receivers, samples), jnp.float32),
            jax.ShapeDtypeStruct((8, LANES), jnp.float32),
        ],
        input_output_aliases={} if onto is None else {len(operands) - 1: 0},
        compiler_params=pltpu.CompilerParams(vmem_limit_bytes=48 * 1024 * 1024),
        cost_estimate=pl.CostEstimate(
            flops=4 * F * shots * rows * samples,
            bytes_accessed=4 * F * shots * rows + 2 * table.size + 4 * shots * rows * samples,
            transcendentals=0,
        ),
        name="update",
    )(*operands)


def swapped(array):
    return lax.all_to_all(array, "shot", split_axis=0, concat_axis=0, tiled=True)


def slots_of(peers):
    half = peers // 2
    return [0, *range(1, min(3, half)), *range(half, peers), *range(3, half)]


def exchanged(arrays):
    peers = len(arrays)
    return [
        lax.ppermute(arrays[slot], "shot", [(i, i ^ slot) for i in range(peers)]) if slot else arrays[0]
        for slot in slots_of(peers)
    ]


def edges(estimate, observed):
    peers = lax.axis_size("shot")
    up = [(i, i + 1) for i in range(peers - 1)]
    down = [(j, i) for i, j in up]
    tail = jnp.concatenate([estimate[-2:], observed[-1:]])
    head = jnp.concatenate([estimate[:2], observed[:1]])
    return lax.ppermute(tail, "shot", up), lax.ppermute(head, "shot", down)


def chunks_of(receivers):
    if receivers == 128:
        return [(16, 0), (16, 1), (32, 1), (32, 2), (16, 6), (16, 7)]
    rows = min(16, receivers)
    return [(rows, index) for index in range(receivers // rows)]


def direct(estimate, observed, delays, thresholds):
    shots, receivers, samples = estimate.shape
    peers = lax.axis_size("shot")
    rank = lax.axis_index("shot")
    share = F // peers
    meta = jnp.concatenate(
        [jnp.reshape(rank * shots, (1,)), rank ^ jnp.arange(peers, dtype=jnp.int32)]
    ).astype(jnp.int32)
    forward, inverse = (jnp.asarray(table) for table in time_tables(samples, peers))
    table = jnp.asarray(shot_table(delays.shape[0]))
    levels = jnp.tile(lax.dynamic_slice_in_dim(thresholds, rank * share, share), 2)[None, :]
    chunks = chunks_of(receivers)
    sides = edges(estimate, observed)
    last, updated, energy = levels, None, 0.0
    lag = 2
    ahead, behind = {}, {}
    for turn in range(len(chunks) + lag + 1):
        if turn < len(chunks):
            rows, index = chunks[turn]
            spectra, power = spectra_of(
                meta,
                delays,
                (estimate, observed, *sides),
                forward,
                rows,
                index,
                index,
                peers,
                last,
            )
            last = power
            energy = energy + power
            ahead[turn] = exchanged(spectra)
        place = turn - lag
        if place in ahead:
            shrunk = shrunk_of(meta, ahead.pop(place), table, levels, last)
            last = shrunk[0]
            behind[place] = exchanged(shrunk)
        place = turn - lag - 1
        if place in behind:
            updated, last = updated_of(
                meta, behind.pop(place), inverse, chunks[place][1], receivers, updated, last
            )
    return updated, energy


def spectral_by_einsum(stepped, forward, inverse, table, level, peers):
    shots, receivers, samples = stepped.shape
    total = table.shape[1]
    share = F // peers
    spectra = jnp.einsum(
        "srt,tdpf->dpfsr",
        stepped,
        forward.reshape(samples, peers, 2, share),
        preferred_element_type=jnp.float32,
    ).astype(jnp.bfloat16)
    mixed = swapped(spectra).transpose(1, 2, 0, 3, 4).reshape(2, share, total, receivers)
    cosine, sine = table[:total], table[total:]
    across = jnp.stack([jnp.stack([cosine, sine]), jnp.stack([-sine, cosine])])
    wave = jnp.einsum("pqks,qfsr->pfkr", across, mixed, preferred_element_type=jnp.float32)
    magnitude = jnp.sqrt(wave[0] * wave[0] + wave[1] * wave[1])
    bound = level[:, None, None]
    factor = jnp.maximum(magnitude - bound, 0.0) / jnp.maximum(magnitude, bound)
    shrunk = (wave * factor[None]).astype(jnp.bfloat16)
    back = jnp.stack([jnp.stack([cosine, -sine]), jnp.stack([sine, cosine])])
    restored = jnp.einsum(
        "pqks,qfkr->pfsr", back, shrunk, preferred_element_type=jnp.float32
    ).astype(jnp.bfloat16)
    restored = restored.reshape(2, share, peers, shots, receivers).transpose(2, 0, 1, 3, 4)
    return jnp.einsum(
        "dpft,dpfsr->srt",
        inverse.reshape(peers, 2, share, samples),
        swapped(restored),
        preferred_element_type=jnp.float32,
    )


def by_einsum(estimate, observed, delays, thresholds):
    shots, receivers, samples = estimate.shape
    peers = lax.axis_size("shot")
    rank = lax.axis_index("shot")
    share = F // peers
    rows = min(16, receivers)
    meta = jnp.reshape(rank * shots, (1,)).astype(jnp.int32)
    sides = edges(estimate, observed)
    energy = 0.0
    parts = []
    for index in range(receivers // rows):
        part, power = stepped_of(meta, delays, (estimate, observed, *sides), rows, index)
        energy = energy + power
        parts.append(part)
    forward, inverse = (jnp.asarray(table) for table in time_tables(samples, peers))
    table = jnp.asarray(shot_table(delays.shape[0]))
    level = lax.dynamic_slice_in_dim(thresholds, rank * share, share)
    stepped = jnp.concatenate(parts, axis=1)
    return spectral_by_einsum(stepped, forward, inverse, table, level, peers), energy


def local(estimate, observed, random_source_delays, thresholds):
    receivers, samples = estimate.shape[1:]
    peers = lax.axis_size("shot")
    filled = peers >= 4 and peers & (peers - 1) == 0 and (2 * F // peers) % LANES == 0
    path = direct if filled else by_einsum
    updated, energy = path(estimate, observed, random_source_delays, thresholds)
    misfit = lax.psum(jnp.sum(energy, axis=1), "patch") / (
        receivers * lax.axis_size("patch") * samples
    )
    return updated, misfit


def solution(mesh):
    in_specs = (P("shot", "patch", None), P("shot", "patch", None), P(), P())
    out_specs = (P("shot", "patch", None), P("shot"))
    return jax.shard_map(local, mesh=mesh, in_specs=in_specs, out_specs=out_specs, check_vma=False)
```

```python
import functools

import jax
import jax.numpy as jnp
import ml_dtypes
import numpy as np
from jax import lax
from jax.experimental import pallas as pl
from jax.experimental.pallas import tpu as pltpu
from jax.sharding import PartitionSpec as P

F = 512
SOURCE_SPACING = 512
JITTER = 256
STEP = 0.5
LANES = 128
NEAR = SOURCE_SPACING - JITTER
FAR = SOURCE_SPACING + JITTER
HALO = 3


def time_tables(samples, blocks):
    freq = np.arange(F, dtype=np.int32)
    sample = np.arange(samples, dtype=np.int32)
    phase = (freq[:, None] * sample[None, :] % samples).astype(np.float32)
    angle = np.float32(2.0 * np.pi) * phase / np.float32(samples)
    root = np.sqrt(np.float32(samples))
    weight = np.where(freq == 0, 1.0, 2.0).astype(np.float32)[:, None] / root
    forward = np.stack([np.cos(angle) / root, -np.sin(angle) / root])
    inverse = np.stack([weight * np.cos(angle), -weight * np.sin(angle)])

    def ordered(table):
        table = table.astype(np.float32).astype(ml_dtypes.bfloat16)
        table = table.reshape(2, blocks, F // blocks, samples).transpose(1, 0, 2, 3)
        return table.reshape(2 * F, samples)

    return np.ascontiguousarray(ordered(forward).T), ordered(inverse)


def shot_table(shots):
    index = np.arange(shots, dtype=np.int32)
    phase = (index[:, None] * index[None, :] % shots).astype(np.float32)
    angle = np.float32(2.0 * np.pi) * phase / np.float32(shots)
    root = np.sqrt(np.float32(shots))
    table = np.concatenate([np.cos(angle) / root, np.sin(angle) / root])
    return table.astype(np.float32).astype(ml_dtypes.bfloat16)


def band(meta_ref, slot, width):
    return pl.ds(pl.multiple_of(meta_ref[1 + slot] * width, width), width)


def blend_into(
    meta_ref, delay_ref, est_ref, obs_ref, before_ref, after_ref, energy_ref, est32, res32, store
):
    shots, rows, samples = est_ref.shape
    columns = samples // LANES
    margin = (FAR - NEAR) // LANES
    inner = (samples - NEAR) // LANES
    skip = NEAR // LANES
    total = delay_ref.shape[0]
    first = meta_ref[0]
    lane = lax.broadcasted_iota(jnp.int32, (1, rows, LANES), 2)

    def ahead(shot):
        shot = jnp.clip(shot, 0, total - 2)
        return jnp.clip(SOURCE_SPACING + delay_ref[shot + 1] - delay_ref[shot], NEAR + 1, FAR - 1)

    def window(field, slot, start):
        column, rest = start // LANES, start % LANES
        wide = field[slot, pl.ds(column, inner + 1)]
        turned = pltpu.roll(
            wide.reshape((inner + 1) * rows, LANES), (LANES - rest) % LANES, 1
        ).reshape(inner + 1, rows, LANES)
        return jnp.where(lane < LANES - rest, turned[:-1], turned[1:])

    def blended(field, slot, shot):
        later = window(field, slot + 1, margin * LANES + NEAR - ahead(shot))
        earlier = window(field, slot - 1, margin * LANES + ahead(shot - 1))
        return later, earlier

    def fill(field, slot, values):
        blank = jnp.zeros((margin, rows, LANES), jnp.float32)
        field[slot, pl.ds(0, margin)] = blank
        field[slot, pl.ds(margin + columns, margin)] = blank
        for column in range(columns):
            field[slot, margin + column] = values(column)

    def cut(ref, shot):
        return lambda column: ref[shot, :, column * LANES : (column + 1) * LANES].astype(jnp.float32)

    for slot in range(2):
        fill(est32, slot, cut(before_ref, slot))
        fill(est32, shots + 2 + slot, cut(after_ref, slot))

    def load(shot, carry):
        fill(est32, shot + 2, cut(est_ref, shot))
        return carry

    lax.fori_loop(0, shots, load, 0, unroll=2)

    def residual(place, values):
        shot = first + place - 1
        inside = jnp.logical_and(shot >= 0, shot < total)
        later, earlier = blended(est32, place + 1, shot)
        power = jnp.zeros((rows, LANES), jnp.float32)
        cells = []
        for column in range(columns):
            cell = est32[place + 1, margin + column]
            if column >= skip:
                cell = cell + later[column - skip]
            if column < inner:
                cell = cell + earlier[column]
            cell = jnp.where(inside, values(column) - cell, 0.0)
            power = power + cell * cell
            cells.append(cell)
        fill(res32, place, lambda column: cells[column])
        return power

    residual(0, cut(before_ref, 2))
    residual(shots + 1, cut(after_ref, 2))

    def middle(shot, carry):
        power = residual(shot + 1, cut(obs_ref, shot))
        energy_ref[pl.ds(shot, 1), :] = jnp.sum(power, axis=0, keepdims=True)
        return carry

    lax.fori_loop(0, shots, middle, 0, unroll=4)

    def step(shot, carry):
        later, earlier = blended(res32, shot + 1, first + shot)
        for column in range(columns):
            cell = res32[shot + 1, margin + column]
            if column >= skip:
                cell = cell + later[column - skip]
            if column < inner:
                cell = cell + earlier[column]
            cell = est32[shot + 2, margin + column] + STEP * cell
            store(shot, column, cell.astype(jnp.bfloat16))
        return carry

    lax.fori_loop(0, shots, step, 0, unroll=4)


def spectra_kernel(
    meta_ref, delay_ref, est_ref, obs_ref, before_ref, after_ref, table_ref, _, *refs
):
    *out_refs, energy_ref, est32, res32, stepped, result = refs
    shots, rows, samples = est_ref.shape
    width = out_refs[0].shape[2]

    def store(shot, column, values):
        start = pl.multiple_of(shot * rows, rows)
        stepped[pl.ds(start, rows), column * LANES : (column + 1) * LANES] = values

    blend_into(
        meta_ref, delay_ref, est_ref, obs_ref, before_ref, after_ref, energy_ref, est32, res32, store
    )
    held = result.shape[0]
    group = held // rows

    def transform(part, carry):
        start = pl.multiple_of(part * held, held)
        result[...] = jnp.dot(
            stepped[pl.ds(start, held), :], table_ref[...], preferred_element_type=jnp.float32
        ).astype(jnp.bfloat16)
        for slot, ref in enumerate(out_refs):
            ref[pl.ds(part * group, group)] = result[:, band(meta_ref, slot, width)].reshape(
                group, rows, width
            )
        return carry

    lax.fori_loop(0, shots // group, transform, 0)


def step_kernel(
    meta_ref, delay_ref, est_ref, obs_ref, before_ref, after_ref, out_ref, energy_ref, est32, res32
):
    def store(shot, column, values):
        out_ref[shot, :, column * LANES : (column + 1) * LANES] = values

    blend_into(
        meta_ref, delay_ref, est_ref, obs_ref, before_ref, after_ref, energy_ref, est32, res32, store
    )


def shots_kernel(meta_ref, table_ref, level_ref, _, *refs):
    *refs, wide, back = refs
    spectra_refs, out_refs = refs[: len(refs) // 2], refs[len(refs) // 2 :]
    held, rows, width = out_refs[0].shape
    shots = wide.shape[0] // rows
    half = width // 2

    def place(slot):
        size = held * rows
        return pl.ds(pl.multiple_of(meta_ref[1 + slot] * size, size), size)

    for slot, ref in zip(slots_of(len(spectra_refs)), spectra_refs):
        wide[place(slot), :] = ref[...].reshape(held * rows, width).astype(jnp.float32)
    level = level_ref[...]
    sign = jnp.where(
        lax.broadcasted_iota(jnp.int32, (1, width), 1) < half, jnp.float32(1.0), jnp.float32(-1.0)
    )

    def pair(index, carry):
        picks = [pl.ds(index * 2 + turn, shots, stride=rows) for turn in range(2)]
        block = jnp.concatenate([wide[pick, :] for pick in picks], axis=1).astype(jnp.bfloat16)
        both = jnp.dot(table_ref[...], block, preferred_element_type=jnp.float32)
        kept = []
        for turn in range(2):
            own = both[:, turn * width : (turn + 1) * width]
            wave = own[:shots] + sign * pltpu.roll(own[shots:], half, 1)
            power = wave * wave
            power = power + pltpu.roll(power, half, 1)
            factor = jnp.maximum(1.0 - level * lax.rsqrt(power), 0.0)
            kept.append((wave * factor).astype(jnp.bfloat16))
        both = jnp.dot(table_ref[...], jnp.concatenate(kept, axis=1), preferred_element_type=jnp.float32)
        for turn in range(2):
            own = both[:, turn * width : (turn + 1) * width]
            back[picks[turn], :] = own[:shots] - sign * pltpu.roll(own[shots:], half, 1)
        return carry

    lax.fori_loop(0, rows // 2, pair, 0, unroll=2)
    for slot, ref in enumerate(out_refs):
        ref[...] = back[place(slot), :].astype(jnp.bfloat16).reshape(held, rows, width)


def update_kernel(inputs, meta_ref, table_ref, _, *refs):
    restored_refs, (out_ref, turn_ref, whole_rows) = refs[:inputs], refs[-3:]
    held, rows, width = restored_refs[0].shape
    for slot, ref in zip(slots_of(inputs), restored_refs):
        whole_rows[:, band(meta_ref, slot, width)] = ref[...].reshape(held * rows, width)
    out_ref[...] = jnp.dot(
        whole_rows[...], table_ref[...], preferred_element_type=jnp.float32
    ).reshape(out_ref.shape)
    turn_ref[...] = jnp.zeros_like(turn_ref)


def whole(shape):
    return pl.BlockSpec(shape, lambda *_: (0,) * len(shape))


def blend_specs(shots, rows, samples, block, edge_block):
    at = lambda step, meta, delays: (0, block, 0)
    edge = lambda step, meta, delays: (0, edge_block, 0)
    return [
        pl.BlockSpec((shots, rows, samples), at),
        pl.BlockSpec((shots, rows, samples), at),
        pl.BlockSpec((HALO, rows, samples), edge),
        pl.BlockSpec((HALO, rows, samples), edge),
    ]


def blend_scratch(shots, rows, samples):
    columns = (samples + 2 * (FAR - NEAR)) // LANES
    return [
        pltpu.VMEM((shots + 4, columns, rows, LANES), jnp.float32),
        pltpu.VMEM((shots + 2, columns, rows, LANES), jnp.float32),
    ]


PARAMS = pltpu.CompilerParams(vmem_limit_bytes=60 * 1024 * 1024)
ANYWHERE = pl.BlockSpec(memory_space=pl.ANY)


def spectra_of(meta, delays, fields, table, rows, block, edge_block, peers, after):
    shots, _, samples = fields[0].shape
    shape = (shots, rows, 2 * F // peers)
    group = min(shots, max(1, 256 // rows))
    *spectra, energy = pl.pallas_call(
        spectra_kernel,
        grid_spec=pltpu.PrefetchScalarGridSpec(
            num_scalar_prefetch=2,
            grid=(1,),
            in_specs=blend_specs(shots, rows, samples, block, edge_block)
            + [whole(table.shape), ANYWHERE],
            out_specs=[whole(shape)] * peers + [whole((shots, LANES))],
            scratch_shapes=blend_scratch(shots, rows, samples)
            + [
                pltpu.VMEM((shots * rows, samples), jnp.bfloat16),
                pltpu.VMEM((group * rows, 2 * F), jnp.bfloat16),
            ],
        ),
        out_shape=[pltpu.HBM(shape, jnp.bfloat16)] * peers + [pltpu.HBM((shots, LANES), jnp.float32)],
        compiler_params=PARAMS,
        cost_estimate=pl.CostEstimate(
            flops=4 * F * shots * rows * samples,
            bytes_accessed=3 * 2 * shots * rows * samples + table.size * 2,
            transcendentals=0,
        ),
        name="spectra",
    )(meta, delays, *fields, table, after)
    return spectra, energy


def stepped_of(meta, delays, fields, rows, index):
    shots, _, samples = fields[0].shape
    return pl.pallas_call(
        step_kernel,
        grid_spec=pltpu.PrefetchScalarGridSpec(
            num_scalar_prefetch=2,
            grid=(1,),
            in_specs=blend_specs(shots, rows, samples, index, index),
            out_specs=[whole((shots, rows, samples)), whole((shots, LANES))],
            scratch_shapes=blend_scratch(shots, rows, samples),
        ),
        out_shape=[
            jax.ShapeDtypeStruct((shots, rows, samples), jnp.bfloat16),
            jax.ShapeDtypeStruct((shots, LANES), jnp.float32),
        ],
        compiler_params=PARAMS,
        name="stepped",
    )(meta, delays, *fields)


def shrunk_of(meta, spectra, table, level, after):
    shape = spectra[0].shape
    held, rows, width = shape
    peers = len(spectra)
    return pl.pallas_call(
        shots_kernel,
        grid_spec=pltpu.PrefetchScalarGridSpec(
            num_scalar_prefetch=1,
            grid=(1,),
            in_specs=[whole(table.shape), whole(level.shape), ANYWHERE]
            + [whole(shape)] * peers,
            out_specs=[whole(shape)] * peers,
            scratch_shapes=[pltpu.VMEM((peers * held * rows, width), jnp.float32)] * 2,
        ),
        out_shape=[pltpu.HBM(shape, jnp.bfloat16)] * peers,
        compiler_params=PARAMS,
        cost_estimate=pl.CostEstimate(
            flops=8 * (peers * held) ** 2 * rows * width,
            bytes_accessed=4 * peers * held * rows * width + 2 * table.size,
            transcendentals=peers * held * rows * width,
        ),
        name="shrink",
    )(meta, table, level, after, *spectra)


def updated_of(meta, restored, table, block, receivers, onto, after):
    shots, rows, width = restored[0].shape
    samples = table.shape[1]
    group = min(shots, max(1, 256 // rows))
    in_specs = [whole(table.shape), ANYWHERE]
    in_specs += [pl.BlockSpec((group, rows, width), lambda step, meta: (step, 0, 0))] * len(restored)
    operands = [meta, table, after, *restored]
    if onto is not None:
        in_specs.append(ANYWHERE)
        operands.append(onto)
    return pl.pallas_call(
        functools.partial(update_kernel, len(restored)),
        grid_spec=pltpu.PrefetchScalarGridSpec(
            num_scalar_prefetch=1,
            grid=(shots // group,),
            in_specs=in_specs,
            out_specs=[
                pl.BlockSpec((group, rows, samples), lambda step, meta: (step, block, 0)),
                whole((8, LANES)),
            ],
            scratch_shapes=[pltpu.VMEM((group * rows, 2 * F), jnp.bfloat16)],
        ),
        out_shape=[
            jax.ShapeDtypeStruct((shots, receivers, samples), jnp.float32),
            jax.ShapeDtypeStruct((8, LANES), jnp.float32),
        ],
        input_output_aliases={} if onto is None else {len(operands) - 1: 0},
        compiler_params=pltpu.CompilerParams(vmem_limit_bytes=48 * 1024 * 1024),
        cost_estimate=pl.CostEstimate(
            flops=4 * F * shots * rows * samples,
            bytes_accessed=4 * F * shots * rows + 2 * table.size + 4 * shots * rows * samples,
            transcendentals=0,
        ),
        name="update",
    )(*operands)


def swapped(array):
    return lax.all_to_all(array, "shot", split_axis=0, concat_axis=0, tiled=True)


def slots_of(peers):
    order = [0]
    for slot in range(peers // 2):
        order += [peers // 2 + slot] + ([slot + 1] if slot + 1 < peers // 2 else [])
    return order


def exchanged(arrays):
    peers = len(arrays)
    return [
        lax.ppermute(arrays[slot], "shot", [(i, i ^ slot) for i in range(peers)]) if slot else arrays[0]
        for slot in slots_of(peers)
    ]


def edges(estimate, observed):
    peers = lax.axis_size("shot")
    up = [(i, i + 1) for i in range(peers - 1)]
    down = [(j, i) for i, j in up]
    tail = jnp.concatenate([estimate[-2:], observed[-1:]])
    head = jnp.concatenate([estimate[:2], observed[:1]])
    return lax.ppermute(tail, "shot", up), lax.ppermute(head, "shot", down)


def chunks_of(receivers):
    if receivers == 128:
        return [(16, 0), (32, 1), (32, 2), (32, 3), (16, 1)]
    rows = min(16, receivers)
    return [(rows, index) for index in range(receivers // rows)]


def direct(estimate, observed, delays, thresholds):
    shots, receivers, samples = estimate.shape
    peers = lax.axis_size("shot")
    rank = lax.axis_index("shot")
    share = F // peers
    meta = jnp.concatenate(
        [jnp.reshape(rank * shots, (1,)), rank ^ jnp.arange(peers, dtype=jnp.int32)]
    ).astype(jnp.int32)
    forward, inverse = (jnp.asarray(table) for table in time_tables(samples, peers))
    table = jnp.asarray(shot_table(delays.shape[0]))
    levels = jnp.tile(lax.dynamic_slice_in_dim(thresholds, rank * share, share), 2)[None, :]
    chunks = chunks_of(receivers)
    sides = edges(estimate, observed)
    last, updated, energy = levels, None, 0.0
    lag = 2
    ahead, behind = {}, {}
    for turn in range(len(chunks) + 2 * lag):
        if turn < len(chunks):
            rows, index = chunks[turn]
            spectra, power = spectra_of(
                meta,
                delays,
                (estimate, observed, *sides),
                forward,
                rows,
                index,
                index,
                peers,
                last,
            )
            last = power
            energy = energy + power
            ahead[turn] = exchanged(spectra)
        place = turn - lag
        if place in ahead:
            shrunk = shrunk_of(meta, ahead.pop(place), table, levels, last)
            last = shrunk[0]
            behind[place] = exchanged(shrunk)
        place = turn - 2 * lag
        if place in behind:
            updated, last = updated_of(
                meta, behind.pop(place), inverse, chunks[place][1], receivers, updated, last
            )
    return updated, energy


def spectral_by_einsum(stepped, forward, inverse, table, level, peers):
    shots, receivers, samples = stepped.shape
    total = table.shape[1]
    share = F // peers
    spectra = jnp.einsum(
        "srt,tdpf->dpfsr",
        stepped,
        forward.reshape(samples, peers, 2, share),
        preferred_element_type=jnp.float32,
    ).astype(jnp.bfloat16)
    mixed = swapped(spectra).transpose(1, 2, 0, 3, 4).reshape(2, share, total, receivers)
    cosine, sine = table[:total], table[total:]
    across = jnp.stack([jnp.stack([cosine, sine]), jnp.stack([-sine, cosine])])
    wave = jnp.einsum("pqks,qfsr->pfkr", across, mixed, preferred_element_type=jnp.float32)
    magnitude = jnp.sqrt(wave[0] * wave[0] + wave[1] * wave[1])
    bound = level[:, None, None]
    factor = jnp.maximum(magnitude - bound, 0.0) / jnp.maximum(magnitude, bound)
    shrunk = (wave * factor[None]).astype(jnp.bfloat16)
    back = jnp.stack([jnp.stack([cosine, -sine]), jnp.stack([sine, cosine])])
    restored = jnp.einsum(
        "pqks,qfkr->pfsr", back, shrunk, preferred_element_type=jnp.float32
    ).astype(jnp.bfloat16)
    restored = restored.reshape(2, share, peers, shots, receivers).transpose(2, 0, 1, 3, 4)
    return jnp.einsum(
        "dpft,dpfsr->srt",
        inverse.reshape(peers, 2, share, samples),
        swapped(restored),
        preferred_element_type=jnp.float32,
    )


def by_einsum(estimate, observed, delays, thresholds):
    shots, receivers, samples = estimate.shape
    peers = lax.axis_size("shot")
    rank = lax.axis_index("shot")
    share = F // peers
    rows = min(16, receivers)
    meta = jnp.reshape(rank * shots, (1,)).astype(jnp.int32)
    sides = edges(estimate, observed)
    energy = 0.0
    parts = []
    for index in range(receivers // rows):
        part, power = stepped_of(meta, delays, (estimate, observed, *sides), rows, index)
        energy = energy + power
        parts.append(part)
    forward, inverse = (jnp.asarray(table) for table in time_tables(samples, peers))
    table = jnp.asarray(shot_table(delays.shape[0]))
    level = lax.dynamic_slice_in_dim(thresholds, rank * share, share)
    stepped = jnp.concatenate(parts, axis=1)
    return spectral_by_einsum(stepped, forward, inverse, table, level, peers), energy


def local(estimate, observed, random_source_delays, thresholds):
    receivers, samples = estimate.shape[1:]
    peers = lax.axis_size("shot")
    filled = peers >= 4 and peers & (peers - 1) == 0 and (2 * F // peers) % LANES == 0
    path = direct if filled else by_einsum
    updated, energy = path(estimate, observed, random_source_delays, thresholds)
    misfit = lax.psum(jnp.sum(energy, axis=1), "patch") / (
        receivers * lax.axis_size("patch") * samples
    )
    return updated, misfit


def solution(mesh):
    in_specs = (P("shot", "patch", None), P("shot", "patch", None), P(), P())
    out_specs = (P("shot", "patch", None), P("shot"))
    return jax.shard_map(local, mesh=mesh, in_specs=in_specs, out_specs=out_specs, check_vma=False)
```

```python
import functools

import jax
import jax.numpy as jnp
import ml_dtypes
import numpy as np
from jax import lax
from jax.experimental import pallas as pl
from jax.experimental.pallas import tpu as pltpu
from jax.sharding import PartitionSpec as P

F = 512
SOURCE_SPACING = 512
JITTER = 256
STEP = 0.5
LANES = 128
NEAR = SOURCE_SPACING - JITTER
FAR = SOURCE_SPACING + JITTER
HALO = 3


def time_tables(samples, blocks):
    freq = np.arange(F, dtype=np.int32)
    sample = np.arange(samples, dtype=np.int32)
    phase = (freq[:, None] * sample[None, :] % samples).astype(np.float32)
    angle = np.float32(2.0 * np.pi) * phase / np.float32(samples)
    root = np.sqrt(np.float32(samples))
    weight = np.where(freq == 0, 1.0, 2.0).astype(np.float32)[:, None] / root
    forward = np.stack([np.cos(angle) / root, -np.sin(angle) / root])
    inverse = np.stack([weight * np.cos(angle), -weight * np.sin(angle)])

    def ordered(table):
        table = table.astype(np.float32).astype(ml_dtypes.bfloat16)
        table = table.reshape(2, blocks, F // blocks, samples).transpose(1, 0, 2, 3)
        return table.reshape(2 * F, samples)

    return np.ascontiguousarray(ordered(forward).T), ordered(inverse)


def shot_table(shots):
    index = np.arange(shots, dtype=np.int32)
    phase = (index[:, None] * index[None, :] % shots).astype(np.float32)
    angle = np.float32(2.0 * np.pi) * phase / np.float32(shots)
    root = np.sqrt(np.float32(shots))
    table = np.concatenate([np.cos(angle) / root, np.sin(angle) / root])
    return table.astype(np.float32).astype(ml_dtypes.bfloat16)


def band(meta_ref, slot, width):
    return pl.ds(pl.multiple_of(meta_ref[1 + slot] * width, width), width)


def group_of(shots, rows):
    group = 1
    while shots % (2 * group) == 0 and 2 * group * rows <= 256:
        group *= 2
    return group


def blend_into(
    meta_ref, delay_ref, est_ref, obs_ref, before_ref, after_ref, energy_ref, est32, res32, store
):
    shots, rows, samples = est_ref.shape
    columns = samples // LANES
    margin = (FAR - NEAR) // LANES
    inner = (samples - NEAR) // LANES
    skip = NEAR // LANES
    total = delay_ref.shape[0]
    first = meta_ref[0]
    lane = lax.broadcasted_iota(jnp.int32, (1, rows, LANES), 2)

    def ahead(shot):
        shot = jnp.clip(shot, 0, total - 2)
        return jnp.clip(SOURCE_SPACING + delay_ref[shot + 1] - delay_ref[shot], NEAR + 1, FAR - 1)

    def window(field, slot, start):
        column, rest = start // LANES, start % LANES
        wide = field[slot, pl.ds(column, inner + 1)]
        turned = pltpu.roll(
            wide.reshape((inner + 1) * rows, LANES), (LANES - rest) % LANES, 1
        ).reshape(inner + 1, rows, LANES)
        return jnp.where(lane < LANES - rest, turned[:-1], turned[1:])

    def blended(field, slot, shot):
        later = window(field, slot + 1, margin * LANES + NEAR - ahead(shot))
        earlier = window(field, slot - 1, margin * LANES + ahead(shot - 1))
        return later, earlier

    def fill(field, slot, values):
        blank = jnp.zeros((margin, rows, LANES), jnp.float32)
        field[slot, pl.ds(0, margin)] = blank
        field[slot, pl.ds(margin + columns, margin)] = blank
        for column in range(columns):
            field[slot, margin + column] = values(column)

    def cut(ref, shot):
        return lambda column: ref[shot, :, column * LANES : (column + 1) * LANES].astype(jnp.float32)

    for slot in range(2):
        fill(est32, slot, cut(before_ref, slot))
        fill(est32, shots + 2 + slot, cut(after_ref, slot))

    def load(shot, carry):
        fill(est32, shot + 2, cut(est_ref, shot))
        return carry

    lax.fori_loop(0, shots, load, 0, unroll=2)

    def residual(place, values):
        shot = first + place - 1
        inside = jnp.logical_and(shot >= 0, shot < total)
        later, earlier = blended(est32, place + 1, shot)
        power = jnp.zeros((rows, LANES), jnp.float32)
        cells = []
        for column in range(columns):
            cell = est32[place + 1, margin + column]
            if column >= skip:
                cell = cell + later[column - skip]
            if column < inner:
                cell = cell + earlier[column]
            cell = jnp.where(inside, values(column) - cell, 0.0)
            power = power + cell * cell
            cells.append(cell)
        fill(res32, place, lambda column: cells[column])
        return power

    residual(0, cut(before_ref, 2))
    residual(shots + 1, cut(after_ref, 2))

    def middle(shot, carry):
        power = residual(shot + 1, cut(obs_ref, shot))
        energy_ref[pl.ds(shot, 1), :] = jnp.sum(power, axis=0, keepdims=True)
        return carry

    lax.fori_loop(0, shots, middle, 0, unroll=4)

    def step(shot, carry):
        later, earlier = blended(res32, shot + 1, first + shot)
        for column in range(columns):
            cell = res32[shot + 1, margin + column]
            if column >= skip:
                cell = cell + later[column - skip]
            if column < inner:
                cell = cell + earlier[column]
            cell = est32[shot + 2, margin + column] + STEP * cell
            store(shot, column, cell.astype(jnp.bfloat16))
        return carry

    lax.fori_loop(0, shots, step, 0, unroll=4)


def spectra_kernel(
    meta_ref, delay_ref, est_ref, obs_ref, before_ref, after_ref, table_ref, _, *refs
):
    *out_refs, energy_ref, est32, res32, stepped, result = refs
    shots, rows, samples = est_ref.shape
    width = out_refs[0].shape[2]

    def store(shot, column, values):
        start = pl.multiple_of(shot * rows, rows)
        stepped[pl.ds(start, rows), column * LANES : (column + 1) * LANES] = values

    blend_into(
        meta_ref, delay_ref, est_ref, obs_ref, before_ref, after_ref, energy_ref, est32, res32, store
    )
    held = result.shape[0]
    group = held // rows

    def transform(part, carry):
        start = pl.multiple_of(part * held, held)
        result[...] = jnp.dot(
            stepped[pl.ds(start, held), :], table_ref[...], preferred_element_type=jnp.float32
        ).astype(jnp.bfloat16)
        for slot, ref in enumerate(out_refs):
            ref[pl.ds(part * group, group)] = result[:, band(meta_ref, slot, width)].reshape(
                group, rows, width
            )
        return carry

    lax.fori_loop(0, shots // group, transform, 0)


def step_kernel(
    meta_ref, delay_ref, est_ref, obs_ref, before_ref, after_ref, out_ref, energy_ref, est32, res32
):
    def store(shot, column, values):
        out_ref[shot, :, column * LANES : (column + 1) * LANES] = values

    blend_into(
        meta_ref, delay_ref, est_ref, obs_ref, before_ref, after_ref, energy_ref, est32, res32, store
    )


def shots_kernel(meta_ref, table_ref, level_ref, _, *refs):
    *refs, wide, back = refs
    spectra_refs, out_refs = refs[: len(refs) // 2], refs[len(refs) // 2 :]
    held, rows, width = out_refs[0].shape
    shots = wide.shape[0] // rows
    half = width // 2

    def place(slot):
        size = held * rows
        return pl.ds(pl.multiple_of(meta_ref[1 + slot] * size, size), size)

    for slot, ref in zip(slots_of(len(spectra_refs)), spectra_refs):
        wide[place(slot), :] = ref[...].reshape(held * rows, width).astype(jnp.float32)
    level = level_ref[...]
    sign = jnp.where(
        lax.broadcasted_iota(jnp.int32, (1, width), 1) < half, jnp.float32(1.0), jnp.float32(-1.0)
    )

    def pair(index, carry):
        picks = [pl.ds(index * 2 + turn, shots, stride=rows) for turn in range(2)]
        block = jnp.concatenate([wide[pick, :] for pick in picks], axis=1).astype(jnp.bfloat16)
        both = jnp.dot(table_ref[...], block, preferred_element_type=jnp.float32)
        kept = []
        for turn in range(2):
            own = both[:, turn * width : (turn + 1) * width]
            wave = own[:shots] + sign * pltpu.roll(own[shots:], half, 1)
            power = wave * wave
            power = power + pltpu.roll(power, half, 1)
            factor = jnp.maximum(1.0 - level * lax.rsqrt(power), 0.0)
            kept.append((wave * factor).astype(jnp.bfloat16))
        both = jnp.dot(table_ref[...], jnp.concatenate(kept, axis=1), preferred_element_type=jnp.float32)
        for turn in range(2):
            own = both[:, turn * width : (turn + 1) * width]
            back[picks[turn], :] = own[:shots] - sign * pltpu.roll(own[shots:], half, 1)
        return carry

    lax.fori_loop(0, rows // 2, pair, 0, unroll=2)
    for slot, ref in enumerate(out_refs):
        ref[...] = back[place(slot), :].astype(jnp.bfloat16).reshape(held, rows, width)


def update_kernel(inputs, meta_ref, table_ref, _, *refs):
    restored_refs, (out_ref, turn_ref, whole_rows) = refs[:inputs], refs[-3:]
    held, rows, width = restored_refs[0].shape
    for slot, ref in zip(slots_of(inputs), restored_refs):
        whole_rows[:, band(meta_ref, slot, width)] = ref[...].reshape(held * rows, width)
    out_ref[...] = jnp.dot(
        whole_rows[...], table_ref[...], preferred_element_type=jnp.float32
    ).reshape(out_ref.shape)
    turn_ref[...] = jnp.zeros_like(turn_ref)


def whole(shape):
    return pl.BlockSpec(shape, lambda *_: (0,) * len(shape))


def blend_specs(shots, rows, samples, block, edge_block):
    at = lambda step, meta, delays: (0, block, 0)
    edge = lambda step, meta, delays: (0, edge_block, 0)
    return [
        pl.BlockSpec((shots, rows, samples), at),
        pl.BlockSpec((shots, rows, samples), at),
        pl.BlockSpec((HALO, rows, samples), edge),
        pl.BlockSpec((HALO, rows, samples), edge),
    ]


def blend_scratch(shots, rows, samples):
    columns = (samples + 2 * (FAR - NEAR)) // LANES
    return [
        pltpu.VMEM((shots + 4, columns, rows, LANES), jnp.float32),
        pltpu.VMEM((shots + 2, columns, rows, LANES), jnp.float32),
    ]


PARAMS = pltpu.CompilerParams(vmem_limit_bytes=60 * 1024 * 1024)
ANYWHERE = pl.BlockSpec(memory_space=pl.ANY)


def spectra_of(meta, delays, fields, table, rows, block, edge_block, peers, after):
    shots, _, samples = fields[0].shape
    shape = (shots, rows, 2 * F // peers)
    group = group_of(shots, rows)
    *spectra, energy = pl.pallas_call(
        spectra_kernel,
        grid_spec=pltpu.PrefetchScalarGridSpec(
            num_scalar_prefetch=2,
            grid=(1,),
            in_specs=blend_specs(shots, rows, samples, block, edge_block)
            + [whole(table.shape), ANYWHERE],
            out_specs=[whole(shape)] * peers + [whole((shots, LANES))],
            scratch_shapes=blend_scratch(shots, rows, samples)
            + [
                pltpu.VMEM((shots * rows, samples), jnp.bfloat16),
                pltpu.VMEM((group * rows, 2 * F), jnp.bfloat16),
            ],
        ),
        out_shape=[pltpu.HBM(shape, jnp.bfloat16)] * peers + [pltpu.HBM((shots, LANES), jnp.float32)],
        compiler_params=PARAMS,
        cost_estimate=pl.CostEstimate(
            flops=4 * F * shots * rows * samples,
            bytes_accessed=3 * 2 * shots * rows * samples + table.size * 2,
            transcendentals=0,
        ),
        name="spectra",
    )(meta, delays, *fields, table, after)
    return spectra, energy


def stepped_of(meta, delays, fields, rows, index):
    shots, _, samples = fields[0].shape
    return pl.pallas_call(
        step_kernel,
        grid_spec=pltpu.PrefetchScalarGridSpec(
            num_scalar_prefetch=2,
            grid=(1,),
            in_specs=blend_specs(shots, rows, samples, index, index),
            out_specs=[whole((shots, rows, samples)), whole((shots, LANES))],
            scratch_shapes=blend_scratch(shots, rows, samples),
        ),
        out_shape=[
            jax.ShapeDtypeStruct((shots, rows, samples), jnp.bfloat16),
            jax.ShapeDtypeStruct((shots, LANES), jnp.float32),
        ],
        compiler_params=PARAMS,
        name="stepped",
    )(meta, delays, *fields)


def shrunk_of(meta, spectra, table, level, after):
    shape = spectra[0].shape
    held, rows, width = shape
    peers = len(spectra)
    return pl.pallas_call(
        shots_kernel,
        grid_spec=pltpu.PrefetchScalarGridSpec(
            num_scalar_prefetch=1,
            grid=(1,),
            in_specs=[whole(table.shape), whole(level.shape), ANYWHERE]
            + [whole(shape)] * peers,
            out_specs=[whole(shape)] * peers,
            scratch_shapes=[pltpu.VMEM((peers * held * rows, width), jnp.float32)] * 2,
        ),
        out_shape=[pltpu.HBM(shape, jnp.bfloat16)] * peers,
        compiler_params=PARAMS,
        cost_estimate=pl.CostEstimate(
            flops=8 * (peers * held) ** 2 * rows * width,
            bytes_accessed=4 * peers * held * rows * width + 2 * table.size,
            transcendentals=peers * held * rows * width,
        ),
        name="shrink",
    )(meta, table, level, after, *spectra)


def updated_of(meta, restored, table, block, receivers, onto, after):
    shots, rows, width = restored[0].shape
    samples = table.shape[1]
    group = group_of(shots, rows)
    in_specs = [whole(table.shape), ANYWHERE]
    in_specs += [pl.BlockSpec((group, rows, width), lambda step, meta: (step, 0, 0))] * len(restored)
    operands = [meta, table, after, *restored]
    if onto is not None:
        in_specs.append(ANYWHERE)
        operands.append(onto)
    return pl.pallas_call(
        functools.partial(update_kernel, len(restored)),
        grid_spec=pltpu.PrefetchScalarGridSpec(
            num_scalar_prefetch=1,
            grid=(shots // group,),
            in_specs=in_specs,
            out_specs=[
                pl.BlockSpec((group, rows, samples), lambda step, meta: (step, block, 0)),
                whole((8, LANES)),
            ],
            scratch_shapes=[pltpu.VMEM((group * rows, 2 * F), jnp.bfloat16)],
        ),
        out_shape=[
            jax.ShapeDtypeStruct((shots, receivers, samples), jnp.float32),
            jax.ShapeDtypeStruct((8, LANES), jnp.float32),
        ],
        input_output_aliases={} if onto is None else {len(operands) - 1: 0},
        compiler_params=pltpu.CompilerParams(vmem_limit_bytes=48 * 1024 * 1024),
        cost_estimate=pl.CostEstimate(
            flops=4 * F * shots * rows * samples,
            bytes_accessed=4 * F * shots * rows + 2 * table.size + 4 * shots * rows * samples,
            transcendentals=0,
        ),
        name="update",
    )(*operands)


def swapped(array):
    return lax.all_to_all(array, "shot", split_axis=0, concat_axis=0, tiled=True)


def slots_of(peers):
    order = [0]
    for slot in range(peers // 2):
        order += [peers // 2 + slot] + ([slot + 1] if slot + 1 < peers // 2 else [])
    return order


def exchanged(arrays):
    peers = len(arrays)
    return [
        lax.ppermute(arrays[slot], "shot", [(i, i ^ slot) for i in range(peers)]) if slot else arrays[0]
        for slot in slots_of(peers)
    ]


def edges(estimate, observed):
    peers = lax.axis_size("shot")
    up = [(i, i + 1) for i in range(peers - 1)]
    down = [(j, i) for i, j in up]
    tail = jnp.concatenate([estimate[-2:], observed[-1:]])
    head = jnp.concatenate([estimate[:2], observed[:1]])
    return lax.ppermute(tail, "shot", up), lax.ppermute(head, "shot", down)


def chunks_of(receivers):
    if receivers == 128:
        return [(16, 6), (48, 0), (48, 1), (16, 7)]
    rows = min(16, receivers)
    return [(rows, index) for index in range(receivers // rows)]


def direct(estimate, observed, delays, thresholds):
    shots, receivers, samples = estimate.shape
    peers = lax.axis_size("shot")
    rank = lax.axis_index("shot")
    share = F // peers
    meta = jnp.concatenate(
        [jnp.reshape(rank * shots, (1,)), rank ^ jnp.arange(peers, dtype=jnp.int32)]
    ).astype(jnp.int32)
    forward, inverse = (jnp.asarray(table) for table in time_tables(samples, peers))
    table = jnp.asarray(shot_table(delays.shape[0]))
    levels = jnp.tile(lax.dynamic_slice_in_dim(thresholds, rank * share, share), 2)[None, :]
    chunks = chunks_of(receivers)
    sides = edges(estimate, observed)
    last, updated, energy = levels, None, 0.0
    lag = 2
    ahead, behind = {}, {}
    for turn in range(len(chunks) + 2 * lag):
        if turn < len(chunks):
            rows, index = chunks[turn]
            spectra, power = spectra_of(
                meta,
                delays,
                (estimate, observed, *sides),
                forward,
                rows,
                index,
                index,
                peers,
                last,
            )
            last = power
            energy = energy + power
            ahead[turn] = exchanged(spectra)
        place = turn - lag
        if place in ahead:
            shrunk = shrunk_of(meta, ahead.pop(place), table, levels, last)
            last = shrunk[0]
            behind[place] = exchanged(shrunk)
        place = turn - 2 * lag
        if place in behind:
            updated, last = updated_of(
                meta, behind.pop(place), inverse, chunks[place][1], receivers, updated, last
            )
    return updated, energy


def spectral_by_einsum(stepped, forward, inverse, table, level, peers):
    shots, receivers, samples = stepped.shape
    total = table.shape[1]
    share = F // peers
    spectra = jnp.einsum(
        "srt,tdpf->dpfsr",
        stepped,
        forward.reshape(samples, peers, 2, share),
        preferred_element_type=jnp.float32,
    ).astype(jnp.bfloat16)
    mixed = swapped(spectra).transpose(1, 2, 0, 3, 4).reshape(2, share, total, receivers)
    cosine, sine = table[:total], table[total:]
    across = jnp.stack([jnp.stack([cosine, sine]), jnp.stack([-sine, cosine])])
    wave = jnp.einsum("pqks,qfsr->pfkr", across, mixed, preferred_element_type=jnp.float32)
    magnitude = jnp.sqrt(wave[0] * wave[0] + wave[1] * wave[1])
    bound = level[:, None, None]
    factor = jnp.maximum(magnitude - bound, 0.0) / jnp.maximum(magnitude, bound)
    shrunk = (wave * factor[None]).astype(jnp.bfloat16)
    back = jnp.stack([jnp.stack([cosine, -sine]), jnp.stack([sine, cosine])])
    restored = jnp.einsum(
        "pqks,qfkr->pfsr", back, shrunk, preferred_element_type=jnp.float32
    ).astype(jnp.bfloat16)
    restored = restored.reshape(2, share, peers, shots, receivers).transpose(2, 0, 1, 3, 4)
    return jnp.einsum(
        "dpft,dpfsr->srt",
        inverse.reshape(peers, 2, share, samples),
        swapped(restored),
        preferred_element_type=jnp.float32,
    )


def by_einsum(estimate, observed, delays, thresholds):
    shots, receivers, samples = estimate.shape
    peers = lax.axis_size("shot")
    rank = lax.axis_index("shot")
    share = F // peers
    rows = min(16, receivers)
    meta = jnp.reshape(rank * shots, (1,)).astype(jnp.int32)
    sides = edges(estimate, observed)
    energy = 0.0
    parts = []
    for index in range(receivers // rows):
        part, power = stepped_of(meta, delays, (estimate, observed, *sides), rows, index)
        energy = energy + power
        parts.append(part)
    forward, inverse = (jnp.asarray(table) for table in time_tables(samples, peers))
    table = jnp.asarray(shot_table(delays.shape[0]))
    level = lax.dynamic_slice_in_dim(thresholds, rank * share, share)
    stepped = jnp.concatenate(parts, axis=1)
    return spectral_by_einsum(stepped, forward, inverse, table, level, peers), energy


def local(estimate, observed, random_source_delays, thresholds):
    receivers, samples = estimate.shape[1:]
    peers = lax.axis_size("shot")
    filled = peers >= 4 and peers & (peers - 1) == 0 and (2 * F // peers) % LANES == 0
    path = direct if filled else by_einsum
    updated, energy = path(estimate, observed, random_source_delays, thresholds)
    misfit = lax.psum(jnp.sum(energy, axis=1), "patch") / (
        receivers * lax.axis_size("patch") * samples
    )
    return updated, misfit


def solution(mesh):
    in_specs = (P("shot", "patch", None), P("shot", "patch", None), P(), P())
    out_specs = (P("shot", "patch", None), P("shot"))
    return jax.shard_map(local, mesh=mesh, in_specs=in_specs, out_specs=out_specs, check_vma=False)
```

```python
import functools

import jax
import jax.numpy as jnp
import ml_dtypes
import numpy as np
from jax import lax
from jax.experimental import pallas as pl
from jax.experimental.pallas import tpu as pltpu
from jax.sharding import PartitionSpec as P

F = 512
SOURCE_SPACING = 512
JITTER = 256
STEP = 0.5
LANES = 128
NEAR = SOURCE_SPACING - JITTER
FAR = SOURCE_SPACING + JITTER
HALO = 3


def time_tables(samples, blocks):
    freq = np.arange(F, dtype=np.int32)
    sample = np.arange(samples, dtype=np.int32)
    phase = (freq[:, None] * sample[None, :] % samples).astype(np.float32)
    angle = np.float32(2.0 * np.pi) * phase / np.float32(samples)
    root = np.sqrt(np.float32(samples))
    weight = np.where(freq == 0, 1.0, 2.0).astype(np.float32)[:, None] / root
    forward = np.stack([np.cos(angle) / root, -np.sin(angle) / root])
    inverse = np.stack([weight * np.cos(angle), -weight * np.sin(angle)])

    def ordered(table):
        table = table.astype(np.float32).astype(ml_dtypes.bfloat16)
        table = table.reshape(2, blocks, F // blocks, samples).transpose(1, 0, 2, 3)
        return table.reshape(2 * F, samples)

    return np.ascontiguousarray(ordered(forward).T), ordered(inverse)


def shot_table(shots):
    index = np.arange(shots, dtype=np.int32)
    phase = (index[:, None] * index[None, :] % shots).astype(np.float32)
    angle = np.float32(2.0 * np.pi) * phase / np.float32(shots)
    root = np.sqrt(np.float32(shots))
    table = np.concatenate([np.cos(angle) / root, np.sin(angle) / root])
    return table.astype(np.float32).astype(ml_dtypes.bfloat16)


def band(meta_ref, slot, width):
    return pl.ds(pl.multiple_of(meta_ref[1 + slot] * width, width), width)


def blend_into(
    meta_ref, delay_ref, est_ref, obs_ref, before_ref, after_ref, energy_ref, est32, res32, store
):
    shots, rows, samples = est_ref.shape
    columns = samples // LANES
    margin = (FAR - NEAR) // LANES
    inner = (samples - NEAR) // LANES
    skip = NEAR // LANES
    total = delay_ref.shape[0]
    first = meta_ref[0]
    lane = lax.broadcasted_iota(jnp.int32, (1, rows, LANES), 2)

    def ahead(shot):
        shot = jnp.clip(shot, 0, total - 2)
        return jnp.clip(SOURCE_SPACING + delay_ref[shot + 1] - delay_ref[shot], NEAR + 1, FAR - 1)

    def window(field, slot, start):
        column, rest = start // LANES, start % LANES
        wide = field[slot, pl.ds(column, inner + 1)]
        turned = pltpu.roll(
            wide.reshape((inner + 1) * rows, LANES), (LANES - rest) % LANES, 1
        ).reshape(inner + 1, rows, LANES)
        return jnp.where(lane < LANES - rest, turned[:-1], turned[1:])

    def blended(field, slot, shot):
        later = window(field, slot + 1, margin * LANES + NEAR - ahead(shot))
        earlier = window(field, slot - 1, margin * LANES + ahead(shot - 1))
        return later, earlier

    def fill(field, slot, values):
        blank = jnp.zeros((margin, rows, LANES), jnp.float32)
        field[slot, pl.ds(0, margin)] = blank
        field[slot, pl.ds(margin + columns, margin)] = blank
        for column in range(columns):
            field[slot, margin + column] = values(column)

    def cut(ref, shot):
        return lambda column: ref[shot, :, column * LANES : (column + 1) * LANES].astype(jnp.float32)

    for slot in range(2):
        fill(est32, slot, cut(before_ref, slot))
        fill(est32, shots + 2 + slot, cut(after_ref, slot))

    def load(shot, carry):
        fill(est32, shot + 2, cut(est_ref, shot))
        return carry

    lax.fori_loop(0, shots, load, 0, unroll=2)

    def residual(place, values):
        shot = first + place - 1
        inside = jnp.logical_and(shot >= 0, shot < total)
        later, earlier = blended(est32, place + 1, shot)
        power = jnp.zeros((rows, LANES), jnp.float32)
        cells = []
        for column in range(columns):
            cell = est32[place + 1, margin + column]
            if column >= skip:
                cell = cell + later[column - skip]
            if column < inner:
                cell = cell + earlier[column]
            cell = jnp.where(inside, values(column) - cell, 0.0)
            power = power + cell * cell
            cells.append(cell)
        fill(res32, place, lambda column: cells[column])
        return power

    residual(0, cut(before_ref, 2))
    residual(shots + 1, cut(after_ref, 2))

    def middle(shot, carry):
        power = residual(shot + 1, cut(obs_ref, shot))
        energy_ref[pl.ds(shot, 1), :] = jnp.sum(power, axis=0, keepdims=True)
        return carry

    lax.fori_loop(0, shots, middle, 0, unroll=4)

    def step(shot, carry):
        later, earlier = blended(res32, shot + 1, first + shot)
        for column in range(columns):
            cell = res32[shot + 1, margin + column]
            if column >= skip:
                cell = cell + later[column - skip]
            if column < inner:
                cell = cell + earlier[column]
            cell = est32[shot + 2, margin + column] + STEP * cell
            store(shot, column, cell.astype(jnp.bfloat16))
        return carry

    lax.fori_loop(0, shots, step, 0, unroll=4)


def spectra_kernel(
    meta_ref, delay_ref, est_ref, obs_ref, before_ref, after_ref, table_ref, _, *refs
):
    *out_refs, energy_ref, est32, res32, stepped, result = refs
    shots, rows, samples = est_ref.shape
    width = out_refs[0].shape[2]

    def store(shot, column, values):
        start = pl.multiple_of(shot * rows, rows)
        stepped[pl.ds(start, rows), column * LANES : (column + 1) * LANES] = values

    blend_into(
        meta_ref, delay_ref, est_ref, obs_ref, before_ref, after_ref, energy_ref, est32, res32, store
    )
    held = result.shape[0]
    group = held // rows

    def transform(part, carry):
        start = pl.multiple_of(part * held, held)
        result[...] = jnp.dot(
            stepped[pl.ds(start, held), :], table_ref[...], preferred_element_type=jnp.float32
        ).astype(jnp.bfloat16)
        for slot, ref in enumerate(out_refs):
            ref[pl.ds(part * group, group)] = result[:, band(meta_ref, slot, width)].reshape(
                group, rows, width
            )
        return carry

    lax.fori_loop(0, shots // group, transform, 0)


def step_kernel(
    meta_ref, delay_ref, est_ref, obs_ref, before_ref, after_ref, out_ref, energy_ref, est32, res32
):
    def store(shot, column, values):
        out_ref[shot, :, column * LANES : (column + 1) * LANES] = values

    blend_into(
        meta_ref, delay_ref, est_ref, obs_ref, before_ref, after_ref, energy_ref, est32, res32, store
    )


def shots_kernel(meta_ref, table_ref, level_ref, _, *refs):
    *refs, wide, back = refs
    spectra_refs, out_refs = refs[: len(refs) // 2], refs[len(refs) // 2 :]
    held, rows, width = out_refs[0].shape
    shots = wide.shape[0] // rows
    half = width // 2

    def place(slot):
        size = held * rows
        return pl.ds(pl.multiple_of(meta_ref[1 + slot] * size, size), size)

    for slot, ref in zip(slots_of(len(spectra_refs)), spectra_refs):
        wide[place(slot), :] = ref[...].reshape(held * rows, width).astype(jnp.float32)
    level = level_ref[...]
    sign = jnp.where(
        lax.broadcasted_iota(jnp.int32, (1, width), 1) < half, jnp.float32(1.0), jnp.float32(-1.0)
    )

    def pair(index, carry):
        picks = [pl.ds(index * 2 + turn, shots, stride=rows) for turn in range(2)]
        block = jnp.concatenate([wide[pick, :] for pick in picks], axis=1).astype(jnp.bfloat16)
        both = jnp.dot(table_ref[...], block, preferred_element_type=jnp.float32)
        kept = []
        for turn in range(2):
            own = both[:, turn * width : (turn + 1) * width]
            wave = own[:shots] + sign * pltpu.roll(own[shots:], half, 1)
            power = wave * wave
            power = power + pltpu.roll(power, half, 1)
            factor = jnp.maximum(1.0 - level * lax.rsqrt(power), 0.0)
            kept.append((wave * factor).astype(jnp.bfloat16))
        both = jnp.dot(table_ref[...], jnp.concatenate(kept, axis=1), preferred_element_type=jnp.float32)
        for turn in range(2):
            own = both[:, turn * width : (turn + 1) * width]
            back[picks[turn], :] = own[:shots] - sign * pltpu.roll(own[shots:], half, 1)
        return carry

    lax.fori_loop(0, rows // 2, pair, 0, unroll=2)
    for slot, ref in enumerate(out_refs):
        ref[...] = back[place(slot), :].astype(jnp.bfloat16).reshape(held, rows, width)


def update_kernel(inputs, meta_ref, table_ref, _, *refs):
    restored_refs, (out_ref, turn_ref, whole_rows) = refs[:inputs], refs[-3:]
    held, rows, width = restored_refs[0].shape
    for slot, ref in zip(slots_of(inputs), restored_refs):
        whole_rows[:, band(meta_ref, slot, width)] = ref[...].reshape(held * rows, width)
    out_ref[...] = jnp.dot(
        whole_rows[...], table_ref[...], preferred_element_type=jnp.float32
    ).reshape(out_ref.shape)
    turn_ref[...] = jnp.zeros_like(turn_ref)


def whole(shape):
    return pl.BlockSpec(shape, lambda *_: (0,) * len(shape))


def blend_specs(shots, rows, samples, block, edge_block):
    at = lambda step, meta, delays: (0, block, 0)
    edge = lambda step, meta, delays: (0, edge_block, 0)
    return [
        pl.BlockSpec((shots, rows, samples), at),
        pl.BlockSpec((shots, rows, samples), at),
        pl.BlockSpec((HALO, rows, samples), edge),
        pl.BlockSpec((HALO, rows, samples), edge),
    ]


def blend_scratch(shots, rows, samples):
    columns = (samples + 2 * (FAR - NEAR)) // LANES
    return [
        pltpu.VMEM((shots + 4, columns, rows, LANES), jnp.float32),
        pltpu.VMEM((shots + 2, columns, rows, LANES), jnp.float32),
    ]


PARAMS = pltpu.CompilerParams(vmem_limit_bytes=60 * 1024 * 1024)
ANYWHERE = pl.BlockSpec(memory_space=pl.ANY)


def spectra_of(meta, delays, fields, table, rows, block, edge_block, peers, after):
    shots, _, samples = fields[0].shape
    shape = (shots, rows, 2 * F // peers)
    group = min(shots, max(1, 256 // rows))
    *spectra, energy = pl.pallas_call(
        spectra_kernel,
        grid_spec=pltpu.PrefetchScalarGridSpec(
            num_scalar_prefetch=2,
            grid=(1,),
            in_specs=blend_specs(shots, rows, samples, block, edge_block)
            + [whole(table.shape), ANYWHERE],
            out_specs=[whole(shape)] * peers + [whole((shots, LANES))],
            scratch_shapes=blend_scratch(shots, rows, samples)
            + [
                pltpu.VMEM((shots * rows, samples), jnp.bfloat16),
                pltpu.VMEM((group * rows, 2 * F), jnp.bfloat16),
            ],
        ),
        out_shape=[pltpu.HBM(shape, jnp.bfloat16)] * peers + [pltpu.HBM((shots, LANES), jnp.float32)],
        compiler_params=PARAMS,
        cost_estimate=pl.CostEstimate(
            flops=4 * F * shots * rows * samples,
            bytes_accessed=3 * 2 * shots * rows * samples + table.size * 2,
            transcendentals=0,
        ),
        name="spectra",
    )(meta, delays, *fields, table, after)
    return spectra, energy


def stepped_of(meta, delays, fields, rows, index):
    shots, _, samples = fields[0].shape
    return pl.pallas_call(
        step_kernel,
        grid_spec=pltpu.PrefetchScalarGridSpec(
            num_scalar_prefetch=2,
            grid=(1,),
            in_specs=blend_specs(shots, rows, samples, index, index),
            out_specs=[whole((shots, rows, samples)), whole((shots, LANES))],
            scratch_shapes=blend_scratch(shots, rows, samples),
        ),
        out_shape=[
            jax.ShapeDtypeStruct((shots, rows, samples), jnp.bfloat16),
            jax.ShapeDtypeStruct((shots, LANES), jnp.float32),
        ],
        compiler_params=PARAMS,
        name="stepped",
    )(meta, delays, *fields)


def shrunk_of(meta, spectra, table, level, after):
    shape = spectra[0].shape
    held, rows, width = shape
    peers = len(spectra)
    return pl.pallas_call(
        shots_kernel,
        grid_spec=pltpu.PrefetchScalarGridSpec(
            num_scalar_prefetch=1,
            grid=(1,),
            in_specs=[whole(table.shape), whole(level.shape), ANYWHERE]
            + [whole(shape)] * peers,
            out_specs=[whole(shape)] * peers,
            scratch_shapes=[pltpu.VMEM((peers * held * rows, width), jnp.float32)] * 2,
        ),
        out_shape=[pltpu.HBM(shape, jnp.bfloat16)] * peers,
        compiler_params=PARAMS,
        cost_estimate=pl.CostEstimate(
            flops=8 * (peers * held) ** 2 * rows * width,
            bytes_accessed=4 * peers * held * rows * width + 2 * table.size,
            transcendentals=peers * held * rows * width,
        ),
        name="shrink",
    )(meta, table, level, after, *spectra)


def updated_of(meta, restored, table, block, receivers, onto, after):
    shots, rows, width = restored[0].shape
    samples = table.shape[1]
    group = min(shots, max(1, 256 // rows))
    in_specs = [whole(table.shape), ANYWHERE]
    in_specs += [pl.BlockSpec((group, rows, width), lambda step, meta: (step, 0, 0))] * len(restored)
    operands = [meta, table, after, *restored]
    if onto is not None:
        in_specs.append(ANYWHERE)
        operands.append(onto)
    return pl.pallas_call(
        functools.partial(update_kernel, len(restored)),
        grid_spec=pltpu.PrefetchScalarGridSpec(
            num_scalar_prefetch=1,
            grid=(shots // group,),
            in_specs=in_specs,
            out_specs=[
                pl.BlockSpec((group, rows, samples), lambda step, meta: (step, block, 0)),
                whole((8, LANES)),
            ],
            scratch_shapes=[pltpu.VMEM((group * rows, 2 * F), jnp.bfloat16)],
        ),
        out_shape=[
            jax.ShapeDtypeStruct((shots, receivers, samples), jnp.float32),
            jax.ShapeDtypeStruct((8, LANES), jnp.float32),
        ],
        input_output_aliases={} if onto is None else {len(operands) - 1: 0},
        compiler_params=pltpu.CompilerParams(vmem_limit_bytes=48 * 1024 * 1024),
        cost_estimate=pl.CostEstimate(
            flops=4 * F * shots * rows * samples,
            bytes_accessed=4 * F * shots * rows + 2 * table.size + 4 * shots * rows * samples,
            transcendentals=0,
        ),
        name="update",
    )(*operands)


def swapped(array):
    return lax.all_to_all(array, "shot", split_axis=0, concat_axis=0, tiled=True)


def slots_of(peers):
    return [0, 1, *range(peers // 2, peers), *range(2, peers // 2)]


def exchanged(arrays):
    peers = len(arrays)
    return [
        lax.ppermute(arrays[slot], "shot", [(i, i ^ slot) for i in range(peers)]) if slot else arrays[0]
        for slot in slots_of(peers)
    ]


def edges(estimate, observed):
    peers = lax.axis_size("shot")
    up = [(i, i + 1) for i in range(peers - 1)]
    down = [(j, i) for i, j in up]
    tail = jnp.concatenate([estimate[-2:], observed[-1:]])
    head = jnp.concatenate([estimate[:2], observed[:1]])
    return lax.ppermute(tail, "shot", up), lax.ppermute(head, "shot", down)


def chunks_of(receivers):
    if receivers == 128:
        return [(16, 0), (32, 1), (32, 2), (32, 3), (16, 1)]
    rows = min(16, receivers)
    return [(rows, index) for index in range(receivers // rows)]


def direct(estimate, observed, delays, thresholds):
    shots, receivers, samples = estimate.shape
    peers = lax.axis_size("shot")
    rank = lax.axis_index("shot")
    share = F // peers
    meta = jnp.concatenate(
        [jnp.reshape(rank * shots, (1,)), rank ^ jnp.arange(peers, dtype=jnp.int32)]
    ).astype(jnp.int32)
    forward, inverse = (jnp.asarray(table) for table in time_tables(samples, peers))
    table = jnp.asarray(shot_table(delays.shape[0]))
    levels = jnp.tile(lax.dynamic_slice_in_dim(thresholds, rank * share, share), 2)[None, :]
    chunks = chunks_of(receivers)
    sides = edges(estimate, observed)
    last, updated, energy = levels, None, 0.0
    lag = 2
    ahead, behind = {}, {}
    for turn in range(len(chunks) + 2 * lag):
        if turn < len(chunks):
            rows, index = chunks[turn]
            spectra, power = spectra_of(
                meta,
                delays,
                (estimate, observed, *sides),
                forward,
                rows,
                index,
                index,
                peers,
                last,
            )
            last = power
            energy = energy + power
            ahead[turn] = exchanged(spectra)
        place = turn - lag
        if place in ahead:
            shrunk = shrunk_of(meta, ahead.pop(place), table, levels, last)
            last = shrunk[0]
            behind[place] = exchanged(shrunk)
        place = turn - 2 * lag
        if place in behind:
            updated, last = updated_of(
                meta, behind.pop(place), inverse, chunks[place][1], receivers, updated, last
            )
    return updated, energy


def spectral_by_einsum(stepped, forward, inverse, table, level, peers):
    shots, receivers, samples = stepped.shape
    total = table.shape[1]
    share = F // peers
    spectra = jnp.einsum(
        "srt,tdpf->dpfsr",
        stepped,
        forward.reshape(samples, peers, 2, share),
        preferred_element_type=jnp.float32,
    ).astype(jnp.bfloat16)
    mixed = swapped(spectra).transpose(1, 2, 0, 3, 4).reshape(2, share, total, receivers)
    cosine, sine = table[:total], table[total:]
    across = jnp.stack([jnp.stack([cosine, sine]), jnp.stack([-sine, cosine])])
    wave = jnp.einsum("pqks,qfsr->pfkr", across, mixed, preferred_element_type=jnp.float32)
    magnitude = jnp.sqrt(wave[0] * wave[0] + wave[1] * wave[1])
    bound = level[:, None, None]
    factor = jnp.maximum(magnitude - bound, 0.0) / jnp.maximum(magnitude, bound)
    shrunk = (wave * factor[None]).astype(jnp.bfloat16)
    back = jnp.stack([jnp.stack([cosine, -sine]), jnp.stack([sine, cosine])])
    restored = jnp.einsum(
        "pqks,qfkr->pfsr", back, shrunk, preferred_element_type=jnp.float32
    ).astype(jnp.bfloat16)
    restored = restored.reshape(2, share, peers, shots, receivers).transpose(2, 0, 1, 3, 4)
    return jnp.einsum(
        "dpft,dpfsr->srt",
        inverse.reshape(peers, 2, share, samples),
        swapped(restored),
        preferred_element_type=jnp.float32,
    )


def by_einsum(estimate, observed, delays, thresholds):
    shots, receivers, samples = estimate.shape
    peers = lax.axis_size("shot")
    rank = lax.axis_index("shot")
    share = F // peers
    rows = min(16, receivers)
    meta = jnp.reshape(rank * shots, (1,)).astype(jnp.int32)
    sides = edges(estimate, observed)
    energy = 0.0
    parts = []
    for index in range(receivers // rows):
        part, power = stepped_of(meta, delays, (estimate, observed, *sides), rows, index)
        energy = energy + power
        parts.append(part)
    forward, inverse = (jnp.asarray(table) for table in time_tables(samples, peers))
    table = jnp.asarray(shot_table(delays.shape[0]))
    level = lax.dynamic_slice_in_dim(thresholds, rank * share, share)
    stepped = jnp.concatenate(parts, axis=1)
    return spectral_by_einsum(stepped, forward, inverse, table, level, peers), energy


def local(estimate, observed, random_source_delays, thresholds):
    receivers, samples = estimate.shape[1:]
    peers = lax.axis_size("shot")
    filled = peers >= 4 and peers & (peers - 1) == 0 and (2 * F // peers) % LANES == 0
    path = direct if filled else by_einsum
    updated, energy = path(estimate, observed, random_source_delays, thresholds)
    misfit = lax.psum(jnp.sum(energy, axis=1), "patch") / (
        receivers * lax.axis_size("patch") * samples
    )
    return updated, misfit


def solution(mesh):
    in_specs = (P("shot", "patch", None), P("shot", "patch", None), P(), P())
    out_specs = (P("shot", "patch", None), P("shot"))
    return jax.shard_map(local, mesh=mesh, in_specs=in_specs, out_specs=out_specs, check_vma=False)
```

```python
import functools

import jax
import jax.numpy as jnp
import ml_dtypes
import numpy as np
from jax import lax
from jax.experimental import pallas as pl
from jax.experimental.pallas import tpu as pltpu
from jax.sharding import PartitionSpec as P

F = 512
SOURCE_SPACING = 512
JITTER = 256
STEP = 0.5
LANES = 128
NEAR = SOURCE_SPACING - JITTER
FAR = SOURCE_SPACING + JITTER
HALO = 3


def time_tables(samples, blocks):
    freq = np.arange(F, dtype=np.int32)
    sample = np.arange(samples, dtype=np.int32)
    phase = (freq[:, None] * sample[None, :] % samples).astype(np.float32)
    angle = np.float32(2.0 * np.pi) * phase / np.float32(samples)
    root = np.sqrt(np.float32(samples))
    weight = np.where(freq == 0, 1.0, 2.0).astype(np.float32)[:, None] / root
    forward = np.stack([np.cos(angle) / root, -np.sin(angle) / root])
    inverse = np.stack([weight * np.cos(angle), -weight * np.sin(angle)])

    def ordered(table):
        table = table.astype(np.float32).astype(ml_dtypes.bfloat16)
        table = table.reshape(2, blocks, F // blocks, samples).transpose(1, 0, 2, 3)
        return table.reshape(2 * F, samples)

    return np.ascontiguousarray(ordered(forward).T), ordered(inverse)


def shot_table(shots):
    index = np.arange(shots, dtype=np.int32)
    phase = (index[:, None] * index[None, :] % shots).astype(np.float32)
    angle = np.float32(2.0 * np.pi) * phase / np.float32(shots)
    root = np.sqrt(np.float32(shots))
    table = np.concatenate([np.cos(angle) / root, np.sin(angle) / root])
    return table.astype(np.float32).astype(ml_dtypes.bfloat16)


def band(meta_ref, slot, width):
    return pl.ds(pl.multiple_of(meta_ref[1 + slot] * width, width), width)


def blend_into(
    meta_ref, delay_ref, est_ref, obs_ref, before_ref, after_ref, energy_ref, est32, res32, store
):
    shots, rows, samples = est_ref.shape
    columns = samples // LANES
    margin = (FAR - NEAR) // LANES
    inner = (samples - NEAR) // LANES
    skip = NEAR // LANES
    total = delay_ref.shape[0]
    first = meta_ref[0]
    lane = lax.broadcasted_iota(jnp.int32, (1, rows, LANES), 2)

    def ahead(shot):
        shot = jnp.clip(shot, 0, total - 2)
        return jnp.clip(SOURCE_SPACING + delay_ref[shot + 1] - delay_ref[shot], NEAR + 1, FAR - 1)

    def window(field, slot, start):
        column, rest = start // LANES, start % LANES
        wide = field[slot, pl.ds(column, inner + 1)]
        turned = pltpu.roll(
            wide.reshape((inner + 1) * rows, LANES), (LANES - rest) % LANES, 1
        ).reshape(inner + 1, rows, LANES)
        return jnp.where(lane < LANES - rest, turned[:-1], turned[1:])

    def blended(field, slot, shot):
        later = window(field, slot + 1, margin * LANES + NEAR - ahead(shot))
        earlier = window(field, slot - 1, margin * LANES + ahead(shot - 1))
        return later, earlier

    def fill(field, slot, values):
        blank = jnp.zeros((margin, rows, LANES), jnp.float32)
        field[slot, pl.ds(0, margin)] = blank
        field[slot, pl.ds(margin + columns, margin)] = blank
        for column in range(columns):
            field[slot, margin + column] = values(column)

    def cut(ref, shot):
        return lambda column: ref[shot, :, column * LANES : (column + 1) * LANES].astype(jnp.float32)

    for slot in range(2):
        fill(est32, slot, cut(before_ref, slot))
        fill(est32, shots + 2 + slot, cut(after_ref, slot))

    def load(shot, carry):
        fill(est32, shot + 2, cut(est_ref, shot))
        return carry

    lax.fori_loop(0, shots, load, 0, unroll=2)

    def residual(place, values):
        shot = first + place - 1
        inside = jnp.logical_and(shot >= 0, shot < total)
        later, earlier = blended(est32, place + 1, shot)
        power = jnp.zeros((rows, LANES), jnp.float32)
        cells = []
        for column in range(columns):
            cell = est32[place + 1, margin + column]
            if column >= skip:
                cell = cell + later[column - skip]
            if column < inner:
                cell = cell + earlier[column]
            cell = jnp.where(inside, values(column) - cell, 0.0)
            power = power + cell * cell
            cells.append(cell)
        fill(res32, place, lambda column: cells[column])
        return power

    residual(0, cut(before_ref, 2))
    residual(shots + 1, cut(after_ref, 2))

    def middle(shot, carry):
        power = residual(shot + 1, cut(obs_ref, shot))
        energy_ref[pl.ds(shot, 1), :] = jnp.sum(power, axis=0, keepdims=True)
        return carry

    lax.fori_loop(0, shots, middle, 0, unroll=4)

    def step(shot, carry):
        later, earlier = blended(res32, shot + 1, first + shot)
        for column in range(columns):
            cell = res32[shot + 1, margin + column]
            if column >= skip:
                cell = cell + later[column - skip]
            if column < inner:
                cell = cell + earlier[column]
            cell = est32[shot + 2, margin + column] + STEP * cell
            store(shot, column, cell.astype(jnp.bfloat16))
        return carry

    lax.fori_loop(0, shots, step, 0, unroll=4)


def spectra_kernel(
    meta_ref, delay_ref, est_ref, obs_ref, before_ref, after_ref, table_ref, _, *refs
):
    *out_refs, energy_ref, est32, res32, stepped, result = refs
    shots, rows, samples = est_ref.shape
    width = out_refs[0].shape[2]

    def store(shot, column, values):
        start = pl.multiple_of(shot * rows, rows)
        stepped[pl.ds(start, rows), column * LANES : (column + 1) * LANES] = values

    blend_into(
        meta_ref, delay_ref, est_ref, obs_ref, before_ref, after_ref, energy_ref, est32, res32, store
    )
    held = result.shape[0]
    group = held // rows

    def transform(part, carry):
        start = pl.multiple_of(part * held, held)
        result[...] = jnp.dot(
            stepped[pl.ds(start, held), :], table_ref[...], preferred_element_type=jnp.float32
        ).astype(jnp.bfloat16)
        for slot, ref in enumerate(out_refs):
            ref[pl.ds(part * group, group)] = result[:, band(meta_ref, slot, width)].reshape(
                group, rows, width
            )
        return carry

    lax.fori_loop(0, shots // group, transform, 0)


def step_kernel(
    meta_ref, delay_ref, est_ref, obs_ref, before_ref, after_ref, out_ref, energy_ref, est32, res32
):
    def store(shot, column, values):
        out_ref[shot, :, column * LANES : (column + 1) * LANES] = values

    blend_into(
        meta_ref, delay_ref, est_ref, obs_ref, before_ref, after_ref, energy_ref, est32, res32, store
    )


def shots_kernel(meta_ref, table_ref, level_ref, _, *refs):
    *refs, wide, back = refs
    spectra_refs, out_refs = refs[: len(refs) // 2], refs[len(refs) // 2 :]
    held, rows, width = out_refs[0].shape
    shots = wide.shape[0] // rows
    half = width // 2

    def place(slot):
        size = held * rows
        return pl.ds(pl.multiple_of(meta_ref[1 + slot] * size, size), size)

    for slot, ref in zip(slots_of(len(spectra_refs)), spectra_refs):
        wide[place(slot), :] = ref[...].reshape(held * rows, width).astype(jnp.float32)
    level = level_ref[...]
    sign = jnp.where(
        lax.broadcasted_iota(jnp.int32, (1, width), 1) < half, jnp.float32(1.0), jnp.float32(-1.0)
    )

    def pair(index, carry):
        picks = [pl.ds(index * 2 + turn, shots, stride=rows) for turn in range(2)]
        block = jnp.concatenate([wide[pick, :] for pick in picks], axis=1).astype(jnp.bfloat16)
        both = jnp.dot(table_ref[...], block, preferred_element_type=jnp.float32)
        kept = []
        for turn in range(2):
            own = both[:, turn * width : (turn + 1) * width]
            wave = own[:shots] + sign * pltpu.roll(own[shots:], half, 1)
            power = wave * wave
            power = power + pltpu.roll(power, half, 1)
            factor = jnp.maximum(1.0 - level * lax.rsqrt(power), 0.0)
            kept.append((wave * factor).astype(jnp.bfloat16))
        both = jnp.dot(table_ref[...], jnp.concatenate(kept, axis=1), preferred_element_type=jnp.float32)
        for turn in range(2):
            own = both[:, turn * width : (turn + 1) * width]
            back[picks[turn], :] = own[:shots] - sign * pltpu.roll(own[shots:], half, 1)
        return carry

    lax.fori_loop(0, rows // 2, pair, 0, unroll=2)
    for slot, ref in enumerate(out_refs):
        ref[...] = back[place(slot), :].astype(jnp.bfloat16).reshape(held, rows, width)


def update_kernel(inputs, meta_ref, table_ref, _, *refs):
    restored_refs, (out_ref, turn_ref, whole_rows) = refs[:inputs], refs[-3:]
    held, rows, width = restored_refs[0].shape
    for slot, ref in zip(slots_of(inputs), restored_refs):
        whole_rows[:, band(meta_ref, slot, width)] = ref[...].reshape(held * rows, width)
    out_ref[...] = jnp.dot(
        whole_rows[...], table_ref[...], preferred_element_type=jnp.float32
    ).reshape(out_ref.shape)
    turn_ref[...] = jnp.zeros_like(turn_ref)


def whole(shape):
    return pl.BlockSpec(shape, lambda *_: (0,) * len(shape))


def blend_specs(shots, rows, samples, block, edge_block):
    at = lambda step, meta, delays: (0, block, 0)
    edge = lambda step, meta, delays: (0, edge_block, 0)
    return [
        pl.BlockSpec((shots, rows, samples), at),
        pl.BlockSpec((shots, rows, samples), at),
        pl.BlockSpec((HALO, rows, samples), edge),
        pl.BlockSpec((HALO, rows, samples), edge),
    ]


def blend_scratch(shots, rows, samples):
    columns = (samples + 2 * (FAR - NEAR)) // LANES
    return [
        pltpu.VMEM((shots + 4, columns, rows, LANES), jnp.float32),
        pltpu.VMEM((shots + 2, columns, rows, LANES), jnp.float32),
    ]


PARAMS = pltpu.CompilerParams(vmem_limit_bytes=60 * 1024 * 1024)
ANYWHERE = pl.BlockSpec(memory_space=pl.ANY)


def spectra_of(meta, delays, fields, table, rows, block, edge_block, peers, after):
    shots, _, samples = fields[0].shape
    shape = (shots, rows, 2 * F // peers)
    group = min(shots, max(1, 256 // rows))
    *spectra, energy = pl.pallas_call(
        spectra_kernel,
        grid_spec=pltpu.PrefetchScalarGridSpec(
            num_scalar_prefetch=2,
            grid=(1,),
            in_specs=blend_specs(shots, rows, samples, block, edge_block)
            + [whole(table.shape), ANYWHERE],
            out_specs=[whole(shape)] * peers + [whole((shots, LANES))],
            scratch_shapes=blend_scratch(shots, rows, samples)
            + [
                pltpu.VMEM((shots * rows, samples), jnp.bfloat16),
                pltpu.VMEM((group * rows, 2 * F), jnp.bfloat16),
            ],
        ),
        out_shape=[pltpu.HBM(shape, jnp.bfloat16)] * peers + [pltpu.HBM((shots, LANES), jnp.float32)],
        compiler_params=PARAMS,
        cost_estimate=pl.CostEstimate(
            flops=4 * F * shots * rows * samples,
            bytes_accessed=3 * 2 * shots * rows * samples + table.size * 2,
            transcendentals=0,
        ),
        name="spectra",
    )(meta, delays, *fields, table, after)
    return spectra, energy


def stepped_of(meta, delays, fields, rows, index):
    shots, _, samples = fields[0].shape
    return pl.pallas_call(
        step_kernel,
        grid_spec=pltpu.PrefetchScalarGridSpec(
            num_scalar_prefetch=2,
            grid=(1,),
            in_specs=blend_specs(shots, rows, samples, index, index),
            out_specs=[whole((shots, rows, samples)), whole((shots, LANES))],
            scratch_shapes=blend_scratch(shots, rows, samples),
        ),
        out_shape=[
            jax.ShapeDtypeStruct((shots, rows, samples), jnp.bfloat16),
            jax.ShapeDtypeStruct((shots, LANES), jnp.float32),
        ],
        compiler_params=PARAMS,
        name="stepped",
    )(meta, delays, *fields)


def shrunk_of(meta, spectra, table, level, after):
    shape = spectra[0].shape
    held, rows, width = shape
    peers = len(spectra)
    return pl.pallas_call(
        shots_kernel,
        grid_spec=pltpu.PrefetchScalarGridSpec(
            num_scalar_prefetch=1,
            grid=(1,),
            in_specs=[whole(table.shape), whole(level.shape), ANYWHERE]
            + [whole(shape)] * peers,
            out_specs=[whole(shape)] * peers,
            scratch_shapes=[pltpu.VMEM((peers * held * rows, width), jnp.float32)] * 2,
        ),
        out_shape=[pltpu.HBM(shape, jnp.bfloat16)] * peers,
        compiler_params=PARAMS,
        cost_estimate=pl.CostEstimate(
            flops=8 * (peers * held) ** 2 * rows * width,
            bytes_accessed=4 * peers * held * rows * width + 2 * table.size,
            transcendentals=peers * held * rows * width,
        ),
        name="shrink",
    )(meta, table, level, after, *spectra)


def updated_of(meta, restored, table, block, receivers, onto, after):
    shots, rows, width = restored[0].shape
    samples = table.shape[1]
    group = min(shots, max(1, 256 // rows))
    in_specs = [whole(table.shape), ANYWHERE]
    in_specs += [pl.BlockSpec((group, rows, width), lambda step, meta: (step, 0, 0))] * len(restored)
    operands = [meta, table, after, *restored]
    if onto is not None:
        in_specs.append(ANYWHERE)
        operands.append(onto)
    return pl.pallas_call(
        functools.partial(update_kernel, len(restored)),
        grid_spec=pltpu.PrefetchScalarGridSpec(
            num_scalar_prefetch=1,
            grid=(shots // group,),
            in_specs=in_specs,
            out_specs=[
                pl.BlockSpec((group, rows, samples), lambda step, meta: (step, block, 0)),
                whole((8, LANES)),
            ],
            scratch_shapes=[pltpu.VMEM((group * rows, 2 * F), jnp.bfloat16)],
        ),
        out_shape=[
            jax.ShapeDtypeStruct((shots, receivers, samples), jnp.float32),
            jax.ShapeDtypeStruct((8, LANES), jnp.float32),
        ],
        input_output_aliases={} if onto is None else {len(operands) - 1: 0},
        compiler_params=pltpu.CompilerParams(vmem_limit_bytes=48 * 1024 * 1024),
        cost_estimate=pl.CostEstimate(
            flops=4 * F * shots * rows * samples,
            bytes_accessed=4 * F * shots * rows + 2 * table.size + 4 * shots * rows * samples,
            transcendentals=0,
        ),
        name="update",
    )(*operands)


def swapped(array):
    return lax.all_to_all(array, "shot", split_axis=0, concat_axis=0, tiled=True)


def slots_of(peers):
    order = [0]
    for slot in range(peers // 2):
        order += ([slot + 1] if slot + 1 < peers // 2 else []) + [peers // 2 + slot]
    return order


def exchanged(arrays):
    peers = len(arrays)
    return [
        lax.ppermute(arrays[slot], "shot", [(i, i ^ slot) for i in range(peers)]) if slot else arrays[0]
        for slot in slots_of(peers)
    ]


def edges(estimate, observed):
    peers = lax.axis_size("shot")
    up = [(i, i + 1) for i in range(peers - 1)]
    down = [(j, i) for i, j in up]
    tail = jnp.concatenate([estimate[-2:], observed[-1:]])
    head = jnp.concatenate([estimate[:2], observed[:1]])
    return lax.ppermute(tail, "shot", up), lax.ppermute(head, "shot", down)


def chunks_of(receivers):
    if receivers == 128:
        return [(16, 0), (32, 1), (32, 2), (32, 3), (16, 1)]
    rows = min(16, receivers)
    return [(rows, index) for index in range(receivers // rows)]


def direct(estimate, observed, delays, thresholds):
    shots, receivers, samples = estimate.shape
    peers = lax.axis_size("shot")
    rank = lax.axis_index("shot")
    share = F // peers
    meta = jnp.concatenate(
        [jnp.reshape(rank * shots, (1,)), rank ^ jnp.arange(peers, dtype=jnp.int32)]
    ).astype(jnp.int32)
    forward, inverse = (jnp.asarray(table) for table in time_tables(samples, peers))
    table = jnp.asarray(shot_table(delays.shape[0]))
    levels = jnp.tile(lax.dynamic_slice_in_dim(thresholds, rank * share, share), 2)[None, :]
    chunks = chunks_of(receivers)
    sides = edges(estimate, observed)
    last, updated, energy = levels, None, 0.0
    lag = 2
    ahead, behind = {}, {}
    for turn in range(len(chunks) + 2 * lag):
        if turn < len(chunks):
            rows, index = chunks[turn]
            spectra, power = spectra_of(
                meta,
                delays,
                (estimate, observed, *sides),
                forward,
                rows,
                index,
                index,
                peers,
                last,
            )
            last = power
            energy = energy + power
            ahead[turn] = exchanged(spectra)
        place = turn - lag
        if place in ahead:
            shrunk = shrunk_of(meta, ahead.pop(place), table, levels, last)
            last = shrunk[0]
            behind[place] = exchanged(shrunk)
        place = turn - 2 * lag
        if place in behind:
            updated, last = updated_of(
                meta, behind.pop(place), inverse, chunks[place][1], receivers, updated, last
            )
    return updated, energy


def spectral_by_einsum(stepped, forward, inverse, table, level, peers):
    shots, receivers, samples = stepped.shape
    total = table.shape[1]
    share = F // peers
    spectra = jnp.einsum(
        "srt,tdpf->dpfsr",
        stepped,
        forward.reshape(samples, peers, 2, share),
        preferred_element_type=jnp.float32,
    ).astype(jnp.bfloat16)
    mixed = swapped(spectra).transpose(1, 2, 0, 3, 4).reshape(2, share, total, receivers)
    cosine, sine = table[:total], table[total:]
    across = jnp.stack([jnp.stack([cosine, sine]), jnp.stack([-sine, cosine])])
    wave = jnp.einsum("pqks,qfsr->pfkr", across, mixed, preferred_element_type=jnp.float32)
    magnitude = jnp.sqrt(wave[0] * wave[0] + wave[1] * wave[1])
    bound = level[:, None, None]
    factor = jnp.maximum(magnitude - bound, 0.0) / jnp.maximum(magnitude, bound)
    shrunk = (wave * factor[None]).astype(jnp.bfloat16)
    back = jnp.stack([jnp.stack([cosine, -sine]), jnp.stack([sine, cosine])])
    restored = jnp.einsum(
        "pqks,qfkr->pfsr", back, shrunk, preferred_element_type=jnp.float32
    ).astype(jnp.bfloat16)
    restored = restored.reshape(2, share, peers, shots, receivers).transpose(2, 0, 1, 3, 4)
    return jnp.einsum(
        "dpft,dpfsr->srt",
        inverse.reshape(peers, 2, share, samples),
        swapped(restored),
        preferred_element_type=jnp.float32,
    )


def by_einsum(estimate, observed, delays, thresholds):
    shots, receivers, samples = estimate.shape
    peers = lax.axis_size("shot")
    rank = lax.axis_index("shot")
    share = F // peers
    rows = min(16, receivers)
    meta = jnp.reshape(rank * shots, (1,)).astype(jnp.int32)
    sides = edges(estimate, observed)
    energy = 0.0
    parts = []
    for index in range(receivers // rows):
        part, power = stepped_of(meta, delays, (estimate, observed, *sides), rows, index)
        energy = energy + power
        parts.append(part)
    forward, inverse = (jnp.asarray(table) for table in time_tables(samples, peers))
    table = jnp.asarray(shot_table(delays.shape[0]))
    level = lax.dynamic_slice_in_dim(thresholds, rank * share, share)
    stepped = jnp.concatenate(parts, axis=1)
    return spectral_by_einsum(stepped, forward, inverse, table, level, peers), energy


def local(estimate, observed, random_source_delays, thresholds):
    receivers, samples = estimate.shape[1:]
    peers = lax.axis_size("shot")
    filled = peers >= 4 and peers & (peers - 1) == 0 and (2 * F // peers) % LANES == 0
    path = direct if filled else by_einsum
    updated, energy = path(estimate, observed, random_source_delays, thresholds)
    misfit = lax.psum(jnp.sum(energy, axis=1), "patch") / (
        receivers * lax.axis_size("patch") * samples
    )
    return updated, misfit


def solution(mesh):
    in_specs = (P("shot", "patch", None), P("shot", "patch", None), P(), P())
    out_specs = (P("shot", "patch", None), P("shot"))
    return jax.shard_map(local, mesh=mesh, in_specs=in_specs, out_specs=out_specs, check_vma=False)
```
